32 devices in a mesh: dp: 4 (over x, core), fsdp: 8 (over z, y).
Axes of the slice: x: 2, y: 2, z: 4, core: 2. Of those that a mesh axis runs over, the one named last changes fastest.
Arguments:
- inputs: bfloat16 [8192, 1024], P(('dp', 'fsdp')), may hold values from -6 to 6
- segment_ids: int32 [8192], P(('dp', 'fsdp')), may hold values from 0 to 511, as said below
- token_mask: int32 [8192], P(('dp', 'fsdp')), may hold values 0 or 1
- cotangent: bfloat16 [8192, 1024], P(('dp', 'fsdp')), may hold values from -6 to 6
- normgain: bfloat16 [2, 1024], P(None, ('dp', 'fsdp')), may hold values from 0.5 to 1.5
- normbias: bfloat16 [2, 1024], P(None, ('dp', 'fsdp')), may hold values from -1.25 to 1.25
- valueproj: bfloat16 [2, 1024, 3072], P(None, ('dp', 'fsdp')), may hold values from -0.1875 to 0.1875
- valuebias: bfloat16 [2, 3072], P(None, ('dp', 'fsdp')), may hold values from -1.25 to 1.25
- reduceproj: bfloat16 [2, 1024, 512], P(None, ('dp', 'fsdp')), may hold values from -0.1875 to 0.1875
- reducebias: bfloat16 [2, 512], P(None, ('dp', 'fsdp')), may hold values from -1.25 to 1.25
- decays: bfloat16 [2, 512], P(None, ('dp', 'fsdp')), may hold values from 0.0039978027 to 0.3984375
- stateinput: bfloat16 [2, 512, 512], P(None, ('dp', 'fsdp')), may hold values from -0.375 to 0.375
- stateoutput: bfloat16 [2, 512, 512], P(None, ('dp', 'fsdp')), may hold values from -0.375 to 0.375
- skipgain: bfloat16 [2, 512], P(None, ('dp', 'fsdp')), may hold values from -3 to 3
- expandproj: bfloat16 [2, 512, 3072], P(None, ('dp', 'fsdp')), may hold values from -0.25 to 0.25
- expandbias: bfloat16 [2, 3072], P(None, ('dp', 'fsdp')), may hold values from -1.25 to 1.25
- outproj: bfloat16 [2, 3072, 1024], P(None, ('dp', 'fsdp')), may hold values from -0.21875 to 0.21875
- outbias: bfloat16 [2, 1024], P(None, ('dp', 'fsdp')), may hold values from -1.25 to 1.25
Outputs:
- outputs: bfloat16 [8192, 1024], P(('dp', 'fsdp'))
- input_grad: float32 [8192, 1024], P(('dp', 'fsdp'))
- normgain_grad: float32 [2, 1024], P(None, ('dp', 'fsdp'))
- normbias_grad: float32 [2, 1024], P(None, ('dp', 'fsdp'))
- valueproj_grad: float32 [2, 1024, 3072], P(None, ('dp', 'fsdp'))
- valuebias_grad: float32 [2, 3072], P(None, ('dp', 'fsdp'))
- reduceproj_grad: float32 [2, 1024, 512], P(None, ('dp', 'fsdp'))
- reducebias_grad: float32 [2, 512], P(None, ('dp', 'fsdp'))
- decays_grad: float32 [2, 512], P(None, ('dp', 'fsdp'))
- stateinput_grad: float32 [2, 512, 512], P(None, ('dp', 'fsdp'))
- stateoutput_grad: float32 [2, 512, 512], P(None, ('dp', 'fsdp'))
- skipgain_grad: float32 [2, 512], P(None, ('dp', 'fsdp'))
- expandproj_grad: float32 [2, 512, 3072], P(None, ('dp', 'fsdp'))
- expandbias_grad: float32 [2, 3072], P(None, ('dp', 'fsdp'))
- outproj_grad: float32 [2, 3072, 1024], P(None, ('dp', 'fsdp'))
- outbias_grad: float32 [2, 1024], P(None, ('dp', 'fsdp'))
The draws below stay inside these ranges and needn't reach their ends.
Inputs may be any that keep to these rules, and one draw needn't show every extreme that they name: `segment_ids`: sequences lie whole inside aligned blocks of 256 rows: the ids never fall inside a block, blocks share no id, and each sequence has 8 rows or more.
All inputs are finite; a program needn't handle non-finite values. No bound on the sum of `token_mask` on one device may be relied on, other than what follows from the above.
Results may differ from the reference program's by a relative error of at most 0.019.
Values may be sent and summed in bfloat16 or wider, within the bound.
A program may use at most 320 MiB of HBM per device.

```python
import math
import jax
import jax.numpy as jnp
from jax import lax

D = 1024
H = 3072
F = 512
N = 512
LAYERS = 2
TOK_DEV = 256
TOKENS = 8192


def draw_segment_ids(key, part):
    blocks = TOKENS // TOK_DEV
    slot = max(TOK_DEV // 16, 4)
    slots = TOK_DEV // slot
    level_key, cut_key, jitter_key = jax.random.split(key, 3)
    levels = jax.random.randint(level_key, (blocks, 1), 0, 5)
    rolls = jax.random.randint(cut_key, (blocks, slots), 0, 16)
    limits = jnp.right_shift(jnp.full((blocks, 1), 16, jnp.int32), levels)
    first = jnp.arange(slots, dtype=jnp.int32)[None, :] >= 1
    cuts = jnp.logical_and(rolls < limits, first).astype(jnp.int32)
    jitter = jax.random.randint(jitter_key, (blocks, slots), 0, slot // 2 + 1)
    places = jnp.arange(slots, dtype=jnp.int32)[None, :] * slot + jitter
    positions = jnp.arange(TOK_DEV, dtype=jnp.int32)
    passed = (places[:, :, None] <= positions[None, None, :]).astype(jnp.int32)
    counts = jnp.sum(passed * cuts[:, :, None], axis=1)
    finals = jnp.sum(cuts, axis=1, keepdims=True)
    is_last = (jnp.arange(blocks, dtype=jnp.int32)[:, None] == blocks - 1).astype(jnp.int32)
    lift = (slots - 1 - finals) * is_last
    base = jnp.arange(blocks, dtype=jnp.int32)[:, None] * slots
    return (base + counts + lift).reshape(TOKENS).astype(jnp.int32)


def plant(values, key, least, high):
    dims = values.shape
    place = [jax.random.randint(jax.random.fold_in(key, axis), (), 0, dims[axis]) for axis in range(len(dims))]
    values = values.at[tuple(place)].set(least)
    longest = dims.index(max(dims))
    place[longest] = (place[longest] + 1) % dims[longest]
    return values.at[tuple(place)].set(high)


def spiked(drawn, stream_key, source, target, parts, factor):
    owner, partner = [(jnp.arange(drawn.shape[axis_at]) // (drawn.shape[axis_at] // parts)).reshape([-1 if axis == axis_at else 1 for axis in range(drawn.ndim)]) for axis_at in (source, target)]
    chosen = jax.random.permutation(stream_key, parts)[partner]
    strong = (owner == chosen) | (owner == (partner + parts // 2) % parts)
    return jnp.where(strong, factor * drawn, drawn)


def steps_of(key, shape, shards, low, high):
    level = 1.0
    for axis_at, parts in shards:
        draws = jax.random.uniform(jax.random.fold_in(jax.random.fold_in(key, 6), axis_at), (parts,), jnp.float32, low / len(shards), high / len(shards))
        level = level * jnp.repeat(jnp.exp(draws), shape[axis_at] // parts).reshape((-1,) + (1,) * (len(shape) - 1 - axis_at))
    return level


def normal_values(key, extent, scale, most, cuts=(), kind=jnp.bfloat16):
    values = scale * jax.random.normal(key, extent, jnp.float32)
    if cuts:
        values = values * steps_of(key, extent, cuts, -0.22, 0.18)
    return jnp.clip(values, -most, most).astype(kind)


def bell_draw_with(stream_key, extent, scale, reach, shards, heavy, kind=jnp.bfloat16):
    drawn = scale * jax.random.normal(stream_key, extent, jnp.float32)
    if shards:
        drawn = drawn * steps_of(stream_key, extent, shards, -0.22, 0.18)
    return jnp.clip(spiked(drawn, jax.random.fold_in(stream_key, 3), *heavy), -reach, reach).astype(kind)


def setup_inputs(seed: int = 0) -> dict:
    keys = jax.random.split(jax.random.key(seed), 19)
    return {
        "inputs": normal_values(keys[0], (TOKENS, D), 1.0, 6.0, ((0, 32),)),
        "segment_ids": draw_segment_ids(jax.random.fold_in(keys[18], 71), 0),
        "token_mask": plant((jax.random.randint(keys[2], (TOKENS,), 0, 8) < 7).astype(jnp.int32), jax.random.fold_in(keys[2], 1), 0, 1),
        "cotangent": bell_draw_with(keys[3], (TOKENS, D), 1.0, 6.0, ((0, 32),), (0, 1, 32, 2.75)),
        "normgain": jnp.clip(1.0 + 0.1 * jax.random.normal(keys[4], (LAYERS, D), jnp.float32), 0.5, 1.5).astype(jnp.bfloat16),
        "normbias": normal_values(keys[5], (LAYERS, D), 0.2, 1.25, ((1, 32),)),
        "valueproj": normal_values(keys[6], (LAYERS, D, H), D ** -0.5, 0.1875, ((1, 32),)),
        "valuebias": normal_values(keys[7], (LAYERS, H), 0.2, 1.25, ((1, 32),)),
        "reduceproj": normal_values(keys[8], (LAYERS, D, F), D ** -0.5, 0.1875, ((1, 32),)),
        "reducebias": normal_values(keys[9], (LAYERS, F), 0.2, 1.25, ((1, 32),)),
        "decays": jnp.clip(jnp.exp(math.log(0.3984375) - 4.6018058 * jax.random.uniform(keys[10], (LAYERS, N), jnp.float32) ** steps_of(keys[10], (LAYERS, N), ((1, 32),), -0.2, 0.2)), 0.0039978027, 0.3984375).astype(jnp.bfloat16),
        "stateinput": normal_values(keys[11], (LAYERS, N, F), 0.06, 0.375, ((1, 32),)),
        "stateoutput": normal_values(keys[12], (LAYERS, N, F), 0.06, 0.375, ((1, 32),)),
        "skipgain": normal_values(keys[13], (LAYERS, F), 0.5, 3.0, ((1, 32),)),
        "expandproj": normal_values(keys[14], (LAYERS, F, H), F ** -0.5, 0.25, ((1, 32),)),
        "expandbias": normal_values(keys[15], (LAYERS, H), 0.2, 1.25, ((1, 32),)),
        "outproj": normal_values(keys[16], (LAYERS, H, D), (H // 4) ** -0.5, 0.21875, ((1, 32),)),
        "outbias": normal_values(keys[17], (LAYERS, D), 0.2, 1.25, ((1, 32),)),
    }


@jax.custom_vjp
def low(v):
    return lax.optimization_barrier(v.astype(jnp.bfloat16)).astype(jnp.float32)

@jax.custom_vjp
def low_back(v):
    return v

def low_keep(v):
    return (low(v), None)

def low_pass(kept, grad):
    return (grad,)

def back_keep(v):
    return (v, None)

def back_low(kept, grad):
    return (low(grad),)
low.defvjp(low_keep, low_pass)
low_back.defvjp(back_keep, back_low)
highest = lax.Precision.HIGHEST

def mixer(labels, signal, decays, stateinput, stateoutput, skipgain):
    rows = signal.shape[0]
    width = min(32, rows)
    count = rows // width
    mixing = stateinput * stateoutput
    offsets = jnp.arange(width, dtype=jnp.float32)
    powers = jnp.exp(-offsets[:, None] * decays[None, :])
    kernel = jnp.dot(powers, mixing, precision=highest)
    positions = jnp.arange(width, dtype=jnp.int32)
    lagged = jnp.maximum(positions[:, None] - positions[None, :], 0)
    toeplitz = jnp.take(kernel, lagged, axis=0)
    causal = positions[:, None] >= positions[None, :]
    leading = jnp.exp(-(offsets[:, None] + 1.0) * decays[None, :])
    trailing = jnp.exp(-(width - 1.0 - offsets[:, None]) * decays[None, :])
    across = jnp.exp(-width * decays)

    def advance(carry, pieces):
        state, before = carry
        block, marks = pieces
        same = jnp.logical_and(marks[:, None] == marks[None, :], causal).astype(signal.dtype)
        inner = lax.optimization_barrier(jnp.sum(toeplitz * same[:, :, None] * block[None, :, :], axis=1))
        joined = (marks == before).astype(signal.dtype)
        carried = jnp.dot(leading, mixing * state, precision=highest) * joined[:, None]
        final = marks[width - 1]
        keep = (final == before).astype(signal.dtype)
        fresh = (marks == final).astype(signal.dtype)
        state = across[:, None] * state * keep + lax.dot_general(trailing * fresh[:, None], block, (((0,), (0,)), ((), ())), precision=highest)
        return ((state, final), inner + carried)
    start = (jnp.zeros(mixing.shape, signal.dtype), jnp.array(-1, jnp.int32))
    ending, mixed = lax.scan(jax.checkpoint(advance), start, (signal.reshape(count, width, -1), labels.reshape(count, width)))
    return mixed.reshape(rows, -1) + skipgain[None, :] * signal

def normalize(rows, gain, shift):
    center = rows - lax.optimization_barrier(jnp.mean(rows, axis=1, keepdims=True))
    spread = lax.optimization_barrier(jnp.mean(center * center, axis=1, keepdims=True))
    return center * lax.rsqrt(spread + 1e-05) * gain + shift

def smooth(values):
    return jax.nn.gelu(values, approximate=False)

def one_layer(rows, labels, flags, weights):
    normgain, normbias, valueproj, valuebias, reduceproj, reducebias, decays, stateinput, stateoutput, skipgain, expandproj, expandbias, outproj, outbias = weights
    normed = low(normalize(rows, normgain, normbias))
    opened = low_back(jnp.dot(normed, valueproj, precision=highest) + valuebias)
    values = smooth(opened)
    reduced = low_back(jnp.dot(normed, reduceproj, precision=highest) + reducebias)
    signal = smooth(reduced) * flags
    mixed = low(mixer(labels, signal, decays, stateinput, stateoutput, skipgain))
    expanded = low_back(jnp.dot(mixed, expandproj, precision=highest) + expandbias)
    gated = low(expanded * values)
    branch = low_back(jnp.dot(gated, outproj, precision=highest) + outbias)
    return rows + flags * branch

def two_layers(rows, labels, flags, params):
    current = rows
    for depth in range(LAYERS):
        current = one_layer(current, labels, flags, tuple((piece[depth] for piece in params)))
    return current

def reference(inputs, segment_ids, token_mask, cotangent, normgain, normbias, valueproj, valuebias, reduceproj, reducebias, decays, stateinput, stateoutput, skipgain, expandproj, expandbias, outproj, outbias):
    params = tuple((piece.astype(jnp.float32) for piece in (normgain, normbias, valueproj, valuebias, reduceproj, reducebias, decays, stateinput, stateoutput, skipgain, expandproj, expandbias, outproj, outbias)))
    blocks = TOKENS // TOK_DEV
    labels_all = segment_ids.reshape(blocks, TOK_DEV)
    flags_all = token_mask.astype(jnp.float32).reshape(blocks, TOK_DEV, 1)

    def forward(flat, weights):

        def per_block(pieces):
            rows, labels, flags = pieces
            return jax.checkpoint(two_layers)(rows, labels, flags, weights)
        stacked = lax.map(per_block, (flat.reshape(blocks, TOK_DEV, D), labels_all, flags_all))
        return stacked.reshape(TOKENS, D)
    result, pullback = jax.vjp(forward, inputs.astype(jnp.float32), params)
    input_grad, grads = pullback(cotangent.astype(jnp.float32))
    return (result.astype(jnp.bfloat16), input_grad, grads[0], grads[1], grads[2], grads[3], grads[4], grads[5], grads[6], grads[7], grads[8], grads[9], grads[10], grads[11], grads[12], grads[13])
```

```python
from functools import partial

import jax
import jax.numpy as jnp
from jax import lax
from jax.experimental import pallas as pl
from jax.experimental.pallas import tpu as pltpu
from jax.sharding import PartitionSpec as P

LAYERS = 2
AXES = ("dp", "fsdp")
GROUP = 4
RINGS = 8
LANES = 128
STRIP = 32
PAD = 32

f32 = jnp.float32
bf16 = jnp.bfloat16
highest = lax.Precision.HIGHEST
rows_dims = (((0,), (0,)), ((), ()))
cols_dims = (((1,), (1,)), ((), ()))

VMEM = pltpu.VMEM


def swap(block, flip):
    size = GROUP * RINGS
    return lax.ppermute(block, AXES, [(i, i ^ flip) for i in range(size)])


def cost(micros):
    return pl.CostEstimate(
        flops=int(micros * 1.0e9), bytes_accessed=1 << 20, transcendentals=0
    )


def params():
    return pltpu.CompilerParams(vmem_limit_bytes=48 << 20)


def whole(shape):
    return pl.BlockSpec(shape, lambda *_: (0,) * len(shape))


def scalars():
    return pl.BlockSpec(memory_space=pltpu.SMEM)


def nt(a, b):
    return lax.dot_general(a, b, cols_dims, preferred_element_type=f32)


def tn(a, b):
    return lax.dot_general(a, b, rows_dims, preferred_element_type=f32)


def nn(a, b):
    return jnp.dot(a, b, preferred_element_type=f32)


def open_value(me, powers, parts):
    rows, width = parts[0].shape
    states = powers.shape[1]
    small = states // (GROUP * RINGS)
    tall = (rows - small) // GROUP
    depth = tall * GROUP * RINGS

    def kernel(me_ref, e_ref, *refs):
        packs, (w_ref, mix_ref, k_ref) = refs[:RINGS], refs[RINGS:]
        dp, fs = me_ref[0], me_ref[1]
        for j in range(RINGS):
            for k in range(GROUP):
                index = (dp ^ k) * RINGS + (fs ^ j)
                w_ref[pl.ds(pl.multiple_of(index * tall, tall), tall), :] = packs[j][
                    k * tall : (k + 1) * tall, :
                ]
                mix_ref[pl.ds(pl.multiple_of(index * small, small), small), :] = packs[j][
                    GROUP * tall :, k * LANES : (k + 1) * LANES
                ]
        k_ref[...] = nn(e_ref[...], mix_ref[...])

    return pl.pallas_call(
        kernel,
        out_shape=(
            jax.ShapeDtypeStruct((depth, width), bf16),
            jax.ShapeDtypeStruct((states, LANES), bf16),
            jax.ShapeDtypeStruct((powers.shape[0], LANES), f32),
        ),
        in_specs=[scalars()] + [pl.BlockSpec(memory_space=VMEM)] * (1 + RINGS),
        out_specs=(pl.BlockSpec(memory_space=VMEM),) * 3,
        compiler_params=params(),
        cost_estimate=cost(2.5),
        name="open_value",
    )(me, powers, *parts)


def open_out(me, parts, tall, small, units):
    width = parts[0].shape[1]
    thirds = units // 256
    across = width // 256

    def kernel(me_ref, *refs):
        packs, (o_ref, e_ref) = refs[:RINGS], refs[RINGS:]
        dp, fs = me_ref[0], me_ref[1]
        for j in range(RINGS):
            o_ref[pl.ds(pl.multiple_of((fs ^ j) * tall, tall), tall), :] = packs[j][:tall, :]
            for k in range(GROUP):
                index = (dp ^ k) * RINGS + (fs ^ j)
                for t in range(thirds):
                    r, c = divmod(k * thirds + t, across)
                    e_ref[
                        pl.ds(pl.multiple_of(index * small, small), small),
                        t * 256 : (t + 1) * 256,
                    ] = packs[j][
                        tall + small * r : tall + small * (r + 1), c * 256 : (c + 1) * 256
                    ]

    return pl.pallas_call(
        kernel,
        out_shape=(
            jax.ShapeDtypeStruct((tall * RINGS, width), bf16),
            jax.ShapeDtypeStruct((small * GROUP * RINGS, units), bf16),
        ),
        in_specs=[scalars()] + [pl.BlockSpec(memory_space=VMEM)] * RINGS,
        out_specs=(pl.BlockSpec(memory_space=VMEM),) * 2,
        compiler_params=params(),
        cost_estimate=cost(2.5),
        name="open_out",
    )(me, *parts)


def forward_in(na, nb, weight, bias, filt, skip, auxa, auxb):
    tokens, depth = na.shape
    width = weight.shape[1]
    units = width - LANES
    strips = tokens // STRIP

    def kernel(
        na_ref, nb_ref, w_ref, b_ref, k_ref, s_ref, xa_ref, xb_ref,
        value_ref, gp_ref, z_ref, g2_ref, y_ref,
        n_scr, a_scr, aux_scr, age_scr, shifted, y_scr,
    ):
        step = pl.program_id(0)

        @pl.when(step == 0)
        def _():
            n_scr[...] = na_ref[...]
            aux_scr[...] = xa_ref[...].astype(f32)

        @pl.when(step == 1)
        def _():
            n_scr[...] = nb_ref[...]
            aux_scr[...] = xb_ref[...].astype(f32)

        a_scr[...] = nn(n_scr[...], w_ref[...])
        age_scr[...] = jnp.broadcast_to(aux_scr[:, 0:1], (tokens, LANES))

        def smooth(i, carry):
            at = pl.ds(pl.multiple_of(i * STRIP, STRIP), STRIP)
            v = a_scr[at, :] + b_ref[...]
            cdf = 0.5 + 0.5 * lax.erf(v * 0.7071067811865476)
            slope = cdf + v * (0.3989422804014327 * jnp.exp(-0.5 * v * v))
            act = v * cdf
            value_ref[at, :] = act[:, :units].astype(bf16)
            gp_ref[at, :] = slope[:, :units].astype(bf16)
            mask = jnp.broadcast_to(aux_scr[at, 2:3], (STRIP, LANES))
            z_ref[at, :] = act[:, units:] * mask
            g2_ref[at, :] = slope[:, units:] * mask
            return carry

        lax.fori_loop(0, strips, smooth, 0)
        z = z_ref[...]
        for b in range(8):
            shifted[b, :PAD, :] = jnp.zeros((PAD, LANES), f32)
            shifted[b, PAD:, :] = z if b == 0 else pltpu.roll(z, b, 0)
        for s in range(strips):
            age = age_scr[s * STRIP : (s + 1) * STRIP, :]

            def lags(a, acc, s=s, age=age):
                base = pl.multiple_of(a * 8, 8)
                left = age - (a * 8).astype(f32)
                for b in range(8):
                    row = k_ref[pl.ds(base + b, 1), :]
                    past = shifted[b, pl.ds(pl.multiple_of(PAD + s * STRIP - base, 8), STRIP), :]
                    acc = acc + jnp.where(left >= b, past, 0.0) * row
                return acc

            y_scr[s * STRIP : (s + 1) * STRIP, :] = lax.fori_loop(
                0, (s + 1) * (STRIP // 8), lags, jnp.zeros((STRIP, LANES), f32)
            )
        y_ref[...] = (y_scr[...] + s_ref[...] * z).astype(bf16)

    half = lambda cols: pl.BlockSpec((tokens, cols), lambda i: (i, 0))
    return pl.pallas_call(
        kernel,
        grid=(2,),
        out_shape=(
            jax.ShapeDtypeStruct((2 * tokens, units), bf16),
            jax.ShapeDtypeStruct((2 * tokens, units), bf16),
            jax.ShapeDtypeStruct((2 * tokens, LANES), f32),
            jax.ShapeDtypeStruct((2 * tokens, LANES), f32),
            jax.ShapeDtypeStruct((2 * tokens, LANES), bf16),
        ),
        in_specs=[
            whole((tokens, depth)), whole((tokens, depth)), whole((depth, width)),
            whole((1, width)), whole(filt.shape), whole((1, LANES)),
            whole((tokens, LANES)), whole((tokens, LANES)),
        ],
        out_specs=(half(units), half(units), half(LANES), half(LANES), half(LANES)),
        scratch_shapes=[
            VMEM((tokens, depth), bf16),
            VMEM((tokens, width), f32),
            VMEM((tokens, LANES), f32),
            VMEM((tokens, LANES), f32),
            VMEM((8, PAD + tokens, LANES), f32),
            VMEM((tokens, LANES), f32),
        ],
        compiler_params=params(),
        cost_estimate=cost(9.0),
        name="forward_in",
    )(na, nb, weight, bias, filt, skip, auxa, auxb)


def forward_out(me, ys, expand, bias, value, outw):
    tokens = ys[0].shape[0] // 2
    feats, units = expand.shape
    depth = outw.shape[1]

    def kernel(
        me_ref, y0, y1, y2, y3, e_ref, b_ref, value_ref, o_ref,
        c_ref, gated_ref, full_ref, first_ref, second_ref,
    ):
        dp = me_ref[0]
        for k, part in enumerate((y0, y1, y2, y3)):
            full_ref[:, pl.ds(pl.multiple_of((dp ^ k) * LANES, LANES), LANES)] = part[...]
        c = nn(full_ref[...], e_ref[...]) + b_ref[...]
        gated = (c * value_ref[...].astype(f32)).astype(bf16)
        c_ref[...] = c.astype(bf16)
        gated_ref[...] = gated
        out = nn(gated, o_ref[...]).astype(bf16)

        @pl.when(pl.program_id(0) == 0)
        def _():
            first_ref[...] = out

        @pl.when(pl.program_id(0) == 1)
        def _():
            second_ref[...] = out

    same = lambda cols: pl.BlockSpec((tokens, cols), lambda i: (i, 0))
    other = lambda cols: pl.BlockSpec((tokens, cols), lambda i: (1 - i, 0))
    return pl.pallas_call(
        kernel,
        grid=(2,),
        out_shape=(
            jax.ShapeDtypeStruct((2 * tokens, units), bf16),
            jax.ShapeDtypeStruct((2 * tokens, units), bf16),
            jax.ShapeDtypeStruct((2 * tokens, feats), bf16),
            jax.ShapeDtypeStruct((tokens, depth), bf16),
            jax.ShapeDtypeStruct((tokens, depth), bf16),
        ),
        in_specs=[
            scalars(), same(LANES), other(LANES), same(LANES), other(LANES),
            whole((feats, units)), whole((1, units)), same(units), whole((units, depth)),
        ],
        out_specs=(same(units), same(units), same(feats), whole((tokens, depth)), whole((tokens, depth))),
        compiler_params=params(),
        cost_estimate=cost(3.5),
        name="forward_out",
    )(me, *ys, expand, bias, value, outw)


def backward_out(me, da, db, outw, expand, value, slope, gate):
    tokens, depth = da.shape
    feats, units = expand.shape

    def kernel(
        me_ref, da_ref, db_ref, o_ref, e_ref, value_ref, gp_ref, c_ref,
        dc_ref, da1_ref, even_ref, odd_ref, sum_ref, d_scr, y_scr,
    ):
        dp = me_ref[0]
        step = pl.program_id(0)

        @pl.when(step == 0)
        def _():
            d_scr[...] = da_ref[...]
            sum_ref[...] = jnp.zeros_like(sum_ref)

        @pl.when(step == 1)
        def _():
            d_scr[...] = db_ref[...]

        dgated = nt(d_scr[...], o_ref[...])
        dc = (dgated * value_ref[...].astype(f32)).astype(bf16)
        dc_ref[...] = dc
        da1_ref[...] = (dgated * c_ref[...].astype(f32) * gp_ref[...].astype(f32)).astype(bf16)
        sum_ref[...] += jnp.sum(dc.astype(f32), axis=0, keepdims=True)
        y_scr[...] = nt(dc, e_ref[...])
        for k, (ref, slot) in enumerate(((even_ref, 0), (odd_ref, 0), (even_ref, 1), (odd_ref, 1))):
            ref[slot] = y_scr[:, pl.ds(pl.multiple_of((dp ^ k) * LANES, LANES), LANES)].astype(bf16)

    same = lambda cols: pl.BlockSpec((tokens, cols), lambda i: (i, 0))
    return pl.pallas_call(
        kernel,
        grid=(2,),
        out_shape=(
            jax.ShapeDtypeStruct((2 * tokens, units), bf16),
            jax.ShapeDtypeStruct((2 * tokens, units), bf16),
            jax.ShapeDtypeStruct((2, 2 * tokens, LANES), bf16),
            jax.ShapeDtypeStruct((2, 2 * tokens, LANES), bf16),
            jax.ShapeDtypeStruct((1, units), f32),
        ),
        in_specs=[
            scalars(), whole((tokens, depth)), whole((tokens, depth)), whole((units, depth)),
            whole((feats, units)), same(units), same(units), same(units),
        ],
        out_specs=(
            same(units), same(units),
            pl.BlockSpec((2, tokens, LANES), lambda i: (0, i, 0)),
            pl.BlockSpec((2, tokens, LANES), lambda i: (0, 1 - i, 0)),
            whole((1, units)),
        ),
        scratch_shapes=[VMEM((tokens, depth), bf16), VMEM((tokens, feats), f32)],
        compiler_params=params(),
        cost_estimate=cost(3.5),
        name="backward_out",
    )(me, da, db, outw, expand, value, slope, gate)


def backward_in(own, near, far, z, slope2, da1, filt, skip, auxa, auxb, weight):
    tokens = auxa.shape[0]
    depth, width = weight.shape
    units = width - LANES
    strips = tokens // STRIP

    def kernel(
        own_ref, near_ref, far_ref, z_ref, g2_ref, da1_ref, k_ref, s_ref, xa_ref, xb_ref, w_ref,
        da_ref, first_ref, second_ref, corr_ref, sum_ref, skip_ref,
        aux_scr, rem_scr, shifted, dz_scr,
    ):
        step = pl.program_id(0)

        @pl.when(step == 0)
        def _():
            aux_scr[...] = xa_ref[...].astype(f32)
            corr_ref[...] = jnp.zeros_like(corr_ref)
            sum_ref[...] = jnp.zeros_like(sum_ref)
            skip_ref[...] = jnp.zeros_like(skip_ref)

        @pl.when(step == 1)
        def _():
            aux_scr[...] = xb_ref[...].astype(f32)

        rem_scr[...] = jnp.broadcast_to(aux_scr[:, 1:2], (tokens, LANES))
        dy = own_ref[0].astype(f32) + near_ref[0].astype(f32) + far_ref[...].astype(f32)
        for b in range(8):
            shifted[b, tokens:, :] = jnp.zeros((PAD, LANES), f32)
            shifted[b, :tokens, :] = dy if b == 0 else pltpu.roll(dy, tokens - b, 0)
        for s in range(strips):
            rem = rem_scr[s * STRIP : (s + 1) * STRIP, :]
            z = z_ref[s * STRIP : (s + 1) * STRIP, :]

            def lags(a, acc, s=s, rem=rem, z=z):
                base = pl.multiple_of(a * 8, 8)
                left = rem - (a * 8).astype(f32)
                for b in range(8):
                    row = k_ref[pl.ds(base + b, 1), :]
                    later = shifted[b, pl.ds(pl.multiple_of(s * STRIP + base, 8), STRIP), :]
                    later = jnp.where(left >= b, later, 0.0)
                    acc = acc + later * row
                    pair = later * z
                    corr_ref[base + b] += (pair[0:8] + pair[8:16]) + (pair[16:24] + pair[24:32])
                return acc

            dz_scr[s * STRIP : (s + 1) * STRIP, :] = lax.fori_loop(
                0, (strips - s) * (STRIP // 8), lags, jnp.zeros((STRIP, LANES), f32)
            )
        z = z_ref[...]
        da2 = ((dz_scr[...] + s_ref[...] * dy) * g2_ref[...]).astype(bf16)
        da_ref[:, :units] = da1_ref[...]
        da_ref[:, units:] = da2
        skip_ref[...] += jnp.sum(z * dy, axis=0, keepdims=True)
        sum_ref[...] += jnp.sum(da_ref[...].astype(f32), axis=0, keepdims=True)
        out = nt(da_ref[...], w_ref[...]).astype(bf16)

        @pl.when(step == 0)
        def _():
            first_ref[...] = out

        @pl.when(step == 1)
        def _():
            second_ref[...] = out

    same = lambda cols: pl.BlockSpec((tokens, cols), lambda i: (i, 0))
    return pl.pallas_call(
        kernel,
        grid=(2,),
        out_shape=(
            jax.ShapeDtypeStruct((2 * tokens, width), bf16),
            jax.ShapeDtypeStruct((tokens, depth), bf16),
            jax.ShapeDtypeStruct((tokens, depth), bf16),
            jax.ShapeDtypeStruct((tokens, 8, LANES), f32),
            jax.ShapeDtypeStruct((1, width), f32),
            jax.ShapeDtypeStruct((1, LANES), f32),
        ),
        in_specs=[
            pl.BlockSpec((1, tokens, LANES), lambda i: (0, i, 0)),
            pl.BlockSpec((1, tokens, LANES), lambda i: (0, i, 0)),
            same(LANES), same(LANES), same(LANES), same(units),
            whole(filt.shape), whole((1, LANES)), whole((tokens, LANES)), whole((tokens, LANES)),
            whole((depth, width)),
        ],
        out_specs=(
            same(width), whole((tokens, depth)), whole((tokens, depth)),
            whole((tokens, 8, LANES)), whole((1, width)), whole((1, LANES)),
        ),
        scratch_shapes=[
            VMEM((tokens, LANES), f32),
            VMEM((tokens, LANES), f32),
            VMEM((8, PAD + tokens, LANES), f32),
            VMEM((tokens, LANES), f32),
        ],
        compiler_params=params(),
        cost_estimate=cost(11.0),
        name="backward_in",
    )(own, near, far, z, slope2, da1, filt, skip, auxa, auxb, weight)


def grads_out(me, gated, douts, full, dc, tall, small):
    tokens, depth = douts[0].shape
    units = dc[0].shape[1]
    feats = full[0].shape[1]
    thirds = units // 256
    across = depth // 256
    rows = tall + small * GROUP * thirds // across

    def kernel(me_ref, g_lo, g_hi, d0, d1, d2, d3, y_lo, y_hi, c_lo, c_hi, *refs):
        outs, (o_scr, e_scr) = refs[:RINGS], refs[RINGS:]
        dp, fs = me_ref[0], me_ref[1]
        step = pl.program_id(0)
        o_scr[pl.ds(pl.multiple_of(step * 256, 256), 256), :] = (
            tn(g_lo[:tokens], d0[...])
            + tn(g_lo[tokens:], d1[...])
            + tn(g_hi[:tokens], d2[...])
            + tn(g_hi[tokens:], d3[...])
        ).astype(bf16)
        e_scr[step] = (tn(y_lo[...], c_lo[...]) + tn(y_hi[...], c_hi[...])).astype(bf16)

        @pl.when(step == thirds - 1)
        def _():
            for j in range(RINGS):
                outs[j][:tall, :] = o_scr[pl.ds(pl.multiple_of((fs ^ j) * tall, tall), tall), :]
                for k in range(GROUP):
                    index = (dp ^ k) * RINGS + (fs ^ j)
                    at = pl.ds(pl.multiple_of(index * small, small), small)
                    for t in range(thirds):
                        r, c = divmod(k * thirds + t, across)
                        outs[j][
                            tall + small * r : tall + small * (r + 1), c * 256 : (c + 1) * 256
                        ] = e_scr[t, at, :]

    column = lambda n: pl.BlockSpec((n, 256), lambda i: (0, i))
    return pl.pallas_call(
        kernel,
        grid=(thirds,),
        out_shape=(jax.ShapeDtypeStruct((rows, depth), bf16),) * RINGS,
        in_specs=[scalars()]
        + [column(2 * tokens)] * 2
        + [whole((tokens, depth))] * 4
        + [whole((2 * tokens, feats))] * 2
        + [column(2 * tokens)] * 2,
        out_specs=(whole((rows, depth)),) * RINGS,
        scratch_shapes=[VMEM((units, depth), bf16), VMEM((thirds, feats, 256), bf16)],
        compiler_params=params(),
        cost_estimate=cost(5.0),
        name="grads_out",
    )(me, *gated, *douts, *full, *dc)


def grads_in(me, norms, das, powers, corr, mixing, tall, small):
    tokens, depth = norms[0].shape
    width = das[0].shape[1]
    states = powers.shape[1]
    rows = tall * GROUP + small
    wide = depth // GROUP

    def kernel(me_ref, n0, n1, n2, n3, a_lo, a_hi, e_ref, corr_ref, mix_ref, *refs):
        outs, (dec_ref, w_scr, m_scr) = refs[:RINGS], refs[RINGS:]
        dp, fs = me_ref[0], me_ref[1]
        step = pl.program_id(0)
        w_scr[...] = (
            tn(n0[...], a_lo[:tokens])
            + tn(n1[...], a_lo[tokens:])
            + tn(n2[...], a_hi[:tokens])
            + tn(n3[...], a_hi[tokens:])
        ).astype(bf16)
        spot = pl.ds(pl.multiple_of((step ^ dp) * tall, tall), tall)
        for j in range(RINGS):
            outs[j][spot, :] = w_scr[pl.ds(pl.multiple_of((fs ^ j) * tall, tall), tall), :]

        @pl.when(step == 0)
        def _():
            corr_f = corr_ref[...]
            m_scr[...] = tn(e_ref[...], corr_f.astype(bf16)).astype(bf16)
            lag = lax.broadcasted_iota(jnp.int32, corr_f.shape, 0).astype(f32)
            dec_ref[...] = -tn(e_ref[...], (corr_f * lag).astype(bf16)) * mix_ref[...].astype(f32)
            for j in range(RINGS):
                outs[j][GROUP * tall :, :] = jnp.zeros((small, width), bf16)
                for k in range(GROUP):
                    index = (dp ^ k) * RINGS + (fs ^ j)
                    outs[j][GROUP * tall :, k * LANES : (k + 1) * LANES] = m_scr[
                        pl.ds(pl.multiple_of(index * small, small), small), :
                    ]

    return pl.pallas_call(
        kernel,
        grid=(GROUP,),
        out_shape=(jax.ShapeDtypeStruct((rows, width), bf16),) * RINGS
        + (jax.ShapeDtypeStruct((states, LANES), f32),),
        in_specs=[scalars()]
        + [pl.BlockSpec((tokens, wide), lambda i: (0, i))] * 4
        + [whole((2 * tokens, width))] * 2
        + [whole(powers.shape), whole(corr.shape), whole(mixing.shape)],
        out_specs=(whole((rows, width)),) * RINGS + (whole((states, LANES)),),
        scratch_shapes=[VMEM((wide, width), bf16), VMEM((states, LANES), bf16)],
        compiler_params=params(),
        cost_estimate=cost(5.0),
        name="grads_in",
    )(me, *norms, *das, powers, corr, mixing)


def finish(me, value_parts, expand_parts, out_parts, stateinput, stateoutput):
    layers, small, states = stateinput.shape
    rows, width = value_parts[0][0].shape
    tall = rows - small
    units = width - LANES
    high, depth = out_parts[0].shape
    feats = LANES * GROUP

    def kernel(me_ref, *refs):
        dp = me_ref[0]
        count = layers * GROUP
        values, expands, outs = refs[:count], refs[count : 2 * count], refs[2 * count : 2 * count + layers]
        si_ref, so_ref, v_ref, r_ref, si_out, so_out, e_ref, o_ref, m_scr = refs[2 * count + layers :]
        for l in range(layers):
            for k in range(GROUP):
                part = values[l * GROUP + k]
                q = dp ^ k
                v_ref[l, :, pl.ds(pl.multiple_of(q * units, LANES), units)] = part[:tall, :units].astype(f32)
                thin = pl.ds(pl.multiple_of(q * LANES, LANES), LANES)
                r_ref[l, :, thin] = part[:tall, units:].astype(f32)
                m_scr[:, thin] = part[tall:, k * LANES : (k + 1) * LANES].astype(f32)
                e_ref[l, :, pl.ds(pl.multiple_of(q * units, LANES), units)] = expands[l * GROUP + k][...].astype(f32)
            si_out[l] = m_scr[...] * so_ref[l].astype(f32)
            so_out[l] = m_scr[...] * si_ref[l].astype(f32)
            o_ref[l] = outs[l][...]

    flat = [p for parts in value_parts for p in parts] + [p for parts in expand_parts for p in parts]
    arrays = flat + list(out_parts) + [stateinput, stateoutput]
    return pl.pallas_call(
        kernel,
        out_shape=(
            jax.ShapeDtypeStruct((layers, tall, units * GROUP), f32),
            jax.ShapeDtypeStruct((layers, tall, feats), f32),
            jax.ShapeDtypeStruct((layers, small, feats), f32),
            jax.ShapeDtypeStruct((layers, small, feats), f32),
            jax.ShapeDtypeStruct((layers, small, units * GROUP), f32),
            jax.ShapeDtypeStruct((layers, high, depth), f32),
        ),
        in_specs=[scalars()] + [pl.BlockSpec(memory_space=VMEM)] * len(arrays),
        out_specs=(pl.BlockSpec(memory_space=VMEM),) * 6,
        scratch_shapes=[VMEM((small, feats), f32)],
        compiler_params=params(),
        cost_estimate=cost(3.0),
        name="finish",
    )(me, *arrays)


def after(block, *others):
    tie = sum(o[(slice(0, 1),) * o.ndim].reshape(1, 1) for o in others)
    return lax.optimization_barrier((block, tie))[0]


def gather_rest(pack):
    along = [pack] + [swap(pack, 2 * k) for k in range(1, RINGS // 2)]
    both = []
    for piece in along:
        both += [piece, swap(piece, 1)]
    return both, along[1:]


def reduce_rest(packs):
    summed = [None] * (RINGS // 2)
    for k in (1, 2, 3, 0):
        summed[k] = packs[2 * k].astype(f32) + swap(packs[2 * k + 1], 1).astype(f32)
    total = summed[0]
    for k in (1, 2, 3):
        total = total + swap(summed[k].astype(bf16), 2 * k).astype(f32)
    return total


def gather_group(block):
    near = swap(block, RINGS)
    far = swap(block, 2 * RINGS)
    return [block, near, far, swap(far, RINGS)]


def return_group(lo, hi):
    ahead = hi[0].astype(f32) + swap(hi[1], RINGS).astype(f32)
    there = swap(ahead.astype(bf16), 2 * RINGS)
    here = lo[0].astype(f32) + swap(lo[1], RINGS).astype(f32)
    return here + there.astype(f32)


def all_rest(block):
    total = block + sum(swap(block, 2 * k) for k in range(1, RINGS // 2))
    return total + swap(total, 1)


def all_group(block):
    return block + sum(swap(block, k * RINGS) for k in range(1, GROUP))


def mixer(labels, signal, decays, stateinput, stateoutput, skipgain):
    rows = signal.shape[0]
    width = min(32, rows)
    count = rows // width
    mixing = stateinput * stateoutput
    offsets = jnp.arange(width, dtype=jnp.float32)
    powers = jnp.exp(-offsets[:, None] * decays[None, :])
    kernel = jnp.dot(powers, mixing, precision=highest)
    positions = jnp.arange(width, dtype=jnp.int32)
    lagged = jnp.maximum(positions[:, None] - positions[None, :], 0)
    toeplitz = jnp.take(kernel, lagged, axis=0)
    causal = positions[:, None] >= positions[None, :]
    leading = jnp.exp(-(offsets[:, None] + 1.0) * decays[None, :])
    trailing = jnp.exp(-(width - 1.0 - offsets[:, None]) * decays[None, :])
    across = jnp.exp(-width * decays)

    def advance(carry, pieces):
        state, before = carry
        block, marks = pieces
        same = jnp.logical_and(marks[:, None] == marks[None, :], causal).astype(signal.dtype)
        inner = jnp.sum(toeplitz * same[:, :, None] * block[None, :, :], axis=1)
        joined = (marks == before).astype(signal.dtype)
        carried = jnp.dot(leading, mixing * state, precision=highest) * joined[:, None]
        final = marks[width - 1]
        keep = (final == before).astype(signal.dtype)
        fresh = (marks == final).astype(signal.dtype)
        state = across[:, None] * state * keep + lax.dot_general(
            trailing * fresh[:, None], block, rows_dims, precision=highest
        )
        return ((state, final), inner + carried)

    start = (jnp.zeros(mixing.shape, signal.dtype), jnp.array(-1, jnp.int32))
    ending, mixed = lax.scan(
        jax.checkpoint(advance),
        start,
        (signal.reshape(count, width, -1), labels.reshape(count, width)),
    )
    return mixed.reshape(rows, -1) + skipgain[None, :] * signal


def normalize(rows, gain, shift):
    center = rows - jnp.mean(rows, axis=1, keepdims=True)
    spread = jnp.mean(center * center, axis=1, keepdims=True)
    return center * lax.rsqrt(spread + 1e-05) * gain + shift


def smooth(values):
    return jax.nn.gelu(values, approximate=False)


def gather_forward(shards, depth):
    return (
        lax.all_gather(shards[0][depth], ("dp", "fsdp"), axis=0, tiled=True),
        lax.all_gather(shards[1][depth], ("dp", "fsdp"), axis=0, tiled=True),
        lax.all_gather(shards[2][depth], ("dp", "fsdp"), axis=0, tiled=True),
        lax.all_gather(shards[3][depth], ("dp", "fsdp"), axis=0, tiled=True),
        lax.all_gather(shards[4][depth], ("dp", "fsdp"), axis=0, tiled=True),
        lax.all_gather(shards[5][depth], ("dp", "fsdp"), axis=0, tiled=True),
        lax.all_gather(shards[6][depth], ("dp", "fsdp"), axis=0, tiled=True),
        lax.all_gather(shards[7][depth], ("dp", "fsdp"), axis=0, tiled=True),
        lax.all_gather(shards[8][depth], ("dp", "fsdp"), axis=0, tiled=True),
        lax.all_gather(shards[9][depth], ("dp", "fsdp"), axis=0, tiled=True),
        lax.all_gather(shards[10][depth], ("dp", "fsdp"), axis=0, tiled=True),
        lax.all_gather(shards[11][depth], ("dp", "fsdp"), axis=0, tiled=True),
        lax.all_gather(shards[12][depth], ("dp", "fsdp"), axis=0, tiled=True),
        lax.all_gather(shards[13][depth], ("dp", "fsdp"), axis=0, tiled=True),
    )


def gather_backward(shards, depth):
    return (
        lax.all_gather(shards[0][depth], ("dp", "fsdp"), axis=0, tiled=True),
        lax.all_gather(shards[1][depth], ("dp", "fsdp"), axis=0, tiled=True),
        lax.all_gather(shards[2][depth], ("dp", "fsdp"), axis=0, tiled=True),
        lax.all_gather(shards[3][depth], ("dp", "fsdp"), axis=0, tiled=True),
        lax.all_gather(shards[4][depth], ("dp", "fsdp"), axis=0, tiled=True),
        lax.all_gather(shards[5][depth], ("dp", "fsdp"), axis=0, tiled=True),
        lax.all_gather(shards[6][depth], ("dp", "fsdp"), axis=0, tiled=True),
        lax.all_gather(shards[7][depth], ("dp", "fsdp"), axis=0, tiled=True),
        lax.all_gather(shards[8][depth], ("dp", "fsdp"), axis=0, tiled=True),
        lax.all_gather(shards[9][depth], ("dp", "fsdp"), axis=0, tiled=True),
        lax.all_gather(shards[10][depth], ("dp", "fsdp"), axis=0, tiled=True),
        lax.all_gather(shards[11][depth], ("dp", "fsdp"), axis=0, tiled=True),
        lax.all_gather(shards[12][depth], ("dp", "fsdp"), axis=0, tiled=True),
        lax.all_gather(shards[13][depth], ("dp", "fsdp"), axis=0, tiled=True),
    )


def scatter_layer(terms):
    return (
        lax.psum_scatter(terms[0], ("dp", "fsdp"), scatter_dimension=0, tiled=True),
        lax.psum_scatter(terms[1], ("dp", "fsdp"), scatter_dimension=0, tiled=True),
        lax.psum_scatter(terms[2], ("dp", "fsdp"), scatter_dimension=0, tiled=True),
        lax.psum_scatter(terms[3], ("dp", "fsdp"), scatter_dimension=0, tiled=True),
        lax.psum_scatter(terms[4], ("dp", "fsdp"), scatter_dimension=0, tiled=True),
        lax.psum_scatter(terms[5], ("dp", "fsdp"), scatter_dimension=0, tiled=True),
        lax.psum_scatter(terms[6], ("dp", "fsdp"), scatter_dimension=0, tiled=True),
        lax.psum_scatter(terms[7], ("dp", "fsdp"), scatter_dimension=0, tiled=True),
        lax.psum_scatter(terms[8], ("dp", "fsdp"), scatter_dimension=0, tiled=True),
        lax.psum_scatter(terms[9], ("dp", "fsdp"), scatter_dimension=0, tiled=True),
        lax.psum_scatter(terms[10], ("dp", "fsdp"), scatter_dimension=0, tiled=True),
        lax.psum_scatter(terms[11], ("dp", "fsdp"), scatter_dimension=0, tiled=True),
        lax.psum_scatter(terms[12], ("dp", "fsdp"), scatter_dimension=0, tiled=True),
        lax.psum_scatter(terms[13], ("dp", "fsdp"), scatter_dimension=0, tiled=True),
    )


def layer_forward(current, labels, flags, weights):
    (
        normgain,
        normbias,
        valueproj,
        valuebias,
        reduceproj,
        reducebias,
        decays,
        stateinput,
        stateoutput,
        skipgain,
        expandproj,
        expandbias,
        outproj,
        outbias,
    ) = weights
    normed, norm_back = jax.vjp(
        normalize, current, normgain.astype(jnp.float32), normbias.astype(jnp.float32)
    )
    normed_low = normed.astype(jnp.bfloat16)
    opened = jnp.dot(normed_low, valueproj, preferred_element_type=jnp.float32) + valuebias.astype(
        jnp.float32
    )
    values, value_back = jax.vjp(smooth, opened)
    reduced = jnp.dot(
        normed_low, reduceproj, preferred_element_type=jnp.float32
    ) + reducebias.astype(jnp.float32)
    smoothed, reduce_back = jax.vjp(smooth, reduced)
    signal = smoothed * flags
    mixed, mix_back = jax.vjp(
        partial(mixer, labels),
        signal,
        decays.astype(jnp.float32),
        stateinput.astype(jnp.float32),
        stateoutput.astype(jnp.float32),
        skipgain.astype(jnp.float32),
    )
    mixed_low = mixed.astype(jnp.bfloat16)
    expanded = jnp.dot(
        mixed_low, expandproj, preferred_element_type=jnp.float32
    ) + expandbias.astype(jnp.float32)
    gated = (expanded * values).astype(jnp.bfloat16)
    branch = jnp.dot(gated, outproj, preferred_element_type=jnp.float32) + outbias.astype(
        jnp.float32
    )
    saved = (
        normed_low,
        values,
        value_back,
        reduce_back,
        mix_back,
        mixed_low,
        expanded,
        gated,
        norm_back,
    )
    return (current + flags * branch, saved)


def layer_backward(upstream, flags, weights, saved):
    (
        normgain,
        normbias,
        valueproj,
        valuebias,
        reduceproj,
        reducebias,
        decays,
        stateinput,
        stateoutput,
        skipgain,
        expandproj,
        expandbias,
        outproj,
        outbias,
    ) = weights
    normed_low, values, value_back, reduce_back, mix_back, mixed_low, expanded, gated, norm_back = (
        saved
    )
    dout = (flags * upstream).astype(jnp.bfloat16)
    outproj_term = lax.dot_general(gated, dout, rows_dims, preferred_element_type=jnp.float32)
    outbias_term = jnp.sum(dout, axis=0, dtype=jnp.float32)
    dgated = lax.dot_general(dout, outproj, cols_dims, preferred_element_type=jnp.float32)
    dexpanded = (dgated * values).astype(jnp.bfloat16)
    dvalues = dgated * expanded
    expandproj_term = lax.dot_general(
        mixed_low, dexpanded, rows_dims, preferred_element_type=jnp.float32
    )
    expandbias_term = jnp.sum(dexpanded, axis=0, dtype=jnp.float32)
    dmixed = lax.dot_general(dexpanded, expandproj, cols_dims, preferred_element_type=jnp.float32)
    dsignal, decays_term, stateinput_term, stateoutput_term, skipgain_term = mix_back(dmixed)
    (dreduced,) = reduce_back(dsignal * flags)
    dreduced_low = dreduced.astype(jnp.bfloat16)
    (dopened,) = value_back(dvalues)
    dopened_low = dopened.astype(jnp.bfloat16)
    valueproj_term = lax.dot_general(
        normed_low, dopened_low, rows_dims, preferred_element_type=jnp.float32
    )
    valuebias_term = jnp.sum(dopened_low, axis=0, dtype=jnp.float32)
    reduceproj_term = lax.dot_general(
        normed_low, dreduced_low, rows_dims, preferred_element_type=jnp.float32
    )
    reducebias_term = jnp.sum(dreduced_low, axis=0, dtype=jnp.float32)
    dnormed = lax.dot_general(dopened_low, valueproj, cols_dims, preferred_element_type=jnp.float32)
    dnormed = dnormed + lax.dot_general(
        dreduced_low, reduceproj, cols_dims, preferred_element_type=jnp.float32
    )
    dcurrent, normgain_term, normbias_term = norm_back(dnormed)
    terms = (
        normgain_term,
        normbias_term,
        valueproj_term,
        valuebias_term,
        reduceproj_term,
        reducebias_term,
        decays_term,
        stateinput_term,
        stateoutput_term,
        skipgain_term,
        expandproj_term,
        expandbias_term,
        outproj_term,
        outbias_term,
    )
    return (upstream + dcurrent, terms)


def plain(
    inputs,
    segment_ids,
    token_mask,
    cotangent,
    normgain,
    normbias,
    valueproj,
    valuebias,
    reduceproj,
    reducebias,
    decays,
    stateinput,
    stateoutput,
    skipgain,
    expandproj,
    expandbias,
    outproj,
    outbias,
):
    shards = (
        normgain,
        normbias,
        valueproj,
        valuebias,
        reduceproj,
        reducebias,
        decays,
        stateinput,
        stateoutput,
        skipgain,
        expandproj,
        expandbias,
        outproj,
        outbias,
    )
    flags = token_mask.astype(jnp.float32)[:, None]
    current = inputs.astype(jnp.float32)
    fetched = []
    stored = []
    for depth in range(LAYERS):
        weights = gather_forward(shards, depth)
        current, saved = layer_forward(current, segment_ids, flags, weights)
        fetched.append(weights)
        stored.append(saved)
    outputs = current.astype(jnp.bfloat16)
    upstream = cotangent.astype(jnp.float32)
    scattered = [None] * LAYERS
    for depth in reversed(range(LAYERS)):
        weights = gather_backward(shards, depth)
        upstream, terms = layer_backward(upstream, flags, weights, stored[depth])
        scattered[depth] = scatter_layer(terms)
    results = tuple(
        (jnp.stack([scattered[depth][index] for depth in range(LAYERS)]) for index in range(14))
    )
    return (outputs, upstream) + tuple(results)


def fast(
    inputs, segment_ids, token_mask, cotangent, normgain, normbias, valueproj, valuebias,
    reduceproj, reducebias, decays, stateinput, stateoutput, skipgain, expandproj, expandbias,
    outproj, outbias,
):
    dp, fs = lax.axis_index("dp"), lax.axis_index("fsdp")
    me = jnp.stack([dp, fs]).astype(jnp.int32)
    tokens, depth = inputs.shape
    tall = valueproj.shape[1]
    small = stateinput.shape[1]
    high = outproj.shape[1]
    hidden = valueproj.shape[2]
    units = hidden // GROUP
    feats = reduceproj.shape[2]
    states = feats
    assert feats == GROUP * LANES
    devices = GROUP * RINGS
    flags = token_mask.astype(f32)[:, None]

    zeros = lambda n: jnp.zeros((n,), bf16)
    rows = []
    for l in range(LAYERS):
        rows.append(jnp.concatenate([normgain[l], normbias[l], outbias[l], decays[l], zeros(16)]))
        rows.append(jnp.concatenate([valuebias[l], reducebias[l], skipgain[l]]))
        rows.append(jnp.concatenate([expandbias[l], zeros(32)]))
    rows += [zeros(LANES)] * 2
    small_pack = jnp.stack(rows)
    stacked = jnp.stack([small_pack] + [swap(small_pack, k * RINGS) for k in range(1, GROUP)])
    stacked = jnp.stack([stacked] + [swap(stacked, 2 * k) for k in range(1, RINGS // 2)])
    stacked = jnp.stack([stacked, swap(stacked, 1)], axis=1)
    number = jnp.arange(devices)
    place = (fs ^ (number % RINGS)) * GROUP + (dp ^ (number // RINGS))
    pick = (place[:, None] == number[None, :]).astype(bf16)
    table = nn(pick, stacked.reshape(devices, -1)).reshape(devices, 8, LANES)

    def vector(row, start, stop):
        return table[:, row, start:stop].reshape(1, -1)

    def quarter(row, start, stop):
        mine = lax.dynamic_slice_in_dim(table, dp * RINGS, RINGS, 0)
        return mine[:, row, start:stop].reshape(1, -1)

    gains = [vector(3 * l, 0, 32) for l in range(LAYERS)]
    shifts = [vector(3 * l, 32, 64) for l in range(LAYERS)]
    outbiases = [vector(3 * l, 64, 96) for l in range(LAYERS)]
    rates = [vector(3 * l, 96, 112) for l in range(LAYERS)]
    inbiases = [
        jnp.concatenate([quarter(3 * l + 1, 0, 96), quarter(3 * l + 1, 96, 112)], axis=1)
        for l in range(LAYERS)
    ]
    skips = [quarter(3 * l + 1, 112, 128) for l in range(LAYERS)]
    gatebiases = [quarter(3 * l + 2, 0, 96) for l in range(LAYERS)]

    value_packs, out_packs = [], []
    for l in range(LAYERS):
        mixing = (stateinput[l].astype(f32) * stateoutput[l].astype(f32)).astype(bf16)
        pieces, expands = [], []
        for k in range(GROUP):
            q = dp ^ k
            top = jnp.concatenate(
                [
                    lax.dynamic_slice_in_dim(valueproj[l], q * units, units, 1),
                    lax.dynamic_slice_in_dim(reduceproj[l], q * LANES, LANES, 1),
                ],
                axis=1,
            )
            thin = lax.dynamic_slice_in_dim(mixing, q * LANES, LANES, 1)
            piece = jnp.concatenate([top, jnp.pad(thin, ((0, 0), (0, units)))], axis=0)
            expand = lax.dynamic_slice_in_dim(expandproj[l], q * units, units, 1)
            pieces.append(swap(piece, k * RINGS) if k else piece)
            expands.append(swap(expand, k * RINGS) if k else expand)
        last = jnp.concatenate(
            [p[tall:, :LANES] for p in pieces] + [jnp.zeros((small, units - 3 * LANES), bf16)], axis=1
        )
        value_packs.append(jnp.concatenate([p[:tall] for p in pieces] + [last], axis=0))
        blocks = [e[:, t * 256 : (t + 1) * 256] for e in expands for t in range(units // 256)]
        across = depth // 256
        strips = [
            jnp.concatenate(blocks[r : r + across], axis=1) for r in range(0, len(blocks), across)
        ]
        out_packs.append(jnp.concatenate([outproj[l]] + strips, axis=0))

    lagged = jnp.arange(tokens, dtype=f32)
    powers = [jnp.exp(-lagged[:, None] * rates[l]).astype(bf16) for l in range(LAYERS)]

    value_w, mixes, filters, out_w, expand_w = [], [], [], [], []
    behind = ()
    for l in range(LAYERS):
        parts, marks = gather_rest(after(value_packs[l], *behind) if behind else value_packs[l])
        w, mix, filt = open_value(me, powers[l], parts)
        value_w.append(w)
        mixes.append(mix)
        filters.append(filt)
        parts, behind = gather_rest(after(out_packs[l], *marks))
        o, e = open_out(me, parts, high, small, units)
        out_w.append(o)
        expand_w.append(e)

    same = (segment_ids[:, None] == segment_ids[None, :]).astype(f32)
    spot = jnp.arange(tokens)
    before = (spot[None, :] < spot[:, None]).astype(f32)
    age = jnp.sum(same * before, axis=1)
    rest = jnp.sum(same * (1.0 - before), axis=1) - 1.0
    aux = jnp.pad(jnp.stack([age, rest, token_mask.astype(f32)], axis=1), ((0, 0), (0, LANES - 3)))
    auxes = gather_group(aux.astype(bf16))

    upstream = cotangent.astype(f32)
    dout = (flags * upstream).astype(bf16)
    douts = gather_group(dout)

    current = inputs.astype(f32)
    saved = []
    for l in range(LAYERS):
        center = current - jnp.mean(current, axis=1, keepdims=True)
        rstd = lax.rsqrt(jnp.mean(center * center, axis=1, keepdims=True) + 1e-05)
        normed = center * rstd
        norms = gather_group((normed * gains[l] + shifts[l]).astype(bf16))
        lo = forward_in(*norms[:2], value_w[l], inbiases[l], filters[l], skips[l], *auxes[:2])
        hi = forward_in(*norms[2:], value_w[l], inbiases[l], filters[l], skips[l], *auxes[2:])
        y_lo, y_hi = lo[4], hi[4]
        far_lo, far_hi = swap(y_lo, 2 * RINGS), swap(y_hi, 2 * RINGS)
        out_hi = forward_out(
            me, (y_hi, swap(y_hi, RINGS), far_lo, swap(far_lo, RINGS)),
            expand_w[l], gatebiases[l], hi[0], out_w[l],
        )
        out_lo = forward_out(
            me, (y_lo, swap(y_lo, RINGS), far_hi, swap(far_hi, RINGS)),
            expand_w[l], gatebiases[l], lo[0], out_w[l],
        )
        branch = return_group(out_lo[3:], out_hi[3:]) + outbiases[l]
        current = current + flags * branch
        saved.append((normed, rstd, norms, lo, hi, out_lo, out_hi))
    outputs = current.astype(bf16)

    value_grads, out_grads, sums_all, sums_rest = [None] * 2, [None] * 2, [None] * 2, [None] * 2
    for l in reversed(range(LAYERS)):
        normed, rstd, norms, lo, hi, out_lo, out_hi = saved[l]
        if l < LAYERS - 1:
            dout = (flags * upstream).astype(bf16)
            douts = gather_group(dout)
        back_lo = backward_out(me, *douts[:2], out_w[l], expand_w[l], lo[0], lo[1], out_lo[0])
        near_lo = swap(back_lo[3], RINGS)
        far_lo = swap((back_lo[2][1].astype(f32) + near_lo[1].astype(f32)).astype(bf16), 2 * RINGS)
        back_hi = backward_out(me, *douts[2:], out_w[l], expand_w[l], hi[0], hi[1], out_hi[0])
        near_hi = swap(back_hi[3], RINGS)
        far_hi = swap((back_hi[2][1].astype(f32) + near_hi[1].astype(f32)).astype(bf16), 2 * RINGS)
        in_hi = backward_in(
            back_hi[2], near_hi, far_lo, hi[2], hi[3], back_hi[1], filters[l], skips[l], *auxes[2:], value_w[l]
        )
        in_lo = backward_in(
            back_lo[2], near_lo, far_hi, lo[2], lo[3], back_lo[1], filters[l], skips[l], *auxes[:2], value_w[l]
        )
        dnrm = return_group(in_lo[1:3], in_hi[1:3])
        out_grads[l] = reduce_rest(
            grads_out(
                me, (out_lo[1], out_hi[1]), douts, (out_lo[2], out_hi[2]), (back_lo[0], back_hi[0]), high, small
            )
        )
        corr = jnp.sum(in_lo[3] + in_hi[3], axis=1)
        *packs, terms = grads_in(me, norms, (in_lo[0], in_hi[0]), powers[l], corr, mixes[l], tall, small)
        value_grads[l] = reduce_rest(packs)
        gain_term = jnp.sum(dnrm * normed, axis=0)
        shift_term = jnp.sum(dnrm, axis=0)
        out_term = jnp.sum(dout.astype(f32), axis=0)
        q = dnrm * gains[l]
        slope = q - jnp.mean(q, axis=1, keepdims=True) - normed * jnp.mean(q * normed, axis=1, keepdims=True)
        upstream = upstream + slope * rstd
        sums_all[l] = jnp.concatenate([gain_term, shift_term, out_term, jnp.sum(terms, axis=1)]).reshape(-1, LANES)
        sums_rest[l] = jnp.concatenate(
            [
                (in_lo[4] + in_hi[4]).reshape(-1, LANES),
                (back_lo[4] + back_hi[4]).reshape(-1, LANES),
                in_lo[5] + in_hi[5],
            ]
        )

    pieces, expands, outs = [], [], []
    for l in range(LAYERS):
        g = value_grads[l]
        parts = []
        for k in range(GROUP):
            part = jnp.concatenate([g[k * tall : (k + 1) * tall], g[GROUP * tall :]], axis=0).astype(bf16)
            parts.append(swap(part, k * RINGS) if k else part)
        pieces.append(parts)
        g = out_grads[l]
        parts = []
        for k in range(GROUP):
            blocks = []
            for t in range(units // 256):
                r, c = divmod(k * (units // 256) + t, depth // 256)
                blocks.append(g[high + small * r : high + small * (r + 1), c * 256 : (c + 1) * 256])
            part = jnp.concatenate(blocks, axis=1).astype(bf16)
            parts.append(swap(part, k * RINGS) if k else part)
        expands.append(parts)
        outs.append(g[:high])
    valueproj_grad, reduceproj_grad, stateinput_grad, stateoutput_grad, expandproj_grad, outproj_grad = finish(
        me, pieces, expands, outs, stateinput, stateoutput
    )

    vectors = []
    for l in range(LAYERS):
        head = sums_all[l].shape[0]
        packed = all_rest(jnp.pad(jnp.concatenate([sums_all[l], sums_rest[l]]), ((0, 6), (0, 0))))
        shared = all_group(packed[:head]).reshape(-1)
        mine = packed[head:].reshape(-1)
        index = dp * RINGS + fs
        take = lambda array, start, n, at: lax.dynamic_slice_in_dim(array, start + at * n, n, 0)
        vectors.append(
            (
                take(shared, 0, depth // devices, index),
                take(shared, depth, depth // devices, index),
                take(mine, 0, units // RINGS, fs),
                take(mine, units, LANES // RINGS, fs),
                take(shared, 3 * depth, states // devices, index),
                take(mine, 2 * units + LANES, LANES // RINGS, fs),
                take(mine, units + LANES, units // RINGS, fs),
                take(shared, 2 * depth, depth // devices, index),
            )
        )
    gain_g, shift_g, vbias_g, rbias_g, decays_g, skip_g, ebias_g, obias_g = (
        jnp.stack([vectors[l][i] for l in range(LAYERS)]) for i in range(8)
    )
    return (
        outputs, upstream, gain_g, shift_g, valueproj_grad, vbias_g, reduceproj_grad, rbias_g, decays_g,
        stateinput_grad, stateoutput_grad, skip_g, expandproj_grad, ebias_g, outproj_grad, obias_g,
    )


def solution(mesh):
    placed = (
        P(("dp", "fsdp"), None),
        P(("dp", "fsdp")),
        P(("dp", "fsdp")),
        P(("dp", "fsdp"), None),
        P(None, ("dp", "fsdp")),
        P(None, ("dp", "fsdp")),
        P(None, ("dp", "fsdp"), None),
        P(None, ("dp", "fsdp")),
        P(None, ("dp", "fsdp"), None),
        P(None, ("dp", "fsdp")),
        P(None, ("dp", "fsdp")),
        P(None, ("dp", "fsdp"), None),
        P(None, ("dp", "fsdp"), None),
        P(None, ("dp", "fsdp")),
        P(None, ("dp", "fsdp"), None),
        P(None, ("dp", "fsdp")),
        P(None, ("dp", "fsdp"), None),
        P(None, ("dp", "fsdp")),
    )
    small = mesh.shape["dp"] == GROUP and mesh.shape["fsdp"] == RINGS
    return jax.shard_map(
        fast if small else plain,
        mesh=mesh,
        in_specs=placed,
        out_specs=(
            P(("dp", "fsdp"), None),
            P(("dp", "fsdp"), None),
            P(None, ("dp", "fsdp")),
            P(None, ("dp", "fsdp")),
            P(None, ("dp", "fsdp"), None),
            P(None, ("dp", "fsdp")),
            P(None, ("dp", "fsdp"), None),
            P(None, ("dp", "fsdp")),
            P(None, ("dp", "fsdp")),
            P(None, ("dp", "fsdp"), None),
            P(None, ("dp", "fsdp"), None),
            P(None, ("dp", "fsdp")),
            P(None, ("dp", "fsdp"), None),
            P(None, ("dp", "fsdp")),
            P(None, ("dp", "fsdp"), None),
            P(None, ("dp", "fsdp")),
        ),
        check_vma=False,
    )
```

```python
from functools import partial

import jax
import jax.numpy as jnp
import numpy as np
from jax import lax
from jax.experimental import pallas as pl
from jax.experimental.pallas import tpu as pltpu
from jax.sharding import PartitionSpec as P

LAYERS = 2
AXES = ("dp", "fsdp")
GROUP = 4
RINGS = 8
LANES = 128
STRIP = 32
PAD = 32

f32 = jnp.float32
bf16 = jnp.bfloat16
highest = lax.Precision.HIGHEST
rows_dims = (((0,), (0,)), ((), ()))
cols_dims = (((1,), (1,)), ((), ()))

VMEM = pltpu.VMEM


def swap(block, flip):
    size = GROUP * RINGS
    return lax.ppermute(block, AXES, [(i, i ^ flip) for i in range(size)])


def cost(micros):
    return pl.CostEstimate(
        flops=int(micros * 1.0e9), bytes_accessed=1 << 20, transcendentals=0
    )


def params():
    return pltpu.CompilerParams(vmem_limit_bytes=48 << 20)


def whole(shape):
    return pl.BlockSpec(shape, lambda *_: (0,) * len(shape))


def scalars():
    return pl.BlockSpec(memory_space=pltpu.SMEM)


def nt(a, b):
    return lax.dot_general(a, b, cols_dims, preferred_element_type=f32)


def tn(a, b):
    return lax.dot_general(a, b, rows_dims, preferred_element_type=f32)


def nn(a, b):
    return jnp.dot(a, b, preferred_element_type=f32)


def open_value(me, powers, parts):
    rows, width = parts[0].shape
    states = powers.shape[1]
    small = states // (GROUP * RINGS)
    tall = (rows - small) // GROUP
    depth = tall * GROUP * RINGS

    def kernel(me_ref, e_ref, *refs):
        packs, (w_ref, mix_ref, k_ref) = refs[:RINGS], refs[RINGS:]
        dp, fs = me_ref[0], me_ref[1]
        for j in range(RINGS):
            for k in range(GROUP):
                index = (dp ^ k) * RINGS + (fs ^ j)
                w_ref[pl.ds(pl.multiple_of(index * tall, tall), tall), :] = packs[j][
                    k * tall : (k + 1) * tall, :
                ]
                mix_ref[pl.ds(pl.multiple_of(index * small, small), small), :] = packs[j][
                    GROUP * tall :, k * LANES : (k + 1) * LANES
                ]
        k_ref[...] = nn(e_ref[...], mix_ref[...])

    return pl.pallas_call(
        kernel,
        out_shape=(
            jax.ShapeDtypeStruct((depth, width), bf16),
            jax.ShapeDtypeStruct((states, LANES), bf16),
            jax.ShapeDtypeStruct((powers.shape[0], LANES), f32),
        ),
        in_specs=[scalars()] + [pl.BlockSpec(memory_space=VMEM)] * (1 + RINGS),
        out_specs=(pl.BlockSpec(memory_space=VMEM),) * 3,
        compiler_params=params(),
        cost_estimate=cost(2.5),
        name="open_value",
    )(me, powers, *parts)


def open_out(me, parts, tall, small, units):
    width = parts[0].shape[1]
    thirds = units // 256
    across = width // 256

    def kernel(me_ref, *refs):
        packs, (o_ref, e_ref) = refs[:RINGS], refs[RINGS:]
        dp, fs = me_ref[0], me_ref[1]
        for j in range(RINGS):
            o_ref[pl.ds(pl.multiple_of((fs ^ j) * tall, tall), tall), :] = packs[j][:tall, :]
            for k in range(GROUP):
                index = (dp ^ k) * RINGS + (fs ^ j)
                for t in range(thirds):
                    r, c = divmod(k * thirds + t, across)
                    e_ref[
                        pl.ds(pl.multiple_of(index * small, small), small),
                        t * 256 : (t + 1) * 256,
                    ] = packs[j][
                        tall + small * r : tall + small * (r + 1), c * 256 : (c + 1) * 256
                    ]

    return pl.pallas_call(
        kernel,
        out_shape=(
            jax.ShapeDtypeStruct((tall * RINGS, width), bf16),
            jax.ShapeDtypeStruct((small * GROUP * RINGS, units), bf16),
        ),
        in_specs=[scalars()] + [pl.BlockSpec(memory_space=VMEM)] * RINGS,
        out_specs=(pl.BlockSpec(memory_space=VMEM),) * 2,
        compiler_params=params(),
        cost_estimate=cost(2.5),
        name="open_out",
    )(me, *parts)


def forward_in(na, nb, weight, bias, filt, skip, auxa, auxb):
    tokens, depth = na.shape
    width = weight.shape[1]
    units = width - LANES
    strips = tokens // STRIP

    def kernel(
        na_ref, nb_ref, w_ref, b_ref, k_ref, s_ref, xa_ref, xb_ref,
        value_ref, gp_ref, z_ref, g2_ref, y_ref,
        n_scr, a_scr, aux_scr, age_scr, shifted, y_scr,
    ):
        step = pl.program_id(0)

        @pl.when(step == 0)
        def _():
            n_scr[...] = na_ref[...]
            aux_scr[...] = xa_ref[...].astype(f32)

        @pl.when(step == 1)
        def _():
            n_scr[...] = nb_ref[...]
            aux_scr[...] = xb_ref[...].astype(f32)

        a_scr[...] = nn(n_scr[...], w_ref[...])
        age_scr[...] = jnp.broadcast_to(aux_scr[:, 0:1], (tokens, LANES))

        def smooth(i, carry):
            at = pl.ds(pl.multiple_of(i * STRIP, STRIP), STRIP)
            v = a_scr[at, :] + b_ref[...]
            cdf = 0.5 + 0.5 * lax.erf(v * 0.7071067811865476)
            slope = cdf + v * (0.3989422804014327 * jnp.exp(-0.5 * v * v))
            act = v * cdf
            value_ref[at, :] = act[:, :units].astype(bf16)
            gp_ref[at, :] = slope[:, :units].astype(bf16)
            mask = jnp.broadcast_to(aux_scr[at, 2:3], (STRIP, LANES))
            z_ref[at, :] = act[:, units:] * mask
            g2_ref[at, :] = slope[:, units:] * mask
            return carry

        lax.fori_loop(0, strips, smooth, 0)
        z = z_ref[...]
        for b in range(8):
            shifted[b, :PAD, :] = jnp.zeros((PAD, LANES), f32)
            shifted[b, PAD:, :] = z if b == 0 else pltpu.roll(z, b, 0)
        for s in range(strips):
            age = age_scr[s * STRIP : (s + 1) * STRIP, :]

            def lags(a, acc, s=s, age=age):
                base = pl.multiple_of(a * 8, 8)
                left = age - (a * 8).astype(f32)
                for b in range(8):
                    row = k_ref[pl.ds(base + b, 1), :]
                    past = shifted[b, pl.ds(pl.multiple_of(PAD + s * STRIP - base, 8), STRIP), :]
                    acc = acc + jnp.where(left >= b, past, 0.0) * row
                return acc

            y_scr[s * STRIP : (s + 1) * STRIP, :] = lax.fori_loop(
                0, (s + 1) * (STRIP // 8), lags, jnp.zeros((STRIP, LANES), f32)
            )
        y_ref[...] = (y_scr[...] + s_ref[...] * z).astype(bf16)

    half = lambda cols: pl.BlockSpec((tokens, cols), lambda i: (i, 0))
    return pl.pallas_call(
        kernel,
        grid=(2,),
        out_shape=(
            jax.ShapeDtypeStruct((2 * tokens, units), bf16),
            jax.ShapeDtypeStruct((2 * tokens, units), bf16),
            jax.ShapeDtypeStruct((2 * tokens, LANES), f32),
            jax.ShapeDtypeStruct((2 * tokens, LANES), f32),
            jax.ShapeDtypeStruct((2 * tokens, LANES), bf16),
        ),
        in_specs=[
            whole((tokens, depth)), whole((tokens, depth)), whole((depth, width)),
            whole((1, width)), whole(filt.shape), whole((1, LANES)),
            whole((tokens, LANES)), whole((tokens, LANES)),
        ],
        out_specs=(half(units), half(units), half(LANES), half(LANES), half(LANES)),
        scratch_shapes=[
            VMEM((tokens, depth), bf16),
            VMEM((tokens, width), f32),
            VMEM((tokens, LANES), f32),
            VMEM((tokens, LANES), f32),
            VMEM((8, PAD + tokens, LANES), f32),
            VMEM((tokens, LANES), f32),
        ],
        compiler_params=params(),
        cost_estimate=cost(9.0),
        name="forward_in",
    )(na, nb, weight, bias, filt, skip, auxa, auxb)


def forward_out(me, ys, expand, bias, value, outw):
    tokens = ys[0].shape[0] // 2
    feats, units = expand.shape
    depth = outw.shape[1]

    def kernel(
        me_ref, y0, y1, y2, y3, e_ref, b_ref, value_ref, o_ref,
        c_ref, gated_ref, full_ref, first_ref, second_ref,
    ):
        dp = me_ref[0]
        for k, part in enumerate((y0, y1, y2, y3)):
            full_ref[:, pl.ds(pl.multiple_of((dp ^ k) * LANES, LANES), LANES)] = part[...]
        c = nn(full_ref[...], e_ref[...]) + b_ref[...]
        gated = (c * value_ref[...].astype(f32)).astype(bf16)
        c_ref[...] = c.astype(bf16)
        gated_ref[...] = gated
        out = nn(gated, o_ref[...]).astype(bf16)

        @pl.when(pl.program_id(0) == 0)
        def _():
            first_ref[...] = out

        @pl.when(pl.program_id(0) == 1)
        def _():
            second_ref[...] = out

    same = lambda cols: pl.BlockSpec((tokens, cols), lambda i: (i, 0))
    other = lambda cols: pl.BlockSpec((tokens, cols), lambda i: (1 - i, 0))
    return pl.pallas_call(
        kernel,
        grid=(2,),
        out_shape=(
            jax.ShapeDtypeStruct((2 * tokens, units), bf16),
            jax.ShapeDtypeStruct((2 * tokens, units), bf16),
            jax.ShapeDtypeStruct((2 * tokens, feats), bf16),
            jax.ShapeDtypeStruct((tokens, depth), bf16),
            jax.ShapeDtypeStruct((tokens, depth), bf16),
        ),
        in_specs=[
            scalars(), same(LANES), other(LANES), same(LANES), other(LANES),
            whole((feats, units)), whole((1, units)), same(units), whole((units, depth)),
        ],
        out_specs=(same(units), same(units), same(feats), whole((tokens, depth)), whole((tokens, depth))),
        compiler_params=params(),
        cost_estimate=cost(3.5),
        name="forward_out",
    )(me, *ys, expand, bias, value, outw)


def backward_out(me, da, db, outw, expand, value, slope, gate):
    tokens, depth = da.shape
    feats, units = expand.shape

    def kernel(
        me_ref, da_ref, db_ref, o_ref, e_ref, value_ref, gp_ref, c_ref,
        dc_ref, da1_ref, even_ref, odd_ref, sum_ref, d_scr, y_scr,
    ):
        dp = me_ref[0]
        step = pl.program_id(0)

        @pl.when(step == 0)
        def _():
            d_scr[...] = da_ref[...]
            sum_ref[...] = jnp.zeros_like(sum_ref)

        @pl.when(step == 1)
        def _():
            d_scr[...] = db_ref[...]

        dgated = nt(d_scr[...], o_ref[...])
        dc = (dgated * value_ref[...].astype(f32)).astype(bf16)
        dc_ref[...] = dc
        da1_ref[...] = (dgated * c_ref[...].astype(f32) * gp_ref[...].astype(f32)).astype(bf16)
        sum_ref[...] += jnp.sum(dc.astype(f32), axis=0, keepdims=True)
        y_scr[...] = nt(dc, e_ref[...])
        for k, (ref, slot) in enumerate(((even_ref, 0), (odd_ref, 0), (even_ref, 1), (odd_ref, 1))):
            ref[slot] = y_scr[:, pl.ds(pl.multiple_of((dp ^ k) * LANES, LANES), LANES)].astype(bf16)

    same = lambda cols: pl.BlockSpec((tokens, cols), lambda i: (i, 0))
    return pl.pallas_call(
        kernel,
        grid=(2,),
        out_shape=(
            jax.ShapeDtypeStruct((2 * tokens, units), bf16),
            jax.ShapeDtypeStruct((2 * tokens, units), bf16),
            jax.ShapeDtypeStruct((2, 2 * tokens, LANES), bf16),
            jax.ShapeDtypeStruct((2, 2 * tokens, LANES), bf16),
            jax.ShapeDtypeStruct((1, units), f32),
        ),
        in_specs=[
            scalars(), whole((tokens, depth)), whole((tokens, depth)), whole((units, depth)),
            whole((feats, units)), same(units), same(units), same(units),
        ],
        out_specs=(
            same(units), same(units),
            pl.BlockSpec((2, tokens, LANES), lambda i: (0, i, 0)),
            pl.BlockSpec((2, tokens, LANES), lambda i: (0, 1 - i, 0)),
            whole((1, units)),
        ),
        scratch_shapes=[VMEM((tokens, depth), bf16), VMEM((tokens, feats), f32)],
        compiler_params=params(),
        cost_estimate=cost(3.5),
        name="backward_out",
    )(me, da, db, outw, expand, value, slope, gate)


def backward_in(own, near, far, z, slope2, da1, filt, skip, auxa, auxb, weight):
    tokens = auxa.shape[0]
    depth, width = weight.shape
    units = width - LANES
    strips = tokens // STRIP

    def kernel(
        own_ref, near_ref, far_ref, z_ref, g2_ref, da1_ref, k_ref, s_ref, xa_ref, xb_ref, w_ref,
        da_ref, first_ref, second_ref, corr_ref, sum_ref, skip_ref,
        aux_scr, rem_scr, shifted, dz_scr,
    ):
        step = pl.program_id(0)

        @pl.when(step == 0)
        def _():
            aux_scr[...] = xa_ref[...].astype(f32)
            corr_ref[...] = jnp.zeros_like(corr_ref)
            sum_ref[...] = jnp.zeros_like(sum_ref)
            skip_ref[...] = jnp.zeros_like(skip_ref)

        @pl.when(step == 1)
        def _():
            aux_scr[...] = xb_ref[...].astype(f32)

        rem_scr[...] = jnp.broadcast_to(aux_scr[:, 1:2], (tokens, LANES))
        dy = own_ref[0].astype(f32) + near_ref[0].astype(f32) + far_ref[...].astype(f32)
        for b in range(8):
            shifted[b, tokens:, :] = jnp.zeros((PAD, LANES), f32)
            shifted[b, :tokens, :] = dy if b == 0 else pltpu.roll(dy, tokens - b, 0)
        for s in range(strips):
            rem = rem_scr[s * STRIP : (s + 1) * STRIP, :]
            z = z_ref[s * STRIP : (s + 1) * STRIP, :]

            def lags(a, acc, s=s, rem=rem, z=z):
                base = pl.multiple_of(a * 8, 8)
                left = rem - (a * 8).astype(f32)
                for b in range(8):
                    row = k_ref[pl.ds(base + b, 1), :]
                    later = shifted[b, pl.ds(pl.multiple_of(s * STRIP + base, 8), STRIP), :]
                    later = jnp.where(left >= b, later, 0.0)
                    acc = acc + later * row
                    pair = later * z
                    corr_ref[base + b] += (pair[0:8] + pair[8:16]) + (pair[16:24] + pair[24:32])
                return acc

            dz_scr[s * STRIP : (s + 1) * STRIP, :] = lax.fori_loop(
                0, (strips - s) * (STRIP // 8), lags, jnp.zeros((STRIP, LANES), f32)
            )
        z = z_ref[...]
        da2 = ((dz_scr[...] + s_ref[...] * dy) * g2_ref[...]).astype(bf16)
        da_ref[:, :units] = da1_ref[...]
        da_ref[:, units:] = da2
        skip_ref[...] += jnp.sum(z * dy, axis=0, keepdims=True)
        sum_ref[...] += jnp.sum(da_ref[...].astype(f32), axis=0, keepdims=True)
        out = nt(da_ref[...], w_ref[...]).astype(bf16)

        @pl.when(step == 0)
        def _():
            first_ref[...] = out

        @pl.when(step == 1)
        def _():
            second_ref[...] = out

    same = lambda cols: pl.BlockSpec((tokens, cols), lambda i: (i, 0))
    return pl.pallas_call(
        kernel,
        grid=(2,),
        out_shape=(
            jax.ShapeDtypeStruct((2 * tokens, width), bf16),
            jax.ShapeDtypeStruct((tokens, depth), bf16),
            jax.ShapeDtypeStruct((tokens, depth), bf16),
            jax.ShapeDtypeStruct((tokens, 8, LANES), f32),
            jax.ShapeDtypeStruct((1, width), f32),
            jax.ShapeDtypeStruct((1, LANES), f32),
        ),
        in_specs=[
            pl.BlockSpec((1, tokens, LANES), lambda i: (0, i, 0)),
            pl.BlockSpec((1, tokens, LANES), lambda i: (0, i, 0)),
            same(LANES), same(LANES), same(LANES), same(units),
            whole(filt.shape), whole((1, LANES)), whole((tokens, LANES)), whole((tokens, LANES)),
            whole((depth, width)),
        ],
        out_specs=(
            same(width), whole((tokens, depth)), whole((tokens, depth)),
            whole((tokens, 8, LANES)), whole((1, width)), whole((1, LANES)),
        ),
        scratch_shapes=[
            VMEM((tokens, LANES), f32),
            VMEM((tokens, LANES), f32),
            VMEM((8, PAD + tokens, LANES), f32),
            VMEM((tokens, LANES), f32),
        ],
        compiler_params=params(),
        cost_estimate=cost(11.0),
        name="backward_in",
    )(own, near, far, z, slope2, da1, filt, skip, auxa, auxb, weight)


def grads_out(me, gated, douts, full, dc, tall, small):
    tokens, depth = douts[0].shape
    units = dc[0].shape[1]
    feats = full[0].shape[1]
    thirds = units // 256
    across = depth // 256
    rows = tall + small * GROUP * thirds // across

    def kernel(me_ref, g_lo, g_hi, d0, d1, d2, d3, y_lo, y_hi, c_lo, c_hi, *refs):
        outs, (o_scr, e_scr) = refs[:RINGS], refs[RINGS:]
        dp, fs = me_ref[0], me_ref[1]
        step = pl.program_id(0)
        o_scr[pl.ds(pl.multiple_of(step * 256, 256), 256), :] = (
            tn(g_lo[:tokens], d0[...])
            + tn(g_lo[tokens:], d1[...])
            + tn(g_hi[:tokens], d2[...])
            + tn(g_hi[tokens:], d3[...])
        ).astype(bf16)
        e_scr[step] = (tn(y_lo[...], c_lo[...]) + tn(y_hi[...], c_hi[...])).astype(bf16)

        @pl.when(step == thirds - 1)
        def _():
            for j in range(RINGS):
                outs[j][:tall, :] = o_scr[pl.ds(pl.multiple_of((fs ^ j) * tall, tall), tall), :]
                for k in range(GROUP):
                    index = (dp ^ k) * RINGS + (fs ^ j)
                    at = pl.ds(pl.multiple_of(index * small, small), small)
                    for t in range(thirds):
                        r, c = divmod(k * thirds + t, across)
                        outs[j][
                            tall + small * r : tall + small * (r + 1), c * 256 : (c + 1) * 256
                        ] = e_scr[t, at, :]

    column = lambda n: pl.BlockSpec((n, 256), lambda i: (0, i))
    return pl.pallas_call(
        kernel,
        grid=(thirds,),
        out_shape=(jax.ShapeDtypeStruct((rows, depth), bf16),) * RINGS,
        in_specs=[scalars()]
        + [column(2 * tokens)] * 2
        + [whole((tokens, depth))] * 4
        + [whole((2 * tokens, feats))] * 2
        + [column(2 * tokens)] * 2,
        out_specs=(whole((rows, depth)),) * RINGS,
        scratch_shapes=[VMEM((units, depth), bf16), VMEM((thirds, feats, 256), bf16)],
        compiler_params=params(),
        cost_estimate=cost(5.0),
        name="grads_out",
    )(me, *gated, *douts, *full, *dc)


def grads_in(me, norms, das, powers, corr, mixing, tall, small):
    tokens, depth = norms[0].shape
    width = das[0].shape[1]
    states = powers.shape[1]
    rows = tall * GROUP + small
    wide = depth // GROUP

    def kernel(me_ref, n0, n1, n2, n3, a_lo, a_hi, e_ref, corr_ref, mix_ref, *refs):
        outs, (dec_ref, w_scr, m_scr) = refs[:RINGS], refs[RINGS:]
        dp, fs = me_ref[0], me_ref[1]
        step = pl.program_id(0)
        w_scr[...] = (
            tn(n0[...], a_lo[:tokens])
            + tn(n1[...], a_lo[tokens:])
            + tn(n2[...], a_hi[:tokens])
            + tn(n3[...], a_hi[tokens:])
        ).astype(bf16)
        spot = pl.ds(pl.multiple_of((step ^ dp) * tall, tall), tall)
        for j in range(RINGS):
            outs[j][spot, :] = w_scr[pl.ds(pl.multiple_of((fs ^ j) * tall, tall), tall), :]

        @pl.when(step == 0)
        def _():
            corr_f = corr_ref[...]
            m_scr[...] = tn(e_ref[...], corr_f.astype(bf16)).astype(bf16)
            lag = lax.broadcasted_iota(jnp.int32, corr_f.shape, 0).astype(f32)
            dec_ref[...] = -tn(e_ref[...], (corr_f * lag).astype(bf16)) * mix_ref[...].astype(f32)
            for j in range(RINGS):
                outs[j][GROUP * tall :, :] = jnp.zeros((small, width), bf16)
                for k in range(GROUP):
                    index = (dp ^ k) * RINGS + (fs ^ j)
                    outs[j][GROUP * tall :, k * LANES : (k + 1) * LANES] = m_scr[
                        pl.ds(pl.multiple_of(index * small, small), small), :
                    ]

    return pl.pallas_call(
        kernel,
        grid=(GROUP,),
        out_shape=(jax.ShapeDtypeStruct((rows, width), bf16),) * RINGS
        + (jax.ShapeDtypeStruct((states, LANES), f32),),
        in_specs=[scalars()]
        + [pl.BlockSpec((tokens, wide), lambda i: (0, i))] * 4
        + [whole((2 * tokens, width))] * 2
        + [whole(powers.shape), whole(corr.shape), whole(mixing.shape)],
        out_specs=(whole((rows, width)),) * RINGS + (whole((states, LANES)),),
        scratch_shapes=[VMEM((wide, width), bf16), VMEM((states, LANES), bf16)],
        compiler_params=params(),
        cost_estimate=cost(5.0),
        name="grads_in",
    )(me, *norms, *das, powers, corr, mixing)


def finish(me, value_parts, expand_parts, out_parts, stateinput, stateoutput):
    layers, small, states = stateinput.shape
    rows, width = value_parts[0][0].shape
    tall = rows - small
    units = width - LANES
    high, depth = out_parts[0].shape
    feats = LANES * GROUP

    def kernel(me_ref, *refs):
        dp = me_ref[0]
        count = layers * GROUP
        values, expands, outs = refs[:count], refs[count : 2 * count], refs[2 * count : 2 * count + layers]
        si_ref, so_ref, v_ref, r_ref, si_out, so_out, e_ref, o_ref, m_scr = refs[2 * count + layers :]
        for l in range(layers):
            for k in range(GROUP):
                part = values[l * GROUP + k]
                q = dp ^ k
                v_ref[l, :, pl.ds(pl.multiple_of(q * units, LANES), units)] = part[:tall, :units].astype(f32)
                thin = pl.ds(pl.multiple_of(q * LANES, LANES), LANES)
                r_ref[l, :, thin] = part[:tall, units:].astype(f32)
                m_scr[:, thin] = part[tall:, k * LANES : (k + 1) * LANES].astype(f32)
                e_ref[l, :, pl.ds(pl.multiple_of(q * units, LANES), units)] = expands[l * GROUP + k][...].astype(f32)
            si_out[l] = m_scr[...] * so_ref[l].astype(f32)
            so_out[l] = m_scr[...] * si_ref[l].astype(f32)
            o_ref[l] = outs[l][...]

    flat = [p for parts in value_parts for p in parts] + [p for parts in expand_parts for p in parts]
    arrays = flat + list(out_parts) + [stateinput, stateoutput]
    return pl.pallas_call(
        kernel,
        out_shape=(
            jax.ShapeDtypeStruct((layers, tall, units * GROUP), f32),
            jax.ShapeDtypeStruct((layers, tall, feats), f32),
            jax.ShapeDtypeStruct((layers, small, feats), f32),
            jax.ShapeDtypeStruct((layers, small, feats), f32),
            jax.ShapeDtypeStruct((layers, small, units * GROUP), f32),
            jax.ShapeDtypeStruct((layers, high, depth), f32),
        ),
        in_specs=[scalars()] + [pl.BlockSpec(memory_space=VMEM)] * len(arrays),
        out_specs=(pl.BlockSpec(memory_space=VMEM),) * 6,
        scratch_shapes=[VMEM((small, feats), f32)],
        compiler_params=params(),
        cost_estimate=cost(3.0),
        name="finish",
    )(me, *arrays)


def after(block, *others):
    tie = sum(o[(slice(0, 1),) * o.ndim].reshape(1, 1) for o in others)
    return lax.optimization_barrier((block, tie))[0]


def gather_rest(pack):
    along = [pack] + [swap(pack, 2 * k) for k in range(1, RINGS // 2)]
    both = []
    for piece in along:
        both += [piece, swap(piece, 1)]
    return both, along[1:]


def reduce_rest(packs):
    summed = [None] * (RINGS // 2)
    for k in (1, 2, 3, 0):
        summed[k] = packs[2 * k].astype(f32) + swap(packs[2 * k + 1], 1).astype(f32)
    total = summed[0]
    for k in (1, 2, 3):
        total = total + swap(summed[k].astype(bf16), 2 * k).astype(f32)
    return total


def gather_group(block):
    near = swap(block, RINGS)
    far = swap(block, 2 * RINGS)
    return [block, near, far, swap(far, RINGS)]


def return_group(lo, hi):
    ahead = hi[0].astype(f32) + swap(hi[1], RINGS).astype(f32)
    there = swap(ahead.astype(bf16), 2 * RINGS)
    here = lo[0].astype(f32) + swap(lo[1], RINGS).astype(f32)
    return here + there.astype(f32)


def all_rest(block):
    total = block + sum(swap(block, 2 * k) for k in range(1, RINGS // 2))
    return total + swap(total, 1)


def all_group(block):
    return block + sum(swap(block, k * RINGS) for k in range(1, GROUP))


def tables(devices):
    out = []
    for count, size in ((devices, 32), (RINGS, 96), (devices, 16)):
        at = np.arange(count * size)
        out.append(jnp.asarray((np.arange(LANES)[:, None] == at[None, :] % size), bf16))
        out.append(jnp.asarray((np.arange(count)[:, None] == at[None, :] // size), f32))
    return out


class Mail:
    def __init__(self, send_sem, recv_sem):
        self.dp, self.fs = lax.axis_index("dp"), lax.axis_index("fsdp")
        self.send_sem, self.recv_sem, self.count, self.sent = send_sem, recv_sem, 0, []

    def peer(self, flip):
        return (self.dp ^ (flip // RINGS), self.fs ^ (flip % RINGS))

    def greet(self, flips):
        barrier = pltpu.get_barrier_semaphore()
        for flip in flips:
            pl.semaphore_signal(
                barrier, inc=1, device_id=self.peer(flip), device_id_type=pl.DeviceIdType.MESH
            )
        pl.semaphore_wait(barrier, len(flips))

    def send(self, src, dst, flip):
        copy = pltpu.make_async_remote_copy(
            src_ref=src, dst_ref=dst, send_sem=self.send_sem.at[self.count],
            recv_sem=self.recv_sem.at[self.count], device_id=self.peer(flip),
            device_id_type=pl.DeviceIdType.MESH,
        )
        self.count += 1
        copy.start()
        self.sent.append(copy)
        return copy

    def finish(self, copy):
        copy.wait_send()
        self.sent = [c for c in self.sent if c is not copy]

    def close(self):
        for copy in self.sent:
            copy.wait_send()


class Spill:
    def __init__(self, sem):
        self.sem, self.open = sem, []

    def put(self, src, dst):
        copy = pltpu.make_async_copy(src, dst, self.sem.at[len(self.open)])
        copy.start()
        self.open.append(copy)

    def close(self):
        for copy in self.open:
            copy.wait()


CORE, CHIP, BOTH = RINGS, 2 * RINGS, 3 * RINGS
FLIPS = (CORE, CHIP, BOTH, 1, 2, 4, 6)


def forward_kernel(sizes, *refs):
    tokens, depth, units, feats, states, tall, small, high = sizes
    width = units + LANES
    top = tall * GROUP
    rows = top + high + small * GROUP * units // depth
    (
        x_ref, aux_ref, dout_ref, v_ref, r_ref, e_ref, o_ref, si_ref, so_ref, vec_ref,
        rep32, put32, rep96, put96, rep16, put16,
    ) = refs[:16]
    (
        out_ref, later_ref, rows_ref, filt_ref, mixn_ref, auxs,
        norm_hbm, value_hbm, gp_hbm, c_hbm, gated_hbm, full_hbm, z_hbm, g2_hbm,
        vw_hbm, ow_hbm, ew_hbm, dout_hbm,
    ) = refs[16:34]
    (
        pieces, ein, packs, vecn, vw, ow, ew, xin, norm, douts,
        value, gp, cbuf, gated, full, z, g2, ybuf, yin, obuf, oin, oadd, ofar, xcur,
        a_scr, age_scr, shifted, y_scr, send_sem, recv_sem, hbm_sem,
    ) = refs[34:]
    mail = Mail(send_sem, recv_sem)
    spill = Spill(hbm_sem)
    dp, fs = mail.dp, mail.fs
    thirds = units // 256
    across = depth // 256

    def lanes(index, size):
        return pl.ds(pl.multiple_of(index * size, LANES), size)

    def place_expand(l, k, part):
        for t in range(thirds):
            r, c = divmod(k * thirds + t, across)
            at = top + high + small * r
            packs[l, 0, at : at + small, c * 256 : (c + 1) * 256] = part[:, t * 256 : (t + 1) * 256]

    for l in range(LAYERS):
        mixing = (si_ref[l].astype(f32) * so_ref[l].astype(f32)).astype(bf16)
        a_scr[:small, :feats] = mixing.astype(f32)
        for k in range(GROUP):
            q = dp ^ k
            dst = packs.at[l, 0, 0:tall] if k == 0 else pieces.at[l, k - 1, 0:tall]
            dst[:, :units] = v_ref[l, :, lanes(q, units)]
            dst[:, units:width] = r_ref[l, :, lanes(q, LANES)]
            dst[:small, width:] = a_scr[:small, lanes(q, LANES)].astype(bf16)
            dst[small:, width:] = vec_ref[l]
            part = e_ref[l, :, lanes(q, units)]
            if k == 0:
                place_expand(l, 0, part)
            else:
                pieces[l, k - 1, tall:, :units] = part
                pieces[l, k - 1, tall:, units:] = jnp.zeros((small, depth - units), bf16)
        packs[l, 0, top : top + high, :] = o_ref[l]
    xin[0] = x_ref[...]
    auxs[0] = aux_ref[...]
    douts[0] = dout_ref[...]

    mail.greet(FLIPS)

    def to_group(l, ks):
        return [
            (
                k,
                mail.send(pieces.at[l, k - 1, 0:tall], packs.at[l, 0, k * tall : (k + 1) * tall], k * RINGS),
                mail.send(pieces.at[l, k - 1, tall : tall + small], ein.at[l, k - 1], k * RINGS),
            )
            for k in ks
        ]

    def from_group(l, copies):
        for k, one, two in copies:
            one.wait_recv()
            two.wait_recv()
            place_expand(l, k, ein[l, k - 1, :, :units])

    def part_rows(part):
        return slice(0, top) if part == 0 else slice(top, rows)

    def along_z(l, part):
        at = part_rows(part)
        return [mail.send(packs.at[l, 0, at], packs.at[l, 2 * k, at], 2 * k) for k in range(1, RINGS // 2)]

    def along_y(l, part, k):
        at = part_rows(part)
        return mail.send(packs.at[l, 2 * k, at], packs.at[l, 2 * k + 1, at], 1)

    first = to_group(0, (2, 3, 1))
    aux_in = [mail.send(aux_ref, auxs.at[k], k * RINGS) for k in (1, 2, 3)]
    x_near = mail.send(x_ref, xin.at[1], CORE)
    from_group(0, first)
    zs = along_z(0, 0)
    ys = [along_y(0, 0, 0)]
    x_far = mail.send(x_ref, xin.at[2], CHIP)
    second = to_group(1, (1,))
    for k in range(1, RINGS // 2):
        zs[k - 1].wait_recv()
        ys.append(along_y(0, 0, k))
    zs_out = along_z(0, 1)
    ys_out = [along_y(0, 1, 0)]
    x_far.wait_recv()
    x_relay = mail.send(xin.at[2], xin.at[3], CORE)
    second += to_group(1, (2, 3))
    dout_near = mail.send(dout_ref, douts.at[1], CORE)

    def open_value(l):
        for j in range(RINGS):
            for k in range(GROUP):
                index = (dp ^ k) * RINGS + (fs ^ j)
                at = slice(k * tall, (k + 1) * tall)
                vw[l, pl.ds(pl.multiple_of(index * tall, tall), tall), :] = packs[l, j, at, :width]
                mixn_ref[l, pl.ds(pl.multiple_of(index * small, small), small), :] = packs[
                    l, j, k * tall : k * tall + small, width:
                ]
                vecn[index] = packs[l, j, k * tall + small : (k + 1) * tall, width:].astype(f32)

        def line(r, rep, put, group=False):
            short = vecn[pl.ds(dp * RINGS, RINGS), r, :] if group else vecn[:, r, :]
            return jnp.sum(nn(short.astype(bf16), rep) * put, axis=0, keepdims=True)

        rows_ref[l] = jnp.zeros(rows_ref.shape[1:], f32)
        for r in range(3):
            rows_ref[l, r : r + 1, :] = line(r, rep32[...], put32[...])
        rates = line(3, rep16[...], put16[...])
        rows_ref[l, 3:4, :states] = rates
        rows_ref[l, 4:5, :units] = line(4, rep96[...], put96[...], True)
        rows_ref[l, 4:5, units:width] = line(5, rep16[:, :LANES], put16[:RINGS, :LANES], True)
        rows_ref[l, 5:6, :LANES] = line(6, rep16[:, :LANES], put16[:RINGS, :LANES], True)
        rows_ref[l, 6:7, :units] = line(7, rep96[...], put96[...], True)
        lag = lax.broadcasted_iota(jnp.int32, (tokens, states), 0).astype(f32)
        filt_ref[l] = nn(jnp.exp(-lag * rates).astype(bf16), mixn_ref[l])

    def open_out(l):
        for j in range(RINGS):
            ow[l, pl.ds(pl.multiple_of((fs ^ j) * high, high), high), :] = packs[l, j, top : top + high, :]
            for k in range(GROUP):
                index = (dp ^ k) * RINGS + (fs ^ j)
                at = pl.ds(pl.multiple_of(index * small, small), small)
                for t in range(thirds):
                    r, c = divmod(k * thirds + t, across)
                    base = top + high + small * r
                    ew[l, at, t * 256 : (t + 1) * 256] = packs[
                        l, j, base : base + small, c * 256 : (c + 1) * 256
                    ]

    def normalize(l, read, dst):
        def strip(i, carry):
            at = pl.ds(pl.multiple_of(i * STRIP, STRIP), STRIP)
            v = read(at)
            center = v - jnp.mean(v, axis=1, keepdims=True)
            scale = lax.rsqrt(jnp.mean(center * center, axis=1, keepdims=True) + 1e-05)
            dst[at, :] = (center * scale * rows_ref[l, 0:1, :] + rows_ref[l, 1:2, :]).astype(bf16)
            return carry

        lax.fori_loop(0, tokens // STRIP, strip, 0)

    def branch_in(l, j):
        base = j * tokens
        a_scr[...] = nn(norm[l, j], vw[l])
        age_scr[...] = jnp.broadcast_to(auxs[j, :, 0:1].astype(f32), (tokens, LANES))

        def smooth(i, carry):
            here = pl.ds(pl.multiple_of(i * STRIP, STRIP), STRIP)
            there = pl.ds(pl.multiple_of(base + i * STRIP, STRIP), STRIP)
            v = a_scr[here, :] + rows_ref[l, 4:5, :width]
            cdf = 0.5 + 0.5 * lax.erf(v * 0.7071067811865476)
            slope = cdf + v * (0.3989422804014327 * jnp.exp(-0.5 * v * v))
            act = v * cdf
            value[l, there, :] = act[:, :units].astype(bf16)
            gp[l, there, :] = slope[:, :units].astype(bf16)
            mask = jnp.broadcast_to(auxs[j, here, 2:3].astype(f32), (STRIP, LANES))
            z[l, there, :] = act[:, units:] * mask
            g2[l, there, :] = slope[:, units:] * mask
            return carry

        lax.fori_loop(0, tokens // STRIP, smooth, 0)
        signal = z[l, base : base + tokens, :]
        for b in range(8):
            shifted[b, PAD:, :] = signal if b == 0 else pltpu.roll(signal, b, 0)

        for s in range(tokens // STRIP):
            age = age_scr[s * STRIP : (s + 1) * STRIP, :]

            def lags(a, acc, s=s, age=age):
                start = pl.multiple_of(a * 8, 8)
                left = age - (a * 8).astype(f32)
                for b in range(8):
                    row = filt_ref[l, pl.ds(start + b, 1), :]
                    past = shifted[b, pl.ds(pl.multiple_of(PAD + s * STRIP - start, 8), STRIP), :]
                    acc = acc + jnp.where(left >= b, past, 0.0) * row
                return acc

            y_scr[s * STRIP : (s + 1) * STRIP, :] = lax.fori_loop(
                0, (s + 1) * (STRIP // 8), lags, jnp.zeros((STRIP, LANES), f32)
            )
        ybuf[l, j] = (y_scr[...] + rows_ref[l, 5:6, :LANES] * signal).astype(bf16)

    def branch_out(l, j):
        at = slice(j * tokens, (j + 1) * tokens)
        for k, part in ((0, ybuf[l, j]), (1, yin[l, 0, j ^ 1]), (2, yin[l, 1, j ^ 2]), (3, yin[l, 2, j ^ 3])):
            full[l, at, lanes(dp ^ k, LANES)] = part
        c = nn(full[l, at, :], ew[l]) + rows_ref[l, 6:7, :units]
        product = (c * value[l, at, :].astype(f32)).astype(bf16)
        cbuf[l, at, :] = c.astype(bf16)
        gated[l, at, :] = product
        obuf[j] = nn(product, ow[l]).astype(bf16)

    for b in range(8):
        shifted[b, :PAD, :] = jnp.zeros((PAD, LANES), f32)

    def layer(l, events):
        def due():
            if events:
                events.pop(0)()

        branch_in(l, 0)
        due()
        branch_in(l, 1)
        near = [mail.send(ybuf.at[l, 0:2], yin.at[l, 0, 0:2], CORE)]
        far = [mail.send(ybuf.at[l, 0:2], yin.at[l, 1, 0:2], CHIP)]
        due()
        return near, far

    def layer_rest(l, near, far, events, ready):
        def due():
            if events:
                events.pop(0)()

        branch_in(l, 2)
        due()
        branch_in(l, 3)
        near.append(mail.send(ybuf.at[l, 2:4], yin.at[l, 0, 2:4], CORE))
        far.append(mail.send(ybuf.at[l, 2:4], yin.at[l, 1, 2:4], CHIP))
        far[0].wait_recv()
        relay = [mail.send(yin.at[l, 1, 0:2], yin.at[l, 2, 0:2], CORE)]
        due()
        ready()
        near[1].wait_recv()
        relay[0].wait_recv()
        branch_out(l, 3)
        core_hi = mail.send(obuf.at[3], oin.at[l, 0], CORE)
        branch_out(l, 2)
        core_hi.wait_recv()
        oadd[l] = (obuf[2].astype(f32) + oin[l, 0].astype(f32)).astype(bf16)
        cross = mail.send(oadd.at[l], ofar.at[l], CHIP)
        far[1].wait_recv()
        relay.append(mail.send(yin.at[l, 1, 2:4], yin.at[l, 2, 2:4], CORE))
        near[0].wait_recv()
        relay[1].wait_recv()
        branch_out(l, 1)
        core_lo = mail.send(obuf.at[1], oin.at[l, 1], CORE)
        branch_out(l, 0)
        core_lo.wait_recv()
        due()
        cross.wait_recv()

        def strip(i, carry):
            at = pl.ds(pl.multiple_of(i * STRIP, STRIP), STRIP)
            branch = obuf[0, at, :].astype(f32) + oin[l, 1, at, :].astype(f32) + ofar[l, at, :].astype(f32)
            mask = auxs[0, at, 2:3].astype(f32)
            before = x_ref[at, :].astype(f32) if l == 0 else xcur[at, :]
            now = before + mask * (branch + rows_ref[l, 2:3, :])
            if l == 0:
                xcur[at, :] = now
                later_ref[at, :] = now
            else:
                out_ref[at, :] = now.astype(bf16)
            return carry

        lax.fori_loop(0, tokens // STRIP, strip, 0)
        mail.finish(core_hi)
        mail.finish(core_lo)
        for buf, hbm in ((cbuf, c_hbm), (gated, gated_hbm), (full, full_hbm)):
            spill.put(buf.at[l], hbm.at[l])

    def spill_in(l):
        for buf, hbm in ((norm, norm_hbm), (value, value_hbm), (gp, gp_hbm), (z, z_hbm), (g2, g2_hbm)):
            spill.put(buf.at[l], hbm.at[l])

    for copy in ys:
        copy.wait_recv()
    open_value(0)
    spill.put(vw.at[0], vw_hbm.at[0])
    for copy in aux_in:
        copy.wait_recv()
    x_near.wait_recv()
    for j in (0, 1):
        normalize(0, lambda at, j=j: xin[j, at, :].astype(f32), norm.at[0, j])

    def out_step(k):
        def event():
            zs_out[k - 1].wait_recv()
            ys_out.append(along_y(0, 1, k))

        return event

    more = {}

    def next_value():
        out_step(3)()
        from_group(1, second)
        more["z"] = along_z(1, 0)
        more["y"] = [along_y(1, 0, 0)]

    near, far = layer(0, [out_step(1), out_step(2)])
    x_relay.wait_recv()
    for j in (2, 3):
        normalize(0, lambda at, j=j: xin[j, at, :].astype(f32), norm.at[0, j])
    dout_far = []

    def ready_out():
        for copy in ys_out:
            copy.wait_recv()
        open_out(0)
        spill.put(ow.at[0], ow_hbm.at[0])
        spill.put(ew.at[0], ew_hbm.at[0])

    def value_step():
        for k in range(1, RINGS // 2):
            more["z"][k - 1].wait_recv()
            more["y"].append(along_y(1, 0, k))
        more["z_out"] = along_z(1, 1)
        more["y_out"] = [along_y(1, 1, 0)]

    layer_rest(0, near, far, [next_value, lambda: None, value_step], ready_out)
    spill_in(0)

    for copy in more["y"]:
        copy.wait_recv()
    open_value(1)
    spill.put(vw.at[1], vw_hbm.at[1])
    normalize(1, lambda at: xcur[at, :], norm.at[1, 0])
    n_far = mail.send(norm.at[1, 0], norm.at[1, 2], CHIP)
    n_near = mail.send(norm.at[1, 0], norm.at[1, 1], CORE)

    def relay_norm():
        n_far.wait_recv()
        more["relay"] = mail.send(norm.at[1, 2], norm.at[1, 3], CORE)

    def out_step_two(k):
        def event():
            more["z_out"][k - 1].wait_recv()
            more["y_out"].append(along_y(1, 1, k))

        return event

    n_near.wait_recv()
    near, far = layer(1, [out_step_two(1), relay_norm])
    more["relay"].wait_recv()
    dout_far = mail.send(dout_ref, douts.at[2], CHIP)

    def ready_out_two():
        out_step_two(3)()
        for copy in more["y_out"]:
            copy.wait_recv()
        open_out(1)
        spill.put(ow.at[1], ow_hbm.at[1])
        spill.put(ew.at[1], ew_hbm.at[1])

    def relay_dout():
        dout_far.wait_recv()
        more["dout"] = mail.send(douts.at[2], douts.at[3], CORE)

    layer_rest(1, near, far, [out_step_two(2), relay_dout], ready_out_two)
    spill_in(1)
    dout_near.wait_recv()
    more["dout"].wait_recv()
    spill.put(douts, dout_hbm)
    mail.close()
    spill.close()


def forward_both(arrays, sizes):
    tokens, depth, units, feats, states, tall, small, high = sizes
    width = units + LANES
    group = tokens * GROUP
    rows = tall * GROUP + high + small * GROUP * units // depth
    shape = jax.ShapeDtypeStruct
    two = lambda *dims: (LAYERS,) + dims
    spilled = [
        (two(GROUP, tokens, depth), bf16), (two(group, units), bf16), (two(group, units), bf16),
        (two(group, units), bf16), (two(group, units), bf16), (two(group, feats), bf16),
        (two(group, LANES), f32), (two(group, LANES), f32),
        (two(depth, width), bf16), (two(units, depth), bf16), (two(feats, units), bf16),
        ((GROUP, tokens, depth), bf16),
    ]
    kept = [
        ((tokens, depth), bf16), ((tokens, depth), f32), (two(8, depth), f32), (two(tokens, LANES), f32),
        (two(states, LANES), bf16), ((GROUP, tokens, LANES), bf16),
    ]
    sems = 80
    return pl.pallas_call(
        partial(forward_kernel, sizes),
        out_shape=[shape(*s) for s in kept + spilled],
        in_specs=[pl.BlockSpec(memory_space=VMEM)] * len(arrays),
        out_specs=[pl.BlockSpec(memory_space=VMEM)] * len(kept)
        + [pl.BlockSpec(memory_space=pl.ANY)] * len(spilled),
        scratch_shapes=[
            VMEM(two(GROUP - 1, tall + small, depth), bf16),
            VMEM(two(GROUP - 1, small, depth), bf16),
            VMEM(two(RINGS, rows, depth), bf16),
            VMEM((GROUP * RINGS, tall - small, LANES), f32),
            VMEM(two(depth, width), bf16),
            VMEM(two(units, depth), bf16),
            VMEM(two(feats, units), bf16),
            VMEM((GROUP, tokens, depth), bf16),
            VMEM(two(GROUP, tokens, depth), bf16),
            VMEM((GROUP, tokens, depth), bf16),
            VMEM(two(group, units), bf16),
            VMEM(two(group, units), bf16),
            VMEM(two(group, units), bf16),
            VMEM(two(group, units), bf16),
            VMEM(two(group, feats), bf16),
            VMEM(two(group, LANES), f32),
            VMEM(two(group, LANES), f32),
            VMEM(two(GROUP, tokens, LANES), bf16),
            VMEM(two(GROUP - 1, GROUP, tokens, LANES), bf16),
            VMEM((GROUP, tokens, depth), bf16),
            VMEM(two(2, tokens, depth), bf16),
            VMEM(two(tokens, depth), bf16),
            VMEM(two(tokens, depth), bf16),
            VMEM((tokens, depth), f32),
            VMEM((tokens, width), f32),
            VMEM((tokens, LANES), f32),
            VMEM((8, PAD + tokens, LANES), f32),
            VMEM((tokens, LANES), f32),
            pltpu.SemaphoreType.DMA((sems,)),
            pltpu.SemaphoreType.DMA((sems,)),
            pltpu.SemaphoreType.DMA((32,)),
        ],
        compiler_params=pltpu.CompilerParams(
            vmem_limit_bytes=60 << 20, collective_id=1, has_side_effects=True
        ),
        cost_estimate=cost(120.0),
        name="forward_both",
    )(*arrays)


def mixer(labels, signal, decays, stateinput, stateoutput, skipgain):
    rows = signal.shape[0]
    width = min(32, rows)
    count = rows // width
    mixing = stateinput * stateoutput
    offsets = jnp.arange(width, dtype=jnp.float32)
    powers = jnp.exp(-offsets[:, None] * decays[None, :])
    kernel = jnp.dot(powers, mixing, precision=highest)
    positions = jnp.arange(width, dtype=jnp.int32)
    lagged = jnp.maximum(positions[:, None] - positions[None, :], 0)
    toeplitz = jnp.take(kernel, lagged, axis=0)
    causal = positions[:, None] >= positions[None, :]
    leading = jnp.exp(-(offsets[:, None] + 1.0) * decays[None, :])
    trailing = jnp.exp(-(width - 1.0 - offsets[:, None]) * decays[None, :])
    across = jnp.exp(-width * decays)

    def advance(carry, pieces):
        state, before = carry
        block, marks = pieces
        same = jnp.logical_and(marks[:, None] == marks[None, :], causal).astype(signal.dtype)
        inner = jnp.sum(toeplitz * same[:, :, None] * block[None, :, :], axis=1)
        joined = (marks == before).astype(signal.dtype)
        carried = jnp.dot(leading, mixing * state, precision=highest) * joined[:, None]
        final = marks[width - 1]
        keep = (final == before).astype(signal.dtype)
        fresh = (marks == final).astype(signal.dtype)
        state = across[:, None] * state * keep + lax.dot_general(
            trailing * fresh[:, None], block, rows_dims, precision=highest
        )
        return ((state, final), inner + carried)

    start = (jnp.zeros(mixing.shape, signal.dtype), jnp.array(-1, jnp.int32))
    ending, mixed = lax.scan(
        jax.checkpoint(advance),
        start,
        (signal.reshape(count, width, -1), labels.reshape(count, width)),
    )
    return mixed.reshape(rows, -1) + skipgain[None, :] * signal


def normalize(rows, gain, shift):
    center = rows - jnp.mean(rows, axis=1, keepdims=True)
    spread = jnp.mean(center * center, axis=1, keepdims=True)
    return center * lax.rsqrt(spread + 1e-05) * gain + shift


def smooth(values):
    return jax.nn.gelu(values, approximate=False)


def gather_forward(shards, depth):
    return (
        lax.all_gather(shards[0][depth], ("dp", "fsdp"), axis=0, tiled=True),
        lax.all_gather(shards[1][depth], ("dp", "fsdp"), axis=0, tiled=True),
        lax.all_gather(shards[2][depth], ("dp", "fsdp"), axis=0, tiled=True),
        lax.all_gather(shards[3][depth], ("dp", "fsdp"), axis=0, tiled=True),
        lax.all_gather(shards[4][depth], ("dp", "fsdp"), axis=0, tiled=True),
        lax.all_gather(shards[5][depth], ("dp", "fsdp"), axis=0, tiled=True),
        lax.all_gather(shards[6][depth], ("dp", "fsdp"), axis=0, tiled=True),
        lax.all_gather(shards[7][depth], ("dp", "fsdp"), axis=0, tiled=True),
        lax.all_gather(shards[8][depth], ("dp", "fsdp"), axis=0, tiled=True),
        lax.all_gather(shards[9][depth], ("dp", "fsdp"), axis=0, tiled=True),
        lax.all_gather(shards[10][depth], ("dp", "fsdp"), axis=0, tiled=True),
        lax.all_gather(shards[11][depth], ("dp", "fsdp"), axis=0, tiled=True),
        lax.all_gather(shards[12][depth], ("dp", "fsdp"), axis=0, tiled=True),
        lax.all_gather(shards[13][depth], ("dp", "fsdp"), axis=0, tiled=True),
    )


def gather_backward(shards, depth):
    return (
        lax.all_gather(shards[0][depth], ("dp", "fsdp"), axis=0, tiled=True),
        lax.all_gather(shards[1][depth], ("dp", "fsdp"), axis=0, tiled=True),
        lax.all_gather(shards[2][depth], ("dp", "fsdp"), axis=0, tiled=True),
        lax.all_gather(shards[3][depth], ("dp", "fsdp"), axis=0, tiled=True),
        lax.all_gather(shards[4][depth], ("dp", "fsdp"), axis=0, tiled=True),
        lax.all_gather(shards[5][depth], ("dp", "fsdp"), axis=0, tiled=True),
        lax.all_gather(shards[6][depth], ("dp", "fsdp"), axis=0, tiled=True),
        lax.all_gather(shards[7][depth], ("dp", "fsdp"), axis=0, tiled=True),
        lax.all_gather(shards[8][depth], ("dp", "fsdp"), axis=0, tiled=True),
        lax.all_gather(shards[9][depth], ("dp", "fsdp"), axis=0, tiled=True),
        lax.all_gather(shards[10][depth], ("dp", "fsdp"), axis=0, tiled=True),
        lax.all_gather(shards[11][depth], ("dp", "fsdp"), axis=0, tiled=True),
        lax.all_gather(shards[12][depth], ("dp", "fsdp"), axis=0, tiled=True),
        lax.all_gather(shards[13][depth], ("dp", "fsdp"), axis=0, tiled=True),
    )


def scatter_layer(terms):
    return (
        lax.psum_scatter(terms[0], ("dp", "fsdp"), scatter_dimension=0, tiled=True),
        lax.psum_scatter(terms[1], ("dp", "fsdp"), scatter_dimension=0, tiled=True),
        lax.psum_scatter(terms[2], ("dp", "fsdp"), scatter_dimension=0, tiled=True),
        lax.psum_scatter(terms[3], ("dp", "fsdp"), scatter_dimension=0, tiled=True),
        lax.psum_scatter(terms[4], ("dp", "fsdp"), scatter_dimension=0, tiled=True),
        lax.psum_scatter(terms[5], ("dp", "fsdp"), scatter_dimension=0, tiled=True),
        lax.psum_scatter(terms[6], ("dp", "fsdp"), scatter_dimension=0, tiled=True),
        lax.psum_scatter(terms[7], ("dp", "fsdp"), scatter_dimension=0, tiled=True),
        lax.psum_scatter(terms[8], ("dp", "fsdp"), scatter_dimension=0, tiled=True),
        lax.psum_scatter(terms[9], ("dp", "fsdp"), scatter_dimension=0, tiled=True),
        lax.psum_scatter(terms[10], ("dp", "fsdp"), scatter_dimension=0, tiled=True),
        lax.psum_scatter(terms[11], ("dp", "fsdp"), scatter_dimension=0, tiled=True),
        lax.psum_scatter(terms[12], ("dp", "fsdp"), scatter_dimension=0, tiled=True),
        lax.psum_scatter(terms[13], ("dp", "fsdp"), scatter_dimension=0, tiled=True),
    )


def layer_forward(current, labels, flags, weights):
    (
        normgain,
        normbias,
        valueproj,
        valuebias,
        reduceproj,
        reducebias,
        decays,
        stateinput,
        stateoutput,
        skipgain,
        expandproj,
        expandbias,
        outproj,
        outbias,
    ) = weights
    normed, norm_back = jax.vjp(
        normalize, current, normgain.astype(jnp.float32), normbias.astype(jnp.float32)
    )
    normed_low = normed.astype(jnp.bfloat16)
    opened = jnp.dot(normed_low, valueproj, preferred_element_type=jnp.float32) + valuebias.astype(
        jnp.float32
    )
    values, value_back = jax.vjp(smooth, opened)
    reduced = jnp.dot(
        normed_low, reduceproj, preferred_element_type=jnp.float32
    ) + reducebias.astype(jnp.float32)
    smoothed, reduce_back = jax.vjp(smooth, reduced)
    signal = smoothed * flags
    mixed, mix_back = jax.vjp(
        partial(mixer, labels),
        signal,
        decays.astype(jnp.float32),
        stateinput.astype(jnp.float32),
        stateoutput.astype(jnp.float32),
        skipgain.astype(jnp.float32),
    )
    mixed_low = mixed.astype(jnp.bfloat16)
    expanded = jnp.dot(
        mixed_low, expandproj, preferred_element_type=jnp.float32
    ) + expandbias.astype(jnp.float32)
    gated = (expanded * values).astype(jnp.bfloat16)
    branch = jnp.dot(gated, outproj, preferred_element_type=jnp.float32) + outbias.astype(
        jnp.float32
    )
    saved = (
        normed_low,
        values,
        value_back,
        reduce_back,
        mix_back,
        mixed_low,
        expanded,
        gated,
        norm_back,
    )
    return (current + flags * branch, saved)


def layer_backward(upstream, flags, weights, saved):
    (
        normgain,
        normbias,
        valueproj,
        valuebias,
        reduceproj,
        reducebias,
        decays,
        stateinput,
        stateoutput,
        skipgain,
        expandproj,
        expandbias,
        outproj,
        outbias,
    ) = weights
    normed_low, values, value_back, reduce_back, mix_back, mixed_low, expanded, gated, norm_back = (
        saved
    )
    dout = (flags * upstream).astype(jnp.bfloat16)
    outproj_term = lax.dot_general(gated, dout, rows_dims, preferred_element_type=jnp.float32)
    outbias_term = jnp.sum(dout, axis=0, dtype=jnp.float32)
    dgated = lax.dot_general(dout, outproj, cols_dims, preferred_element_type=jnp.float32)
    dexpanded = (dgated * values).astype(jnp.bfloat16)
    dvalues = dgated * expanded
    expandproj_term = lax.dot_general(
        mixed_low, dexpanded, rows_dims, preferred_element_type=jnp.float32
    )
    expandbias_term = jnp.sum(dexpanded, axis=0, dtype=jnp.float32)
    dmixed = lax.dot_general(dexpanded, expandproj, cols_dims, preferred_element_type=jnp.float32)
    dsignal, decays_term, stateinput_term, stateoutput_term, skipgain_term = mix_back(dmixed)
    (dreduced,) = reduce_back(dsignal * flags)
    dreduced_low = dreduced.astype(jnp.bfloat16)
    (dopened,) = value_back(dvalues)
    dopened_low = dopened.astype(jnp.bfloat16)
    valueproj_term = lax.dot_general(
        normed_low, dopened_low, rows_dims, preferred_element_type=jnp.float32
    )
    valuebias_term = jnp.sum(dopened_low, axis=0, dtype=jnp.float32)
    reduceproj_term = lax.dot_general(
        normed_low, dreduced_low, rows_dims, preferred_element_type=jnp.float32
    )
    reducebias_term = jnp.sum(dreduced_low, axis=0, dtype=jnp.float32)
    dnormed = lax.dot_general(dopened_low, valueproj, cols_dims, preferred_element_type=jnp.float32)
    dnormed = dnormed + lax.dot_general(
        dreduced_low, reduceproj, cols_dims, preferred_element_type=jnp.float32
    )
    dcurrent, normgain_term, normbias_term = norm_back(dnormed)
    terms = (
        normgain_term,
        normbias_term,
        valueproj_term,
        valuebias_term,
        reduceproj_term,
        reducebias_term,
        decays_term,
        stateinput_term,
        stateoutput_term,
        skipgain_term,
        expandproj_term,
        expandbias_term,
        outproj_term,
        outbias_term,
    )
    return (upstream + dcurrent, terms)


def plain(
    inputs,
    segment_ids,
    token_mask,
    cotangent,
    normgain,
    normbias,
    valueproj,
    valuebias,
    reduceproj,
    reducebias,
    decays,
    stateinput,
    stateoutput,
    skipgain,
    expandproj,
    expandbias,
    outproj,
    outbias,
):
    shards = (
        normgain,
        normbias,
        valueproj,
        valuebias,
        reduceproj,
        reducebias,
        decays,
        stateinput,
        stateoutput,
        skipgain,
        expandproj,
        expandbias,
        outproj,
        outbias,
    )
    flags = token_mask.astype(jnp.float32)[:, None]
    current = inputs.astype(jnp.float32)
    fetched = []
    stored = []
    for depth in range(LAYERS):
        weights = gather_forward(shards, depth)
        current, saved = layer_forward(current, segment_ids, flags, weights)
        fetched.append(weights)
        stored.append(saved)
    outputs = current.astype(jnp.bfloat16)
    upstream = cotangent.astype(jnp.float32)
    scattered = [None] * LAYERS
    for depth in reversed(range(LAYERS)):
        weights = gather_backward(shards, depth)
        upstream, terms = layer_backward(upstream, flags, weights, stored[depth])
        scattered[depth] = scatter_layer(terms)
    results = tuple(
        (jnp.stack([scattered[depth][index] for depth in range(LAYERS)]) for index in range(14))
    )
    return (outputs, upstream) + tuple(results)


def fast(
    inputs, segment_ids, token_mask, cotangent, normgain, normbias, valueproj, valuebias,
    reduceproj, reducebias, decays, stateinput, stateoutput, skipgain, expandproj, expandbias,
    outproj, outbias,
):
    dp, fs = lax.axis_index("dp"), lax.axis_index("fsdp")
    me = jnp.stack([dp, fs]).astype(jnp.int32)
    tokens, depth = inputs.shape
    tall = valueproj.shape[1]
    small = stateinput.shape[1]
    high = outproj.shape[1]
    units = valueproj.shape[2] // GROUP
    feats = reduceproj.shape[2]
    states = feats
    devices = GROUP * RINGS
    group = tokens * GROUP
    flags = token_mask.astype(f32)[:, None]
    sizes = (tokens, depth, units, feats, states, tall, small, high)

    same = (segment_ids[:, None] == segment_ids[None, :]).astype(f32)
    spot = jnp.arange(tokens)
    before = (spot[None, :] < spot[:, None]).astype(f32)
    age = jnp.sum(same * before, axis=1)
    rest = jnp.sum(same * (1.0 - before), axis=1) - 1.0
    aux = jnp.pad(jnp.stack([age, rest, token_mask.astype(f32)], axis=1), ((0, 0), (0, LANES - 3)))
    upstream = cotangent.astype(f32)
    dout = (flags * upstream).astype(bf16)
    shorts = (normgain, normbias, outbias, decays, valuebias, reducebias, skipgain, expandbias)
    vec = jnp.stack([jnp.pad(v, ((0, 0), (0, LANES - v.shape[1]))) for v in shorts], axis=1)
    vec = jnp.pad(vec, ((0, 0), (0, tall - small - len(shorts)), (0, 0)))

    (
        outputs, later, rows, filt, mixes, auxes,
        norms, value, slope, gate, gated, full, z, slope2, value_w, out_w, expand_w, douts,
    ) = forward_both(
        (
            inputs, aux.astype(bf16), dout, valueproj, reduceproj, expandproj, outproj,
            stateinput, stateoutput, vec, *tables(devices),
        ),
        sizes,
    )
    half = tokens * 2
    douts = [douts[k] for k in range(GROUP)]
    auxes = [auxes[k] for k in range(GROUP)]
    lagged = jnp.arange(tokens, dtype=f32)

    value_grads, out_grads, sums_all, sums_rest = [None] * 2, [None] * 2, [None] * 2, [None] * 2
    for l in reversed(range(LAYERS)):
        current = inputs.astype(f32) if l == 0 else later
        center = current - jnp.mean(current, axis=1, keepdims=True)
        rstd = lax.rsqrt(jnp.mean(center * center, axis=1, keepdims=True) + 1e-05)
        normed = center * rstd
        gain = rows[l, 0:1, :]
        skip = rows[l, 5:6, :LANES]
        powers = jnp.exp(-lagged[:, None] * rows[l, 3:4, :states]).astype(bf16)
        lo = [a[l, :half] for a in (value, slope, z, slope2)]
        hi = [a[l, half:] for a in (value, slope, z, slope2)]
        out_lo = [a[l, :half] for a in (gate, gated, full)]
        out_hi = [a[l, half:] for a in (gate, gated, full)]
        if l < LAYERS - 1:
            dout = (flags * upstream).astype(bf16)
            douts = gather_group(dout)
        back_lo = backward_out(me, *douts[:2], out_w[l], expand_w[l], lo[0], lo[1], out_lo[0])
        near_lo = swap(back_lo[3], RINGS)
        far_lo = swap((back_lo[2][1].astype(f32) + near_lo[1].astype(f32)).astype(bf16), 2 * RINGS)
        back_hi = backward_out(me, *douts[2:], out_w[l], expand_w[l], hi[0], hi[1], out_hi[0])
        near_hi = swap(back_hi[3], RINGS)
        far_hi = swap((back_hi[2][1].astype(f32) + near_hi[1].astype(f32)).astype(bf16), 2 * RINGS)
        in_hi = backward_in(
            back_hi[2], near_hi, far_lo, hi[2], hi[3], back_hi[1], filt[l], skip, *auxes[2:], value_w[l]
        )
        in_lo = backward_in(
            back_lo[2], near_lo, far_hi, lo[2], lo[3], back_lo[1], filt[l], skip, *auxes[:2], value_w[l]
        )
        dnrm = return_group(in_lo[1:3], in_hi[1:3])
        out_grads[l] = reduce_rest(
            grads_out(
                me, (out_lo[1], out_hi[1]), douts, (out_lo[2], out_hi[2]), (back_lo[0], back_hi[0]), high, small
            )
        )
        corr = jnp.sum(in_lo[3] + in_hi[3], axis=1)
        *packs, terms = grads_in(
            me, [norms[l, k] for k in range(GROUP)], (in_lo[0], in_hi[0]), powers, corr, mixes[l], tall, small
        )
        value_grads[l] = reduce_rest(packs)
        gain_term = jnp.sum(dnrm * normed, axis=0)
        shift_term = jnp.sum(dnrm, axis=0)
        out_term = jnp.sum(dout.astype(f32), axis=0)
        q = dnrm * gain
        tilt = q - jnp.mean(q, axis=1, keepdims=True) - normed * jnp.mean(q * normed, axis=1, keepdims=True)
        upstream = upstream + tilt * rstd
        sums_all[l] = jnp.concatenate([gain_term, shift_term, out_term, jnp.sum(terms, axis=1)]).reshape(-1, LANES)
        sums_rest[l] = jnp.concatenate(
            [
                (in_lo[4] + in_hi[4]).reshape(-1, LANES),
                (back_lo[4] + back_hi[4]).reshape(-1, LANES),
                in_lo[5] + in_hi[5],
            ]
        )

    pieces, expands, outs = [], [], []
    for l in range(LAYERS):
        g = value_grads[l]
        parts = []
        for k in range(GROUP):
            part = jnp.concatenate([g[k * tall : (k + 1) * tall], g[GROUP * tall :]], axis=0).astype(bf16)
            parts.append(swap(part, k * RINGS) if k else part)
        pieces.append(parts)
        g = out_grads[l]
        parts = []
        for k in range(GROUP):
            blocks = []
            for t in range(units // 256):
                r, c = divmod(k * (units // 256) + t, depth // 256)
                blocks.append(g[high + small * r : high + small * (r + 1), c * 256 : (c + 1) * 256])
            part = jnp.concatenate(blocks, axis=1).astype(bf16)
            parts.append(swap(part, k * RINGS) if k else part)
        expands.append(parts)
        outs.append(g[:high])
    valueproj_grad, reduceproj_grad, stateinput_grad, stateoutput_grad, expandproj_grad, outproj_grad = finish(
        me, pieces, expands, outs, stateinput, stateoutput
    )

    vectors = []
    for l in range(LAYERS):
        head = sums_all[l].shape[0]
        packed = all_rest(jnp.pad(jnp.concatenate([sums_all[l], sums_rest[l]]), ((0, 6), (0, 0))))
        shared = all_group(packed[:head]).reshape(-1)
        mine = packed[head:].reshape(-1)
        index = dp * RINGS + fs
        take = lambda array, start, n, at: lax.dynamic_slice_in_dim(array, start + at * n, n, 0)
        vectors.append(
            (
                take(shared, 0, depth // devices, index),
                take(shared, depth, depth // devices, index),
                take(mine, 0, units // RINGS, fs),
                take(mine, units, LANES // RINGS, fs),
                take(shared, 3 * depth, states // devices, index),
                take(mine, 2 * units + LANES, LANES // RINGS, fs),
                take(mine, units + LANES, units // RINGS, fs),
                take(shared, 2 * depth, depth // devices, index),
            )
        )
    gain_g, shift_g, vbias_g, rbias_g, decays_g, skip_g, ebias_g, obias_g = (
        jnp.stack([vectors[l][i] for l in range(LAYERS)]) for i in range(8)
    )
    return (
        outputs, upstream, gain_g, shift_g, valueproj_grad, vbias_g, reduceproj_grad, rbias_g, decays_g,
        stateinput_grad, stateoutput_grad, skip_g, expandproj_grad, ebias_g, outproj_grad, obias_g,
    )


def solution(mesh):
    placed = (
        P(("dp", "fsdp"), None),
        P(("dp", "fsdp")),
        P(("dp", "fsdp")),
        P(("dp", "fsdp"), None),
        P(None, ("dp", "fsdp")),
        P(None, ("dp", "fsdp")),
        P(None, ("dp", "fsdp"), None),
        P(None, ("dp", "fsdp")),
        P(None, ("dp", "fsdp"), None),
        P(None, ("dp", "fsdp")),
        P(None, ("dp", "fsdp")),
        P(None, ("dp", "fsdp"), None),
        P(None, ("dp", "fsdp"), None),
        P(None, ("dp", "fsdp")),
        P(None, ("dp", "fsdp"), None),
        P(None, ("dp", "fsdp")),
        P(None, ("dp", "fsdp"), None),
        P(None, ("dp", "fsdp")),
    )
    small = mesh.shape["dp"] == GROUP and mesh.shape["fsdp"] == RINGS
    return jax.shard_map(
        fast if small else plain,
        mesh=mesh,
        in_specs=placed,
        out_specs=(
            P(("dp", "fsdp"), None),
            P(("dp", "fsdp"), None),
            P(None, ("dp", "fsdp")),
            P(None, ("dp", "fsdp")),
            P(None, ("dp", "fsdp"), None),
            P(None, ("dp", "fsdp")),
            P(None, ("dp", "fsdp"), None),
            P(None, ("dp", "fsdp")),
            P(None, ("dp", "fsdp")),
            P(None, ("dp", "fsdp"), None),
            P(None, ("dp", "fsdp"), None),
            P(None, ("dp", "fsdp")),
            P(None, ("dp", "fsdp"), None),
            P(None, ("dp", "fsdp")),
            P(None, ("dp", "fsdp"), None),
            P(None, ("dp", "fsdp")),
        ),
        check_vma=False,
    )
```

```python
from functools import partial

import jax
import jax.numpy as jnp
import numpy as np
from jax import lax
from jax.experimental import pallas as pl
from jax.experimental.pallas import tpu as pltpu
from jax.sharding import PartitionSpec as P

LAYERS = 2
AXES = ("dp", "fsdp")
GROUP = 4
RINGS = 8
LANES = 128
STRIP = 32
PAD = 32

f32 = jnp.float32
bf16 = jnp.bfloat16
highest = lax.Precision.HIGHEST
rows_dims = (((0,), (0,)), ((), ()))
cols_dims = (((1,), (1,)), ((), ()))

VMEM = pltpu.VMEM


def cost(micros):
    return pl.CostEstimate(
        flops=int(micros * 1.0e9), bytes_accessed=1 << 20, transcendentals=0
    )


def nt(a, b):
    return lax.dot_general(a, b, cols_dims, preferred_element_type=f32)


def tn(a, b):
    return lax.dot_general(a, b, rows_dims, preferred_element_type=f32)


def nn(a, b):
    return jnp.dot(a, b, preferred_element_type=f32)


def tables(devices):
    out = []
    for count, size in ((devices, 32), (RINGS, 96), (devices, 16)):
        at = np.arange(count * size)
        out.append(jnp.asarray((np.arange(LANES)[:, None] == at[None, :] % size), bf16))
        out.append(jnp.asarray((np.arange(count)[:, None] == at[None, :] // size), f32))
    return out


class Mail:
    def __init__(self, send_sem, recv_sem):
        self.dp, self.fs = lax.axis_index("dp"), lax.axis_index("fsdp")
        self.send_sem, self.recv_sem, self.count, self.sent = send_sem, recv_sem, 0, []

    def peer(self, flip):
        return (self.dp ^ (flip // RINGS), self.fs ^ (flip % RINGS))

    def greet(self, flips):
        barrier = pltpu.get_barrier_semaphore()
        for flip in flips:
            pl.semaphore_signal(
                barrier, inc=1, device_id=self.peer(flip), device_id_type=pl.DeviceIdType.MESH
            )
        pl.semaphore_wait(barrier, len(flips))

    def send(self, src, dst, flip):
        copy = pltpu.make_async_remote_copy(
            src_ref=src, dst_ref=dst, send_sem=self.send_sem.at[self.count],
            recv_sem=self.recv_sem.at[self.count], device_id=self.peer(flip),
            device_id_type=pl.DeviceIdType.MESH,
        )
        self.count += 1
        copy.start()
        self.sent.append(copy)
        return copy

    def finish(self, copy):
        copy.wait_send()
        self.sent = [c for c in self.sent if c is not copy]

    def close(self):
        for copy in self.sent:
            copy.wait_send()


class Spill:
    def __init__(self, sem):
        self.sem, self.open = sem, []

    def put(self, src, dst):
        copy = pltpu.make_async_copy(src, dst, self.sem.at[len(self.open)])
        copy.start()
        self.open.append(copy)

    def close(self):
        for copy in self.open:
            copy.wait()


CORE, CHIP, BOTH = RINGS, 2 * RINGS, 3 * RINGS
FLIPS = (CORE, CHIP, BOTH, 1, 2, 4, 6)


def forward_kernel(sizes, *refs):
    tokens, depth, units, feats, states, tall, small, high = sizes
    width = units + LANES
    top = tall * GROUP
    rows = top + high + small * GROUP * units // depth
    (
        x_ref, aux_ref, dout_ref, v_ref, r_ref, e_ref, o_ref, si_ref, so_ref, vec_ref,
        rep32, put32, rep96, put96, rep16, put16,
    ) = refs[:16]
    (
        out_ref, later_ref, rows_ref, filt_ref, mixn_ref, auxs,
        norm_hbm, value_hbm, gp_hbm, c_hbm, full_hbm, z_hbm, g2_hbm,
        vw_hbm, ow_hbm, ew_hbm, dout_hbm,
    ) = refs[16:33]
    (
        pieces, ein, packs, vecn, vw, ow, ew, xin, norm, douts,
        value, gp, cbuf, full, z, g2, ybuf, yin, obuf, oin, oadd, ofar, xcur,
        a_scr, age_scr, shifted, y_scr, send_sem, recv_sem, hbm_sem,
    ) = refs[33:]
    mail = Mail(send_sem, recv_sem)
    spill = Spill(hbm_sem)
    dp, fs = mail.dp, mail.fs
    thirds = units // 256
    across = depth // 256

    def lanes(index, size):
        return pl.ds(pl.multiple_of(index * size, LANES), size)

    def place_expand(l, k, part):
        for t in range(thirds):
            r, c = divmod(k * thirds + t, across)
            at = top + high + small * r
            packs[l, 0, at : at + small, c * 256 : (c + 1) * 256] = part[:, t * 256 : (t + 1) * 256]

    for l in range(LAYERS):
        mixing = (si_ref[l].astype(f32) * so_ref[l].astype(f32)).astype(bf16)
        a_scr[:small, :feats] = mixing.astype(f32)
        for k in range(GROUP):
            q = dp ^ k
            dst = packs.at[l, 0, 0:tall] if k == 0 else pieces.at[l, k - 1, 0:tall]
            dst[:, :units] = v_ref[l, :, lanes(q, units)]
            dst[:, units:width] = r_ref[l, :, lanes(q, LANES)]
            dst[:small, width:] = a_scr[:small, lanes(q, LANES)].astype(bf16)
            dst[small:, width:] = vec_ref[l]
            part = e_ref[l, :, lanes(q, units)]
            if k == 0:
                place_expand(l, 0, part)
            else:
                pieces[l, k - 1, tall:, :units] = part
                pieces[l, k - 1, tall:, units:] = jnp.zeros((small, depth - units), bf16)
        packs[l, 0, top : top + high, :] = o_ref[l]
    xin[0] = x_ref[...]
    auxs[0] = aux_ref[...]
    douts[0] = dout_ref[...]

    mail.greet(FLIPS)

    def to_group(l, ks):
        return [
            (
                k,
                mail.send(pieces.at[l, k - 1, 0:tall], packs.at[l, 0, k * tall : (k + 1) * tall], k * RINGS),
                mail.send(pieces.at[l, k - 1, tall : tall + small], ein.at[l, k - 1], k * RINGS),
            )
            for k in ks
        ]

    def from_group(l, copies):
        for k, one, two in copies:
            one.wait_recv()
            two.wait_recv()
            place_expand(l, k, ein[l, k - 1, :, :units])

    def part_rows(part):
        return slice(0, top) if part == 0 else slice(top, rows)

    def along_z(l, part):
        at = part_rows(part)
        return [mail.send(packs.at[l, 0, at], packs.at[l, 2 * k, at], 2 * k) for k in range(1, RINGS // 2)]

    def along_y(l, part, k):
        at = part_rows(part)
        return mail.send(packs.at[l, 2 * k, at], packs.at[l, 2 * k + 1, at], 1)

    first = to_group(0, (2, 3, 1))
    aux_in = [mail.send(aux_ref, auxs.at[k], k * RINGS) for k in (1, 2, 3)]
    x_near = mail.send(x_ref, xin.at[1], CORE)
    from_group(0, first)
    zs = along_z(0, 0)
    ys = [along_y(0, 0, 0)]
    x_far = mail.send(x_ref, xin.at[2], CHIP)
    second = to_group(1, (1,))
    for k in range(1, RINGS // 2):
        zs[k - 1].wait_recv()
        ys.append(along_y(0, 0, k))
    zs_out = along_z(0, 1)
    ys_out = [along_y(0, 1, 0)]
    x_far.wait_recv()
    x_relay = mail.send(xin.at[2], xin.at[3], CORE)
    second += to_group(1, (2, 3))
    dout_near = mail.send(dout_ref, douts.at[1], CORE)

    def open_value(l):
        for j in range(RINGS):
            for k in range(GROUP):
                index = (dp ^ k) * RINGS + (fs ^ j)
                at = slice(k * tall, (k + 1) * tall)
                vw[l, pl.ds(pl.multiple_of(index * tall, tall), tall), :] = packs[l, j, at, :width]
                mixn_ref[l, pl.ds(pl.multiple_of(index * small, small), small), :] = packs[
                    l, j, k * tall : k * tall + small, width:
                ]
                vecn[index] = packs[l, j, k * tall + small : (k + 1) * tall, width:].astype(f32)

        def line(r, rep, put, group=False):
            short = vecn[pl.ds(dp * RINGS, RINGS), r, :] if group else vecn[:, r, :]
            return jnp.sum(nn(short.astype(bf16), rep) * put, axis=0, keepdims=True)

        rows_ref[l] = jnp.zeros(rows_ref.shape[1:], f32)
        for r in range(3):
            rows_ref[l, r : r + 1, :] = line(r, rep32[...], put32[...])
        rates = line(3, rep16[...], put16[...])
        rows_ref[l, 3:4, :states] = rates
        rows_ref[l, 4:5, :units] = line(4, rep96[...], put96[...], True)
        rows_ref[l, 4:5, units:width] = line(5, rep16[:, :LANES], put16[:RINGS, :LANES], True)
        rows_ref[l, 5:6, :LANES] = line(6, rep16[:, :LANES], put16[:RINGS, :LANES], True)
        rows_ref[l, 6:7, :units] = line(7, rep96[...], put96[...], True)
        lag = lax.broadcasted_iota(jnp.int32, (tokens, states), 0).astype(f32)
        filt_ref[l] = nn(jnp.exp(-lag * rates).astype(bf16), mixn_ref[l])

    def open_out(l):
        for j in range(RINGS):
            ow[l, pl.ds(pl.multiple_of((fs ^ j) * high, high), high), :] = packs[l, j, top : top + high, :]
            for k in range(GROUP):
                index = (dp ^ k) * RINGS + (fs ^ j)
                at = pl.ds(pl.multiple_of(index * small, small), small)
                for t in range(thirds):
                    r, c = divmod(k * thirds + t, across)
                    base = top + high + small * r
                    ew[l, at, t * 256 : (t + 1) * 256] = packs[
                        l, j, base : base + small, c * 256 : (c + 1) * 256
                    ]

    def normalize(l, read, dst):
        def strip(i, carry):
            at = pl.ds(pl.multiple_of(i * STRIP, STRIP), STRIP)
            v = read(at)
            center = v - jnp.mean(v, axis=1, keepdims=True)
            scale = lax.rsqrt(jnp.mean(center * center, axis=1, keepdims=True) + 1e-05)
            dst[at, :] = (center * scale * rows_ref[l, 0:1, :] + rows_ref[l, 1:2, :]).astype(bf16)
            return carry

        lax.fori_loop(0, tokens // STRIP, strip, 0)

    def branch_in(l, j):
        base = j * tokens
        a_scr[...] = nn(norm[l, j], vw[l])
        age_scr[...] = jnp.broadcast_to(auxs[j, :, 0:1].astype(f32), (tokens, LANES))

        def smooth(i, carry):
            here = pl.ds(pl.multiple_of(i * STRIP, STRIP), STRIP)
            there = pl.ds(pl.multiple_of(base + i * STRIP, STRIP), STRIP)
            v = a_scr[here, :] + rows_ref[l, 4:5, :width]
            cdf = 0.5 + 0.5 * lax.erf(v * 0.7071067811865476)
            slope = cdf + v * (0.3989422804014327 * jnp.exp(-0.5 * v * v))
            act = v * cdf
            value[l, there, :] = act[:, :units].astype(bf16)
            gp[l, there, :] = slope[:, :units].astype(bf16)
            mask = jnp.broadcast_to(auxs[j, here, 2:3].astype(f32), (STRIP, LANES))
            z[l, there, :] = act[:, units:] * mask
            g2[l, there, :] = slope[:, units:] * mask
            return carry

        lax.fori_loop(0, tokens // STRIP, smooth, 0)
        signal = z[l, base : base + tokens, :]
        for b in range(8):
            shifted[b, PAD:, :] = signal if b == 0 else pltpu.roll(signal, b, 0)

        for s in range(tokens // STRIP):
            age = age_scr[s * STRIP : (s + 1) * STRIP, :]

            def lags(a, acc, s=s, age=age):
                start = pl.multiple_of(a * 8, 8)
                left = age - (a * 8).astype(f32)
                for b in range(8):
                    row = filt_ref[l, pl.ds(start + b, 1), :]
                    past = shifted[b, pl.ds(pl.multiple_of(PAD + s * STRIP - start, 8), STRIP), :]
                    acc = acc + jnp.where(left >= b, past, 0.0) * row
                return acc

            y_scr[s * STRIP : (s + 1) * STRIP, :] = lax.fori_loop(
                0, (s + 1) * (STRIP // 8), lags, jnp.zeros((STRIP, LANES), f32)
            )
        ybuf[l, j] = (y_scr[...] + rows_ref[l, 5:6, :LANES] * signal).astype(bf16)

    def branch_out(l, j):
        at = slice(j * tokens, (j + 1) * tokens)
        for k, part in ((0, ybuf[l, j]), (1, yin[l, 0, j ^ 1]), (2, yin[l, 1, j ^ 2]), (3, yin[l, 2, j ^ 3])):
            full[l, at, lanes(dp ^ k, LANES)] = part
        c = nn(full[l, at, :], ew[l]) + rows_ref[l, 6:7, :units]
        product = (c * value[l, at, :].astype(f32)).astype(bf16)
        cbuf[l, at, :] = c.astype(bf16)
        obuf[j] = nn(product, ow[l]).astype(bf16)

    for b in range(8):
        shifted[b, :PAD, :] = jnp.zeros((PAD, LANES), f32)

    def layer(l, events):
        def due():
            if events:
                events.pop(0)()

        branch_in(l, 0)
        due()
        branch_in(l, 1)
        near = [mail.send(ybuf.at[l, 0:2], yin.at[l, 0, 0:2], CORE)]
        far = [mail.send(ybuf.at[l, 0:2], yin.at[l, 1, 0:2], CHIP)]
        due()
        return near, far

    def layer_rest(l, near, far, events, ready):
        def due():
            if events:
                events.pop(0)()

        branch_in(l, 2)
        due()
        branch_in(l, 3)
        near.append(mail.send(ybuf.at[l, 2:4], yin.at[l, 0, 2:4], CORE))
        far.append(mail.send(ybuf.at[l, 2:4], yin.at[l, 1, 2:4], CHIP))
        far[0].wait_recv()
        relay = [mail.send(yin.at[l, 1, 0:2], yin.at[l, 2, 0:2], CORE)]
        due()
        ready()
        near[1].wait_recv()
        relay[0].wait_recv()
        branch_out(l, 3)
        core_hi = mail.send(obuf.at[3], oin.at[l, 0], CORE)
        branch_out(l, 2)
        core_hi.wait_recv()
        oadd[l] = (obuf[2].astype(f32) + oin[l, 0].astype(f32)).astype(bf16)
        cross = mail.send(oadd.at[l], ofar.at[l], CHIP)
        far[1].wait_recv()
        relay.append(mail.send(yin.at[l, 1, 2:4], yin.at[l, 2, 2:4], CORE))
        near[0].wait_recv()
        relay[1].wait_recv()
        branch_out(l, 1)
        core_lo = mail.send(obuf.at[1], oin.at[l, 1], CORE)
        branch_out(l, 0)
        core_lo.wait_recv()
        due()
        cross.wait_recv()

        def strip(i, carry):
            at = pl.ds(pl.multiple_of(i * STRIP, STRIP), STRIP)
            branch = obuf[0, at, :].astype(f32) + oin[l, 1, at, :].astype(f32) + ofar[l, at, :].astype(f32)
            mask = auxs[0, at, 2:3].astype(f32)
            before = x_ref[at, :].astype(f32) if l == 0 else xcur[at, :]
            now = before + mask * (branch + rows_ref[l, 2:3, :])
            if l == 0:
                xcur[at, :] = now
                later_ref[at, :] = now
            else:
                out_ref[at, :] = now.astype(bf16)
            return carry

        lax.fori_loop(0, tokens // STRIP, strip, 0)
        mail.finish(core_hi)
        mail.finish(core_lo)
        for buf, hbm in ((cbuf, c_hbm), (full, full_hbm)):
            spill.put(buf.at[l], hbm.at[l])

    def spill_in(l):
        for buf, hbm in ((norm, norm_hbm), (value, value_hbm), (gp, gp_hbm), (z, z_hbm), (g2, g2_hbm)):
            spill.put(buf.at[l], hbm.at[l])

    for copy in ys:
        copy.wait_recv()
    open_value(0)
    spill.put(vw.at[0], vw_hbm.at[0])
    for copy in aux_in:
        copy.wait_recv()
    x_near.wait_recv()
    for j in (0, 1):
        normalize(0, lambda at, j=j: xin[j, at, :].astype(f32), norm.at[0, j])

    def out_step(k):
        def event():
            zs_out[k - 1].wait_recv()
            ys_out.append(along_y(0, 1, k))

        return event

    more = {}

    def next_value():
        out_step(3)()
        from_group(1, second)
        more["z"] = along_z(1, 0)
        more["y"] = [along_y(1, 0, 0)]

    near, far = layer(0, [out_step(1), out_step(2)])
    x_relay.wait_recv()
    for j in (2, 3):
        normalize(0, lambda at, j=j: xin[j, at, :].astype(f32), norm.at[0, j])
    dout_far = []

    def ready_out():
        for copy in ys_out:
            copy.wait_recv()
        open_out(0)
        spill.put(ow.at[0], ow_hbm.at[0])
        spill.put(ew.at[0], ew_hbm.at[0])

    def value_step():
        for k in range(1, RINGS // 2):
            more["z"][k - 1].wait_recv()
            more["y"].append(along_y(1, 0, k))
        more["z_out"] = along_z(1, 1)
        more["y_out"] = [along_y(1, 1, 0)]

    layer_rest(0, near, far, [next_value, lambda: None, value_step], ready_out)
    spill_in(0)

    for copy in more["y"]:
        copy.wait_recv()
    open_value(1)
    spill.put(vw.at[1], vw_hbm.at[1])
    normalize(1, lambda at: xcur[at, :], norm.at[1, 0])
    n_far = mail.send(norm.at[1, 0], norm.at[1, 2], CHIP)
    n_near = mail.send(norm.at[1, 0], norm.at[1, 1], CORE)

    def relay_norm():
        n_far.wait_recv()
        more["relay"] = mail.send(norm.at[1, 2], norm.at[1, 3], CORE)

    def out_step_two(k):
        def event():
            more["z_out"][k - 1].wait_recv()
            more["y_out"].append(along_y(1, 1, k))

        return event

    n_near.wait_recv()
    near, far = layer(1, [out_step_two(1), relay_norm])
    more["relay"].wait_recv()
    dout_far = mail.send(dout_ref, douts.at[2], CHIP)

    def ready_out_two():
        out_step_two(3)()
        for copy in more["y_out"]:
            copy.wait_recv()
        open_out(1)
        spill.put(ow.at[1], ow_hbm.at[1])
        spill.put(ew.at[1], ew_hbm.at[1])

    def relay_dout():
        dout_far.wait_recv()
        more["dout"] = mail.send(douts.at[2], douts.at[3], CORE)

    layer_rest(1, near, far, [out_step_two(2), relay_dout], ready_out_two)
    spill_in(1)
    dout_near.wait_recv()
    more["dout"].wait_recv()
    spill.put(douts, dout_hbm)
    mail.close()
    spill.close()


def forward_both(arrays, sizes):
    tokens, depth, units, feats, states, tall, small, high = sizes
    width = units + LANES
    group = tokens * GROUP
    rows = tall * GROUP + high + small * GROUP * units // depth
    shape = jax.ShapeDtypeStruct
    two = lambda *dims: (LAYERS,) + dims
    spilled = [
        (two(GROUP, tokens, depth), bf16), (two(group, units), bf16), (two(group, units), bf16),
        (two(group, units), bf16), (two(group, feats), bf16),
        (two(group, LANES), f32), (two(group, LANES), f32),
        (two(depth, width), bf16), (two(units, depth), bf16), (two(feats, units), bf16),
        ((GROUP, tokens, depth), bf16),
    ]
    kept = [
        ((tokens, depth), bf16), ((tokens, depth), f32), (two(8, depth), f32), (two(tokens, LANES), f32),
        (two(states, LANES), bf16), ((GROUP, tokens, LANES), bf16),
    ]
    sems = 80
    return pl.pallas_call(
        partial(forward_kernel, sizes),
        out_shape=[shape(*s) for s in kept + spilled],
        in_specs=[pl.BlockSpec(memory_space=VMEM)] * len(arrays),
        out_specs=[pl.BlockSpec(memory_space=VMEM)] * len(kept)
        + [pl.BlockSpec(memory_space=pl.ANY)] * len(spilled),
        scratch_shapes=[
            VMEM(two(GROUP - 1, tall + small, depth), bf16),
            VMEM(two(GROUP - 1, small, depth), bf16),
            VMEM(two(RINGS, rows, depth), bf16),
            VMEM((GROUP * RINGS, tall - small, LANES), f32),
            VMEM(two(depth, width), bf16),
            VMEM(two(units, depth), bf16),
            VMEM(two(feats, units), bf16),
            VMEM((GROUP, tokens, depth), bf16),
            VMEM(two(GROUP, tokens, depth), bf16),
            VMEM((GROUP, tokens, depth), bf16),
            VMEM(two(group, units), bf16),
            VMEM(two(group, units), bf16),
            VMEM(two(group, units), bf16),
            VMEM(two(group, feats), bf16),
            VMEM(two(group, LANES), f32),
            VMEM(two(group, LANES), f32),
            VMEM(two(GROUP, tokens, LANES), bf16),
            VMEM(two(GROUP - 1, GROUP, tokens, LANES), bf16),
            VMEM((GROUP, tokens, depth), bf16),
            VMEM(two(2, tokens, depth), bf16),
            VMEM(two(tokens, depth), bf16),
            VMEM(two(tokens, depth), bf16),
            VMEM((tokens, depth), f32),
            VMEM((tokens, width), f32),
            VMEM((tokens, LANES), f32),
            VMEM((8, PAD + tokens, LANES), f32),
            VMEM((tokens, LANES), f32),
            pltpu.SemaphoreType.DMA((sems,)),
            pltpu.SemaphoreType.DMA((sems,)),
            pltpu.SemaphoreType.DMA((32,)),
        ],
        compiler_params=pltpu.CompilerParams(
            vmem_limit_bytes=60 << 20, collective_id=1, has_side_effects=True
        ),
        cost_estimate=cost(120.0),
        name="forward_both",
    )(*arrays)


class Fetch:
    def __init__(self, sem):
        self.sem, self.count = sem, 0

    def get(self, src, dst):
        copy = pltpu.make_async_copy(src, dst, self.sem.at[self.count])
        self.count += 1
        copy.start()
        return copy


def backward_kernel(sizes, *refs):
    tokens, depth, units, feats, states, tall, small, high = sizes
    width = units + LANES
    top = tall * GROUP
    rows = top + high + small * GROUP * units // depth
    devices = GROUP * RINGS
    (
        cot_ref, x_ref, later_ref, rows_ref, filt_ref, mixn_ref, auxs, si_ref, so_ref,
        norm_hbm, value_hbm, gp_hbm, c_hbm, full_hbm, z_hbm, g2_hbm, vw_hbm, ow_hbm, ew_hbm, dout_hbm,
    ) = refs[:20]
    (
        dx_ref, gain_ref, shift_ref, v_ref, vb_ref, r_ref, rb_ref, dec_ref, si_out, so_out, skip_ref,
        e_ref, eb_ref, o_ref, ob_ref,
    ) = refs[20:35]
    (
        norm, value, gp, cbuf, full, z, g2, vw, ow, ew, dout, dcb, da,
        qe, qo, near, cross, far, dnbuf, din, dadd, dfar,
        packs, ysum, zsum, gsend, grecv, vsend, vin, vsum, vgrp,
        rem_scr, shifted, dz_scr, corr, y_scr, w_scr, o_scr, m_scr,
        send_sem, recv_sem, hbm_sem,
    ) = refs[35:]
    mail = Mail(send_sem, recv_sem)
    fetch = Fetch(hbm_sem)
    dp, fs = mail.dp, mail.fs
    index = dp * RINGS + fs
    thirds = units // 256
    across = depth // 256
    strips = tokens // STRIP

    def lanes(at, size):
        return pl.ds(pl.multiple_of(at * size, LANES), size)

    def block(j):
        return pl.ds(pl.multiple_of(j * tokens, tokens), tokens)

    def load_out(l):
        return [
            fetch.get(ow_hbm.at[l], ow), fetch.get(ew_hbm.at[l], ew), fetch.get(value_hbm.at[l], value),
            fetch.get(gp_hbm.at[l], gp), fetch.get(c_hbm.at[l], cbuf), fetch.get(full_hbm.at[l], full),
        ]

    def load_in(l):
        return [
            fetch.get(z_hbm.at[l], z), fetch.get(g2_hbm.at[l], g2), fetch.get(vw_hbm.at[l], vw),
            fetch.get(norm_hbm.at[l], norm),
        ]

    first = fetch.get(dout_hbm, dout.at[LAYERS - 1])
    loads = load_out(LAYERS - 1)
    more_loads = load_in(LAYERS - 1)
    vsend[...] = jnp.zeros(vsend.shape, f32)
    for b in range(8):
        shifted[b, tokens:, :] = jnp.zeros((PAD, LANES), f32)

    def start_dx(i, carry):
        at = pl.ds(pl.multiple_of(i * STRIP, STRIP), STRIP)
        up = cot_ref[at, :].astype(f32)
        dx_ref[at, :] = up
        low = (up * auxs[0, at, 2:3].astype(f32)).astype(bf16).astype(f32)
        return carry + jnp.sum(low, axis=0, keepdims=True)

    vsend[LAYERS - 1, 2:3, :] = lax.fori_loop(0, strips, start_dx, jnp.zeros((1, depth), f32))

    mail.greet((CORE, CHIP, BOTH, 1, 2, 3, 4, 5, 6, 7))

    def back_out(l, j):
        at = block(j)
        dgated = nt(dout[l, at, :], ow[...])
        val = value[at, :].astype(f32)
        gate = cbuf[at, :].astype(f32)
        dc = (dgated * val).astype(bf16)
        dcb[at, :] = dc
        da[at, :units] = (dgated * gate * gp[at, :].astype(f32)).astype(bf16)
        cbuf[at, :] = (gate * val).astype(bf16)
        vsend[l, 5:6, :units] += jnp.sum(dc.astype(f32), axis=0, keepdims=True)
        y_scr[...] = nt(dc, ew[...])
        for k in range(GROUP):
            part = y_scr[:, lanes(dp ^ k, LANES)].astype(bf16)
            if k % 2:
                qo[k // 2, j ^ 1] = part
            else:
                qe[k // 2, j] = part

    def back_in(l, j):
        at = block(j)
        rem_scr[...] = jnp.broadcast_to(auxs[j, :, 1:2].astype(f32), (tokens, LANES))
        dy = qe[0, j].astype(f32) + near[0, j].astype(f32) + far[j].astype(f32)
        for b in range(8):
            shifted[b, :tokens, :] = dy if b == 0 else pltpu.roll(dy, tokens - b, 0)
        for s in range(strips):
            rem = rem_scr[s * STRIP : (s + 1) * STRIP, :]
            past = z[pl.ds(pl.multiple_of(j * tokens + s * STRIP, STRIP), STRIP), :]

            def lags(a, acc, s=s, rem=rem, past=past):
                base = pl.multiple_of(a * 8, 8)
                left = rem - (a * 8).astype(f32)
                for b in range(8):
                    row = filt_ref[l, pl.ds(base + b, 1), :]
                    later = shifted[b, pl.ds(pl.multiple_of(s * STRIP + base, 8), STRIP), :]
                    later = jnp.where(left >= b, later, 0.0)
                    acc = acc + later * row
                    pair = later * past
                    corr[pl.ds(pl.multiple_of(base * 8 + b * 8, 8), 8), :] += (pair[0:8] + pair[8:16]) + (
                        pair[16:24] + pair[24:32]
                    )
                return acc

            dz_scr[s * STRIP : (s + 1) * STRIP, :] = lax.fori_loop(
                0, (strips - s) * (STRIP // 8), lags, jnp.zeros((STRIP, LANES), f32)
            )
        da2 = (dz_scr[...] + rows_ref[l, 5:6, :LANES] * dy) * g2[at, :]
        da[at, units:] = da2.astype(bf16)
        vsend[l, 5:6, units:width] += jnp.sum(z[at, :] * dy, axis=0, keepdims=True)
        vsend[l, 4:5, :width] += jnp.sum(da[at, :].astype(f32), axis=0, keepdims=True)
        dnbuf[j] = nt(da[at, :], vw[...]).astype(bf16)

    def grads_out_of(l):
        wide = high * GROUP
        for i in range(RINGS // GROUP):
            o_scr[...] = tn(cbuf[:, i * wide : (i + 1) * wide], dout[l]).astype(bf16)
            for g in range(GROUP):
                spot = fs ^ (i * GROUP + g)
                packs[l, spot, top : top + high, :] = o_scr[g * high : (g + 1) * high, :]
        for t in range(thirds):
            w_scr[: 2 * tokens, :256] = tn(full[...], dcb[:, t * 256 : (t + 1) * 256]).astype(bf16)
            for j in range(RINGS):
                for k in range(GROUP):
                    r, c = divmod(k * thirds + t, across)
                    owner = (dp ^ k) * RINGS + (fs ^ j)
                    packs[l, j, top + high + small * r : top + high + small * (r + 1), c * 256 : (c + 1) * 256] = (
                        w_scr[pl.ds(pl.multiple_of(owner * small, small), small), :256]
                    )

    def grads_in_of(l):
        wide = depth // GROUP
        for d in range(GROUP):
            w_scr[:wide, :] = tn(norm[:, d * wide : (d + 1) * wide], da[...]).astype(bf16)
            at = pl.ds(pl.multiple_of((dp ^ d) * tall, tall), tall)
            for j in range(RINGS):
                packs[l, j, at, :width] = w_scr[pl.ds(pl.multiple_of((fs ^ j) * tall, tall), tall), :]
        lag = lax.broadcasted_iota(jnp.int32, (tokens, tokens * 8), 0)
        part = lax.broadcasted_iota(jnp.int32, (tokens, tokens * 8), 1) // 8
        total = nn((lag == part).astype(bf16), corr[...].astype(bf16))
        steps = lax.broadcasted_iota(jnp.int32, (tokens, states), 0).astype(f32)
        powers = jnp.exp(-steps * rows_ref[l, 3:4, :states]).astype(bf16)
        m_scr[...] = tn(powers, total.astype(bf16)).astype(bf16)
        steps = lax.broadcasted_iota(jnp.int32, (tokens, LANES), 0).astype(f32)
        terms = tn(powers, (total * steps).astype(bf16)) * mixn_ref[l].astype(f32)
        vsend[l, 3:4, :states] = -lax.dot_general(
            jnp.ones((8, LANES), f32), terms, cols_dims, precision=highest, preferred_element_type=f32
        )[0:1]
        for j in range(RINGS):
            for k in range(GROUP):
                owner = (dp ^ k) * RINGS + (fs ^ j)
                packs[l, j, k * tall : k * tall + small, width:] = m_scr[
                    pl.ds(pl.multiple_of(owner * small, small), small), :
                ]
                packs[l, j, k * tall + small : (k + 1) * tall, width:] = jnp.zeros((tall - small, LANES), bf16)

    state = {}

    def part_rows(part):
        return slice(0, top) if part == 0 else slice(top, rows)

    def along_y(l, part):
        at = part_rows(part)
        for k in (1, 2, 3, 0):
            state[l, part, "y", k] = mail.send(packs.at[l, 2 * k + 1, at], ysum.at[l, k, at], 1)

    def step_y(l, part, k):
        at = part_rows(part)
        state[l, part, "y", k].wait_recv()
        packs[l, 2 * k, at, :] = (packs[l, 2 * k, at, :].astype(f32) + ysum[l, k, at, :].astype(f32)).astype(bf16)
        if k:
            state[l, part, "z", k] = mail.send(packs.at[l, 2 * k, at], zsum.at[l, k - 1, at], 2 * k)

    def total_of(l, at, lane=slice(None)):
        out = packs[l, 0, at, lane].astype(f32)
        for k in range(RINGS // 2 - 1):
            out = out + zsum[l, k, at, lane].astype(f32)
        return out

    def step_z_out(l):
        for k in (1, 2, 3):
            state[l, 1, "z", k].wait_recv()
        o_ref[l] = total_of(l, slice(top, top + high))
        for k in range(GROUP):
            for t in range(thirds):
                r, c = divmod(k * thirds + t, across)
                base = top + high + small * r
                piece = total_of(l, slice(base, base + small), slice(c * 256, (c + 1) * 256))
                if k == 0:
                    e_ref[l, :, pl.ds(pl.multiple_of(dp * units + t * 256, 256), 256)] = piece
                else:
                    gsend[l, k - 1, tall:, t * 256 : (t + 1) * 256] = piece.astype(bf16)
            if k:
                gsend[l, k - 1, tall:, units:] = jnp.zeros((small, depth - units), bf16)
                state[l, "e", k] = mail.send(
                    gsend.at[l, k - 1, tall : tall + small], grecv.at[l, k - 1, tall : tall + small], k * RINGS
                )

    def last_out(l):
        for k in range(1, GROUP):
            state[l, "e", k].wait_recv()
            e_ref[l, :, lanes(dp ^ k, units)] = grecv[l, k - 1, tall:, :units].astype(f32)

    def step_z_in(l):
        for k in (1, 2, 3):
            state[l, 0, "z", k].wait_recv()
        for k in (2, 3, 1, 0):
            piece = total_of(l, slice(k * tall, (k + 1) * tall))
            if k == 0:
                place_in(l, 0, piece)
            else:
                gsend[l, k - 1, :tall, :] = piece.astype(bf16)
                state[l, "v", k] = mail.send(gsend.at[l, k - 1, 0:tall], grecv.at[l, k - 1, 0:tall], k * RINGS)

    def place_in(l, k, piece):
        v_ref[l, :, lanes(dp ^ k, units)] = piece[:, :units]
        r_ref[l, :, lanes(dp ^ k, LANES)] = piece[:, units:width]
        thin = lanes(dp ^ k, LANES)
        mine = piece[:small, width:]
        si_out[l, :, thin] = mine * so_ref[l, :, thin].astype(f32)
        so_out[l, :, thin] = mine * si_ref[l, :, thin].astype(f32)

    def last_in(l):
        for k in range(1, GROUP):
            state[l, "v", k].wait_recv()
            place_in(l, k, grecv[l, k - 1, :tall, :].astype(f32))

    def vector_rest(l):
        state[l, "vr"] = [mail.send(vsend.at[l], vin.at[l, j - 1], j) for j in range(1, RINGS)]

    def vector_group(l):
        for copy in state[l, "vr"]:
            copy.wait_recv()
        total = vsend[l]
        for j in range(RINGS - 1):
            total = total + vin[l, j]
        vsum[l] = total
        state[l, "vg"] = [mail.send(vsum.at[l], vgrp.at[l, k - 1], k * RINGS) for k in range(1, GROUP)]

    def vector_last(l):
        for copy in state[l, "vg"]:
            copy.wait_recv()
        mine = vsum[l]
        total = mine
        for k in range(GROUP - 1):
            total = total + vgrp[l, k]
        apart = lax.broadcasted_iota(jnp.int32, (depth, LANES), 0) - lax.broadcasted_iota(
            jnp.int32, (depth, LANES), 1
        )

        def pick(array, start):
            return jnp.dot(array, (apart == start).astype(f32), precision=highest, preferred_element_type=f32)

        long = depth // devices
        got = pick(total, index * long)
        for r, ref in enumerate((gain_ref, shift_ref, ob_ref)):
            ref[l : l + 1, :] = got[r : r + 1, :long]
        short = states // devices
        dec_ref[l : l + 1, :] = pick(total, index * short)[3:4, :short]
        own = units // RINGS
        got = pick(mine, fs * own)
        vb_ref[l : l + 1, :] = got[4:5, :own]
        eb_ref[l : l + 1, :] = got[5:6, :own]
        got = pick(mine, units + fs * short)
        rb_ref[l : l + 1, :] = got[4:5, :short]
        skip_ref[l : l + 1, :] = got[5:6, :short]

    def pair(fn, lo):
        def body(i, carry):
            fn(lo + i)
            return carry

        lax.fori_loop(0, 2, body, 0)

    def exchange_dy(half):
        return mail.send(qo.at[:, half], near.at[:, half], CORE)

    def cross_dy(half, other, copy):
        copy.wait_recv()
        cross[half] = (qe[1, half].astype(f32) + near[1, half].astype(f32)).astype(bf16)
        return mail.send(cross.at[half], far.at[other], CHIP)

    lo, hi = slice(0, 2), slice(2, 4)

    def layer(l, loads, more_loads, events, wait_far, keep):
        def due():
            if events:
                events.pop(0)()

        for copy in loads:
            copy.wait()
        corr[...] = jnp.zeros(corr.shape, f32)
        pair(lambda j: back_out(l, j), 0)
        near_lo = exchange_dy(lo)
        due()
        wait_far()
        pair(lambda j: back_out(l, j), 2)
        near_hi = exchange_dy(hi)
        cross_lo = cross_dy(lo, hi, near_lo)
        due()
        cross_hi = cross_dy(hi, lo, near_hi)
        grads_out_of(l)
        along_y(l, 1)
        next_loads = load_out(l - 1) if l else []
        for copy in more_loads:
            copy.wait()
        due()
        cross_lo.wait_recv()
        back_in(l, 3)
        core_hi = mail.send(dnbuf.at[3], din.at[0], CORE)
        due()
        back_in(l, 2)
        core_hi.wait_recv()
        dadd[...] = (dnbuf[2].astype(f32) + din[0].astype(f32)).astype(bf16)
        chip = mail.send(dadd, dfar, CHIP)
        due()
        cross_hi.wait_recv()
        back_in(l, 1)
        core_lo = mail.send(dnbuf.at[1], din.at[1], CORE)
        due()
        back_in(l, 0)
        due()
        grads_in_of(l)
        along_y(l, 0)
        next_more = load_in(l - 1) if l else []
        due()
        core_lo.wait_recv()
        chip.wait_recv()

        def strip(i, carry):
            gain_sum, shift_sum, out_sum = carry
            at = pl.ds(pl.multiple_of(i * STRIP, STRIP), STRIP)
            v = later_ref[at, :] if l else x_ref[at, :].astype(f32)
            center = v - jnp.mean(v, axis=1, keepdims=True)
            scale = lax.rsqrt(jnp.mean(center * center, axis=1, keepdims=True) + 1e-05)
            normed = center * scale
            grad = dnbuf[0, at, :].astype(f32) + din[1, at, :].astype(f32) + dfar[at, :].astype(f32)
            q = grad * rows_ref[l, 0:1, :]
            tilt = q - jnp.mean(q, axis=1, keepdims=True) - normed * jnp.mean(q * normed, axis=1, keepdims=True)
            up = dx_ref[at, :] + tilt * scale
            dx_ref[at, :] = up
            if l:
                low = (up * auxs[0, at, 2:3].astype(f32)).astype(bf16)
                dout[l - 1, at, :] = low
                out_sum = out_sum + jnp.sum(low.astype(f32), axis=0, keepdims=True)
            return (
                gain_sum + jnp.sum(grad * normed, axis=0, keepdims=True),
                shift_sum + jnp.sum(grad, axis=0, keepdims=True),
                out_sum,
            )

        zero = jnp.zeros((1, depth), f32)
        gain_sum, shift_sum, out_sum = lax.fori_loop(0, strips, strip, (zero, zero, zero))
        vsend[l, 0:1, :] = gain_sum
        vsend[l, 1:2, :] = shift_sum
        if l:
            vsend[l - 1, 2:3, :] = out_sum
        for copy in (near_lo, near_hi, cross_lo, cross_hi, core_hi, core_lo, chip):
            mail.finish(copy)
        return next_loads, next_more

    first.wait()
    due_one = lambda l, part, k: (lambda: step_y(l, part, k))
    nothing = lambda: None
    events = [nothing, nothing, nothing] + [due_one(1, 1, 1), due_one(1, 1, 2), due_one(1, 1, 3), due_one(1, 1, 0)]
    loads, more_loads = layer(1, loads, more_loads, events, nothing, None)

    dout_chip = mail.send(dout.at[0, pl.ds(0, tokens)], dout.at[0, pl.ds(2 * tokens, tokens)], CHIP)
    dout_core = mail.send(dout.at[0, pl.ds(0, tokens)], dout.at[0, pl.ds(tokens, tokens)], CORE)
    vector_rest(1)

    def dout_far():
        step_z_out(1)
        dout_chip.wait_recv()
        relay = mail.send(dout.at[0, pl.ds(2 * tokens, tokens)], dout.at[0, pl.ds(3 * tokens, tokens)], CORE)
        step_y(1, 0, 2)
        relay.wait_recv()

    def then(*steps):
        def event():
            for step in steps:
                step()

        return event

    events = [
        due_one(1, 0, 1),
        due_one(1, 0, 3),
        then(due_one(1, 0, 0), lambda: vector_group(1)),
        due_one(0, 1, 1),
        then(due_one(0, 1, 2), lambda: last_out(1)),
        then(due_one(0, 1, 3), lambda: step_z_in(1)),
        then(due_one(0, 1, 0)),
        nothing,
    ]
    dout_core.wait_recv()
    layer(0, loads, more_loads, events, dout_far, None)
    vector_rest(0)
    last_in(1)
    vector_last(1)
    step_z_out(0)
    step_y(0, 0, 1)
    vector_group(0)
    step_y(0, 0, 2)
    step_y(0, 0, 3)
    step_y(0, 0, 0)
    last_out(0)
    vector_last(0)
    step_z_in(0)
    last_in(0)
    mail.close()


def backward_both(arrays, sizes):
    tokens, depth, units, feats, states, tall, small, high = sizes
    width = units + LANES
    group = tokens * GROUP
    rows = tall * GROUP + high + small * GROUP * units // depth
    devices = GROUP * RINGS
    hidden = units * GROUP
    shape = jax.ShapeDtypeStruct
    two = lambda *dims: (LAYERS,) + dims
    outs = [
        (tokens, depth), two(depth // devices), two(depth // devices), two(tall, hidden), two(units // RINGS),
        two(tall, feats), two(LANES // RINGS), two(states // devices), two(small, feats), two(small, feats),
        two(LANES // RINGS), two(small, hidden), two(units // RINGS), two(high, depth), two(depth // devices),
    ]
    return pl.pallas_call(
        partial(backward_kernel, sizes),
        out_shape=[shape(s, f32) for s in outs],
        in_specs=[pl.BlockSpec(memory_space=VMEM)] * 9 + [pl.BlockSpec(memory_space=pl.ANY)] * 11,
        out_specs=[pl.BlockSpec(memory_space=VMEM)] * len(outs),
        scratch_shapes=[
            VMEM((group, depth), bf16),
            VMEM((group, units), bf16),
            VMEM((group, units), bf16),
            VMEM((group, units), bf16),
            VMEM((group, feats), bf16),
            VMEM((group, LANES), f32),
            VMEM((group, LANES), f32),
            VMEM((depth, width), bf16),
            VMEM((units, depth), bf16),
            VMEM((feats, units), bf16),
            VMEM(two(group, depth), bf16),
            VMEM((group, units), bf16),
            VMEM((group, width), bf16),
            VMEM((2, GROUP, tokens, LANES), bf16),
            VMEM((2, GROUP, tokens, LANES), bf16),
            VMEM((2, GROUP, tokens, LANES), bf16),
            VMEM((GROUP, tokens, LANES), bf16),
            VMEM((GROUP, tokens, LANES), bf16),
            VMEM((GROUP, tokens, depth), bf16),
            VMEM((2, tokens, depth), bf16),
            VMEM((tokens, depth), bf16),
            VMEM((tokens, depth), bf16),
            VMEM(two(RINGS, rows, depth), bf16),
            VMEM(two(RINGS // 2, rows, depth), bf16),
            VMEM(two(RINGS // 2 - 1, rows, depth), bf16),
            VMEM(two(GROUP - 1, tall + small, depth), bf16),
            VMEM(two(GROUP - 1, tall + small, depth), bf16),
            VMEM(two(8, depth), f32),
            VMEM(two(RINGS - 1, 8, depth), f32),
            VMEM(two(8, depth), f32),
            VMEM(two(GROUP - 1, 8, depth), f32),
            VMEM((tokens, LANES), f32),
            VMEM((8, PAD + tokens, LANES), f32),
            VMEM((tokens, LANES), f32),
            VMEM((tokens * 8, LANES), f32),
            VMEM((tokens, feats), f32),
            VMEM((2 * tokens, width), bf16),
            VMEM((high * GROUP, depth), bf16),
            VMEM((states, LANES), bf16),
            pltpu.SemaphoreType.DMA((100,)),
            pltpu.SemaphoreType.DMA((100,)),
            pltpu.SemaphoreType.DMA((24,)),
        ],
        compiler_params=pltpu.CompilerParams(
            vmem_limit_bytes=60 << 20, collective_id=2, has_side_effects=True
        ),
        cost_estimate=cost(140.0),
        name="backward_both",
    )(*arrays)


def mixer(labels, signal, decays, stateinput, stateoutput, skipgain):
    rows = signal.shape[0]
    width = min(32, rows)
    count = rows // width
    mixing = stateinput * stateoutput
    offsets = jnp.arange(width, dtype=jnp.float32)
    powers = jnp.exp(-offsets[:, None] * decays[None, :])
    kernel = jnp.dot(powers, mixing, precision=highest)
    positions = jnp.arange(width, dtype=jnp.int32)
    lagged = jnp.maximum(positions[:, None] - positions[None, :], 0)
    toeplitz = jnp.take(kernel, lagged, axis=0)
    causal = positions[:, None] >= positions[None, :]
    leading = jnp.exp(-(offsets[:, None] + 1.0) * decays[None, :])
    trailing = jnp.exp(-(width - 1.0 - offsets[:, None]) * decays[None, :])
    across = jnp.exp(-width * decays)

    def advance(carry, pieces):
        state, before = carry
        block, marks = pieces
        same = jnp.logical_and(marks[:, None] == marks[None, :], causal).astype(signal.dtype)
        inner = jnp.sum(toeplitz * same[:, :, None] * block[None, :, :], axis=1)
        joined = (marks == before).astype(signal.dtype)
        carried = jnp.dot(leading, mixing * state, precision=highest) * joined[:, None]
        final = marks[width - 1]
        keep = (final == before).astype(signal.dtype)
        fresh = (marks == final).astype(signal.dtype)
        state = across[:, None] * state * keep + lax.dot_general(
            trailing * fresh[:, None], block, rows_dims, precision=highest
        )
        return ((state, final), inner + carried)

    start = (jnp.zeros(mixing.shape, signal.dtype), jnp.array(-1, jnp.int32))
    ending, mixed = lax.scan(
        jax.checkpoint(advance),
        start,
        (signal.reshape(count, width, -1), labels.reshape(count, width)),
    )
    return mixed.reshape(rows, -1) + skipgain[None, :] * signal


def normalize(rows, gain, shift):
    center = rows - jnp.mean(rows, axis=1, keepdims=True)
    spread = jnp.mean(center * center, axis=1, keepdims=True)
    return center * lax.rsqrt(spread + 1e-05) * gain + shift


def smooth(values):
    return jax.nn.gelu(values, approximate=False)


def gather_forward(shards, depth):
    return (
        lax.all_gather(shards[0][depth], ("dp", "fsdp"), axis=0, tiled=True),
        lax.all_gather(shards[1][depth], ("dp", "fsdp"), axis=0, tiled=True),
        lax.all_gather(shards[2][depth], ("dp", "fsdp"), axis=0, tiled=True),
        lax.all_gather(shards[3][depth], ("dp", "fsdp"), axis=0, tiled=True),
        lax.all_gather(shards[4][depth], ("dp", "fsdp"), axis=0, tiled=True),
        lax.all_gather(shards[5][depth], ("dp", "fsdp"), axis=0, tiled=True),
        lax.all_gather(shards[6][depth], ("dp", "fsdp"), axis=0, tiled=True),
        lax.all_gather(shards[7][depth], ("dp", "fsdp"), axis=0, tiled=True),
        lax.all_gather(shards[8][depth], ("dp", "fsdp"), axis=0, tiled=True),
        lax.all_gather(shards[9][depth], ("dp", "fsdp"), axis=0, tiled=True),
        lax.all_gather(shards[10][depth], ("dp", "fsdp"), axis=0, tiled=True),
        lax.all_gather(shards[11][depth], ("dp", "fsdp"), axis=0, tiled=True),
        lax.all_gather(shards[12][depth], ("dp", "fsdp"), axis=0, tiled=True),
        lax.all_gather(shards[13][depth], ("dp", "fsdp"), axis=0, tiled=True),
    )


def gather_backward(shards, depth):
    return (
        lax.all_gather(shards[0][depth], ("dp", "fsdp"), axis=0, tiled=True),
        lax.all_gather(shards[1][depth], ("dp", "fsdp"), axis=0, tiled=True),
        lax.all_gather(shards[2][depth], ("dp", "fsdp"), axis=0, tiled=True),
        lax.all_gather(shards[3][depth], ("dp", "fsdp"), axis=0, tiled=True),
        lax.all_gather(shards[4][depth], ("dp", "fsdp"), axis=0, tiled=True),
        lax.all_gather(shards[5][depth], ("dp", "fsdp"), axis=0, tiled=True),
        lax.all_gather(shards[6][depth], ("dp", "fsdp"), axis=0, tiled=True),
        lax.all_gather(shards[7][depth], ("dp", "fsdp"), axis=0, tiled=True),
        lax.all_gather(shards[8][depth], ("dp", "fsdp"), axis=0, tiled=True),
        lax.all_gather(shards[9][depth], ("dp", "fsdp"), axis=0, tiled=True),
        lax.all_gather(shards[10][depth], ("dp", "fsdp"), axis=0, tiled=True),
        lax.all_gather(shards[11][depth], ("dp", "fsdp"), axis=0, tiled=True),
        lax.all_gather(shards[12][depth], ("dp", "fsdp"), axis=0, tiled=True),
        lax.all_gather(shards[13][depth], ("dp", "fsdp"), axis=0, tiled=True),
    )


def scatter_layer(terms):
    return (
        lax.psum_scatter(terms[0], ("dp", "fsdp"), scatter_dimension=0, tiled=True),
        lax.psum_scatter(terms[1], ("dp", "fsdp"), scatter_dimension=0, tiled=True),
        lax.psum_scatter(terms[2], ("dp", "fsdp"), scatter_dimension=0, tiled=True),
        lax.psum_scatter(terms[3], ("dp", "fsdp"), scatter_dimension=0, tiled=True),
        lax.psum_scatter(terms[4], ("dp", "fsdp"), scatter_dimension=0, tiled=True),
        lax.psum_scatter(terms[5], ("dp", "fsdp"), scatter_dimension=0, tiled=True),
        lax.psum_scatter(terms[6], ("dp", "fsdp"), scatter_dimension=0, tiled=True),
        lax.psum_scatter(terms[7], ("dp", "fsdp"), scatter_dimension=0, tiled=True),
        lax.psum_scatter(terms[8], ("dp", "fsdp"), scatter_dimension=0, tiled=True),
        lax.psum_scatter(terms[9], ("dp", "fsdp"), scatter_dimension=0, tiled=True),
        lax.psum_scatter(terms[10], ("dp", "fsdp"), scatter_dimension=0, tiled=True),
        lax.psum_scatter(terms[11], ("dp", "fsdp"), scatter_dimension=0, tiled=True),
        lax.psum_scatter(terms[12], ("dp", "fsdp"), scatter_dimension=0, tiled=True),
        lax.psum_scatter(terms[13], ("dp", "fsdp"), scatter_dimension=0, tiled=True),
    )


def layer_forward(current, labels, flags, weights):
    (
        normgain,
        normbias,
        valueproj,
        valuebias,
        reduceproj,
        reducebias,
        decays,
        stateinput,
        stateoutput,
        skipgain,
        expandproj,
        expandbias,
        outproj,
        outbias,
    ) = weights
    normed, norm_back = jax.vjp(
        normalize, current, normgain.astype(jnp.float32), normbias.astype(jnp.float32)
    )
    normed_low = normed.astype(jnp.bfloat16)
    opened = jnp.dot(normed_low, valueproj, preferred_element_type=jnp.float32) + valuebias.astype(
        jnp.float32
    )
    values, value_back = jax.vjp(smooth, opened)
    reduced = jnp.dot(
        normed_low, reduceproj, preferred_element_type=jnp.float32
    ) + reducebias.astype(jnp.float32)
    smoothed, reduce_back = jax.vjp(smooth, reduced)
    signal = smoothed * flags
    mixed, mix_back = jax.vjp(
        partial(mixer, labels),
        signal,
        decays.astype(jnp.float32),
        stateinput.astype(jnp.float32),
        stateoutput.astype(jnp.float32),
        skipgain.astype(jnp.float32),
    )
    mixed_low = mixed.astype(jnp.bfloat16)
    expanded = jnp.dot(
        mixed_low, expandproj, preferred_element_type=jnp.float32
    ) + expandbias.astype(jnp.float32)
    gated = (expanded * values).astype(jnp.bfloat16)
    branch = jnp.dot(gated, outproj, preferred_element_type=jnp.float32) + outbias.astype(
        jnp.float32
    )
    saved = (
        normed_low,
        values,
        value_back,
        reduce_back,
        mix_back,
        mixed_low,
        expanded,
        gated,
        norm_back,
    )
    return (current + flags * branch, saved)


def layer_backward(upstream, flags, weights, saved):
    (
        normgain,
        normbias,
        valueproj,
        valuebias,
        reduceproj,
        reducebias,
        decays,
        stateinput,
        stateoutput,
        skipgain,
        expandproj,
        expandbias,
        outproj,
        outbias,
    ) = weights
    normed_low, values, value_back, reduce_back, mix_back, mixed_low, expanded, gated, norm_back = (
        saved
    )
    dout = (flags * upstream).astype(jnp.bfloat16)
    outproj_term = lax.dot_general(gated, dout, rows_dims, preferred_element_type=jnp.float32)
    outbias_term = jnp.sum(dout, axis=0, dtype=jnp.float32)
    dgated = lax.dot_general(dout, outproj, cols_dims, preferred_element_type=jnp.float32)
    dexpanded = (dgated * values).astype(jnp.bfloat16)
    dvalues = dgated * expanded
    expandproj_term = lax.dot_general(
        mixed_low, dexpanded, rows_dims, preferred_element_type=jnp.float32
    )
    expandbias_term = jnp.sum(dexpanded, axis=0, dtype=jnp.float32)
    dmixed = lax.dot_general(dexpanded, expandproj, cols_dims, preferred_element_type=jnp.float32)
    dsignal, decays_term, stateinput_term, stateoutput_term, skipgain_term = mix_back(dmixed)
    (dreduced,) = reduce_back(dsignal * flags)
    dreduced_low = dreduced.astype(jnp.bfloat16)
    (dopened,) = value_back(dvalues)
    dopened_low = dopened.astype(jnp.bfloat16)
    valueproj_term = lax.dot_general(
        normed_low, dopened_low, rows_dims, preferred_element_type=jnp.float32
    )
    valuebias_term = jnp.sum(dopened_low, axis=0, dtype=jnp.float32)
    reduceproj_term = lax.dot_general(
        normed_low, dreduced_low, rows_dims, preferred_element_type=jnp.float32
    )
    reducebias_term = jnp.sum(dreduced_low, axis=0, dtype=jnp.float32)
    dnormed = lax.dot_general(dopened_low, valueproj, cols_dims, preferred_element_type=jnp.float32)
    dnormed = dnormed + lax.dot_general(
        dreduced_low, reduceproj, cols_dims, preferred_element_type=jnp.float32
    )
    dcurrent, normgain_term, normbias_term = norm_back(dnormed)
    terms = (
        normgain_term,
        normbias_term,
        valueproj_term,
        valuebias_term,
        reduceproj_term,
        reducebias_term,
        decays_term,
        stateinput_term,
        stateoutput_term,
        skipgain_term,
        expandproj_term,
        expandbias_term,
        outproj_term,
        outbias_term,
    )
    return (upstream + dcurrent, terms)


def plain(
    inputs,
    segment_ids,
    token_mask,
    cotangent,
    normgain,
    normbias,
    valueproj,
    valuebias,
    reduceproj,
    reducebias,
    decays,
    stateinput,
    stateoutput,
    skipgain,
    expandproj,
    expandbias,
    outproj,
    outbias,
):
    shards = (
        normgain,
        normbias,
        valueproj,
        valuebias,
        reduceproj,
        reducebias,
        decays,
        stateinput,
        stateoutput,
        skipgain,
        expandproj,
        expandbias,
        outproj,
        outbias,
    )
    flags = token_mask.astype(jnp.float32)[:, None]
    current = inputs.astype(jnp.float32)
    fetched = []
    stored = []
    for depth in range(LAYERS):
        weights = gather_forward(shards, depth)
        current, saved = layer_forward(current, segment_ids, flags, weights)
        fetched.append(weights)
        stored.append(saved)
    outputs = current.astype(jnp.bfloat16)
    upstream = cotangent.astype(jnp.float32)
    scattered = [None] * LAYERS
    for depth in reversed(range(LAYERS)):
        weights = gather_backward(shards, depth)
        upstream, terms = layer_backward(upstream, flags, weights, stored[depth])
        scattered[depth] = scatter_layer(terms)
    results = tuple(
        (jnp.stack([scattered[depth][index] for depth in range(LAYERS)]) for index in range(14))
    )
    return (outputs, upstream) + tuple(results)


def fast(
    inputs, segment_ids, token_mask, cotangent, normgain, normbias, valueproj, valuebias,
    reduceproj, reducebias, decays, stateinput, stateoutput, skipgain, expandproj, expandbias,
    outproj, outbias,
):
    tokens, depth = inputs.shape
    tall = valueproj.shape[1]
    small = stateinput.shape[1]
    high = outproj.shape[1]
    units = valueproj.shape[2] // GROUP
    feats = reduceproj.shape[2]
    states = stateinput.shape[1] * GROUP * RINGS
    group = tokens * GROUP
    sizes = (tokens, depth, units, feats, states, tall, small, high)

    same = (segment_ids[:, None] == segment_ids[None, :]).astype(f32)
    spot = jnp.arange(tokens)
    before = (spot[None, :] < spot[:, None]).astype(f32)
    age = jnp.sum(same * before, axis=1)
    rest = jnp.sum(same * (1.0 - before), axis=1) - 1.0
    aux = jnp.pad(jnp.stack([age, rest, token_mask.astype(f32)], axis=1), ((0, 0), (0, LANES - 3)))
    dout = (token_mask.astype(f32)[:, None] * cotangent.astype(f32)).astype(bf16)
    shorts = (normgain, normbias, outbias, decays, valuebias, reducebias, skipgain, expandbias)
    vec = jnp.stack([jnp.pad(v, ((0, 0), (0, LANES - v.shape[1]))) for v in shorts], axis=1)
    vec = jnp.pad(vec, ((0, 0), (0, tall - small - len(shorts)), (0, 0)))

    (
        outputs, later, rows, filt, mixes, auxes,
        norms, value, slope, gate, full, z, slope2, value_w, out_w, expand_w, douts,
    ) = forward_both(
        (
            inputs, aux.astype(bf16), dout, valueproj, reduceproj, expandproj, outproj,
            stateinput, stateoutput, vec, *tables(GROUP * RINGS),
        ),
        sizes,
    )
    grads = backward_both(
        (
            cotangent, inputs, later, rows, filt, mixes, auxes, stateinput, stateoutput,
            norms.reshape(LAYERS, group, depth), value, slope, gate, full, z, slope2,
            value_w, out_w, expand_w, douts.reshape(group, depth),
        ),
        sizes,
    )
    return (outputs, *grads)


def solution(mesh):
    placed = (
        P(("dp", "fsdp"), None),
        P(("dp", "fsdp")),
        P(("dp", "fsdp")),
        P(("dp", "fsdp"), None),
        P(None, ("dp", "fsdp")),
        P(None, ("dp", "fsdp")),
        P(None, ("dp", "fsdp"), None),
        P(None, ("dp", "fsdp")),
        P(None, ("dp", "fsdp"), None),
        P(None, ("dp", "fsdp")),
        P(None, ("dp", "fsdp")),
        P(None, ("dp", "fsdp"), None),
        P(None, ("dp", "fsdp"), None),
        P(None, ("dp", "fsdp")),
        P(None, ("dp", "fsdp"), None),
        P(None, ("dp", "fsdp")),
        P(None, ("dp", "fsdp"), None),
        P(None, ("dp", "fsdp")),
    )
    small = mesh.shape["dp"] == GROUP and mesh.shape["fsdp"] == RINGS
    return jax.shard_map(
        fast if small else plain,
        mesh=mesh,
        in_specs=placed,
        out_specs=(
            P(("dp", "fsdp"), None),
            P(("dp", "fsdp"), None),
            P(None, ("dp", "fsdp")),
            P(None, ("dp", "fsdp")),
            P(None, ("dp", "fsdp"), None),
            P(None, ("dp", "fsdp")),
            P(None, ("dp", "fsdp"), None),
            P(None, ("dp", "fsdp")),
            P(None, ("dp", "fsdp")),
            P(None, ("dp", "fsdp"), None),
            P(None, ("dp", "fsdp"), None),
            P(None, ("dp", "fsdp")),
            P(None, ("dp", "fsdp"), None),
            P(None, ("dp", "fsdp")),
            P(None, ("dp", "fsdp"), None),
            P(None, ("dp", "fsdp")),
        ),
        check_vma=False,
    )
```

```python
from functools import partial

import jax
import jax.numpy as jnp
import numpy as np
from jax import lax
from jax.experimental import pallas as pl
from jax.experimental.pallas import tpu as pltpu
from jax.sharding import PartitionSpec as P

LAYERS = 2
AXES = ("dp", "fsdp")
GROUP = 4
RINGS = 8
LANES = 128
STRIP = 32
PAD = 32

f32 = jnp.float32
bf16 = jnp.bfloat16
highest = lax.Precision.HIGHEST
rows_dims = (((0,), (0,)), ((), ()))
cols_dims = (((1,), (1,)), ((), ()))

VMEM = pltpu.VMEM


def cost(micros):
    return pl.CostEstimate(
        flops=int(micros * 1.0e9), bytes_accessed=1 << 20, transcendentals=0
    )


def nt(a, b):
    return lax.dot_general(a, b, cols_dims, preferred_element_type=f32)


def tn(a, b):
    return lax.dot_general(a, b, rows_dims, preferred_element_type=f32)


def nn(a, b):
    return jnp.dot(a, b, preferred_element_type=f32)


def tables(devices):
    out = []
    for count, size in ((devices, 32), (RINGS, 96), (devices, 16)):
        at = np.arange(count * size)
        out.append(jnp.asarray((np.arange(LANES)[:, None] == at[None, :] % size), bf16))
        out.append(jnp.asarray((np.arange(count)[:, None] == at[None, :] // size), f32))
    return out


class Mail:
    def __init__(self, send_sem, recv_sem):
        self.dp, self.fs = lax.axis_index("dp"), lax.axis_index("fsdp")
        self.z, self.y = self.fs // 2, self.fs % 2
        self.send_sem, self.recv_sem, self.count, self.sent = send_sem, recv_sem, 0, []

    def peer(self, flip):
        return (self.dp ^ (flip // RINGS), self.fs ^ (flip % RINGS))

    def along(self, way):
        return (self.dp, self.fs + 2 * way)

    def greet(self, flips):
        barrier = pltpu.get_barrier_semaphore()

        def hail(device):
            pl.semaphore_signal(barrier, inc=1, device_id=device, device_id_type=pl.DeviceIdType.MESH)

        for flip in flips:
            hail(self.peer(flip))
        ahead, behind = self.z < LINE - 1, self.z > 0
        pl.when(ahead)(lambda: hail(self.along(1)))
        pl.when(behind)(lambda: hail(self.along(-1)))
        pl.semaphore_wait(barrier, len(flips) + ahead.astype(jnp.int32) + behind.astype(jnp.int32))

    def copy(self, src, dst, device):
        made = pltpu.make_async_remote_copy(
            src_ref=src, dst_ref=dst, send_sem=self.send_sem.at[self.count],
            recv_sem=self.recv_sem.at[self.count], device_id=device,
            device_id_type=pl.DeviceIdType.MESH,
        )
        self.count += 1
        return made

    def start(self, copy, when=None):
        only(when, copy.start)
        self.sent.append((copy, when))

    def send(self, src, dst, flip):
        copy = self.copy(src, dst, self.peer(flip))
        self.start(copy)
        return copy

    def finish(self, copy):
        copy.wait_send()
        self.sent = [(c, w) for c, w in self.sent if c is not copy]

    def close(self):
        for copy, when in self.sent:
            only(when, copy.wait_send)


def only(when, step):
    if when is None:
        step()
    else:
        pl.when(when)(step)


class Gather:
    def __init__(self, mail, packs, l, begin, cut, end):
        self.mail, self.packs, self.l = mail, packs, l
        self.early, self.late = slice(begin, cut), slice(cut, end)
        self.steps, self.across = {}, []

    def line(self, rows, both, step):
        m = self.mail
        for way in (1, -1):
            held = m.z - way * (step - 1)
            can = (held >= 0) & (m.z < LINE - 1) if way == 1 else (held <= LINE - 1) & (m.z > 0)
            at = jnp.clip(held, 0, LINE - 1)
            ref = self.packs.at[self.l, at, :, rows] if both else self.packs.at[self.l, at, m.y, rows]
            copy = m.copy(ref, ref, m.along(way))
            m.start(copy, can)
            self.steps[both, step, way] = copy

    def over(self, rows, at, when):
        m = self.mail
        ref = self.packs.at[self.l, at, m.y, rows]
        copy = m.copy(ref, ref, m.peer(1))
        m.start(copy, when)
        self.across.append((copy, when))
        return copy

    def begin(self):
        self.first = self.over(self.early, self.mail.z, None)
        self.across = []
        self.line(self.late, False, 1)
        self.over(self.late, self.mail.z, None)

    def come(self, both, step):
        m = self.mail
        out = []
        for way in (1, -1):
            source = m.z - way * step
            when = source >= 0 if way == 1 else source <= LINE - 1
            only(when, self.steps[both, step, way].wait_recv)
            out.append((jnp.clip(source, 0, LINE - 1), when))
        return out

    def step(self, step):
        held = self.come(False, step)
        if step < LINE - 1:
            self.line(self.late, False, step + 1)
        for at, when in held:
            self.over(self.late, at, when)
        if step == 1:
            self.first.wait_recv()
        else:
            self.come(True, step - 1)
        self.line(self.early, True, step)

    def end(self):
        self.come(True, LINE - 1)
        for copy, when in self.across:
            only(when, copy.wait_recv)


class Spill:
    def __init__(self, sem):
        self.sem, self.open = sem, []

    def put(self, src, dst):
        copy = pltpu.make_async_copy(src, dst, self.sem.at[len(self.open)])
        copy.start()
        self.open.append(copy)

    def close(self):
        for copy in self.open:
            copy.wait()


CORE, CHIP, BOTH = RINGS, 2 * RINGS, 3 * RINGS
FLIPS = (CORE, CHIP, BOTH, 1)
LINE = RINGS // 2


def forward_kernel(sizes, *refs):
    tokens, depth, units, feats, states, tall, small, high = sizes
    width = units + LANES
    top = tall * GROUP
    rows = top + high + small * GROUP * units // depth
    (
        x_ref, seg_ref, mask_ref, cot_ref, v_ref, r_ref, e_ref, o_ref, si_ref, so_ref,
        *short_refs, rep32, put32, rep96, put96, rep16, put16,
    ) = refs[:24]
    (
        out_ref, cross_ref, later_ref, rows_ref, filt_ref, mixn_ref, auxs,
        norm_hbm, value_hbm, gp_hbm, c_hbm, full_hbm, z_hbm, g2_hbm,
        vw_hbm, ow_hbm, ew_hbm, dout_hbm,
    ) = refs[24:42]
    (
        pieces, ein, packs, vecn, vw, ow, ew, xin, norm, douts,
        value, gp, cbuf, full, z, g2, ybuf, yin, obuf, oin, oadd, ofar, xcur,
        a_scr, age_scr, shifted, y_scr, vec_scr, send_sem, recv_sem, hbm_sem,
    ) = refs[42:]
    mail = Mail(send_sem, recv_sem)
    spill = Spill(hbm_sem)
    dp, z_at, y_at = mail.dp, mail.z, mail.y
    thirds = units // 256
    across = depth // 256

    def lanes(index, size):
        return pl.ds(pl.multiple_of(index * size, LANES), size)

    def place_expand(l, k, part):
        for t in range(thirds):
            r, c = divmod(k * thirds + t, across)
            at = top + high + small * r
            packs[l, z_at, y_at, at : at + small, c * 256 : (c + 1) * 256] = part[:, t * 256 : (t + 1) * 256]

    def line_up(ref):
        row = jnp.concatenate([ref[i : i + 1, :] for i in range(tokens // LANES)], axis=1).astype(f32)
        return jnp.broadcast_to(row, (tokens, tokens))

    ids = line_up(seg_ref)
    here = lax.broadcasted_iota(jnp.int32, (tokens, tokens), 0)
    there = lax.broadcasted_iota(jnp.int32, (tokens, tokens), 1)
    same = (ids == ids.T).astype(f32)
    age = jnp.sum(jnp.where(there < here, same, 0.0), axis=1, keepdims=True)
    rest = jnp.sum(jnp.where(there > here, same, 0.0), axis=1, keepdims=True)
    mask = line_up(mask_ref).T[:, :LANES]
    lane = lax.broadcasted_iota(jnp.int32, (tokens, LANES), 1)
    auxs[0] = jnp.where(lane == 0, age, jnp.where(lane == 1, rest, jnp.where(lane == 2, mask, 0.0))).astype(bf16)
    age_scr[...] = mask

    vec_scr[...] = jnp.zeros(vec_scr.shape, f32)
    for l in range(LAYERS):
        for r, ref in enumerate(short_refs):
            vec_scr[8 * l + r : 8 * l + r + 1, : ref.shape[1]] = ref[l : l + 1, :].astype(f32)
    for l in range(LAYERS):
        a_scr[:small, :feats] = si_ref[l].astype(f32) * so_ref[l].astype(f32)
        for k in range(GROUP):
            q = dp ^ k
            dst = packs.at[l, z_at, y_at, 0:tall] if k == 0 else pieces.at[l, k - 1, 0:tall]
            dst[:, :units] = v_ref[l, :, lanes(q, units)]
            dst[:, units:width] = r_ref[l, :, lanes(q, LANES)]
            dst[:small, width:] = a_scr[:small, lanes(q, LANES)].astype(bf16)
            dst[small:, width:] = vec_scr[...].astype(bf16)
            part = e_ref[l, :, lanes(q, units)]
            if k == 0:
                place_expand(l, 0, part)
            else:
                pieces[l, k - 1, tall:, :units] = part
                pieces[l, k - 1, tall:, units:] = jnp.zeros((small, depth - units), bf16)
        packs[l, z_at, y_at, top : top + high, :] = o_ref[l]

    mail.greet(FLIPS)

    def to_group(l, ks):
        return [
            (
                k,
                mail.send(
                    pieces.at[l, k - 1, 0:tall], packs.at[l, z_at, y_at, k * tall : (k + 1) * tall], k * RINGS
                ),
                mail.send(pieces.at[l, k - 1, tall : tall + small], ein.at[l, k - 1], k * RINGS),
            )
            for k in ks
        ]

    def from_group(l, copies):
        for k, one, two in copies:
            one.wait_recv()
            two.wait_recv()
            place_expand(l, k, ein[l, k - 1, :, :units])

    gathers = [
        [Gather(mail, packs, l, 0, 16, top), Gather(mail, packs, l, top, top + 32, rows)] for l in range(LAYERS)
    ]
    first = to_group(0, (2, 3, 1))
    xin[0] = x_ref[...]

    def start_dout(i, carry):
        at = pl.ds(pl.multiple_of(i * STRIP, STRIP), STRIP)
        flags = jnp.broadcast_to(age_scr[at, 0:1], (STRIP, depth))
        douts[0, at, :] = (cot_ref[at, :].astype(f32) * flags).astype(bf16)
        return carry

    lax.fori_loop(0, tokens // STRIP, start_dout, 0)
    from_group(0, first)
    gathers[0][0].begin()
    aux_in = [mail.send(auxs.at[0], auxs.at[k], k * RINGS) for k in (1, 2, 3)]
    x_near = mail.send(x_ref, xin.at[1], CORE)
    x_far = mail.send(x_ref, xin.at[2], CHIP)
    second = to_group(1, (1,))
    dout_near = mail.send(douts.at[0], douts.at[1], CORE)
    gathers[0][0].step(1)
    gathers[0][0].step(2)
    gathers[0][1].begin()
    x_far.wait_recv()
    x_relay = mail.send(xin.at[2], xin.at[3], CORE)
    second += to_group(1, (2, 3))
    dout_far = mail.send(douts.at[0], douts.at[2], CHIP)
    gathers[0][0].step(3)

    def open_value(l):
        for j in range(RINGS):
            for k in range(GROUP):
                index = (dp ^ k) * RINGS + j
                at = slice(k * tall, (k + 1) * tall)
                source = packs.at[l, j // 2, j % 2]
                vw[l, pl.ds(pl.multiple_of(index * tall, tall), tall), :] = source[at, :width]
                mixn_ref[l, pl.ds(pl.multiple_of(index * small, small), small), :] = source[
                    k * tall : k * tall + small, width:
                ]
                if l == 0:
                    vecn[index] = source[k * tall + small : (k + 1) * tall, width:].astype(f32)

        if l == 0:
            for each in range(LAYERS):
                open_vectors(each)
        lag = lax.broadcasted_iota(jnp.int32, (tokens, states), 0).astype(f32)
        filt_ref[l] = nn(jnp.exp(-lag * rows_ref[l, 3:4, :states]).astype(bf16), mixn_ref[l])

    def open_vectors(l):
        def line(r, rep, put, group=False):
            r = r + 8 * l
            short = vecn[pl.ds(dp * RINGS, RINGS), r, :] if group else vecn[:, r, :]
            return jnp.sum(nn(short.astype(bf16), rep) * put, axis=0, keepdims=True)

        rows_ref[l] = jnp.zeros(rows_ref.shape[1:], f32)
        for r in range(3):
            rows_ref[l, r : r + 1, :] = line(r, rep32[...], put32[...])
        rows_ref[l, 3:4, :states] = line(3, rep16[...], put16[...])
        rows_ref[l, 4:5, :units] = line(4, rep96[...], put96[...], True)
        rows_ref[l, 4:5, units:width] = line(5, rep16[:, :LANES], put16[:RINGS, :LANES], True)
        rows_ref[l, 5:6, :LANES] = line(6, rep16[:, :LANES], put16[:RINGS, :LANES], True)
        rows_ref[l, 6:7, :units] = line(7, rep96[...], put96[...], True)

    def open_out(l):
        for j in range(RINGS):
            source = packs.at[l, j // 2, j % 2]
            ow[l, j * high : (j + 1) * high, :] = source[top : top + high, :]
            for k in range(GROUP):
                index = (dp ^ k) * RINGS + j
                at = pl.ds(pl.multiple_of(index * small, small), small)
                for t in range(thirds):
                    r, c = divmod(k * thirds + t, across)
                    base = top + high + small * r
                    ew[l, at, t * 256 : (t + 1) * 256] = source[
                        base : base + small, c * 256 : (c + 1) * 256
                    ]

    def normalize(l, read, dst):
        def strip(i, carry):
            at = pl.ds(pl.multiple_of(i * STRIP, STRIP), STRIP)
            v = read(at)
            center = v - jnp.mean(v, axis=1, keepdims=True)
            scale = lax.rsqrt(jnp.mean(center * center, axis=1, keepdims=True) + 1e-05)
            dst[at, :] = (center * scale * rows_ref[l, 0:1, :] + rows_ref[l, 1:2, :]).astype(bf16)
            return carry

        lax.fori_loop(0, tokens // STRIP, strip, 0)

    def branch_in(l, j):
        base = j * tokens
        a_scr[...] = nn(norm[l, j], vw[l])
        age_scr[...] = jnp.broadcast_to(auxs[j, :, 0:1].astype(f32), (tokens, LANES))

        def smooth(i, carry):
            here = pl.ds(pl.multiple_of(i * STRIP, STRIP), STRIP)
            there = pl.ds(pl.multiple_of(base + i * STRIP, STRIP), STRIP)
            v = a_scr[here, :] + rows_ref[l, 4:5, :width]
            cdf = 0.5 + 0.5 * lax.erf(v * 0.7071067811865476)
            slope = cdf + v * (0.3989422804014327 * jnp.exp(-0.5 * v * v))
            act = v * cdf
            value[l, there, :] = act[:, :units].astype(bf16)
            gp[l, there, :] = slope[:, :units].astype(bf16)
            mask = jnp.broadcast_to(auxs[j, here, 2:3].astype(f32), (STRIP, LANES))
            z[l, there, :] = act[:, units:] * mask
            g2[l, there, :] = slope[:, units:] * mask
            return carry

        lax.fori_loop(0, tokens // STRIP, smooth, 0)
        signal = z[l, base : base + tokens, :]
        for b in range(8):
            shifted[b, PAD:, :] = signal if b == 0 else pltpu.roll(signal, b, 0)

        for s in range(tokens // STRIP):
            age = age_scr[s * STRIP : (s + 1) * STRIP, :]

            def lags(a, acc, s=s, age=age):
                start = pl.multiple_of(a * 8, 8)
                left = age - (a * 8).astype(f32)
                for b in range(8):
                    row = filt_ref[l, pl.ds(start + b, 1), :]
                    past = shifted[b, pl.ds(pl.multiple_of(PAD + s * STRIP - start, 8), STRIP), :]
                    acc = acc + jnp.where(left >= b, past, 0.0) * row
                return acc

            y_scr[s * STRIP : (s + 1) * STRIP, :] = lax.fori_loop(
                0, (s + 1) * (STRIP // 8), lags, jnp.zeros((STRIP, LANES), f32)
            )
        ybuf[l, j] = (y_scr[...] + rows_ref[l, 5:6, :LANES] * signal).astype(bf16)

    def branch_out(l, j):
        at = slice(j * tokens, (j + 1) * tokens)
        for k, part in ((0, ybuf[l, j]), (1, yin[l, 0, j ^ 1]), (2, yin[l, 1, j ^ 2]), (3, yin[l, 2, j ^ 3])):
            full[l, at, lanes(dp ^ k, LANES)] = part
        c = nn(full[l, at, :], ew[l]) + rows_ref[l, 6:7, :units]
        product = (c * value[l, at, :].astype(f32)).astype(bf16)
        cbuf[l, at, :] = c.astype(bf16)
        obuf[j] = nn(product, ow[l]).astype(bf16)

    for b in range(8):
        shifted[b, :PAD, :] = jnp.zeros((PAD, LANES), f32)

    def layer(l, events):
        def due():
            if events:
                events.pop(0)()

        branch_in(l, 0)
        due()
        branch_in(l, 1)
        near = [mail.send(ybuf.at[l, 0:2], yin.at[l, 0, 0:2], CORE)]
        far = [mail.send(ybuf.at[l, 0:2], yin.at[l, 1, 0:2], CHIP)]
        due()
        return near, far

    def layer_rest(l, near, far, events, ready):
        def due():
            if events:
                events.pop(0)()

        branch_in(l, 2)
        due()
        branch_in(l, 3)
        near.append(mail.send(ybuf.at[l, 2:4], yin.at[l, 0, 2:4], CORE))
        far.append(mail.send(ybuf.at[l, 2:4], yin.at[l, 1, 2:4], CHIP))
        far[0].wait_recv()
        relay = [mail.send(yin.at[l, 1, 0:2], yin.at[l, 2, 0:2], CORE)]
        due()
        ready()
        near[1].wait_recv()
        relay[0].wait_recv()
        branch_out(l, 3)
        core_hi = mail.send(obuf.at[3], oin.at[l, 0], CORE)
        branch_out(l, 2)
        core_hi.wait_recv()
        both = (obuf[2].astype(f32) + oin[l, 0].astype(f32)).astype(bf16)
        if l == 0:
            oadd[...] = both
            cross = mail.send(oadd, ofar, CHIP)
        else:
            cross_ref[...] = both
        due()
        far[1].wait_recv()
        relay.append(mail.send(yin.at[l, 1, 2:4], yin.at[l, 2, 2:4], CORE))
        near[0].wait_recv()
        relay[1].wait_recv()
        branch_out(l, 1)
        core_lo = mail.send(obuf.at[1], oin.at[l, 1], CORE)
        branch_out(l, 0)
        core_lo.wait_recv()
        due()
        if l == 0:
            cross.wait_recv()

        def strip(i, carry):
            at = pl.ds(pl.multiple_of(i * STRIP, STRIP), STRIP)
            branch = obuf[0, at, :].astype(f32) + oin[l, 1, at, :].astype(f32)
            if l == 0:
                branch = branch + ofar[at, :].astype(f32)
            mask = auxs[0, at, 2:3].astype(f32)
            before = x_ref[at, :].astype(f32) if l == 0 else xcur[at, :]
            now = before + mask * (branch + rows_ref[l, 2:3, :])
            if l == 0:
                xcur[at, :] = now
                later_ref[at, :] = now
            else:
                out_ref[at, :] = now
            return carry

        lax.fori_loop(0, tokens // STRIP, strip, 0)
        mail.finish(core_hi)
        mail.finish(core_lo)
        for buf, hbm in ((cbuf, c_hbm), (full, full_hbm)):
            spill.put(buf.at[l], hbm.at[l])

    def spill_in(l):
        for buf, hbm in ((norm, norm_hbm), (value, value_hbm), (gp, gp_hbm), (z, z_hbm), (g2, g2_hbm)):
            spill.put(buf.at[l], hbm.at[l])

    def then(*steps):
        def event():
            for step in steps:
                step()

        return event

    nothing = then()

    gathers[0][0].end()
    open_value(0)
    spill.put(vw.at[0], vw_hbm.at[0])
    for copy in aux_in:
        copy.wait_recv()
    x_near.wait_recv()
    for j in (0, 1):
        normalize(0, lambda at, j=j: xin[j, at, :].astype(f32), norm.at[0, j])
    gathers[0][1].step(1)

    more = {}

    def next_value():
        from_group(1, second)
        gathers[1][0].begin()

    def relay_dout():
        dout_far.wait_recv()
        more["dout"] = mail.send(douts.at[2], douts.at[3], CORE)

    near, far = layer(0, [lambda: gathers[0][1].step(2), next_value])
    x_relay.wait_recv()
    for j in (2, 3):
        normalize(0, lambda at, j=j: xin[j, at, :].astype(f32), norm.at[0, j])

    def ready_out(l):
        def event():
            gathers[l][1].end()
            open_out(l)
            spill.put(ow.at[l], ow_hbm.at[l])
            spill.put(ew.at[l], ew_hbm.at[l])

        return event

    events = [
        then(lambda: gathers[0][1].step(3), relay_dout),
        nothing,
        lambda: gathers[1][0].step(1),
        then(lambda: gathers[1][0].step(2), lambda: gathers[1][1].begin()),
    ]
    layer_rest(0, near, far, events, ready_out(0))
    spill_in(0)

    gathers[1][0].step(3)
    normalize(1, lambda at: xcur[at, :], norm.at[1, 0])
    n_far = mail.send(norm.at[1, 0], norm.at[1, 2], CHIP)
    n_near = mail.send(norm.at[1, 0], norm.at[1, 1], CORE)
    gathers[1][0].end()
    open_value(1)
    spill.put(vw.at[1], vw_hbm.at[1])
    def relay_norm():
        n_far.wait_recv()
        more["relay"] = mail.send(norm.at[1, 2], norm.at[1, 3], CORE)

    n_near.wait_recv()
    gathers[1][1].step(1)
    near, far = layer(1, [then(relay_norm, lambda: gathers[1][1].step(2)), nothing])
    more["relay"].wait_recv()

    layer_rest(1, near, far, [lambda: gathers[1][1].step(3), nothing, nothing, nothing], ready_out(1))
    spill_in(1)
    dout_near.wait_recv()
    more["dout"].wait_recv()
    spill.put(douts, dout_hbm)
    mail.close()
    spill.close()


def forward_both(arrays, sizes):
    tokens, depth, units, feats, states, tall, small, high = sizes
    width = units + LANES
    group = tokens * GROUP
    rows = tall * GROUP + high + small * GROUP * units // depth
    shape = jax.ShapeDtypeStruct
    two = lambda *dims: (LAYERS,) + dims
    spilled = [
        (two(GROUP, tokens, depth), bf16), (two(group, units), bf16), (two(group, units), bf16),
        (two(group, units), bf16), (two(group, feats), bf16),
        (two(group, LANES), f32), (two(group, LANES), f32),
        (two(depth, width), bf16), (two(units, depth), bf16), (two(feats, units), bf16),
        ((GROUP, tokens, depth), bf16),
    ]
    kept = [
        ((tokens, depth), f32), ((tokens, depth), bf16), ((tokens, depth), f32), (two(8, depth), f32),
        (two(tokens, LANES), f32),
        (two(states, LANES), bf16), ((GROUP, tokens, LANES), bf16),
    ]
    sems = 160
    return pl.pallas_call(
        partial(forward_kernel, sizes),
        out_shape=[shape(*s) for s in kept + spilled],
        in_specs=[pl.BlockSpec(memory_space=VMEM)] * len(arrays),
        out_specs=[pl.BlockSpec(memory_space=VMEM)] * len(kept)
        + [pl.BlockSpec(memory_space=pl.ANY)] * len(spilled),
        scratch_shapes=[
            VMEM(two(GROUP - 1, tall + small, depth), bf16),
            VMEM(two(GROUP - 1, small, depth), bf16),
            VMEM(two(LINE, 2, rows, depth), bf16),
            VMEM((GROUP * RINGS, tall - small, LANES), f32),
            VMEM(two(depth, width), bf16),
            VMEM(two(units, depth), bf16),
            VMEM(two(feats, units), bf16),
            VMEM((GROUP, tokens, depth), bf16),
            VMEM(two(GROUP, tokens, depth), bf16),
            VMEM((GROUP, tokens, depth), bf16),
            VMEM(two(group, units), bf16),
            VMEM(two(group, units), bf16),
            VMEM(two(group, units), bf16),
            VMEM(two(group, feats), bf16),
            VMEM(two(group, LANES), f32),
            VMEM(two(group, LANES), f32),
            VMEM(two(GROUP, tokens, LANES), bf16),
            VMEM(two(GROUP - 1, GROUP, tokens, LANES), bf16),
            VMEM((GROUP, tokens, depth), bf16),
            VMEM(two(2, tokens, depth), bf16),
            VMEM((tokens, depth), bf16),
            VMEM((tokens, depth), bf16),
            VMEM((tokens, depth), f32),
            VMEM((tokens, width), f32),
            VMEM((tokens, LANES), f32),
            VMEM((8, PAD + tokens, LANES), f32),
            VMEM((tokens, LANES), f32),
            VMEM((tall - small, LANES), f32),
            pltpu.SemaphoreType.DMA((sems,)),
            pltpu.SemaphoreType.DMA((sems,)),
            pltpu.SemaphoreType.DMA((32,)),
        ],
        compiler_params=pltpu.CompilerParams(
            vmem_limit_bytes=60 << 20, collective_id=1, has_side_effects=True
        ),
        cost_estimate=cost(120.0),
        name="forward_both",
    )(*arrays)


class Fetch:
    def __init__(self, sem):
        self.sem, self.count = sem, 0

    def get(self, src, dst):
        copy = pltpu.make_async_copy(src, dst, self.sem.at[self.count])
        self.count += 1
        copy.start()
        return copy


class Reduce:
    def __init__(self, mail, packs, ysum, zin, zother, l, begin, cut, end, lanes):
        self.mail, self.packs, self.ysum, self.zin, self.zother = mail, packs, ysum, zin, zother
        self.l, self.early, self.late, self.lanes = l, slice(begin, cut), slice(cut, end), lanes
        self.has_early = cut > begin
        self.other = slice(0, cut - begin) if begin == 0 else slice(16, 16 + cut - begin)
        self.over, self.steps = [], {}
        z = mail.z
        low = z < LINE // 2
        self.order = [
            jnp.where(low, 3, 0), jnp.where(low, 2, 1), jnp.where(low, 1 - z, 5 - z), z,
        ]

    def at(self, z, y, rows):
        return self.packs.at[self.l, z, y, rows, self.lanes]

    def add(self, z, y, rows, more):
        ref = self.at(z, y, rows)
        ref[...] = (ref[...].astype(f32) + more[...].astype(f32)).astype(bf16)

    def slots(self, step, early):
        out = []
        m = self.mail
        rows = self.early if early else self.late
        for side, way in enumerate((1, -1)):
            held = 4 + m.z - step if way == 1 else m.z - 4 + step
            if way == 1:
                can = (m.z + 1 <= step) & (m.z < LINE - 1)
            else:
                can = (LINE - m.z <= step) & (m.z > 0)
            at = jnp.clip(held, 0, LINE - 1)
            out.append((way, side, can, at, m.y, rows, self.zin.at[self.l, step - 1, side, rows, self.lanes], 0))
            if early:
                spot = self.zother.at[self.l, step - 1, side, self.other, self.lanes]
                out.append((way, side, can, at, 1 - m.y, rows, spot, 1))
        return out

    def pass_on(self, step, early):
        for way, side, can, at, y, rows, spot, which in self.slots(step, early):
            copy = self.mail.copy(self.at(at, y, rows), spot, self.mail.along(way))
            self.mail.start(copy, can)
            self.steps[early, step, side, which] = copy

    def take(self, step, early):
        z = self.mail.z
        for way, side, can, at, y, rows, spot, which in self.slots(step, early):
            copy = self.steps[early, step, side, which]
            if way == 1:
                when, mine = (z >= 1) & (step >= z), 3 + z - step
            else:
                when, mine = (z <= LINE - 2) & (step >= LINE - 1 - z), z - 3 + step

            def arrive(copy=copy, mine=mine, y=y, rows=rows, spot=spot):
                copy.wait_recv()
                self.add(jnp.clip(mine, 0, LINE - 1), y, rows, spot)

            only(when, arrive)

    def begin(self):
        m = self.mail
        if self.has_early:
            self.pass_on(1, True)
        for i, z in enumerate(self.order):
            copy = m.copy(
                self.at(z, 1 - m.y, self.late), self.ysum.at[self.l, i, self.late, self.lanes], m.peer(1)
            )
            m.start(copy)
            self.over.append(copy)

    def step(self, i):
        m = self.mail
        if i < LINE:
            self.over[i].wait_recv()
            self.add(self.order[i], m.y, self.late, self.ysum.at[self.l, i, self.late, self.lanes])
            if i:
                self.take(i, False)
            if i < LINE - 1:
                self.pass_on(i + 1, False)
            if self.has_early and i:
                self.take(i, True)
                if i < LINE - 1:
                    self.pass_on(i + 1, True)
                else:
                    self.last = m.copy(
                        self.at(m.z, 1 - m.y, self.early), self.ysum.at[self.l, 0, self.early, self.lanes], m.peer(1)
                    )
                    m.start(self.last)
        elif self.has_early:
            self.last.wait_recv()
            self.add(m.z, m.y, self.early, self.ysum.at[self.l, 0, self.early, self.lanes])


def backward_kernel(sizes, *refs):
    tokens, depth, units, feats, states, tall, small, high = sizes
    width = units + LANES
    top = tall * GROUP
    rows = top + high + small * GROUP * units // depth
    devices = GROUP * RINGS
    (
        cot_ref, x_ref, later_ref, rows_ref, filt_ref, mixn_ref, auxs, oadd_ref,
        norm_hbm, value_hbm, gp_hbm, c_hbm, full_hbm, z_hbm, g2_hbm, vw_hbm, ow_hbm, ew_hbm, dout_hbm,
    ) = refs[:19]
    dx_ref, vmine_ref, vtotal_ref, o_ref, raw_hbm, ofar_hbm = refs[19:25]
    (
        norm, value, gp, cbuf, full, z, g2, vw, ow, ew, dout, dcb, da,
        qe, qo, near, cross, far, ofar, dnbuf, din, dadd, dfar,
        packs, ysum, zin, zother, gsend, grecv, vsend, vin, vgrp,
        rem_scr, shifted, dz_scr, corr, y_scr, w_scr, o_scr, m_scr,
        send_sem, recv_sem, hbm_sem,
    ) = refs[25:]
    mail = Mail(send_sem, recv_sem)
    fetch = Fetch(hbm_sem)
    dp, z_at, y_at = mail.dp, mail.z, mail.y
    thirds = units // 256
    across = depth // 256
    strips = tokens // STRIP

    def lanes(at, size):
        return pl.ds(pl.multiple_of(at * size, LANES), size)

    def block(j):
        return pl.ds(pl.multiple_of(j * tokens, tokens), tokens)

    def load_out(l):
        return [
            fetch.get(ow_hbm.at[l], ow), fetch.get(ew_hbm.at[l], ew), fetch.get(value_hbm.at[l], value),
            fetch.get(gp_hbm.at[l], gp), fetch.get(c_hbm.at[l], cbuf), fetch.get(full_hbm.at[l], full),
        ]

    def load_in(l):
        return [
            fetch.get(z_hbm.at[l], z), fetch.get(g2_hbm.at[l], g2), fetch.get(vw_hbm.at[l], vw),
            fetch.get(norm_hbm.at[l], norm),
        ]

    first = fetch.get(dout_hbm, dout)
    loads = load_out(LAYERS - 1)
    more_loads = load_in(LAYERS - 1)
    vsend[...] = jnp.zeros(vsend.shape, f32)
    for b in range(8):
        shifted[b, tokens:, :] = jnp.zeros((PAD, LANES), f32)

    def start_dx(i, carry):
        at = pl.ds(pl.multiple_of(i * STRIP, STRIP), STRIP)
        up = cot_ref[at, :].astype(f32)
        dx_ref[at, :] = up
        low = (up * auxs[0, at, 2:3].astype(f32)).astype(bf16).astype(f32)
        return carry + jnp.sum(low, axis=0, keepdims=True)

    vsend[LAYERS - 1, 2:3, :] = lax.fori_loop(0, strips, start_dx, jnp.zeros((1, depth), f32))

    mail.greet((CORE, CHIP, BOTH, 1, 2, 3, 4, 5, 6, 7))

    def back_out(l, j):
        at = block(j)
        dgated = nt(dout[at, :], ow[...])
        val = value[at, :].astype(f32)
        gate = cbuf[at, :].astype(f32)
        dc = (dgated * val).astype(bf16)
        dcb[at, :] = dc
        da[at, :units] = (dgated * gate * gp[at, :].astype(f32)).astype(bf16)
        cbuf[at, :] = (gate * val).astype(bf16)
        vsend[l, 5:6, :units] += jnp.sum(dc.astype(f32), axis=0, keepdims=True)
        y_scr[...] = nt(dc, ew[...])
        for k in range(GROUP):
            part = y_scr[:, lanes(dp ^ k, LANES)].astype(bf16)
            if k % 2:
                qo[k // 2, j ^ 1] = part
            else:
                qe[k // 2, j] = part

    def back_in(l, j):
        at = block(j)
        rem_scr[...] = jnp.broadcast_to(auxs[j, :, 1:2].astype(f32), (tokens, LANES))
        dy = qe[0, j].astype(f32) + near[0, j].astype(f32) + far[j].astype(f32)
        for b in range(8):
            shifted[b, :tokens, :] = dy if b == 0 else pltpu.roll(dy, tokens - b, 0)
        for s in range(strips):
            rem = rem_scr[s * STRIP : (s + 1) * STRIP, :]
            past = z[pl.ds(pl.multiple_of(j * tokens + s * STRIP, STRIP), STRIP), :]

            def lags(a, acc, s=s, rem=rem, past=past):
                base = pl.multiple_of(a * 8, 8)
                left = rem - (a * 8).astype(f32)
                for b in range(8):
                    row = filt_ref[l, pl.ds(base + b, 1), :]
                    later = shifted[b, pl.ds(pl.multiple_of(s * STRIP + base, 8), STRIP), :]
                    later = jnp.where(left >= b, later, 0.0)
                    acc = acc + later * row
                    pair = later * past
                    corr[pl.ds(pl.multiple_of(base * 8 + b * 8, 8), 8), :] += (pair[0:8] + pair[8:16]) + (
                        pair[16:24] + pair[24:32]
                    )
                return acc

            dz_scr[s * STRIP : (s + 1) * STRIP, :] = lax.fori_loop(
                0, (strips - s) * (STRIP // 8), lags, jnp.zeros((STRIP, LANES), f32)
            )
        da2 = (dz_scr[...] + rows_ref[l, 5:6, :LANES] * dy) * g2[at, :]
        da[at, units:] = da2.astype(bf16)
        vsend[l, 5:6, units:width] += jnp.sum(z[at, :] * dy, axis=0, keepdims=True)
        vsend[l, 4:5, :width] += jnp.sum(da[at, :].astype(f32), axis=0, keepdims=True)
        dnbuf[j] = nt(da[at, :], vw[...]).astype(bf16)

    def grads_out_of(l):
        wide = high * GROUP
        for i in range(RINGS // GROUP):
            o_scr[...] = tn(cbuf[:, i * wide : (i + 1) * wide], dout[...]).astype(bf16)
            for g in range(GROUP):
                at = i * GROUP + g
                packs[l, at // 2, at % 2, top : top + high, :] = o_scr[g * high : (g + 1) * high, :]
        for t in range(thirds):
            w_scr[: 2 * tokens, :256] = tn(full[...], dcb[:, t * 256 : (t + 1) * 256]).astype(bf16)
            for j in range(RINGS):
                for k in range(GROUP):
                    r, c = divmod(k * thirds + t, across)
                    owner = (dp ^ k) * RINGS + j
                    base = top + high + small * r
                    packs[l, j // 2, j % 2, base : base + small, c * 256 : (c + 1) * 256] = w_scr[
                        pl.ds(pl.multiple_of(owner * small, small), small), :256
                    ]

    def grads_in_of(l, lane):
        wide = depth // GROUP
        size = lane.stop - lane.start
        for d in range(GROUP):
            w_scr[:wide, :size] = tn(norm[:, d * wide : (d + 1) * wide], da[:, lane]).astype(bf16)
            at = pl.ds(pl.multiple_of((dp ^ d) * tall, tall), tall)
            for j in range(RINGS):
                packs[l, j // 2, j % 2, at, lane] = w_scr[j * tall : (j + 1) * tall, :size]

    def mixing_of(l):
        lag = lax.broadcasted_iota(jnp.int32, (tokens, tokens * 8), 0)
        part = lax.broadcasted_iota(jnp.int32, (tokens, tokens * 8), 1) // 8
        total = nn((lag == part).astype(bf16), corr[...].astype(bf16))
        steps = lax.broadcasted_iota(jnp.int32, (tokens, states), 0).astype(f32)
        powers = jnp.exp(-steps * rows_ref[l, 3:4, :states]).astype(bf16)
        m_scr[...] = tn(powers, total.astype(bf16)).astype(bf16)
        for j in range(RINGS):
            for k in range(GROUP):
                owner = (dp ^ k) * RINGS + j
                side = packs.at[l, j // 2, j % 2, k * tall : (k + 1) * tall]
                side[:small, width:] = m_scr[pl.ds(pl.multiple_of(owner * small, small), small), :]
                side[small:, width:] = jnp.zeros((tall - small, LANES), bf16)
        steps = lax.broadcasted_iota(jnp.int32, (tokens, LANES), 0).astype(f32)
        terms = tn(powers, (total * steps).astype(bf16)) * mixn_ref[l].astype(f32)
        vsend[l, 3:4, :states] = -lax.dot_general(
            jnp.ones((8, LANES), f32), terms, cols_dims, precision=highest, preferred_element_type=f32
        )[0:1]

    state = {}
    bufs = (mail, packs, ysum, zin, zother)
    sums = [
        {
            "out": Reduce(*bufs, l, top, top + 32, rows, slice(0, depth)),
            "value": Reduce(*bufs, l, 0, 16, top, slice(0, units)),
            "rest": Reduce(*bufs, l, 0, 0, top, slice(units, depth)),
        }
        for l in range(LAYERS)
    ]

    def own(l, at, lane=slice(None)):
        return packs[l, z_at, y_at, at, lane]

    def group_out(l):
        sums[l]["out"].step(4)
        o_ref[l] = own(l, slice(top, top + high))
        for k in range(GROUP):
            dst = grecv.at[l, 0, tall : tall + small] if k == 0 else gsend.at[l, k - 1]
            for t in range(thirds):
                r, c = divmod(k * thirds + t, across)
                base = top + high + small * r
                dst[:, t * 256 : (t + 1) * 256] = own(l, slice(base, base + small), slice(c * 256, (c + 1) * 256))
            dst[:, units:] = jnp.zeros((small, depth - units), bf16)
            if k:
                state[l, "out", k] = mail.send(
                    gsend.at[l, k - 1], grecv.at[l, k, tall : tall + small], k * RINGS
                )

    def group_in(l, name):
        sums[l][name].step(4)
        lane = sums[l][name].lanes
        for k in (2, 3, 1):
            state[l, name, k] = mail.send(
                packs.at[l, z_at, y_at, k * tall : (k + 1) * tall, lane], grecv.at[l, k, 0:tall, lane], k * RINGS
            )
        grecv[l, 0, :tall, lane] = own(l, slice(0, tall), lane)

    def group_last(l):
        for name in ("out", "value", "rest"):
            for k in range(1, GROUP):
                state[l, name, k].wait_recv()
        state[l, "raw"] = fetch.get(grecv.at[l], raw_hbm.at[l])

    def vector_rest(l):
        state[l, "vr"] = [mail.send(vsend.at[l], vin.at[l, j - 1], j) for j in range(1, RINGS)]

    def vector_group(l):
        for copy in state[l, "vr"]:
            copy.wait_recv()
        total = vsend[l]
        for j in range(RINGS - 1):
            total = total + vin[l, j]
        vmine_ref[l] = total
        vgrp[l, 0] = total
        state[l, "vg"] = [mail.send(vgrp.at[l, 0], vgrp.at[l, k], k * RINGS) for k in range(1, GROUP)]

    def vector_last(l):
        for copy in state[l, "vg"]:
            copy.wait_recv()
        total = vgrp[l, 0]
        for k in range(1, GROUP):
            total = total + vgrp[l, k]
        vtotal_ref[l] = total

    def pair(fn, lo):
        def body(i, carry):
            fn(lo + i)
            return carry

        lax.fori_loop(0, 2, body, 0)

    def exchange_dy(half):
        return mail.send(qo.at[:, half], near.at[:, half], CORE)

    def cross_dy(half, other, copy):
        copy.wait_recv()
        cross[half] = (qe[1, half].astype(f32) + near[1, half].astype(f32)).astype(bf16)
        return mail.send(cross.at[half], far.at[other], CHIP)

    lo, hi = slice(0, 2), slice(2, 4)

    def layer(l, loads, more_loads, events, wait_far):
        def due():
            if events:
                events.pop(0)()

        for copy in loads:
            copy.wait()
        corr[...] = jnp.zeros(corr.shape, f32)
        pair(lambda j: back_out(l, j), 0)
        near_lo = exchange_dy(lo)
        wait_far()
        pair(lambda j: back_out(l, j), 2)
        near_hi = exchange_dy(hi)
        cross_lo = cross_dy(lo, hi, near_lo)
        cross_hi = cross_dy(hi, lo, near_hi)
        if l:
            state["o"] = mail.send(oadd_ref, ofar, CHIP)
        due()
        grads_out_of(l)
        sums[l]["out"].begin()
        next_loads = load_out(l - 1) if l else []
        for copy in more_loads:
            copy.wait()
        due()
        grads_in_of(l, slice(0, units))
        sums[l]["value"].begin()
        due()
        cross_lo.wait_recv()
        back_in(l, 3)
        core_hi = mail.send(dnbuf.at[3], din.at[0], CORE)
        due()
        back_in(l, 2)
        core_hi.wait_recv()
        dadd[...] = (dnbuf[2].astype(f32) + din[0].astype(f32)).astype(bf16)
        chip = mail.send(dadd, dfar, CHIP)
        due()
        cross_hi.wait_recv()
        back_in(l, 1)
        core_lo = mail.send(dnbuf.at[1], din.at[1], CORE)
        due()
        back_in(l, 0)
        due()
        grads_in_of(l, slice(units, width))
        mixing_of(l)
        sums[l]["rest"].begin()
        next_more = load_in(l - 1) if l else []
        due()
        core_lo.wait_recv()
        chip.wait_recv()

        def strip(i, carry):
            gain_sum, shift_sum, out_sum = carry
            at = pl.ds(pl.multiple_of(i * STRIP, STRIP), STRIP)
            v = later_ref[at, :] if l else x_ref[at, :].astype(f32)
            center = v - jnp.mean(v, axis=1, keepdims=True)
            scale = lax.rsqrt(jnp.mean(center * center, axis=1, keepdims=True) + 1e-05)
            normed = center * scale
            grad = dnbuf[0, at, :].astype(f32) + din[1, at, :].astype(f32) + dfar[at, :].astype(f32)
            q = grad * rows_ref[l, 0:1, :]
            tilt = q - jnp.mean(q, axis=1, keepdims=True) - normed * jnp.mean(q * normed, axis=1, keepdims=True)
            up = dx_ref[at, :] + tilt * scale
            dx_ref[at, :] = up
            if l:
                low = (up * auxs[0, at, 2:3].astype(f32)).astype(bf16)
                dout[at, :] = low
                out_sum = out_sum + jnp.sum(low.astype(f32), axis=0, keepdims=True)
            return (
                gain_sum + jnp.sum(grad * normed, axis=0, keepdims=True),
                shift_sum + jnp.sum(grad, axis=0, keepdims=True),
                out_sum,
            )

        zero = jnp.zeros((1, depth), f32)
        gain_sum, shift_sum, out_sum = lax.fori_loop(0, strips, strip, (zero, zero, zero))
        vsend[l, 0:1, :] = gain_sum
        vsend[l, 1:2, :] = shift_sum
        if l:
            vsend[l - 1, 2:3, :] = out_sum
        for copy in (near_lo, near_hi, cross_lo, cross_hi, core_hi, core_lo, chip):
            mail.finish(copy)
        return next_loads, next_more

    first.wait()

    def then(*steps):
        def event():
            for step in steps:
                step()

        return event

    nothing = then()

    def step(l, name, i):
        return lambda: sums[l][name].step(i)

    events = [
        nothing, nothing, nothing, step(1, "out", 0), step(1, "out", 1), step(1, "out", 2), step(1, "out", 3), nothing,
    ]
    loads, more_loads = layer(1, loads, more_loads, events, nothing)

    dout_chip = mail.send(dout.at[pl.ds(0, tokens)], dout.at[pl.ds(2 * tokens, tokens)], CHIP)
    dout_core = mail.send(dout.at[pl.ds(0, tokens)], dout.at[pl.ds(tokens, tokens)], CORE)
    vector_rest(1)
    state["o"].wait_recv()
    far_out = fetch.get(ofar, ofar_hbm)
    step(1, "value", 0)()

    def dout_far():
        step(1, "value", 1)()
        dout_chip.wait_recv()
        relay = mail.send(dout.at[pl.ds(2 * tokens, tokens)], dout.at[pl.ds(3 * tokens, tokens)], CORE)
        step(1, "value", 2)()
        relay.wait_recv()

    events = [
        then(step(1, "value", 3), lambda: group_out(1)),
        then(step(1, "rest", 0), step(1, "rest", 1), lambda: vector_group(1)),
        then(step(1, "rest", 2), step(1, "rest", 3), lambda: group_in(1, "value")),
        then(step(0, "out", 0), lambda: group_in(1, "rest")),
        step(0, "out", 1),
        then(step(0, "out", 2), lambda: vector_last(1)),
        then(step(0, "out", 3), lambda: group_last(1)),
        then(step(0, "value", 0), step(0, "value", 1)),
    ]
    dout_core.wait_recv()
    layer(0, loads, more_loads, events, dout_far)
    vector_rest(0)
    step(0, "value", 2)()
    group_out(0)
    step(0, "value", 3)()
    vector_group(0)
    step(0, "rest", 0)()
    step(0, "rest", 1)()
    group_in(0, "value")
    step(0, "rest", 2)()
    step(0, "rest", 3)()
    group_in(0, "rest")
    vector_last(0)
    group_last(0)
    mail.close()
    far_out.wait()
    for l in range(LAYERS):
        state[l, "raw"].wait()


def backward_both(arrays, sizes):
    tokens, depth, units, feats, states, tall, small, high = sizes
    width = units + LANES
    group = tokens * GROUP
    rows = tall * GROUP + high + small * GROUP * units // depth
    shape = jax.ShapeDtypeStruct
    two = lambda *dims: (LAYERS,) + dims
    outs = [
        ((tokens, depth), f32), (two(8, depth), f32), (two(8, depth), f32), (two(high, depth), bf16),
        (two(GROUP, tall + small, depth), bf16), ((tokens, depth), bf16),
    ]
    return pl.pallas_call(
        partial(backward_kernel, sizes),
        out_shape=[shape(*s) for s in outs],
        in_specs=[pl.BlockSpec(memory_space=VMEM)] * 8 + [pl.BlockSpec(memory_space=pl.ANY)] * 11,
        out_specs=[pl.BlockSpec(memory_space=VMEM)] * 4 + [pl.BlockSpec(memory_space=pl.ANY)] * 2,
        scratch_shapes=[
            VMEM((group, depth), bf16),
            VMEM((group, units), bf16),
            VMEM((group, units), bf16),
            VMEM((group, units), bf16),
            VMEM((group, feats), bf16),
            VMEM((group, LANES), f32),
            VMEM((group, LANES), f32),
            VMEM((depth, width), bf16),
            VMEM((units, depth), bf16),
            VMEM((feats, units), bf16),
            VMEM((group, depth), bf16),
            VMEM((group, units), bf16),
            VMEM((group, width), bf16),
            VMEM((2, GROUP, tokens, LANES), bf16),
            VMEM((2, GROUP, tokens, LANES), bf16),
            VMEM((2, GROUP, tokens, LANES), bf16),
            VMEM((GROUP, tokens, LANES), bf16),
            VMEM((GROUP, tokens, LANES), bf16),
            VMEM((tokens, depth), bf16),
            VMEM((GROUP, tokens, depth), bf16),
            VMEM((2, tokens, depth), bf16),
            VMEM((tokens, depth), bf16),
            VMEM((tokens, depth), bf16),
            VMEM(two(LINE, 2, rows, depth), bf16),
            VMEM(two(LINE, rows, depth), bf16),
            VMEM(two(LINE - 1, 2, rows, depth), bf16),
            VMEM(two(LINE - 1, 2, 48, depth), bf16),
            VMEM(two(GROUP - 1, small, depth), bf16),
            VMEM(two(GROUP, tall + small, depth), bf16),
            VMEM(two(8, depth), f32),
            VMEM(two(RINGS - 1, 8, depth), f32),
            VMEM(two(GROUP, 8, depth), f32),
            VMEM((tokens, LANES), f32),
            VMEM((8, PAD + tokens, LANES), f32),
            VMEM((tokens, LANES), f32),
            VMEM((tokens * 8, LANES), f32),
            VMEM((tokens, feats), f32),
            VMEM((2 * tokens, width), bf16),
            VMEM((high * GROUP, depth), bf16),
            VMEM((states, LANES), bf16),
            pltpu.SemaphoreType.DMA((220,)),
            pltpu.SemaphoreType.DMA((220,)),
            pltpu.SemaphoreType.DMA((26,)),
        ],
        compiler_params=pltpu.CompilerParams(
            vmem_limit_bytes=60 << 20, collective_id=2, has_side_effects=True
        ),
        cost_estimate=cost(140.0),
        name="backward_both",
    )(*arrays)


def finish(me, arrays, sizes):
    tokens, depth, units, feats, states, tall, small, high = sizes
    width = units + LANES
    devices = GROUP * RINGS
    hidden = units * GROUP

    def kernel(me_ref, *refs):
        hbm = refs[: len(arrays)]
        (
            last_ref, dx_ref, gain_ref, shift_ref, v_ref, vb_ref, r_ref, rb_ref, dec_ref, si_out, so_out,
            skip_ref, e_ref, eb_ref, o_ref, ob_ref,
        ) = refs[len(arrays) : len(arrays) + 16]
        here, sem = refs[len(arrays) + 16 : -1], refs[-1]
        copies = [pltpu.make_async_copy(a, b, sem.at[i]) for i, (a, b) in enumerate(zip(hbm, here))]
        for copy in copies:
            copy.start()
        for copy in copies:
            copy.wait()
        raw, out_part, mine_ref, total_ref, dx_in, last_in, far_in, aux_ref, si_ref, so_ref = here
        dp, fs = me_ref[0], me_ref[1]
        index = dp * RINGS + fs

        def lanes(at, size):
            return pl.ds(pl.multiple_of(at * size, LANES), size)

        flags = aux_ref[0, :, 2:3].astype(f32)
        last_ref[...] = (last_in[...] + flags * far_in[...].astype(f32)).astype(bf16)
        dx_ref[...] = dx_in[...]
        o_ref[...] = out_part[...].astype(f32)
        apart = lax.broadcasted_iota(jnp.int32, (depth, LANES), 0) - lax.broadcasted_iota(
            jnp.int32, (depth, LANES), 1
        )
        for l in range(LAYERS):
            for k in range(GROUP):
                q = dp ^ k
                v_ref[l, :, lanes(q, units)] = raw[l, k, :tall, :units].astype(f32)
                r_ref[l, :, lanes(q, LANES)] = raw[l, k, :tall, units:width].astype(f32)
                e_ref[l, :, lanes(q, units)] = raw[l, k, tall:, :units].astype(f32)
                part = raw[l, k, :small, width:].astype(f32)
                si_out[l, :, lanes(q, LANES)] = part * so_ref[l, :, lanes(q, LANES)].astype(f32)
                so_out[l, :, lanes(q, LANES)] = part * si_ref[l, :, lanes(q, LANES)].astype(f32)

            def pick(ref, start):
                return jnp.dot(
                    ref[l], (apart == start).astype(f32), precision=highest, preferred_element_type=f32
                )

            long, short, mid = depth // devices, states // devices, units // RINGS
            got = pick(total_ref, index * long)
            for r, ref in enumerate((gain_ref, shift_ref, ob_ref)):
                ref[l : l + 1, :] = got[r : r + 1, :long]
            dec_ref[l : l + 1, :] = pick(total_ref, index * short)[3:4, :short]
            got = pick(mine_ref, fs * mid)
            vb_ref[l : l + 1, :] = got[4:5, :mid]
            eb_ref[l : l + 1, :] = got[5:6, :mid]
            got = pick(mine_ref, units + fs * short)
            rb_ref[l : l + 1, :] = got[4:5, :short]
            skip_ref[l : l + 1, :] = got[5:6, :short]

    two = lambda *dims: (LAYERS,) + dims
    outs = [
        (tokens, depth), two(depth // devices), two(depth // devices), two(tall, hidden), two(units // RINGS),
        two(tall, feats), two(LANES // RINGS), two(states // devices), two(small, feats), two(small, feats),
        two(LANES // RINGS), two(small, hidden), two(units // RINGS), two(high, depth), two(depth // devices),
    ]
    return pl.pallas_call(
        kernel,
        out_shape=[jax.ShapeDtypeStruct((tokens, depth), bf16)] + [jax.ShapeDtypeStruct(s, f32) for s in outs],
        in_specs=[pl.BlockSpec(memory_space=pltpu.SMEM)] + [pl.BlockSpec(memory_space=pl.ANY)] * len(arrays),
        out_specs=[pl.BlockSpec(memory_space=VMEM)] * 16,
        scratch_shapes=[VMEM(a.shape, a.dtype) for a in arrays] + [pltpu.SemaphoreType.DMA((len(arrays),))],
        compiler_params=pltpu.CompilerParams(vmem_limit_bytes=60 << 20),
        cost_estimate=cost(4.0),
        name="finish",
    )(me, *arrays)


def mixer(labels, signal, decays, stateinput, stateoutput, skipgain):
    rows = signal.shape[0]
    width = min(32, rows)
    count = rows // width
    mixing = stateinput * stateoutput
    offsets = jnp.arange(width, dtype=jnp.float32)
    powers = jnp.exp(-offsets[:, None] * decays[None, :])
    kernel = jnp.dot(powers, mixing, precision=highest)
    positions = jnp.arange(width, dtype=jnp.int32)
    lagged = jnp.maximum(positions[:, None] - positions[None, :], 0)
    toeplitz = jnp.take(kernel, lagged, axis=0)
    causal = positions[:, None] >= positions[None, :]
    leading = jnp.exp(-(offsets[:, None] + 1.0) * decays[None, :])
    trailing = jnp.exp(-(width - 1.0 - offsets[:, None]) * decays[None, :])
    across = jnp.exp(-width * decays)

    def advance(carry, pieces):
        state, before = carry
        block, marks = pieces
        same = jnp.logical_and(marks[:, None] == marks[None, :], causal).astype(signal.dtype)
        inner = jnp.sum(toeplitz * same[:, :, None] * block[None, :, :], axis=1)
        joined = (marks == before).astype(signal.dtype)
        carried = jnp.dot(leading, mixing * state, precision=highest) * joined[:, None]
        final = marks[width - 1]
        keep = (final == before).astype(signal.dtype)
        fresh = (marks == final).astype(signal.dtype)
        state = across[:, None] * state * keep + lax.dot_general(
            trailing * fresh[:, None], block, rows_dims, precision=highest
        )
        return ((state, final), inner + carried)

    start = (jnp.zeros(mixing.shape, signal.dtype), jnp.array(-1, jnp.int32))
    ending, mixed = lax.scan(
        jax.checkpoint(advance),
        start,
        (signal.reshape(count, width, -1), labels.reshape(count, width)),
    )
    return mixed.reshape(rows, -1) + skipgain[None, :] * signal


def normalize(rows, gain, shift):
    center = rows - jnp.mean(rows, axis=1, keepdims=True)
    spread = jnp.mean(center * center, axis=1, keepdims=True)
    return center * lax.rsqrt(spread + 1e-05) * gain + shift


def smooth(values):
    return jax.nn.gelu(values, approximate=False)


def gather_forward(shards, depth):
    return (
        lax.all_gather(shards[0][depth], ("dp", "fsdp"), axis=0, tiled=True),
        lax.all_gather(shards[1][depth], ("dp", "fsdp"), axis=0, tiled=True),
        lax.all_gather(shards[2][depth], ("dp", "fsdp"), axis=0, tiled=True),
        lax.all_gather(shards[3][depth], ("dp", "fsdp"), axis=0, tiled=True),
        lax.all_gather(shards[4][depth], ("dp", "fsdp"), axis=0, tiled=True),
        lax.all_gather(shards[5][depth], ("dp", "fsdp"), axis=0, tiled=True),
        lax.all_gather(shards[6][depth], ("dp", "fsdp"), axis=0, tiled=True),
        lax.all_gather(shards[7][depth], ("dp", "fsdp"), axis=0, tiled=True),
        lax.all_gather(shards[8][depth], ("dp", "fsdp"), axis=0, tiled=True),
        lax.all_gather(shards[9][depth], ("dp", "fsdp"), axis=0, tiled=True),
        lax.all_gather(shards[10][depth], ("dp", "fsdp"), axis=0, tiled=True),
        lax.all_gather(shards[11][depth], ("dp", "fsdp"), axis=0, tiled=True),
        lax.all_gather(shards[12][depth], ("dp", "fsdp"), axis=0, tiled=True),
        lax.all_gather(shards[13][depth], ("dp", "fsdp"), axis=0, tiled=True),
    )


def gather_backward(shards, depth):
    return (
        lax.all_gather(shards[0][depth], ("dp", "fsdp"), axis=0, tiled=True),
        lax.all_gather(shards[1][depth], ("dp", "fsdp"), axis=0, tiled=True),
        lax.all_gather(shards[2][depth], ("dp", "fsdp"), axis=0, tiled=True),
        lax.all_gather(shards[3][depth], ("dp", "fsdp"), axis=0, tiled=True),
        lax.all_gather(shards[4][depth], ("dp", "fsdp"), axis=0, tiled=True),
        lax.all_gather(shards[5][depth], ("dp", "fsdp"), axis=0, tiled=True),
        lax.all_gather(shards[6][depth], ("dp", "fsdp"), axis=0, tiled=True),
        lax.all_gather(shards[7][depth], ("dp", "fsdp"), axis=0, tiled=True),
        lax.all_gather(shards[8][depth], ("dp", "fsdp"), axis=0, tiled=True),
        lax.all_gather(shards[9][depth], ("dp", "fsdp"), axis=0, tiled=True),
        lax.all_gather(shards[10][depth], ("dp", "fsdp"), axis=0, tiled=True),
        lax.all_gather(shards[11][depth], ("dp", "fsdp"), axis=0, tiled=True),
        lax.all_gather(shards[12][depth], ("dp", "fsdp"), axis=0, tiled=True),
        lax.all_gather(shards[13][depth], ("dp", "fsdp"), axis=0, tiled=True),
    )


def scatter_layer(terms):
    return (
        lax.psum_scatter(terms[0], ("dp", "fsdp"), scatter_dimension=0, tiled=True),
        lax.psum_scatter(terms[1], ("dp", "fsdp"), scatter_dimension=0, tiled=True),
        lax.psum_scatter(terms[2], ("dp", "fsdp"), scatter_dimension=0, tiled=True),
        lax.psum_scatter(terms[3], ("dp", "fsdp"), scatter_dimension=0, tiled=True),
        lax.psum_scatter(terms[4], ("dp", "fsdp"), scatter_dimension=0, tiled=True),
        lax.psum_scatter(terms[5], ("dp", "fsdp"), scatter_dimension=0, tiled=True),
        lax.psum_scatter(terms[6], ("dp", "fsdp"), scatter_dimension=0, tiled=True),
        lax.psum_scatter(terms[7], ("dp", "fsdp"), scatter_dimension=0, tiled=True),
        lax.psum_scatter(terms[8], ("dp", "fsdp"), scatter_dimension=0, tiled=True),
        lax.psum_scatter(terms[9], ("dp", "fsdp"), scatter_dimension=0, tiled=True),
        lax.psum_scatter(terms[10], ("dp", "fsdp"), scatter_dimension=0, tiled=True),
        lax.psum_scatter(terms[11], ("dp", "fsdp"), scatter_dimension=0, tiled=True),
        lax.psum_scatter(terms[12], ("dp", "fsdp"), scatter_dimension=0, tiled=True),
        lax.psum_scatter(terms[13], ("dp", "fsdp"), scatter_dimension=0, tiled=True),
    )


def layer_forward(current, labels, flags, weights):
    (
        normgain,
        normbias,
        valueproj,
        valuebias,
        reduceproj,
        reducebias,
        decays,
        stateinput,
        stateoutput,
        skipgain,
        expandproj,
        expandbias,
        outproj,
        outbias,
    ) = weights
    normed, norm_back = jax.vjp(
        normalize, current, normgain.astype(jnp.float32), normbias.astype(jnp.float32)
    )
    normed_low = normed.astype(jnp.bfloat16)
    opened = jnp.dot(normed_low, valueproj, preferred_element_type=jnp.float32) + valuebias.astype(
        jnp.float32
    )
    values, value_back = jax.vjp(smooth, opened)
    reduced = jnp.dot(
        normed_low, reduceproj, preferred_element_type=jnp.float32
    ) + reducebias.astype(jnp.float32)
    smoothed, reduce_back = jax.vjp(smooth, reduced)
    signal = smoothed * flags
    mixed, mix_back = jax.vjp(
        partial(mixer, labels),
        signal,
        decays.astype(jnp.float32),
        stateinput.astype(jnp.float32),
        stateoutput.astype(jnp.float32),
        skipgain.astype(jnp.float32),
    )
    mixed_low = mixed.astype(jnp.bfloat16)
    expanded = jnp.dot(
        mixed_low, expandproj, preferred_element_type=jnp.float32
    ) + expandbias.astype(jnp.float32)
    gated = (expanded * values).astype(jnp.bfloat16)
    branch = jnp.dot(gated, outproj, preferred_element_type=jnp.float32) + outbias.astype(
        jnp.float32
    )
    saved = (
        normed_low,
        values,
        value_back,
        reduce_back,
        mix_back,
        mixed_low,
        expanded,
        gated,
        norm_back,
    )
    return (current + flags * branch, saved)


def layer_backward(upstream, flags, weights, saved):
    (
        normgain,
        normbias,
        valueproj,
        valuebias,
        reduceproj,
        reducebias,
        decays,
        stateinput,
        stateoutput,
        skipgain,
        expandproj,
        expandbias,
        outproj,
        outbias,
    ) = weights
    normed_low, values, value_back, reduce_back, mix_back, mixed_low, expanded, gated, norm_back = (
        saved
    )
    dout = (flags * upstream).astype(jnp.bfloat16)
    outproj_term = lax.dot_general(gated, dout, rows_dims, preferred_element_type=jnp.float32)
    outbias_term = jnp.sum(dout, axis=0, dtype=jnp.float32)
    dgated = lax.dot_general(dout, outproj, cols_dims, preferred_element_type=jnp.float32)
    dexpanded = (dgated * values).astype(jnp.bfloat16)
    dvalues = dgated * expanded
    expandproj_term = lax.dot_general(
        mixed_low, dexpanded, rows_dims, preferred_element_type=jnp.float32
    )
    expandbias_term = jnp.sum(dexpanded, axis=0, dtype=jnp.float32)
    dmixed = lax.dot_general(dexpanded, expandproj, cols_dims, preferred_element_type=jnp.float32)
    dsignal, decays_term, stateinput_term, stateoutput_term, skipgain_term = mix_back(dmixed)
    (dreduced,) = reduce_back(dsignal * flags)
    dreduced_low = dreduced.astype(jnp.bfloat16)
    (dopened,) = value_back(dvalues)
    dopened_low = dopened.astype(jnp.bfloat16)
    valueproj_term = lax.dot_general(
        normed_low, dopened_low, rows_dims, preferred_element_type=jnp.float32
    )
    valuebias_term = jnp.sum(dopened_low, axis=0, dtype=jnp.float32)
    reduceproj_term = lax.dot_general(
        normed_low, dreduced_low, rows_dims, preferred_element_type=jnp.float32
    )
    reducebias_term = jnp.sum(dreduced_low, axis=0, dtype=jnp.float32)
    dnormed = lax.dot_general(dopened_low, valueproj, cols_dims, preferred_element_type=jnp.float32)
    dnormed = dnormed + lax.dot_general(
        dreduced_low, reduceproj, cols_dims, preferred_element_type=jnp.float32
    )
    dcurrent, normgain_term, normbias_term = norm_back(dnormed)
    terms = (
        normgain_term,
        normbias_term,
        valueproj_term,
        valuebias_term,
        reduceproj_term,
        reducebias_term,
        decays_term,
        stateinput_term,
        stateoutput_term,
        skipgain_term,
        expandproj_term,
        expandbias_term,
        outproj_term,
        outbias_term,
    )
    return (upstream + dcurrent, terms)


def plain(
    inputs,
    segment_ids,
    token_mask,
    cotangent,
    normgain,
    normbias,
    valueproj,
    valuebias,
    reduceproj,
    reducebias,
    decays,
    stateinput,
    stateoutput,
    skipgain,
    expandproj,
    expandbias,
    outproj,
    outbias,
):
    shards = (
        normgain,
        normbias,
        valueproj,
        valuebias,
        reduceproj,
        reducebias,
        decays,
        stateinput,
        stateoutput,
        skipgain,
        expandproj,
        expandbias,
        outproj,
        outbias,
    )
    flags = token_mask.astype(jnp.float32)[:, None]
    current = inputs.astype(jnp.float32)
    fetched = []
    stored = []
    for depth in range(LAYERS):
        weights = gather_forward(shards, depth)
        current, saved = layer_forward(current, segment_ids, flags, weights)
        fetched.append(weights)
        stored.append(saved)
    outputs = current.astype(jnp.bfloat16)
    upstream = cotangent.astype(jnp.float32)
    scattered = [None] * LAYERS
    for depth in reversed(range(LAYERS)):
        weights = gather_backward(shards, depth)
        upstream, terms = layer_backward(upstream, flags, weights, stored[depth])
        scattered[depth] = scatter_layer(terms)
    results = tuple(
        (jnp.stack([scattered[depth][index] for depth in range(LAYERS)]) for index in range(14))
    )
    return (outputs, upstream) + tuple(results)


def fast(
    inputs, segment_ids, token_mask, cotangent, normgain, normbias, valueproj, valuebias,
    reduceproj, reducebias, decays, stateinput, stateoutput, skipgain, expandproj, expandbias,
    outproj, outbias,
):
    tokens, depth = inputs.shape
    tall = valueproj.shape[1]
    small = stateinput.shape[1]
    high = outproj.shape[1]
    units = valueproj.shape[2] // GROUP
    feats = reduceproj.shape[2]
    states = stateinput.shape[1] * GROUP * RINGS
    group = tokens * GROUP
    sizes = (tokens, depth, units, feats, states, tall, small, high)

    lined = lambda v: v.reshape(tokens // LANES, LANES)
    shorts = (normgain, normbias, outbias, decays, valuebias, reducebias, skipgain, expandbias)
    (
        last, across, later, rows, filt, mixes, auxes,
        norms, value, slope, gate, full, z, slope2, value_w, out_w, expand_w, douts,
    ) = forward_both(
        (
            inputs, lined(segment_ids), lined(token_mask), cotangent, valueproj, reduceproj, expandproj,
            outproj, stateinput, stateoutput, *shorts, *tables(GROUP * RINGS),
        ),
        sizes,
    )
    dx, mine, total, out_part, raw, arrived = backward_both(
        (
            cotangent, inputs, later, rows, filt, mixes, auxes, across,
            norms.reshape(LAYERS, group, depth), value, slope, gate, full, z, slope2,
            value_w, out_w, expand_w, douts.reshape(group, depth),
        ),
        sizes,
    )
    me = jnp.stack([lax.axis_index("dp"), lax.axis_index("fsdp")]).astype(jnp.int32)
    arrays = (raw, out_part, mine, total, dx, last, arrived, auxes, stateinput, stateoutput)
    return tuple(finish(me, arrays, sizes))


def solution(mesh):
    placed = (
        P(("dp", "fsdp"), None),
        P(("dp", "fsdp")),
        P(("dp", "fsdp")),
        P(("dp", "fsdp"), None),
        P(None, ("dp", "fsdp")),
        P(None, ("dp", "fsdp")),
        P(None, ("dp", "fsdp"), None),
        P(None, ("dp", "fsdp")),
        P(None, ("dp", "fsdp"), None),
        P(None, ("dp", "fsdp")),
        P(None, ("dp", "fsdp")),
        P(None, ("dp", "fsdp"), None),
        P(None, ("dp", "fsdp"), None),
        P(None, ("dp", "fsdp")),
        P(None, ("dp", "fsdp"), None),
        P(None, ("dp", "fsdp")),
        P(None, ("dp", "fsdp"), None),
        P(None, ("dp", "fsdp")),
    )
    small = mesh.shape["dp"] == GROUP and mesh.shape["fsdp"] == RINGS
    return jax.shard_map(
        fast if small else plain,
        mesh=mesh,
        in_specs=placed,
        out_specs=(
            P(("dp", "fsdp"), None),
            P(("dp", "fsdp"), None),
            P(None, ("dp", "fsdp")),
            P(None, ("dp", "fsdp")),
            P(None, ("dp", "fsdp"), None),
            P(None, ("dp", "fsdp")),
            P(None, ("dp", "fsdp"), None),
            P(None, ("dp", "fsdp")),
            P(None, ("dp", "fsdp")),
            P(None, ("dp", "fsdp"), None),
            P(None, ("dp", "fsdp"), None),
            P(None, ("dp", "fsdp")),
            P(None, ("dp", "fsdp"), None),
            P(None, ("dp", "fsdp")),
            P(None, ("dp", "fsdp"), None),
            P(None, ("dp", "fsdp")),
        ),
        check_vma=False,
    )
```

```python
from functools import partial

import jax
import jax.numpy as jnp
import numpy as np
from jax import lax
from jax.experimental import pallas as pl
from jax.experimental.pallas import tpu as pltpu
from jax.sharding import PartitionSpec as P

LAYERS = 2
AXES = ("dp", "fsdp")
GROUP = 4
RINGS = 8
LANES = 128
STRIP = 32
PAD = 32

f32 = jnp.float32
bf16 = jnp.bfloat16
highest = lax.Precision.HIGHEST
rows_dims = (((0,), (0,)), ((), ()))
cols_dims = (((1,), (1,)), ((), ()))

VMEM = pltpu.VMEM


def cost(micros):
    return pl.CostEstimate(
        flops=int(micros * 1.0e9), bytes_accessed=1 << 20, transcendentals=0
    )


def nt(a, b):
    return lax.dot_general(a, b, cols_dims, preferred_element_type=f32)


def tn(a, b):
    return lax.dot_general(a, b, rows_dims, preferred_element_type=f32)


def nn(a, b):
    return jnp.dot(a, b, preferred_element_type=f32)


def tables(devices):
    out = []
    for count, size in ((devices, 32), (RINGS, 96), (devices, 16)):
        at = np.arange(count * size)
        out.append(jnp.asarray((np.arange(LANES)[:, None] == at[None, :] % size), bf16))
        out.append(jnp.asarray((np.arange(count)[:, None] == at[None, :] // size), f32))
    return out


class Mail:
    def __init__(self, send_sem, recv_sem):
        self.dp, self.fs = lax.axis_index("dp"), lax.axis_index("fsdp")
        self.z, self.y = self.fs // 2, self.fs % 2
        self.send_sem, self.recv_sem, self.count, self.sent = send_sem, recv_sem, 0, []

    def peer(self, flip):
        return (self.dp ^ (flip // RINGS), self.fs ^ (flip % RINGS))

    def along(self, way):
        return (self.dp, self.fs + 2 * way)

    def greet(self, flips):
        barrier = pltpu.get_barrier_semaphore()

        def hail(device):
            pl.semaphore_signal(barrier, inc=1, device_id=device, device_id_type=pl.DeviceIdType.MESH)

        for flip in flips:
            hail(self.peer(flip))
        ahead, behind = self.z < LINE - 1, self.z > 0
        pl.when(ahead)(lambda: hail(self.along(1)))
        pl.when(behind)(lambda: hail(self.along(-1)))
        pl.semaphore_wait(barrier, len(flips) + ahead.astype(jnp.int32) + behind.astype(jnp.int32))

    def copy(self, src, dst, device):
        made = pltpu.make_async_remote_copy(
            src_ref=src, dst_ref=dst, send_sem=self.send_sem.at[self.count],
            recv_sem=self.recv_sem.at[self.count], device_id=device,
            device_id_type=pl.DeviceIdType.MESH,
        )
        self.count += 1
        return made

    def start(self, copy, when=None):
        only(when, copy.start)
        self.sent.append((copy, when))

    def send(self, src, dst, flip):
        copy = self.copy(src, dst, self.peer(flip))
        self.start(copy)
        return copy

    def finish(self, copy):
        copy.wait_send()
        self.sent = [(c, w) for c, w in self.sent if c is not copy]

    def close(self):
        for copy, when in self.sent:
            only(when, copy.wait_send)


def only(when, step):
    if when is None:
        step()
    else:
        pl.when(when)(step)


class Gather:
    def __init__(self, mail, packs, l, begin, cut, end):
        self.mail, self.packs, self.l = mail, packs, l
        self.early, self.late = slice(begin, cut), slice(cut, end)
        self.steps, self.across = {}, []

    def line(self, rows, both, step):
        m = self.mail
        for way in (1, -1):
            held = m.z - way * (step - 1)
            can = (held >= 0) & (m.z < LINE - 1) if way == 1 else (held <= LINE - 1) & (m.z > 0)
            at = jnp.clip(held, 0, LINE - 1)
            ref = self.packs.at[self.l, at, :, rows] if both else self.packs.at[self.l, at, m.y, rows]
            copy = m.copy(ref, ref, m.along(way))
            m.start(copy, can)
            self.steps[both, step, way] = copy

    def over(self, rows, at, when):
        m = self.mail
        ref = self.packs.at[self.l, at, m.y, rows]
        copy = m.copy(ref, ref, m.peer(1))
        m.start(copy, when)
        self.across.append((copy, when))
        return copy

    def begin(self):
        self.first = self.over(self.early, self.mail.z, None)
        self.across = []
        self.line(self.late, False, 1)
        self.over(self.late, self.mail.z, None)

    def come(self, both, step):
        m = self.mail
        out = []
        for way in (1, -1):
            source = m.z - way * step
            when = source >= 0 if way == 1 else source <= LINE - 1
            only(when, self.steps[both, step, way].wait_recv)
            out.append((jnp.clip(source, 0, LINE - 1), when))
        return out

    def step(self, step):
        held = self.come(False, step)
        if step < LINE - 1:
            self.line(self.late, False, step + 1)
        for at, when in held:
            self.over(self.late, at, when)
        if step == 1:
            self.first.wait_recv()
        else:
            self.come(True, step - 1)
        self.line(self.early, True, step)

    def end(self):
        self.come(True, LINE - 1)
        for copy, when in self.across:
            only(when, copy.wait_recv)


class Spill:
    def __init__(self, sem):
        self.sem, self.open = sem, []

    def put(self, src, dst):
        copy = pltpu.make_async_copy(src, dst, self.sem.at[len(self.open)])
        copy.start()
        self.open.append(copy)

    def close(self):
        for copy in self.open:
            copy.wait()


CORE, CHIP, BOTH = RINGS, 2 * RINGS, 3 * RINGS
FLIPS = (CORE, CHIP, BOTH, 1)
LINE = RINGS // 2


def forward_kernel(sizes, *refs):
    tokens, depth, units, feats, states, tall, small, high = sizes
    width = units + LANES
    top = tall * GROUP
    rows = top + high + small * GROUP * units // depth
    (
        x_ref, seg_ref, mask_ref, cot_ref, v_ref, r_ref, e_ref, o_ref, si_ref, so_ref,
        *short_refs, rep32, put32, rep96, put96, rep16, put16,
    ) = refs[:24]
    (
        out_ref, cross_ref, later_ref, rows_ref, filt_ref, mixn_ref, auxs,
        norm_hbm, value_hbm, gp_hbm, c_hbm, full_hbm, z_hbm, g2_hbm,
        vw_hbm, ow_hbm, ew_hbm, dout_hbm,
    ) = refs[24:42]
    (
        pieces, ein, packs, vecn, vw, ow, ew, xin, norm, douts,
        value, gp, cbuf, full, z, g2, ybuf, yin, obuf, oin, oadd, ofar, xcur,
        a_scr, age_scr, shifted, y_scr, vec_scr, lead_scr, trail_scr, send_sem, recv_sem, hbm_sem,
    ) = refs[42:]
    mail = Mail(send_sem, recv_sem)
    spill = Spill(hbm_sem)
    dp, z_at, y_at = mail.dp, mail.z, mail.y
    thirds = units // 256
    across = depth // 256

    def lanes(index, size):
        return pl.ds(pl.multiple_of(index * size, LANES), size)

    def place_expand(l, k, part):
        for t in range(thirds):
            r, c = divmod(k * thirds + t, across)
            at = top + high + small * r
            packs[l, z_at, y_at, at : at + small, c * 256 : (c + 1) * 256] = part[:, t * 256 : (t + 1) * 256]

    vec_scr[...] = jnp.zeros(vec_scr.shape, f32)
    for l in range(LAYERS):
        for r, ref in enumerate(short_refs):
            vec_scr[8 * l + r : 8 * l + r + 1, : ref.shape[1]] = ref[l : l + 1, :].astype(f32)
    for l in range(LAYERS):
        a_scr[:small, :feats] = si_ref[l].astype(f32) * so_ref[l].astype(f32)
        for k in range(GROUP):
            q = dp ^ k
            dst = packs.at[l, z_at, y_at, 0:tall] if k == 0 else pieces.at[l, k - 1, 0:tall]
            dst[:, :units] = v_ref[l, :, lanes(q, units)]
            dst[:, units:width] = r_ref[l, :, lanes(q, LANES)]
            dst[:small, width:] = a_scr[:small, lanes(q, LANES)].astype(bf16)
            dst[small:, width:] = vec_scr[...].astype(bf16)
            part = e_ref[l, :, lanes(q, units)]
            if k == 0:
                place_expand(l, 0, part)
            else:
                pieces[l, k - 1, tall:, :units] = part
                pieces[l, k - 1, tall:, units:] = jnp.zeros((small, depth - units), bf16)
        packs[l, z_at, y_at, top : top + high, :] = o_ref[l]

    mail.greet(FLIPS)

    def to_group(l, ks):
        return [
            (
                k,
                mail.send(
                    pieces.at[l, k - 1, 0:tall], packs.at[l, z_at, y_at, k * tall : (k + 1) * tall], k * RINGS
                ),
                mail.send(pieces.at[l, k - 1, tall : tall + small], ein.at[l, k - 1], k * RINGS),
            )
            for k in ks
        ]

    def from_group(l, copies):
        for k, one, two in copies:
            one.wait_recv()
            two.wait_recv()
            place_expand(l, k, ein[l, k - 1, :, :units])

    gathers = [
        [Gather(mail, packs, l, 0, 16, top), Gather(mail, packs, l, top, top + 32, rows)] for l in range(LAYERS)
    ]
    first = to_group(0, (2, 3, 1))
    xin[0] = x_ref[...]

    def line_up(ref):
        row = jnp.concatenate([ref[i : i + 1, :] for i in range(tokens // LANES)], axis=1).astype(f32)
        return jnp.broadcast_to(row, (tokens, tokens))

    ids = line_up(seg_ref)
    here = lax.broadcasted_iota(jnp.int32, (tokens, tokens), 0)
    there = lax.broadcasted_iota(jnp.int32, (tokens, tokens), 1)
    same = (ids == ids.T).astype(f32)
    age = jnp.sum(jnp.where(there < here, same, 0.0), axis=1, keepdims=True)
    rest = jnp.sum(jnp.where(there > here, same, 0.0), axis=1, keepdims=True)
    mask = line_up(mask_ref).T[:, :LANES]
    lane = lax.broadcasted_iota(jnp.int32, (tokens, LANES), 1)
    auxs[0] = jnp.where(lane == 0, age, jnp.where(lane == 1, rest, jnp.where(lane == 2, mask, 0.0))).astype(bf16)
    age_scr[...] = mask

    from_group(0, first)
    gathers[0][0].begin()
    aux_in = [mail.send(auxs.at[0], auxs.at[k], k * RINGS) for k in (1, 2, 3)]
    x_near = mail.send(x_ref, xin.at[1], CORE)
    x_far = mail.send(x_ref, xin.at[2], CHIP)
    second = to_group(1, (1,))

    def start_dout(i, carry):
        at = pl.ds(pl.multiple_of(i * STRIP, STRIP), STRIP)
        flags = jnp.broadcast_to(age_scr[at, 0:1], (STRIP, depth))
        douts[0, at, :] = (cot_ref[at, :].astype(f32) * flags).astype(bf16)
        return carry

    lax.fori_loop(0, tokens // STRIP, start_dout, 0)
    dout_near = mail.send(douts.at[0], douts.at[1], CORE)
    gathers[0][0].step(1)
    gathers[0][0].step(2)
    gathers[0][1].begin()
    x_far.wait_recv()
    x_relay = mail.send(xin.at[2], xin.at[3], CORE)
    second += to_group(1, (2, 3))
    dout_far = mail.send(douts.at[0], douts.at[2], CHIP)
    gathers[0][0].step(3)

    def open_value(l):
        for j in range(RINGS):
            for k in range(GROUP):
                index = (dp ^ k) * RINGS + j
                at = slice(k * tall, (k + 1) * tall)
                source = packs.at[l, j // 2, j % 2]
                vw[l, pl.ds(pl.multiple_of(index * tall, tall), tall), :] = source[at, :width]
                mixn_ref[l, pl.ds(pl.multiple_of(index * small, small), small), :] = source[
                    k * tall : k * tall + small, width:
                ]
                if l == 0:
                    vecn[index] = source[k * tall + small : (k + 1) * tall, width:].astype(f32)

        if l == 0:
            for each in range(LAYERS):
                open_vectors(each)
        lag = lax.broadcasted_iota(jnp.int32, (tokens, states), 0).astype(f32)
        filt_ref[l] = nn(jnp.exp(-lag * rows_ref[l, 3:4, :states]).astype(bf16), mixn_ref[l])
        half = tokens // 2
        step = lax.broadcasted_iota(jnp.int32, (half, states), 0).astype(f32)
        lead_scr[...] = jnp.exp(-(step + 1.0) * rows_ref[l, 3:4, :states]).astype(bf16)
        trail_scr[...] = jnp.exp(-(half - 1.0 - step) * rows_ref[l, 3:4, :states]).astype(bf16)

    def open_vectors(l):
        def line(r, rep, put, group=False):
            r = r + 8 * l
            short = vecn[pl.ds(dp * RINGS, RINGS), r, :] if group else vecn[:, r, :]
            return jnp.sum(nn(short.astype(bf16), rep) * put, axis=0, keepdims=True)

        rows_ref[l] = jnp.zeros(rows_ref.shape[1:], f32)
        for r in range(3):
            rows_ref[l, r : r + 1, :] = line(r, rep32[...], put32[...])
        rows_ref[l, 3:4, :states] = line(3, rep16[...], put16[...])
        rows_ref[l, 4:5, :units] = line(4, rep96[...], put96[...], True)
        rows_ref[l, 4:5, units:width] = line(5, rep16[:, :LANES], put16[:RINGS, :LANES], True)
        rows_ref[l, 5:6, :LANES] = line(6, rep16[:, :LANES], put16[:RINGS, :LANES], True)
        rows_ref[l, 6:7, :units] = line(7, rep96[...], put96[...], True)

    def open_out(l):
        for j in range(RINGS):
            source = packs.at[l, j // 2, j % 2]
            ow[l, j * high : (j + 1) * high, :] = source[top : top + high, :]
            for k in range(GROUP):
                index = (dp ^ k) * RINGS + j
                at = pl.ds(pl.multiple_of(index * small, small), small)
                for t in range(thirds):
                    r, c = divmod(k * thirds + t, across)
                    base = top + high + small * r
                    ew[l, at, t * 256 : (t + 1) * 256] = source[
                        base : base + small, c * 256 : (c + 1) * 256
                    ]

    def normalize(l, read, dst):
        def strip(i, carry):
            at = pl.ds(pl.multiple_of(i * STRIP, STRIP), STRIP)
            v = read(at)
            center = v - jnp.mean(v, axis=1, keepdims=True)
            scale = lax.rsqrt(jnp.mean(center * center, axis=1, keepdims=True) + 1e-05)
            dst[at, :] = (center * scale * rows_ref[l, 0:1, :] + rows_ref[l, 1:2, :]).astype(bf16)
            return carry

        lax.fori_loop(0, tokens // STRIP, strip, 0)

    def branch_in(l, j, middle):
        base = j * tokens
        a_scr[...] = nn(norm[l, j], vw[l])
        half = tokens // 2
        spot = lax.broadcasted_iota(jnp.int32, (tokens, LANES), 0)
        ages = jnp.broadcast_to(auxs[j, :, 0:1].astype(f32), (tokens, LANES))
        age_scr[...] = jnp.minimum(ages, (spot % half).astype(f32))

        def smooth(i, carry):
            here = pl.ds(pl.multiple_of(i * STRIP, STRIP), STRIP)
            there = pl.ds(pl.multiple_of(base + i * STRIP, STRIP), STRIP)
            v = a_scr[here, :] + rows_ref[l, 4:5, :width]
            cdf = 0.5 + 0.5 * lax.erf(v * 0.7071067811865476)
            slope = cdf + v * (0.3989422804014327 * jnp.exp(-0.5 * v * v))
            act = v * cdf
            value[l, there, :] = act[:, :units].astype(bf16)
            gp[l, there, :] = slope[:, :units].astype(bf16)
            mask = jnp.broadcast_to(auxs[j, here, 2:3].astype(f32), (STRIP, LANES))
            z[l, there, :] = act[:, units:] * mask
            g2[l, there, :] = slope[:, units:] * mask
            return carry

        lax.fori_loop(0, tokens // STRIP, smooth, 0)
        middle()
        signal = z[l, base : base + tokens, :]
        for b in range(8):
            shifted[b, PAD:, :] = signal if b == 0 else pltpu.roll(signal, b, 0)

        for s in range(tokens // STRIP):
            age = age_scr[s * STRIP : (s + 1) * STRIP, :]

            def lags(a, acc, s=s, age=age):
                start = pl.multiple_of(a * 8, 8)
                left = age - (a * 8).astype(f32)
                for b in range(8):
                    row = filt_ref[l, pl.ds(start + b, 1), :]
                    past = shifted[b, pl.ds(pl.multiple_of(PAD + s * STRIP - start, 8), STRIP), :]
                    acc = acc + jnp.where(left >= b, past, 0.0) * row
                return acc

            y_scr[s * STRIP : (s + 1) * STRIP, :] = lax.fori_loop(
                0, (s % (half // STRIP) + 1) * (STRIP // 8), lags, jnp.zeros((STRIP, LANES), f32)
            )
        place = lax.broadcasted_iota(jnp.int32, (half, LANES), 0).astype(f32)
        left = jnp.broadcast_to(auxs[j, :half, 1:2].astype(f32), (half, LANES))
        ages = jnp.broadcast_to(auxs[j, half:, 0:1].astype(f32), (half, LANES))
        carry = jnp.where(place + left >= half - 1.0, signal[:half, :], 0.0).astype(bf16)
        held = (tn(trail_scr[...], carry) * mixn_ref[l].astype(f32)).astype(bf16)
        y_scr[half:, :] += jnp.where(place + 1.0 <= ages, nn(lead_scr[...], held), 0.0)
        ybuf[l, j] = (y_scr[...] + rows_ref[l, 5:6, :LANES] * signal).astype(bf16)

    def branch_out(l, j):
        at = slice(j * tokens, (j + 1) * tokens)
        for k, part in ((0, ybuf[l, j]), (1, yin[l, 0, j ^ 1]), (2, yin[l, 1, j ^ 2]), (3, yin[l, 2, j ^ 3])):
            full[l, at, lanes(dp ^ k, LANES)] = part
        c = nn(full[l, at, :], ew[l]) + rows_ref[l, 6:7, :units]
        product = (c * value[l, at, :].astype(f32)).astype(bf16)
        cbuf[l, at, :] = c.astype(bf16)
        obuf[j] = nn(product, ow[l]).astype(bf16)

    for b in range(8):
        shifted[b, :PAD, :] = jnp.zeros((PAD, LANES), f32)

    def layer(l, events):
        def due():
            if events:
                events.pop(0)()

        branch_in(l, 0, due)
        due()
        branch_in(l, 1, due)
        near = [mail.send(ybuf.at[l, 0:2], yin.at[l, 0, 0:2], CORE)]
        far = [mail.send(ybuf.at[l, 0:2], yin.at[l, 1, 0:2], CHIP)]
        due()
        return near, far

    def layer_rest(l, near, far, events, ready):
        def due():
            if events:
                events.pop(0)()

        branch_in(l, 2, due)
        due()
        branch_in(l, 3, due)
        near.append(mail.send(ybuf.at[l, 2:4], yin.at[l, 0, 2:4], CORE))
        far.append(mail.send(ybuf.at[l, 2:4], yin.at[l, 1, 2:4], CHIP))
        far[0].wait_recv()
        relay = [mail.send(yin.at[l, 1, 0:2], yin.at[l, 2, 0:2], CORE)]
        due()
        ready()
        near[1].wait_recv()
        relay[0].wait_recv()
        branch_out(l, 3)
        core_hi = mail.send(obuf.at[3], oin.at[l, 0], CORE)
        branch_out(l, 2)
        core_hi.wait_recv()
        both = (obuf[2].astype(f32) + oin[l, 0].astype(f32)).astype(bf16)
        if l == 0:
            oadd[...] = both
            cross = mail.send(oadd, ofar, CHIP)
        else:
            cross_ref[...] = both
        due()
        far[1].wait_recv()
        relay.append(mail.send(yin.at[l, 1, 2:4], yin.at[l, 2, 2:4], CORE))
        near[0].wait_recv()
        relay[1].wait_recv()
        branch_out(l, 1)
        core_lo = mail.send(obuf.at[1], oin.at[l, 1], CORE)
        branch_out(l, 0)
        core_lo.wait_recv()
        due()
        if l == 0:
            cross.wait_recv()

        def strip(i, carry):
            at = pl.ds(pl.multiple_of(i * STRIP, STRIP), STRIP)
            branch = obuf[0, at, :].astype(f32) + oin[l, 1, at, :].astype(f32)
            if l == 0:
                branch = branch + ofar[at, :].astype(f32)
            mask = auxs[0, at, 2:3].astype(f32)
            before = x_ref[at, :].astype(f32) if l == 0 else xcur[at, :]
            now = before + mask * (branch + rows_ref[l, 2:3, :])
            if l == 0:
                xcur[at, :] = now
                later_ref[at, :] = now
            else:
                out_ref[at, :] = now
            return carry

        lax.fori_loop(0, tokens // STRIP, strip, 0)
        mail.finish(core_hi)
        mail.finish(core_lo)
        for buf, hbm in ((cbuf, c_hbm), (full, full_hbm)):
            spill.put(buf.at[l], hbm.at[l])

    def spill_in(l):
        for buf, hbm in ((norm, norm_hbm), (value, value_hbm), (gp, gp_hbm), (z, z_hbm), (g2, g2_hbm)):
            spill.put(buf.at[l], hbm.at[l])

    def then(*steps):
        def event():
            for step in steps:
                step()

        return event

    nothing = then()

    gathers[0][0].end()
    open_value(0)
    spill.put(vw.at[0], vw_hbm.at[0])
    for copy in aux_in:
        copy.wait_recv()
    x_near.wait_recv()
    for j in (0, 1):
        normalize(0, lambda at, j=j: xin[j, at, :].astype(f32), norm.at[0, j])
    gathers[0][1].step(1)

    more = {}

    def next_value():
        from_group(1, second)
        gathers[1][0].begin()

    def relay_dout():
        dout_far.wait_recv()
        more["dout"] = mail.send(douts.at[2], douts.at[3], CORE)

    near, far = layer(
        0, [nothing, lambda: gathers[0][1].step(2), next_value, lambda: gathers[0][1].step(3)]
    )
    x_relay.wait_recv()
    for j in (2, 3):
        normalize(0, lambda at, j=j: xin[j, at, :].astype(f32), norm.at[0, j])

    def ready_out(l):
        def event():
            gathers[l][1].end()
            open_out(l)
            spill.put(ow.at[l], ow_hbm.at[l])
            spill.put(ew.at[l], ew_hbm.at[l])
            spill_in(l)

        return event

    events = [
        relay_dout,
        lambda: gathers[1][0].step(1),
        nothing,
        lambda: gathers[1][0].step(2),
        then(lambda: gathers[1][1].begin(), lambda: gathers[1][0].step(3)),
        lambda: gathers[1][1].step(1),
    ]
    layer_rest(0, near, far, events, ready_out(0))

    normalize(1, lambda at: xcur[at, :], norm.at[1, 0])
    n_far = mail.send(norm.at[1, 0], norm.at[1, 2], CHIP)
    n_near = mail.send(norm.at[1, 0], norm.at[1, 1], CORE)
    gathers[1][0].end()
    open_value(1)
    spill.put(vw.at[1], vw_hbm.at[1])
    def relay_norm():
        n_far.wait_recv()
        more["relay"] = mail.send(norm.at[1, 2], norm.at[1, 3], CORE)

    n_near.wait_recv()
    near, far = layer(
        1, [lambda: gathers[1][1].step(2), nothing, lambda: gathers[1][1].step(3), relay_norm]
    )
    more["relay"].wait_recv()
    dout_near.wait_recv()
    more["dout"].wait_recv()
    spill.put(douts, dout_hbm)
    layer_rest(1, near, far, [nothing] * 6, ready_out(1))
    mail.close()
    spill.close()


def forward_both(arrays, sizes):
    tokens, depth, units, feats, states, tall, small, high = sizes
    width = units + LANES
    group = tokens * GROUP
    rows = tall * GROUP + high + small * GROUP * units // depth
    shape = jax.ShapeDtypeStruct
    two = lambda *dims: (LAYERS,) + dims
    spilled = [
        (two(GROUP, tokens, depth), bf16), (two(group, units), bf16), (two(group, units), bf16),
        (two(group, units), bf16), (two(group, feats), bf16),
        (two(group, LANES), f32), (two(group, LANES), f32),
        (two(depth, width), bf16), (two(units, depth), bf16), (two(feats, units), bf16),
        ((GROUP, tokens, depth), bf16),
    ]
    kept = [
        ((tokens, depth), f32), ((tokens, depth), bf16), ((tokens, depth), f32), (two(8, depth), f32),
        (two(tokens, LANES), f32),
        (two(states, LANES), bf16), ((GROUP, tokens, LANES), bf16),
    ]
    sems = 160
    return pl.pallas_call(
        partial(forward_kernel, sizes),
        out_shape=[shape(*s) for s in kept + spilled],
        in_specs=[pl.BlockSpec(memory_space=VMEM)] * len(arrays),
        out_specs=[pl.BlockSpec(memory_space=VMEM)] * len(kept)
        + [pl.BlockSpec(memory_space=pl.ANY)] * len(spilled),
        scratch_shapes=[
            VMEM(two(GROUP - 1, tall + small, depth), bf16),
            VMEM(two(GROUP - 1, small, depth), bf16),
            VMEM(two(LINE, 2, rows, depth), bf16),
            VMEM((GROUP * RINGS, tall - small, LANES), f32),
            VMEM(two(depth, width), bf16),
            VMEM(two(units, depth), bf16),
            VMEM(two(feats, units), bf16),
            VMEM((GROUP, tokens, depth), bf16),
            VMEM(two(GROUP, tokens, depth), bf16),
            VMEM((GROUP, tokens, depth), bf16),
            VMEM(two(group, units), bf16),
            VMEM(two(group, units), bf16),
            VMEM(two(group, units), bf16),
            VMEM(two(group, feats), bf16),
            VMEM(two(group, LANES), f32),
            VMEM(two(group, LANES), f32),
            VMEM(two(GROUP, tokens, LANES), bf16),
            VMEM(two(GROUP - 1, GROUP, tokens, LANES), bf16),
            VMEM((GROUP, tokens, depth), bf16),
            VMEM(two(2, tokens, depth), bf16),
            VMEM((tokens, depth), bf16),
            VMEM((tokens, depth), bf16),
            VMEM((tokens, depth), f32),
            VMEM((tokens, width), f32),
            VMEM((tokens, LANES), f32),
            VMEM((8, PAD + tokens, LANES), f32),
            VMEM((tokens, LANES), f32),
            VMEM((tall - small, LANES), f32),
            VMEM((tokens // 2, states), bf16),
            VMEM((tokens // 2, states), bf16),
            pltpu.SemaphoreType.DMA((sems,)),
            pltpu.SemaphoreType.DMA((sems,)),
            pltpu.SemaphoreType.DMA((32,)),
        ],
        compiler_params=pltpu.CompilerParams(
            vmem_limit_bytes=60 << 20, collective_id=1, has_side_effects=True
        ),
        cost_estimate=cost(120.0),
        name="forward_both",
    )(*arrays)


class Fetch:
    def __init__(self, sem):
        self.sem, self.count = sem, 0

    def get(self, src, dst):
        copy = pltpu.make_async_copy(src, dst, self.sem.at[self.count])
        self.count += 1
        copy.start()
        return copy


class Reduce:
    def __init__(self, mail, packs, ysum, zin, zother, l, begin, cut, end, lanes, spot):
        self.mail, self.packs, self.ysum, self.zin, self.zother = mail, packs, ysum, zin, zother
        self.l, self.early, self.late, self.lanes = l, slice(begin, cut), slice(cut, end), lanes
        self.has_early = cut > begin
        self.other = slice(spot, spot + cut - begin)
        self.over, self.steps = [], {}
        z = mail.z
        low = z < LINE // 2
        self.order = [
            jnp.where(low, 3, 0), jnp.where(low, 2, 1), jnp.where(low, 1 - z, 5 - z), z,
        ]

    def at(self, z, y, rows):
        return self.packs.at[self.l, z, y, rows, self.lanes]

    def add(self, z, y, rows, more):
        ref = self.at(z, y, rows)
        ref[...] = (ref[...].astype(f32) + more[...].astype(f32)).astype(bf16)

    def slots(self, step, early):
        out = []
        m = self.mail
        rows = self.early if early else self.late
        for side, way in enumerate((1, -1)):
            held = 4 + m.z - step if way == 1 else m.z - 4 + step
            if way == 1:
                can = (m.z + 1 <= step) & (m.z < LINE - 1)
            else:
                can = (LINE - m.z <= step) & (m.z > 0)
            at = jnp.clip(held, 0, LINE - 1)
            out.append((way, side, can, at, m.y, rows, self.zin.at[self.l, step - 1, side, rows, self.lanes], 0))
            if early:
                spot = self.zother.at[self.l, step - 1, side, self.other, self.lanes]
                out.append((way, side, can, at, 1 - m.y, rows, spot, 1))
        return out

    def pass_on(self, step, early):
        for way, side, can, at, y, rows, spot, which in self.slots(step, early):
            copy = self.mail.copy(self.at(at, y, rows), spot, self.mail.along(way))
            self.mail.start(copy, can)
            self.steps[early, step, side, which] = copy

    def take(self, step, early):
        z = self.mail.z
        for way, side, can, at, y, rows, spot, which in self.slots(step, early):
            copy = self.steps[early, step, side, which]
            if way == 1:
                when, mine = (z >= 1) & (step >= z), 3 + z - step
            else:
                when, mine = (z <= LINE - 2) & (step >= LINE - 1 - z), z - 3 + step

            def arrive(copy=copy, mine=mine, y=y, rows=rows, spot=spot):
                copy.wait_recv()
                self.add(jnp.clip(mine, 0, LINE - 1), y, rows, spot)

            only(when, arrive)

    def begin(self):
        m = self.mail
        if self.has_early:
            self.pass_on(1, True)
        for i, z in enumerate(self.order):
            copy = m.copy(
                self.at(z, 1 - m.y, self.late), self.ysum.at[self.l, i, self.late, self.lanes], m.peer(1)
            )
            m.start(copy)
            self.over.append(copy)

    def step(self, i):
        m = self.mail
        if i < LINE:
            self.over[i].wait_recv()
            self.add(self.order[i], m.y, self.late, self.ysum.at[self.l, i, self.late, self.lanes])
            if i:
                self.take(i, False)
            if i < LINE - 1:
                self.pass_on(i + 1, False)
            if self.has_early and i:
                self.take(i, True)
                if i < LINE - 1:
                    self.pass_on(i + 1, True)
                else:
                    self.last = m.copy(
                        self.at(m.z, 1 - m.y, self.early), self.ysum.at[self.l, 0, self.early, self.lanes], m.peer(1)
                    )
                    m.start(self.last)
        elif self.has_early:
            self.last.wait_recv()
            self.add(m.z, m.y, self.early, self.ysum.at[self.l, 0, self.early, self.lanes])


def backward_kernel(sizes, *refs):
    tokens, depth, units, feats, states, tall, small, high = sizes
    width = units + LANES
    top = tall * GROUP
    rows = top + high + small * GROUP * units // depth
    devices = GROUP * RINGS
    (
        cot_ref, x_ref, later_ref, rows_ref, filt_ref, mixn_ref, auxs, oadd_ref,
        norm_hbm, value_hbm, gp_hbm, c_hbm, full_hbm, z_hbm, g2_hbm, vw_hbm, ow_hbm, ew_hbm, dout_hbm,
    ) = refs[:19]
    dx_ref, vmine_ref, vtotal_ref, o_ref, raw_hbm, ofar_hbm = refs[19:25]
    (
        norm, value, gp, cbuf, full, z, g2, vw, ow, ew, dout, dcb, da,
        qe, qo, near, cross, far, ofar, dnbuf, din, dadd, dfar,
        packs, ysum, zin, zother, gsend, grecv, vsend, vin, vgrp,
        rem_scr, shifted, dz_scr, corr, y_scr, w_scr, o_scr, m_scr,
        send_sem, recv_sem, hbm_sem,
    ) = refs[25:]
    mail = Mail(send_sem, recv_sem)
    fetch = Fetch(hbm_sem)
    dp, z_at, y_at = mail.dp, mail.z, mail.y
    thirds = units // 256
    across = depth // 256
    strips = tokens // STRIP

    def lanes(at, size):
        return pl.ds(pl.multiple_of(at * size, LANES), size)

    def block(j):
        return pl.ds(pl.multiple_of(j * tokens, tokens), tokens)

    def load_out(l):
        return [
            fetch.get(ow_hbm.at[l], ow), fetch.get(ew_hbm.at[l], ew), fetch.get(value_hbm.at[l], value),
            fetch.get(gp_hbm.at[l], gp), fetch.get(c_hbm.at[l], cbuf), fetch.get(full_hbm.at[l], full),
        ]

    def load_in(l):
        return [
            fetch.get(z_hbm.at[l], z), fetch.get(g2_hbm.at[l], g2), fetch.get(vw_hbm.at[l], vw),
            fetch.get(norm_hbm.at[l], norm),
        ]

    first = fetch.get(dout_hbm, dout)
    loads = load_out(LAYERS - 1)
    more_loads = load_in(LAYERS - 1)
    vsend[...] = jnp.zeros(vsend.shape, f32)
    for b in range(8):
        shifted[b, tokens:, :] = jnp.zeros((PAD, LANES), f32)

    def start_dx(i, carry):
        at = pl.ds(pl.multiple_of(i * STRIP, STRIP), STRIP)
        up = cot_ref[at, :].astype(f32)
        dx_ref[at, :] = up
        low = (up * auxs[0, at, 2:3].astype(f32)).astype(bf16).astype(f32)
        return carry + jnp.sum(low, axis=0, keepdims=True)

    vsend[LAYERS - 1, 2:3, :] = lax.fori_loop(0, strips, start_dx, jnp.zeros((1, depth), f32))

    mail.greet((CORE, CHIP, BOTH, 1, 2, 3, 4, 5, 6, 7))

    def back_out(l, j):
        at = block(j)
        dgated = nt(dout[at, :], ow[...])
        val = value[at, :].astype(f32)
        gate = cbuf[at, :].astype(f32)
        dc = (dgated * val).astype(bf16)
        dcb[at, :] = dc
        da[at, :units] = (dgated * gate * gp[at, :].astype(f32)).astype(bf16)

        def keep():
            cbuf[at, :] = (gate * val).astype(bf16)

        pl.when(j < 2)(keep)
        vsend[l, 5:6, :units] += jnp.sum(dc.astype(f32), axis=0, keepdims=True)
        y_scr[...] = nt(dc, ew[...])
        for k in range(GROUP):
            part = y_scr[:, lanes(dp ^ k, LANES)].astype(bf16)
            if k % 2:
                qo[k // 2, j ^ 1] = part
            else:
                qe[k // 2, j] = part

    def back_in(l, j, middle):
        at = block(j)
        rem_scr[...] = jnp.broadcast_to(auxs[j, :, 1:2].astype(f32), (tokens, LANES))
        dy = qe[0, j].astype(f32) + near[0, j].astype(f32) + far[j].astype(f32)
        for b in range(8):
            shifted[b, :tokens, :] = dy if b == 0 else pltpu.roll(dy, tokens - b, 0)
        for s in range(strips):
            rem = rem_scr[s * STRIP : (s + 1) * STRIP, :]
            past = z[pl.ds(pl.multiple_of(j * tokens + s * STRIP, STRIP), STRIP), :]

            def lags(a, acc, s=s, rem=rem, past=past):
                base = pl.multiple_of(a * 8, 8)
                left = rem - (a * 8).astype(f32)
                for b in range(8):
                    row = filt_ref[l, pl.ds(base + b, 1), :]
                    later = shifted[b, pl.ds(pl.multiple_of(s * STRIP + base, 8), STRIP), :]
                    later = jnp.where(left >= b, later, 0.0)
                    acc = acc + later * row
                    pair = later * past
                    corr[pl.ds(pl.multiple_of(base * 8 + b * 8, 8), 8), :] += (pair[0:8] + pair[8:16]) + (
                        pair[16:24] + pair[24:32]
                    )
                return acc

            dz_scr[s * STRIP : (s + 1) * STRIP, :] = lax.fori_loop(
                0, (strips - s) * (STRIP // 8), lags, jnp.zeros((STRIP, LANES), f32)
            )
            if s == 2:
                middle()
        da2 = (dz_scr[...] + rows_ref[l, 5:6, :LANES] * dy) * g2[at, :]
        da[at, units:] = da2.astype(bf16)
        vsend[l, 5:6, units:width] += jnp.sum(z[at, :] * dy, axis=0, keepdims=True)
        vsend[l, 4:5, :width] += jnp.sum(da[at, :].astype(f32), axis=0, keepdims=True)
        dnbuf[j] = nt(da[at, :], vw[...]).astype(bf16)

    def grads_proj(l):
        half, wide = 2 * tokens, high * GROUP
        for j in (2, 3):
            at = slice(j * tokens, (j + 1) * tokens)
            dcb[at, :] = (cbuf[at, :].astype(f32) * value[at, :].astype(f32)).astype(bf16)
        for i in range(RINGS // GROUP):
            lane = slice(i * wide, (i + 1) * wide)
            o_scr[...] = (tn(cbuf[:half, lane], dout[:half, :]) + tn(dcb[half:, lane], dout[half:, :])).astype(bf16)
            for g in range(GROUP):
                at = i * GROUP + g
                packs[l, at // 2, at % 2, top : top + high, :] = o_scr[g * high : (g + 1) * high, :]
        sums[l]["proj"].begin()

    def grads_expand(l):
        for t in range(thirds):
            w_scr[: 2 * tokens, :256] = tn(full[...], dcb[:, t * 256 : (t + 1) * 256]).astype(bf16)
            for j in range(RINGS):
                for k in range(GROUP):
                    r, c = divmod(k * thirds + t, across)
                    owner = (dp ^ k) * RINGS + j
                    base = top + high + small * r
                    packs[l, j // 2, j % 2, base : base + small, c * 256 : (c + 1) * 256] = w_scr[
                        pl.ds(pl.multiple_of(owner * small, small), small), :256
                    ]
        sums[l]["expand"].begin()

    def grads_in_of(l, lane):
        wide = depth // GROUP
        size = lane.stop - lane.start
        for d in range(GROUP):
            w_scr[:wide, :size] = tn(norm[:, d * wide : (d + 1) * wide], da[:, lane]).astype(bf16)
            at = pl.ds(pl.multiple_of((dp ^ d) * tall, tall), tall)
            for j in range(RINGS):
                packs[l, j // 2, j % 2, at, lane] = w_scr[j * tall : (j + 1) * tall, :size]

    def mixing_of(l):
        lag = lax.broadcasted_iota(jnp.int32, (tokens, tokens * 8), 0)
        part = lax.broadcasted_iota(jnp.int32, (tokens, tokens * 8), 1) // 8
        total = nn((lag == part).astype(bf16), corr[...].astype(bf16))
        steps = lax.broadcasted_iota(jnp.int32, (tokens, states), 0).astype(f32)
        powers = jnp.exp(-steps * rows_ref[l, 3:4, :states]).astype(bf16)
        m_scr[...] = tn(powers, total.astype(bf16)).astype(bf16)
        for j in range(RINGS):
            for k in range(GROUP):
                owner = (dp ^ k) * RINGS + j
                side = packs.at[l, j // 2, j % 2, k * tall : (k + 1) * tall]
                side[:small, width:] = m_scr[pl.ds(pl.multiple_of(owner * small, small), small), :]
                side[small:, width:] = jnp.zeros((tall - small, LANES), bf16)
        steps = lax.broadcasted_iota(jnp.int32, (tokens, LANES), 0).astype(f32)
        terms = tn(powers, (total * steps).astype(bf16)) * mixn_ref[l].astype(f32)
        vsend[l, 3:4, :states] = -lax.dot_general(
            jnp.ones((8, LANES), f32), terms, cols_dims, precision=highest, preferred_element_type=f32
        )[0:1]

    state = {}
    bufs = (mail, packs, ysum, zin, zother)
    sums = [
        {
            "proj": Reduce(*bufs, l, top, top + 16, top + high, slice(0, depth), 16),
            "expand": Reduce(*bufs, l, top + high, top + high + 16, rows, slice(0, depth), 32),
            "value": Reduce(*bufs, l, 0, 16, top, slice(0, units), 0),
            "rest": Reduce(*bufs, l, 0, 0, top, slice(units, depth), 0),
        }
        for l in range(LAYERS)
    ]

    def own(l, at, lane=slice(None)):
        return packs[l, z_at, y_at, at, lane]

    def group_proj(l):
        sums[l]["proj"].step(4)
        o_ref[l] = own(l, slice(top, top + high))

    def group_out(l):
        sums[l]["expand"].step(4)
        for k in range(GROUP):
            dst = grecv.at[l, 0, tall : tall + small] if k == 0 else gsend.at[l, k - 1]
            for t in range(thirds):
                r, c = divmod(k * thirds + t, across)
                base = top + high + small * r
                dst[:, t * 256 : (t + 1) * 256] = own(l, slice(base, base + small), slice(c * 256, (c + 1) * 256))
            dst[:, units:] = jnp.zeros((small, depth - units), bf16)
            if k:
                state[l, "out", k] = mail.send(
                    gsend.at[l, k - 1], grecv.at[l, k, tall : tall + small], k * RINGS
                )

    def group_in(l, name):
        sums[l][name].step(4)
        lane = sums[l][name].lanes
        for k in (2, 3, 1):
            state[l, name, k] = mail.send(
                packs.at[l, z_at, y_at, k * tall : (k + 1) * tall, lane], grecv.at[l, k, 0:tall, lane], k * RINGS
            )
        grecv[l, 0, :tall, lane] = own(l, slice(0, tall), lane)

    def group_last(l):
        for name in ("out", "value", "rest"):
            for k in range(1, GROUP):
                state[l, name, k].wait_recv()
        state[l, "raw"] = fetch.get(grecv.at[l], raw_hbm.at[l])

    def vector_rest(l):
        state[l, "vr"] = [mail.send(vsend.at[l], vin.at[l, j - 1], j) for j in range(1, RINGS)]

    def vector_group(l):
        for copy in state[l, "vr"]:
            copy.wait_recv()
        total = vsend[l]
        for j in range(RINGS - 1):
            total = total + vin[l, j]
        vmine_ref[l] = total
        vgrp[l, 0] = total
        state[l, "vg"] = [mail.send(vgrp.at[l, 0], vgrp.at[l, k], k * RINGS) for k in range(1, GROUP)]

    def vector_last(l):
        for copy in state[l, "vg"]:
            copy.wait_recv()
        total = vgrp[l, 0]
        for k in range(1, GROUP):
            total = total + vgrp[l, k]
        vtotal_ref[l] = total

    def pair(fn, lo):
        def body(i, carry):
            fn(lo + i)
            return carry

        lax.fori_loop(0, 2, body, 0)

    def exchange_dy(half):
        return mail.send(qo.at[:, half], near.at[:, half], CORE)

    def cross_dy(half, other, copy):
        copy.wait_recv()
        cross[half] = (qe[1, half].astype(f32) + near[1, half].astype(f32)).astype(bf16)
        return mail.send(cross.at[half], far.at[other], CHIP)

    lo, hi = slice(0, 2), slice(2, 4)

    def grads_value(l):
        grads_in_of(l, slice(0, units))
        sums[l]["value"].begin()

    def grads_rest(l):
        grads_in_of(l, slice(units, width))
        mixing_of(l)
        sums[l]["rest"].begin()

    def layer(l, loads, more_loads, events, wait_far):
        def due():
            if events:
                events.pop(0)()

        for copy in loads:
            copy.wait()
        corr[...] = jnp.zeros(corr.shape, f32)
        pair(lambda j: back_out(l, j), 0)
        near_lo = exchange_dy(lo)
        wait_far()
        grads_proj(l)
        pair(lambda j: back_out(l, j), 2)
        near_hi = exchange_dy(hi)
        cross_lo = cross_dy(lo, hi, near_lo)
        cross_hi = cross_dy(hi, lo, near_hi)
        if l:
            state["o"] = mail.send(oadd_ref, ofar, CHIP)
        due()
        grads_expand(l)
        next_loads = load_out(l - 1) if l else []
        for copy in more_loads:
            copy.wait()
        due()
        grads_value(l)
        due()
        cross_lo.wait_recv()
        back_in(l, 3, due)
        core_hi = mail.send(dnbuf.at[3], din.at[0], CORE)
        due()
        back_in(l, 2, due)
        core_hi.wait_recv()
        dadd[...] = (dnbuf[2].astype(f32) + din[0].astype(f32)).astype(bf16)
        chip = mail.send(dadd, dfar, CHIP)
        due()
        cross_hi.wait_recv()
        back_in(l, 1, due)
        core_lo = mail.send(dnbuf.at[1], din.at[1], CORE)
        due()
        back_in(l, 0, due)
        due()
        if l == 0:
            grads_rest(l)
        due()
        core_lo.wait_recv()
        chip.wait_recv()

        def strip(i, carry):
            gain_sum, shift_sum, out_sum = carry
            at = pl.ds(pl.multiple_of(i * STRIP, STRIP), STRIP)
            v = later_ref[at, :] if l else x_ref[at, :].astype(f32)
            center = v - jnp.mean(v, axis=1, keepdims=True)
            scale = lax.rsqrt(jnp.mean(center * center, axis=1, keepdims=True) + 1e-05)
            normed = center * scale
            grad = dnbuf[0, at, :].astype(f32) + din[1, at, :].astype(f32) + dfar[at, :].astype(f32)
            q = grad * rows_ref[l, 0:1, :]
            tilt = q - jnp.mean(q, axis=1, keepdims=True) - normed * jnp.mean(q * normed, axis=1, keepdims=True)
            up = dx_ref[at, :] + tilt * scale
            dx_ref[at, :] = up
            if l:
                low = (up * auxs[0, at, 2:3].astype(f32)).astype(bf16)
                dout[at, :] = low
                out_sum = out_sum + jnp.sum(low.astype(f32), axis=0, keepdims=True)
            return (
                gain_sum + jnp.sum(grad * normed, axis=0, keepdims=True),
                shift_sum + jnp.sum(grad, axis=0, keepdims=True),
                out_sum,
            )

        zero = jnp.zeros((1, depth), f32)
        gain_sum, shift_sum, out_sum = lax.fori_loop(0, strips, strip, (zero, zero, zero))
        vsend[l, 0:1, :] = gain_sum
        vsend[l, 1:2, :] = shift_sum
        if l:
            vsend[l - 1, 2:3, :] = out_sum
        for copy in (near_lo, near_hi, cross_lo, cross_hi, core_hi, core_lo, chip):
            mail.finish(copy)
        return next_loads

    first.wait()

    def then(*steps):
        def event():
            for step in steps:
                step()

        return event

    nothing = then()

    def step(l, name, i):
        return lambda: sums[l][name].step(i)

    def steps(l, name, *which):
        return then(*(step(l, name, i) for i in which))

    events = [
        then(),
        then(),
        then(step(1, "proj", 0)),
        then(),
        then(step(1, "proj", 1)),
        then(),
        then(step(1, "proj", 2), step(1, "expand", 0)),
        then(),
        then(step(1, "proj", 3), step(1, "expand", 1)),
        then(),
        then(step(1, "expand", 2), step(1, "value", 0)),
        then(lambda: group_proj(1), step(1, "expand", 3)),
    ]
    loads = layer(1, loads, more_loads, events, nothing)

    dout_chip = mail.send(dout.at[pl.ds(0, tokens)], dout.at[pl.ds(2 * tokens, tokens)], CHIP)
    dout_core = mail.send(dout.at[pl.ds(0, tokens)], dout.at[pl.ds(tokens, tokens)], CORE)
    grads_rest(1)
    more_loads = load_in(0)
    vector_rest(1)
    state["o"].wait_recv()
    far_out = fetch.get(ofar, ofar_hbm)

    step(1, "value", 1)()

    def dout_far():
        group_out(1)
        step(1, "value", 2)()
        dout_chip.wait_recv()
        relay = mail.send(dout.at[pl.ds(2 * tokens, tokens)], dout.at[pl.ds(3 * tokens, tokens)], CORE)
        step(1, "value", 3)()
        step(1, "rest", 0)()
        relay.wait_recv()

    events = [
        then(step(1, "rest", 1)),
        then(step(0, "proj", 0)),
        then(lambda: group_in(1, "value"), step(1, "rest", 2)),
        then(step(0, "proj", 1)),
        then(lambda: vector_group(1), step(1, "rest", 3)),
        then(step(0, "proj", 2), step(0, "expand", 0)),
        then(lambda: group_in(1, "rest")),
        then(step(0, "proj", 3), step(0, "expand", 1)),
        then(step(0, "value", 0)),
        then(step(0, "expand", 2), lambda: group_proj(0), step(0, "value", 1)),
        then(lambda: vector_last(1)),
        then(step(0, "expand", 3), step(0, "value", 2), lambda: group_last(1)),
    ]
    dout_core.wait_recv()
    layer(0, loads, more_loads, events, dout_far)
    step(0, "value", 3)()
    vector_rest(0)
    step(0, "rest", 0)()
    group_out(0)
    group_in(0, "value")
    step(0, "rest", 1)()
    vector_group(0)
    steps(0, "rest", 2, 3)()
    group_in(0, "rest")
    vector_last(0)
    group_last(0)
    mail.close()
    far_out.wait()
    for l in range(LAYERS):
        state[l, "raw"].wait()


def backward_both(arrays, sizes):
    tokens, depth, units, feats, states, tall, small, high = sizes
    width = units + LANES
    group = tokens * GROUP
    rows = tall * GROUP + high + small * GROUP * units // depth
    shape = jax.ShapeDtypeStruct
    two = lambda *dims: (LAYERS,) + dims
    outs = [
        ((tokens, depth), f32), (two(8, depth), f32), (two(8, depth), f32), (two(high, depth), bf16),
        (two(GROUP, tall + small, depth), bf16), ((tokens, depth), bf16),
    ]
    return pl.pallas_call(
        partial(backward_kernel, sizes),
        out_shape=[shape(*s) for s in outs],
        in_specs=[pl.BlockSpec(memory_space=VMEM)] * 8 + [pl.BlockSpec(memory_space=pl.ANY)] * 11,
        out_specs=[pl.BlockSpec(memory_space=VMEM)] * 4 + [pl.BlockSpec(memory_space=pl.ANY)] * 2,
        scratch_shapes=[
            VMEM((group, depth), bf16),
            VMEM((group, units), bf16),
            VMEM((group, units), bf16),
            VMEM((group, units), bf16),
            VMEM((group, feats), bf16),
            VMEM((group, LANES), f32),
            VMEM((group, LANES), f32),
            VMEM((depth, width), bf16),
            VMEM((units, depth), bf16),
            VMEM((feats, units), bf16),
            VMEM((group, depth), bf16),
            VMEM((group, units), bf16),
            VMEM((group, width), bf16),
            VMEM((2, GROUP, tokens, LANES), bf16),
            VMEM((2, GROUP, tokens, LANES), bf16),
            VMEM((2, GROUP, tokens, LANES), bf16),
            VMEM((GROUP, tokens, LANES), bf16),
            VMEM((GROUP, tokens, LANES), bf16),
            VMEM((tokens, depth), bf16),
            VMEM((GROUP, tokens, depth), bf16),
            VMEM((2, tokens, depth), bf16),
            VMEM((tokens, depth), bf16),
            VMEM((tokens, depth), bf16),
            VMEM(two(LINE, 2, rows, depth), bf16),
            VMEM(two(LINE, rows, depth), bf16),
            VMEM(two(LINE - 1, 2, rows, depth), bf16),
            VMEM(two(LINE - 1, 2, 48, depth), bf16),
            VMEM(two(GROUP - 1, small, depth), bf16),
            VMEM(two(GROUP, tall + small, depth), bf16),
            VMEM(two(8, depth), f32),
            VMEM(two(RINGS - 1, 8, depth), f32),
            VMEM(two(GROUP, 8, depth), f32),
            VMEM((tokens, LANES), f32),
            VMEM((8, PAD + tokens, LANES), f32),
            VMEM((tokens, LANES), f32),
            VMEM((tokens * 8, LANES), f32),
            VMEM((tokens, feats), f32),
            VMEM((2 * tokens, width), bf16),
            VMEM((high * GROUP, depth), bf16),
            VMEM((states, LANES), bf16),
            pltpu.SemaphoreType.DMA((220,)),
            pltpu.SemaphoreType.DMA((220,)),
            pltpu.SemaphoreType.DMA((26,)),
        ],
        compiler_params=pltpu.CompilerParams(
            vmem_limit_bytes=60 << 20, collective_id=2, has_side_effects=True
        ),
        cost_estimate=cost(140.0),
        name="backward_both",
    )(*arrays)


def finish(me, arrays, sizes):
    tokens, depth, units, feats, states, tall, small, high = sizes
    width = units + LANES
    devices = GROUP * RINGS
    hidden = units * GROUP

    def kernel(me_ref, *refs):
        hbm = refs[: len(arrays)]
        (
            last_ref, dx_ref, gain_ref, shift_ref, v_ref, vb_ref, r_ref, rb_ref, dec_ref, si_out, so_out,
            skip_ref, e_ref, eb_ref, o_ref, ob_ref,
        ) = refs[len(arrays) : len(arrays) + 16]
        here, sem = refs[len(arrays) + 16 : -1], refs[-1]
        to = (*here, dx_ref)
        copies = [pltpu.make_async_copy(a, b, sem.at[i]) for i, (a, b) in enumerate(zip(hbm, to))]
        for copy in copies:
            copy.start()
        raw, out_part, mine_ref, total_ref, last_in, far_in, aux_ref, si_ref, so_ref = here
        for copy in copies[:-1]:
            copy.wait()
        dp, fs = me_ref[0], me_ref[1]
        index = dp * RINGS + fs

        def lanes(at, size):
            return pl.ds(pl.multiple_of(at * size, LANES), size)

        flags = aux_ref[0, :, 2:3].astype(f32)
        last_ref[...] = (last_in[...] + flags * far_in[...].astype(f32)).astype(bf16)
        o_ref[...] = out_part[...].astype(f32)
        apart = lax.broadcasted_iota(jnp.int32, (depth, LANES), 0) - lax.broadcasted_iota(
            jnp.int32, (depth, LANES), 1
        )
        both = jnp.concatenate([total_ref[0], total_ref[1], mine_ref[0], mine_ref[1]], axis=0)
        high_part = both.astype(bf16)
        low_part = (both - high_part.astype(f32)).astype(bf16)

        def pick(start):
            chosen = (apart == start).astype(bf16)
            return nn(high_part, chosen) + nn(low_part, chosen)

        short, mid = states // devices, units // RINGS
        long_all, short_all = pick(index * (depth // devices)), pick(index * short)
        mid_all, rest_all = pick(fs * mid), pick(units + fs * short)
        for l in range(LAYERS):
            for k in range(GROUP):
                q = dp ^ k
                v_ref[l, :, lanes(q, units)] = raw[l, k, :tall, :units].astype(f32)
                r_ref[l, :, lanes(q, LANES)] = raw[l, k, :tall, units:width].astype(f32)
                e_ref[l, :, lanes(q, units)] = raw[l, k, tall:, :units].astype(f32)
                part = raw[l, k, :small, width:].astype(f32)
                si_out[l, :, lanes(q, LANES)] = part * so_ref[l, :, lanes(q, LANES)].astype(f32)
                so_out[l, :, lanes(q, LANES)] = part * si_ref[l, :, lanes(q, LANES)].astype(f32)

            for r, ref in enumerate((gain_ref, shift_ref, ob_ref)):
                ref[l : l + 1, :] = long_all[8 * l + r : 8 * l + r + 1, : depth // devices]
            dec_ref[l : l + 1, :] = short_all[8 * l + 3 : 8 * l + 4, :short]
            own = 8 * (LAYERS + l)
            vb_ref[l : l + 1, :] = mid_all[own + 4 : own + 5, :mid]
            eb_ref[l : l + 1, :] = mid_all[own + 5 : own + 6, :mid]
            rb_ref[l : l + 1, :] = rest_all[own + 4 : own + 5, :short]
            skip_ref[l : l + 1, :] = rest_all[own + 5 : own + 6, :short]
        copies[-1].wait()

    two = lambda *dims: (LAYERS,) + dims
    outs = [
        (tokens, depth), two(depth // devices), two(depth // devices), two(tall, hidden), two(units // RINGS),
        two(tall, feats), two(LANES // RINGS), two(states // devices), two(small, feats), two(small, feats),
        two(LANES // RINGS), two(small, hidden), two(units // RINGS), two(high, depth), two(depth // devices),
    ]
    return pl.pallas_call(
        kernel,
        out_shape=[jax.ShapeDtypeStruct((tokens, depth), bf16)] + [jax.ShapeDtypeStruct(s, f32) for s in outs],
        in_specs=[pl.BlockSpec(memory_space=pltpu.SMEM)] + [pl.BlockSpec(memory_space=pl.ANY)] * len(arrays),
        out_specs=[pl.BlockSpec(memory_space=VMEM)] * 16,
        scratch_shapes=[VMEM(a.shape, a.dtype) for a in arrays[:-1]] + [pltpu.SemaphoreType.DMA((len(arrays),))],
        compiler_params=pltpu.CompilerParams(vmem_limit_bytes=60 << 20),
        cost_estimate=cost(4.0),
        name="finish",
    )(me, *arrays)


def mixer(labels, signal, decays, stateinput, stateoutput, skipgain):
    rows = signal.shape[0]
    width = min(32, rows)
    count = rows // width
    mixing = stateinput * stateoutput
    offsets = jnp.arange(width, dtype=jnp.float32)
    powers = jnp.exp(-offsets[:, None] * decays[None, :])
    kernel = jnp.dot(powers, mixing, precision=highest)
    positions = jnp.arange(width, dtype=jnp.int32)
    lagged = jnp.maximum(positions[:, None] - positions[None, :], 0)
    toeplitz = jnp.take(kernel, lagged, axis=0)
    causal = positions[:, None] >= positions[None, :]
    leading = jnp.exp(-(offsets[:, None] + 1.0) * decays[None, :])
    trailing = jnp.exp(-(width - 1.0 - offsets[:, None]) * decays[None, :])
    across = jnp.exp(-width * decays)

    def advance(carry, pieces):
        state, before = carry
        block, marks = pieces
        same = jnp.logical_and(marks[:, None] == marks[None, :], causal).astype(signal.dtype)
        inner = jnp.sum(toeplitz * same[:, :, None] * block[None, :, :], axis=1)
        joined = (marks == before).astype(signal.dtype)
        carried = jnp.dot(leading, mixing * state, precision=highest) * joined[:, None]
        final = marks[width - 1]
        keep = (final == before).astype(signal.dtype)
        fresh = (marks == final).astype(signal.dtype)
        state = across[:, None] * state * keep + lax.dot_general(
            trailing * fresh[:, None], block, rows_dims, precision=highest
        )
        return ((state, final), inner + carried)

    start = (jnp.zeros(mixing.shape, signal.dtype), jnp.array(-1, jnp.int32))
    ending, mixed = lax.scan(
        jax.checkpoint(advance),
        start,
        (signal.reshape(count, width, -1), labels.reshape(count, width)),
    )
    return mixed.reshape(rows, -1) + skipgain[None, :] * signal


def normalize(rows, gain, shift):
    center = rows - jnp.mean(rows, axis=1, keepdims=True)
    spread = jnp.mean(center * center, axis=1, keepdims=True)
    return center * lax.rsqrt(spread + 1e-05) * gain + shift


def smooth(values):
    return jax.nn.gelu(values, approximate=False)


def gather_forward(shards, depth):
    return (
        lax.all_gather(shards[0][depth], ("dp", "fsdp"), axis=0, tiled=True),
        lax.all_gather(shards[1][depth], ("dp", "fsdp"), axis=0, tiled=True),
        lax.all_gather(shards[2][depth], ("dp", "fsdp"), axis=0, tiled=True),
        lax.all_gather(shards[3][depth], ("dp", "fsdp"), axis=0, tiled=True),
        lax.all_gather(shards[4][depth], ("dp", "fsdp"), axis=0, tiled=True),
        lax.all_gather(shards[5][depth], ("dp", "fsdp"), axis=0, tiled=True),
        lax.all_gather(shards[6][depth], ("dp", "fsdp"), axis=0, tiled=True),
        lax.all_gather(shards[7][depth], ("dp", "fsdp"), axis=0, tiled=True),
        lax.all_gather(shards[8][depth], ("dp", "fsdp"), axis=0, tiled=True),
        lax.all_gather(shards[9][depth], ("dp", "fsdp"), axis=0, tiled=True),
        lax.all_gather(shards[10][depth], ("dp", "fsdp"), axis=0, tiled=True),
        lax.all_gather(shards[11][depth], ("dp", "fsdp"), axis=0, tiled=True),
        lax.all_gather(shards[12][depth], ("dp", "fsdp"), axis=0, tiled=True),
        lax.all_gather(shards[13][depth], ("dp", "fsdp"), axis=0, tiled=True),
    )


def gather_backward(shards, depth):
    return (
        lax.all_gather(shards[0][depth], ("dp", "fsdp"), axis=0, tiled=True),
        lax.all_gather(shards[1][depth], ("dp", "fsdp"), axis=0, tiled=True),
        lax.all_gather(shards[2][depth], ("dp", "fsdp"), axis=0, tiled=True),
        lax.all_gather(shards[3][depth], ("dp", "fsdp"), axis=0, tiled=True),
        lax.all_gather(shards[4][depth], ("dp", "fsdp"), axis=0, tiled=True),
        lax.all_gather(shards[5][depth], ("dp", "fsdp"), axis=0, tiled=True),
        lax.all_gather(shards[6][depth], ("dp", "fsdp"), axis=0, tiled=True),
        lax.all_gather(shards[7][depth], ("dp", "fsdp"), axis=0, tiled=True),
        lax.all_gather(shards[8][depth], ("dp", "fsdp"), axis=0, tiled=True),
        lax.all_gather(shards[9][depth], ("dp", "fsdp"), axis=0, tiled=True),
        lax.all_gather(shards[10][depth], ("dp", "fsdp"), axis=0, tiled=True),
        lax.all_gather(shards[11][depth], ("dp", "fsdp"), axis=0, tiled=True),
        lax.all_gather(shards[12][depth], ("dp", "fsdp"), axis=0, tiled=True),
        lax.all_gather(shards[13][depth], ("dp", "fsdp"), axis=0, tiled=True),
    )


def scatter_layer(terms):
    return (
        lax.psum_scatter(terms[0], ("dp", "fsdp"), scatter_dimension=0, tiled=True),
        lax.psum_scatter(terms[1], ("dp", "fsdp"), scatter_dimension=0, tiled=True),
        lax.psum_scatter(terms[2], ("dp", "fsdp"), scatter_dimension=0, tiled=True),
        lax.psum_scatter(terms[3], ("dp", "fsdp"), scatter_dimension=0, tiled=True),
        lax.psum_scatter(terms[4], ("dp", "fsdp"), scatter_dimension=0, tiled=True),
        lax.psum_scatter(terms[5], ("dp", "fsdp"), scatter_dimension=0, tiled=True),
        lax.psum_scatter(terms[6], ("dp", "fsdp"), scatter_dimension=0, tiled=True),
        lax.psum_scatter(terms[7], ("dp", "fsdp"), scatter_dimension=0, tiled=True),
        lax.psum_scatter(terms[8], ("dp", "fsdp"), scatter_dimension=0, tiled=True),
        lax.psum_scatter(terms[9], ("dp", "fsdp"), scatter_dimension=0, tiled=True),
        lax.psum_scatter(terms[10], ("dp", "fsdp"), scatter_dimension=0, tiled=True),
        lax.psum_scatter(terms[11], ("dp", "fsdp"), scatter_dimension=0, tiled=True),
        lax.psum_scatter(terms[12], ("dp", "fsdp"), scatter_dimension=0, tiled=True),
        lax.psum_scatter(terms[13], ("dp", "fsdp"), scatter_dimension=0, tiled=True),
    )


def layer_forward(current, labels, flags, weights):
    (
        normgain,
        normbias,
        valueproj,
        valuebias,
        reduceproj,
        reducebias,
        decays,
        stateinput,
        stateoutput,
        skipgain,
        expandproj,
        expandbias,
        outproj,
        outbias,
    ) = weights
    normed, norm_back = jax.vjp(
        normalize, current, normgain.astype(jnp.float32), normbias.astype(jnp.float32)
    )
    normed_low = normed.astype(jnp.bfloat16)
    opened = jnp.dot(normed_low, valueproj, preferred_element_type=jnp.float32) + valuebias.astype(
        jnp.float32
    )
    values, value_back = jax.vjp(smooth, opened)
    reduced = jnp.dot(
        normed_low, reduceproj, preferred_element_type=jnp.float32
    ) + reducebias.astype(jnp.float32)
    smoothed, reduce_back = jax.vjp(smooth, reduced)
    signal = smoothed * flags
    mixed, mix_back = jax.vjp(
        partial(mixer, labels),
        signal,
        decays.astype(jnp.float32),
        stateinput.astype(jnp.float32),
        stateoutput.astype(jnp.float32),
        skipgain.astype(jnp.float32),
    )
    mixed_low = mixed.astype(jnp.bfloat16)
    expanded = jnp.dot(
        mixed_low, expandproj, preferred_element_type=jnp.float32
    ) + expandbias.astype(jnp.float32)
    gated = (expanded * values).astype(jnp.bfloat16)
    branch = jnp.dot(gated, outproj, preferred_element_type=jnp.float32) + outbias.astype(
        jnp.float32
    )
    saved = (
        normed_low,
        values,
        value_back,
        reduce_back,
        mix_back,
        mixed_low,
        expanded,
        gated,
        norm_back,
    )
    return (current + flags * branch, saved)


def layer_backward(upstream, flags, weights, saved):
    (
        normgain,
        normbias,
        valueproj,
        valuebias,
        reduceproj,
        reducebias,
        decays,
        stateinput,
        stateoutput,
        skipgain,
        expandproj,
        expandbias,
        outproj,
        outbias,
    ) = weights
    normed_low, values, value_back, reduce_back, mix_back, mixed_low, expanded, gated, norm_back = (
        saved
    )
    dout = (flags * upstream).astype(jnp.bfloat16)
    outproj_term = lax.dot_general(gated, dout, rows_dims, preferred_element_type=jnp.float32)
    outbias_term = jnp.sum(dout, axis=0, dtype=jnp.float32)
    dgated = lax.dot_general(dout, outproj, cols_dims, preferred_element_type=jnp.float32)
    dexpanded = (dgated * values).astype(jnp.bfloat16)
    dvalues = dgated * expanded
    expandproj_term = lax.dot_general(
        mixed_low, dexpanded, rows_dims, preferred_element_type=jnp.float32
    )
    expandbias_term = jnp.sum(dexpanded, axis=0, dtype=jnp.float32)
    dmixed = lax.dot_general(dexpanded, expandproj, cols_dims, preferred_element_type=jnp.float32)
    dsignal, decays_term, stateinput_term, stateoutput_term, skipgain_term = mix_back(dmixed)
    (dreduced,) = reduce_back(dsignal * flags)
    dreduced_low = dreduced.astype(jnp.bfloat16)
    (dopened,) = value_back(dvalues)
    dopened_low = dopened.astype(jnp.bfloat16)
    valueproj_term = lax.dot_general(
        normed_low, dopened_low, rows_dims, preferred_element_type=jnp.float32
    )
    valuebias_term = jnp.sum(dopened_low, axis=0, dtype=jnp.float32)
    reduceproj_term = lax.dot_general(
        normed_low, dreduced_low, rows_dims, preferred_element_type=jnp.float32
    )
    reducebias_term = jnp.sum(dreduced_low, axis=0, dtype=jnp.float32)
    dnormed = lax.dot_general(dopened_low, valueproj, cols_dims, preferred_element_type=jnp.float32)
    dnormed = dnormed + lax.dot_general(
        dreduced_low, reduceproj, cols_dims, preferred_element_type=jnp.float32
    )
    dcurrent, normgain_term, normbias_term = norm_back(dnormed)
    terms = (
        normgain_term,
        normbias_term,
        valueproj_term,
        valuebias_term,
        reduceproj_term,
        reducebias_term,
        decays_term,
        stateinput_term,
        stateoutput_term,
        skipgain_term,
        expandproj_term,
        expandbias_term,
        outproj_term,
        outbias_term,
    )
    return (upstream + dcurrent, terms)


def plain(
    inputs,
    segment_ids,
    token_mask,
    cotangent,
    normgain,
    normbias,
    valueproj,
    valuebias,
    reduceproj,
    reducebias,
    decays,
    stateinput,
    stateoutput,
    skipgain,
    expandproj,
    expandbias,
    outproj,
    outbias,
):
    shards = (
        normgain,
        normbias,
        valueproj,
        valuebias,
        reduceproj,
        reducebias,
        decays,
        stateinput,
        stateoutput,
        skipgain,
        expandproj,
        expandbias,
        outproj,
        outbias,
    )
    flags = token_mask.astype(jnp.float32)[:, None]
    current = inputs.astype(jnp.float32)
    fetched = []
    stored = []
    for depth in range(LAYERS):
        weights = gather_forward(shards, depth)
        current, saved = layer_forward(current, segment_ids, flags, weights)
        fetched.append(weights)
        stored.append(saved)
    outputs = current.astype(jnp.bfloat16)
    upstream = cotangent.astype(jnp.float32)
    scattered = [None] * LAYERS
    for depth in reversed(range(LAYERS)):
        weights = gather_backward(shards, depth)
        upstream, terms = layer_backward(upstream, flags, weights, stored[depth])
        scattered[depth] = scatter_layer(terms)
    results = tuple(
        (jnp.stack([scattered[depth][index] for depth in range(LAYERS)]) for index in range(14))
    )
    return (outputs, upstream) + tuple(results)


def fast(
    inputs, segment_ids, token_mask, cotangent, normgain, normbias, valueproj, valuebias,
    reduceproj, reducebias, decays, stateinput, stateoutput, skipgain, expandproj, expandbias,
    outproj, outbias,
):
    tokens, depth = inputs.shape
    tall = valueproj.shape[1]
    small = stateinput.shape[1]
    high = outproj.shape[1]
    units = valueproj.shape[2] // GROUP
    feats = reduceproj.shape[2]
    states = stateinput.shape[1] * GROUP * RINGS
    group = tokens * GROUP
    sizes = (tokens, depth, units, feats, states, tall, small, high)

    lined = lambda v: v.reshape(tokens // LANES, LANES)
    shorts = (normgain, normbias, outbias, decays, valuebias, reducebias, skipgain, expandbias)
    (
        last, across, later, rows, filt, mixes, auxes,
        norms, value, slope, gate, full, z, slope2, value_w, out_w, expand_w, douts,
    ) = forward_both(
        (
            inputs, lined(segment_ids), lined(token_mask), cotangent, valueproj, reduceproj, expandproj,
            outproj, stateinput, stateoutput, *shorts, *tables(GROUP * RINGS),
        ),
        sizes,
    )
    dx, mine, total, out_part, raw, arrived = backward_both(
        (
            cotangent, inputs, later, rows, filt, mixes, auxes, across,
            norms.reshape(LAYERS, group, depth), value, slope, gate, full, z, slope2,
            value_w, out_w, expand_w, douts.reshape(group, depth),
        ),
        sizes,
    )
    me = jnp.stack([lax.axis_index("dp"), lax.axis_index("fsdp")]).astype(jnp.int32)
    arrays = (raw, out_part, mine, total, last, arrived, auxes, stateinput, stateoutput, dx)
    return tuple(finish(me, arrays, sizes))


def solution(mesh):
    placed = (
        P(("dp", "fsdp"), None),
        P(("dp", "fsdp")),
        P(("dp", "fsdp")),
        P(("dp", "fsdp"), None),
        P(None, ("dp", "fsdp")),
        P(None, ("dp", "fsdp")),
        P(None, ("dp", "fsdp"), None),
        P(None, ("dp", "fsdp")),
        P(None, ("dp", "fsdp"), None),
        P(None, ("dp", "fsdp")),
        P(None, ("dp", "fsdp")),
        P(None, ("dp", "fsdp"), None),
        P(None, ("dp", "fsdp"), None),
        P(None, ("dp", "fsdp")),
        P(None, ("dp", "fsdp"), None),
        P(None, ("dp", "fsdp")),
        P(None, ("dp", "fsdp"), None),
        P(None, ("dp", "fsdp")),
    )
    small = mesh.shape["dp"] == GROUP and mesh.shape["fsdp"] == RINGS
    return jax.shard_map(
        fast if small else plain,
        mesh=mesh,
        in_specs=placed,
        out_specs=(
            P(("dp", "fsdp"), None),
            P(("dp", "fsdp"), None),
            P(None, ("dp", "fsdp")),
            P(None, ("dp", "fsdp")),
            P(None, ("dp", "fsdp"), None),
            P(None, ("dp", "fsdp")),
            P(None, ("dp", "fsdp"), None),
            P(None, ("dp", "fsdp")),
            P(None, ("dp", "fsdp")),
            P(None, ("dp", "fsdp"), None),
            P(None, ("dp", "fsdp"), None),
            P(None, ("dp", "fsdp")),
            P(None, ("dp", "fsdp"), None),
            P(None, ("dp", "fsdp")),
            P(None, ("dp", "fsdp"), None),
            P(None, ("dp", "fsdp")),
        ),
        check_vma=False,
    )
```

```python
from functools import partial

import jax
import jax.numpy as jnp
import numpy as np
from jax import lax
from jax.experimental import pallas as pl
from jax.experimental.pallas import tpu as pltpu
from jax.sharding import PartitionSpec as P

LAYERS = 2
AXES = ("dp", "fsdp")
GROUP = 4
RINGS = 8
LANES = 128
STRIP = 32
PAD = 32

f32 = jnp.float32
bf16 = jnp.bfloat16
highest = lax.Precision.HIGHEST
rows_dims = (((0,), (0,)), ((), ()))
cols_dims = (((1,), (1,)), ((), ()))

VMEM = pltpu.VMEM


def cost(micros):
    return pl.CostEstimate(
        flops=int(micros * 1.0e9), bytes_accessed=1 << 20, transcendentals=0
    )


def nt(a, b):
    return lax.dot_general(a, b, cols_dims, preferred_element_type=f32)


def tn(a, b):
    return lax.dot_general(a, b, rows_dims, preferred_element_type=f32)


def nn(a, b):
    return jnp.dot(a, b, preferred_element_type=f32)


def tables(devices):
    out = []
    for count, size in ((devices, 32), (RINGS, 96), (devices, 16)):
        at = np.arange(count * size)
        out.append(jnp.asarray((np.arange(LANES)[:, None] == at[None, :] % size), bf16))
        out.append(jnp.asarray((np.arange(count)[:, None] == at[None, :] // size), f32))
    return out


class Mail:
    def __init__(self, send_sem, recv_sem):
        self.dp, self.fs = lax.axis_index("dp"), lax.axis_index("fsdp")
        self.z, self.y = self.fs // 2, self.fs % 2
        self.send_sem, self.recv_sem, self.count, self.sent = send_sem, recv_sem, 0, []

    def peer(self, flip):
        return (self.dp ^ (flip // RINGS), self.fs ^ (flip % RINGS))

    def along(self, way):
        return (self.dp, self.fs + 2 * way)

    def greet(self, flips):
        barrier = pltpu.get_barrier_semaphore()

        def hail(device):
            pl.semaphore_signal(barrier, inc=1, device_id=device, device_id_type=pl.DeviceIdType.MESH)

        for flip in flips:
            hail(self.peer(flip))
        ahead, behind = self.z < LINE - 1, self.z > 0
        pl.when(ahead)(lambda: hail(self.along(1)))
        pl.when(behind)(lambda: hail(self.along(-1)))
        pl.semaphore_wait(barrier, len(flips) + ahead.astype(jnp.int32) + behind.astype(jnp.int32))

    def copy(self, src, dst, device):
        made = pltpu.make_async_remote_copy(
            src_ref=src, dst_ref=dst, send_sem=self.send_sem.at[self.count],
            recv_sem=self.recv_sem.at[self.count], device_id=device,
            device_id_type=pl.DeviceIdType.MESH,
        )
        self.count += 1
        return made

    def start(self, copy, when=None):
        only(when, copy.start)
        self.sent.append((copy, when))

    def send(self, src, dst, flip):
        copy = self.copy(src, dst, self.peer(flip))
        self.start(copy)
        return copy

    def finish(self, copy):
        copy.wait_send()
        self.sent = [(c, w) for c, w in self.sent if c is not copy]

    def close(self):
        for copy, when in self.sent:
            only(when, copy.wait_send)


def only(when, step):
    if when is None:
        step()
    else:
        pl.when(when)(step)


class Gather:
    def __init__(self, mail, packs, l, begin, cut, end):
        self.mail, self.packs, self.l = mail, packs, l
        self.early, self.late = slice(begin, cut), slice(cut, end)
        self.steps, self.across = {}, []

    def line(self, rows, both, step):
        m = self.mail
        for way in (1, -1):
            held = m.z - way * (step - 1)
            can = (held >= 0) & (m.z < LINE - 1) if way == 1 else (held <= LINE - 1) & (m.z > 0)
            at = jnp.clip(held, 0, LINE - 1)
            ref = self.packs.at[self.l, at, :, rows] if both else self.packs.at[self.l, at, m.y, rows]
            copy = m.copy(ref, ref, m.along(way))
            m.start(copy, can)
            self.steps[both, step, way] = copy

    def over(self, rows, at, when):
        m = self.mail
        ref = self.packs.at[self.l, at, m.y, rows]
        copy = m.copy(ref, ref, m.peer(1))
        m.start(copy, when)
        self.across.append((copy, when))
        return copy

    def begin(self):
        self.first = self.over(self.early, self.mail.z, None)
        self.across = []
        self.line(self.late, False, 1)
        self.over(self.late, self.mail.z, None)

    def come(self, both, step):
        m = self.mail
        out = []
        for way in (1, -1):
            source = m.z - way * step
            when = source >= 0 if way == 1 else source <= LINE - 1
            only(when, self.steps[both, step, way].wait_recv)
            out.append((jnp.clip(source, 0, LINE - 1), when))
        return out

    def step(self, step):
        held = self.come(False, step)
        if step < LINE - 1:
            self.line(self.late, False, step + 1)
        for at, when in held:
            self.over(self.late, at, when)
        if step == 1:
            self.first.wait_recv()
        else:
            self.come(True, step - 1)
        self.line(self.early, True, step)

    def end(self):
        self.come(True, LINE - 1)
        for copy, when in self.across:
            only(when, copy.wait_recv)


class Spill:
    def __init__(self, sem):
        self.sem, self.open = sem, []

    def put(self, src, dst):
        copy = pltpu.make_async_copy(src, dst, self.sem.at[len(self.open)])
        copy.start()
        self.open.append(copy)

    def close(self):
        for copy in self.open:
            copy.wait()


CORE, CHIP, BOTH = RINGS, 2 * RINGS, 3 * RINGS
FLIPS = (CORE, CHIP, BOTH, 1)
LINE = RINGS // 2


def forward_kernel(sizes, *refs):
    tokens, depth, units, feats, states, tall, small, high = sizes
    width = units + LANES
    top = tall * GROUP
    rows = top + high + small * GROUP * units // depth
    (
        x_ref, seg_ref, mask_ref, cot_ref, v_ref, r_ref, e_ref, o_ref, si_ref, so_ref,
        *short_refs, rep32, put32, rep96, put96, rep16, put16,
    ) = refs[:24]
    (
        out_ref, cross_ref, later_ref, rows_ref, filt_ref, mixn_ref, auxs,
        norm_hbm, value_hbm, gp_hbm, c_hbm, full_hbm, z_hbm, g2_hbm,
        vw_hbm, ow_hbm, ew_hbm, dout_hbm,
    ) = refs[24:42]
    (
        pieces, ein, packs, vecn, vw, ow, ew, xin, norm, douts,
        value, gp, cbuf, full, z, g2, ybuf, yin, obuf, oin, oadd, ofar, xcur,
        a_scr, age_scr, shifted, y_scr, vec_scr, lead_scr, trail_scr, send_sem, recv_sem, hbm_sem,
    ) = refs[42:]
    mail = Mail(send_sem, recv_sem)
    spill = Spill(hbm_sem)
    dp, z_at, y_at = mail.dp, mail.z, mail.y
    thirds = units // 256
    across = depth // 256

    def lanes(index, size):
        return pl.ds(pl.multiple_of(index * size, LANES), size)

    def place_expand(l, k, part):
        for t in range(thirds):
            r, c = divmod(k * thirds + t, across)
            at = top + high + small * r
            packs[l, z_at, y_at, at : at + small, c * 256 : (c + 1) * 256] = part[:, t * 256 : (t + 1) * 256]

    vec_scr[...] = jnp.zeros(vec_scr.shape, f32)
    for l in range(LAYERS):
        for r, ref in enumerate(short_refs):
            vec_scr[8 * l + r : 8 * l + r + 1, : ref.shape[1]] = ref[l : l + 1, :].astype(f32)
    for l in range(LAYERS):
        a_scr[:small, :feats] = si_ref[l].astype(f32) * so_ref[l].astype(f32)
        for k in range(GROUP):
            q = dp ^ k
            dst = packs.at[l, z_at, y_at, 0:tall] if k == 0 else pieces.at[l, k - 1, 0:tall]
            dst[:, :units] = v_ref[l, :, lanes(q, units)]
            dst[:, units:width] = r_ref[l, :, lanes(q, LANES)]
            dst[:small, width:] = a_scr[:small, lanes(q, LANES)].astype(bf16)
            dst[small:, width:] = vec_scr[...].astype(bf16)
            part = e_ref[l, :, lanes(q, units)]
            if k == 0:
                place_expand(l, 0, part)
            else:
                pieces[l, k - 1, tall:, :units] = part
                pieces[l, k - 1, tall:, units:] = jnp.zeros((small, depth - units), bf16)
        packs[l, z_at, y_at, top : top + high, :] = o_ref[l]

    mail.greet(FLIPS)

    def to_group(l, ks):
        return [
            (
                k,
                mail.send(
                    pieces.at[l, k - 1, 0:tall], packs.at[l, z_at, y_at, k * tall : (k + 1) * tall], k * RINGS
                ),
                mail.send(pieces.at[l, k - 1, tall : tall + small], ein.at[l, k - 1], k * RINGS),
            )
            for k in ks
        ]

    def from_group(l, copies):
        for k, one, two in copies:
            one.wait_recv()
            two.wait_recv()
            place_expand(l, k, ein[l, k - 1, :, :units])

    gathers = [
        [Gather(mail, packs, l, 0, 16, top), Gather(mail, packs, l, top, top + 32, rows)] for l in range(LAYERS)
    ]
    first = to_group(0, (2, 3, 1))
    xin[0] = x_ref[...]

    def line_up(ref):
        row = jnp.concatenate([ref[i : i + 1, :] for i in range(tokens // LANES)], axis=1).astype(f32)
        return jnp.broadcast_to(row, (tokens, tokens))

    ids = line_up(seg_ref)
    here = lax.broadcasted_iota(jnp.int32, (tokens, tokens), 0)
    there = lax.broadcasted_iota(jnp.int32, (tokens, tokens), 1)
    same = (ids == ids.T).astype(f32)
    age = jnp.sum(jnp.where(there < here, same, 0.0), axis=1, keepdims=True)
    rest = jnp.sum(jnp.where(there > here, same, 0.0), axis=1, keepdims=True)
    mask = line_up(mask_ref).T[:, :LANES]
    lane = lax.broadcasted_iota(jnp.int32, (tokens, LANES), 1)
    auxs[0] = jnp.where(lane == 0, age, jnp.where(lane == 1, rest, jnp.where(lane == 2, mask, 0.0))).astype(bf16)
    age_scr[...] = mask

    from_group(0, first)
    gathers[0][0].begin()
    aux_in = [mail.send(auxs.at[0], auxs.at[k], k * RINGS) for k in (1, 2, 3)]
    x_near = mail.send(x_ref, xin.at[1], CORE)
    x_far = mail.send(x_ref, xin.at[2], CHIP)
    second = to_group(1, (1,))

    def start_dout(i, carry):
        at = pl.ds(pl.multiple_of(i * STRIP, STRIP), STRIP)
        flags = jnp.broadcast_to(age_scr[at, 0:1], (STRIP, depth))
        douts[0, at, :] = (cot_ref[at, :].astype(f32) * flags).astype(bf16)
        return carry

    lax.fori_loop(0, tokens // STRIP, start_dout, 0)
    dout_near = mail.send(douts.at[0], douts.at[1], CORE)
    gathers[0][0].step(1)
    gathers[0][0].step(2)
    gathers[0][1].begin()
    x_far.wait_recv()
    x_relay = mail.send(xin.at[2], xin.at[3], CORE)
    second += to_group(1, (2, 3))
    dout_far = mail.send(douts.at[0], douts.at[2], CHIP)
    gathers[0][0].step(3)

    def open_value(l):
        for j in range(RINGS):
            for k in range(GROUP):
                index = (dp ^ k) * RINGS + j
                at = slice(k * tall, (k + 1) * tall)
                source = packs.at[l, j // 2, j % 2]
                vw[l, pl.ds(pl.multiple_of(index * tall, tall), tall), :] = source[at, :width]
                mixn_ref[l, pl.ds(pl.multiple_of(index * small, small), small), :] = source[
                    k * tall : k * tall + small, width:
                ]
                if l == 0:
                    vecn[index] = source[k * tall + small : (k + 1) * tall, width:].astype(f32)

        if l == 0:
            for each in range(LAYERS):
                open_vectors(each)
        lag = lax.broadcasted_iota(jnp.int32, (tokens, states), 0).astype(f32)
        filt_ref[l] = nn(jnp.exp(-lag * rows_ref[l, 3:4, :states]).astype(bf16), mixn_ref[l])
        half = tokens // 2
        step = lax.broadcasted_iota(jnp.int32, (half, states), 0).astype(f32)
        lead_scr[...] = jnp.exp(-(step + 1.0) * rows_ref[l, 3:4, :states]).astype(bf16)
        trail_scr[...] = jnp.exp(-(half - 1.0 - step) * rows_ref[l, 3:4, :states]).astype(bf16)

    def open_vectors(l):
        def line(r, rep, put, group=False):
            r = r + 8 * l
            short = vecn[pl.ds(dp * RINGS, RINGS), r, :] if group else vecn[:, r, :]
            return jnp.sum(nn(short.astype(bf16), rep) * put, axis=0, keepdims=True)

        rows_ref[l] = jnp.zeros(rows_ref.shape[1:], f32)
        for r in range(3):
            rows_ref[l, r : r + 1, :] = line(r, rep32[...], put32[...])
        rows_ref[l, 3:4, :states] = line(3, rep16[...], put16[...])
        rows_ref[l, 4:5, :units] = line(4, rep96[...], put96[...], True)
        rows_ref[l, 4:5, units:width] = line(5, rep16[:, :LANES], put16[:RINGS, :LANES], True)
        rows_ref[l, 5:6, :LANES] = line(6, rep16[:, :LANES], put16[:RINGS, :LANES], True)
        rows_ref[l, 6:7, :units] = line(7, rep96[...], put96[...], True)

    def open_out(l):
        for j in range(RINGS):
            source = packs.at[l, j // 2, j % 2]
            ow[l, j * high : (j + 1) * high, :] = source[top : top + high, :]
            for k in range(GROUP):
                index = (dp ^ k) * RINGS + j
                at = pl.ds(pl.multiple_of(index * small, small), small)
                for t in range(thirds):
                    r, c = divmod(k * thirds + t, across)
                    base = top + high + small * r
                    ew[l, at, t * 256 : (t + 1) * 256] = source[
                        base : base + small, c * 256 : (c + 1) * 256
                    ]

    halves = [slice(h * tokens // 2, (h + 1) * tokens // 2) for h in range(2)]

    def normalize(l, read, dst, begin=0, end=tokens // STRIP):
        def strip(i, carry):
            at = pl.ds(pl.multiple_of(i * STRIP, STRIP), STRIP)
            v = read(at)
            center = v - jnp.mean(v, axis=1, keepdims=True)
            scale = lax.rsqrt(jnp.mean(center * center, axis=1, keepdims=True) + 1e-05)
            dst[at, :] = (center * scale * rows_ref[l, 0:1, :] + rows_ref[l, 1:2, :]).astype(bf16)
            return carry

        lax.fori_loop(begin, end, strip, 0)

    def branch_in(l, j, middle):
        base = j * tokens
        a_scr[...] = nn(norm[l, j], vw[l])
        half = tokens // 2
        spot = lax.broadcasted_iota(jnp.int32, (tokens, LANES), 0)
        ages = jnp.broadcast_to(auxs[j, :, 0:1].astype(f32), (tokens, LANES))
        age_scr[...] = jnp.minimum(ages, (spot % half).astype(f32))

        def smooth(i, carry):
            here = pl.ds(pl.multiple_of(i * STRIP, STRIP), STRIP)
            there = pl.ds(pl.multiple_of(base + i * STRIP, STRIP), STRIP)
            v = a_scr[here, :] + rows_ref[l, 4:5, :width]
            cdf = 0.5 + 0.5 * lax.erf(v * 0.7071067811865476)
            slope = cdf + v * (0.3989422804014327 * jnp.exp(-0.5 * v * v))
            act = v * cdf
            value[l, there, :] = act[:, :units].astype(bf16)
            gp[l, there, :] = slope[:, :units].astype(bf16)
            mask = jnp.broadcast_to(auxs[j, here, 2:3].astype(f32), (STRIP, LANES))
            z[l, there, :] = act[:, units:] * mask
            g2[l, there, :] = slope[:, units:] * mask
            return carry

        lax.fori_loop(0, tokens // STRIP, smooth, 0)
        middle()
        signal = z[l, base : base + tokens, :]
        for b in range(8):
            shifted[b, PAD:, :] = signal if b == 0 else pltpu.roll(signal, b, 0)

        for s in range(tokens // STRIP):
            age = age_scr[s * STRIP : (s + 1) * STRIP, :]

            def lags(a, acc, s=s, age=age):
                start = pl.multiple_of(a * 8, 8)
                left = age - (a * 8).astype(f32)
                for b in range(8):
                    row = filt_ref[l, pl.ds(start + b, 1), :]
                    past = shifted[b, pl.ds(pl.multiple_of(PAD + s * STRIP - start, 8), STRIP), :]
                    acc = acc + jnp.where(left >= b, past, 0.0) * row
                return acc

            y_scr[s * STRIP : (s + 1) * STRIP, :] = lax.fori_loop(
                0, (s % (half // STRIP) + 1) * (STRIP // 8), lags, jnp.zeros((STRIP, LANES), f32)
            )
        place = lax.broadcasted_iota(jnp.int32, (half, LANES), 0).astype(f32)
        left = jnp.broadcast_to(auxs[j, :half, 1:2].astype(f32), (half, LANES))
        ages = jnp.broadcast_to(auxs[j, half:, 0:1].astype(f32), (half, LANES))
        carry = jnp.where(place + left >= half - 1.0, signal[:half, :], 0.0).astype(bf16)
        held = (tn(trail_scr[...], carry) * mixn_ref[l].astype(f32)).astype(bf16)
        y_scr[half:, :] += jnp.where(place + 1.0 <= ages, nn(lead_scr[...], held), 0.0)
        ybuf[l, j] = (y_scr[...] + rows_ref[l, 5:6, :LANES] * signal).astype(bf16)

    def branch_out(l, j):
        at = slice(j * tokens, (j + 1) * tokens)
        for k, part in ((0, ybuf[l, j]), (1, yin[l, 0, j ^ 1]), (2, yin[l, 1, j ^ 2]), (3, yin[l, 2, j ^ 3])):
            full[l, at, lanes(dp ^ k, LANES)] = part
        c = nn(full[l, at, :], ew[l]) + rows_ref[l, 6:7, :units]
        product = (c * value[l, at, :].astype(f32)).astype(bf16)
        cbuf[l, at, :] = c.astype(bf16)
        obuf[j] = nn(product, ow[l]).astype(bf16)

    for b in range(8):
        shifted[b, :PAD, :] = jnp.zeros((PAD, LANES), f32)

    def layer(l, events):
        def due():
            if events:
                events.pop(0)()

        branch_in(l, 0, due)
        due()
        branch_in(l, 1, due)
        near = [mail.send(ybuf.at[l, 0:2], yin.at[l, 0, 0:2], CORE)]
        far = [mail.send(ybuf.at[l, 0:2], yin.at[l, 1, 0:2], CHIP)]
        due()
        return near, far

    n_far = []

    def on_half(h):
        size = tokens // STRIP // 2
        normalize(1, lambda at: xcur[at, :], norm.at[1, 0], h * size, (h + 1) * size)
        n_far.append(mail.send(norm.at[1, 0, halves[h]], norm.at[1, 2, halves[h]], CHIP))

    def layer_rest(l, near, far, events, ready):
        def due():
            if events:
                events.pop(0)()

        branch_in(l, 2, due)
        due()
        branch_in(l, 3, due)
        near.append(mail.send(ybuf.at[l, 2:4], yin.at[l, 0, 2:4], CORE))
        far.append(mail.send(ybuf.at[l, 2:4], yin.at[l, 1, 2:4], CHIP))
        far[0].wait_recv()
        relay = [mail.send(yin.at[l, 1, 0:2], yin.at[l, 2, 0:2], CORE)]
        due()
        ready()
        near[1].wait_recv()
        relay[0].wait_recv()
        branch_out(l, 3)
        core_hi = mail.send(obuf.at[3], oin.at[l, 0], CORE)
        branch_out(l, 2)
        core_hi.wait_recv()
        if l == 0:
            cross = []
            for at in halves:
                oadd[at] = (obuf[2, at].astype(f32) + oin[l, 0, at].astype(f32)).astype(bf16)
                cross.append(mail.send(oadd.at[at], ofar.at[at], CHIP))
        else:
            cross_ref[...] = (obuf[2].astype(f32) + oin[l, 0].astype(f32)).astype(bf16)
        due()
        far[1].wait_recv()
        relay.append(mail.send(yin.at[l, 1, 2:4], yin.at[l, 2, 2:4], CORE))
        near[0].wait_recv()
        relay[1].wait_recv()
        branch_out(l, 1)
        core_lo = mail.send(obuf.at[1], oin.at[l, 1], CORE)
        branch_out(l, 0)
        core_lo.wait_recv()
        due()

        def strip(i, carry):
            at = pl.ds(pl.multiple_of(i * STRIP, STRIP), STRIP)
            branch = obuf[0, at, :].astype(f32) + oin[l, 1, at, :].astype(f32)
            if l == 0:
                branch = branch + ofar[at, :].astype(f32)
            mask = auxs[0, at, 2:3].astype(f32)
            before = x_ref[at, :].astype(f32) if l == 0 else xcur[at, :]
            now = before + mask * (branch + rows_ref[l, 2:3, :])
            if l == 0:
                xcur[at, :] = now
                later_ref[at, :] = now
            else:
                out_ref[at, :] = now
            return carry

        for h in range(2):
            if l == 0:
                cross[h].wait_recv()
            lax.fori_loop(h * tokens // STRIP // 2, (h + 1) * tokens // STRIP // 2, strip, 0)
            if l == 0:
                on_half(h)
        mail.finish(core_hi)
        mail.finish(core_lo)
        for buf, hbm in ((cbuf, c_hbm), (full, full_hbm)):
            spill.put(buf.at[l], hbm.at[l])

    def spill_in(l):
        for buf, hbm in ((norm, norm_hbm), (value, value_hbm), (gp, gp_hbm), (z, z_hbm), (g2, g2_hbm)):
            spill.put(buf.at[l], hbm.at[l])

    def then(*steps):
        def event():
            for step in steps:
                step()

        return event

    nothing = then()

    gathers[0][0].end()
    open_value(0)
    spill.put(vw.at[0], vw_hbm.at[0])
    for copy in aux_in:
        copy.wait_recv()
    x_near.wait_recv()
    for j in (0, 1):
        normalize(0, lambda at, j=j: xin[j, at, :].astype(f32), norm.at[0, j])
    gathers[0][1].step(1)

    more = {}

    def next_value():
        from_group(1, second)
        gathers[1][0].begin()

    def relay_dout():
        dout_far.wait_recv()
        more["dout"] = mail.send(douts.at[2], douts.at[3], CORE)

    near, far = layer(
        0, [nothing, lambda: gathers[0][1].step(2), next_value, lambda: gathers[0][1].step(3)]
    )
    x_relay.wait_recv()
    for j in (2, 3):
        normalize(0, lambda at, j=j: xin[j, at, :].astype(f32), norm.at[0, j])

    def ready_out(l):
        def event():
            gathers[l][1].end()
            open_out(l)
            spill.put(ow.at[l], ow_hbm.at[l])
            spill.put(ew.at[l], ew_hbm.at[l])
            spill_in(l)

        return event

    events = [
        relay_dout,
        lambda: gathers[1][0].step(1),
        nothing,
        lambda: gathers[1][0].step(2),
        then(lambda: gathers[1][1].begin(), lambda: gathers[1][0].step(3)),
        lambda: gathers[1][1].step(1),
    ]
    layer_rest(0, near, far, events, ready_out(0))

    n_near = mail.send(norm.at[1, 0], norm.at[1, 1], CORE)
    gathers[1][0].end()
    open_value(1)
    spill.put(vw.at[1], vw_hbm.at[1])
    def relay_norm():
        more["relay"] = []
        for at, copy in zip(halves, n_far):
            copy.wait_recv()
            more["relay"].append(mail.send(norm.at[1, 2, at], norm.at[1, 3, at], CORE))

    n_near.wait_recv()
    near, far = layer(
        1, [lambda: gathers[1][1].step(2), nothing, lambda: gathers[1][1].step(3), relay_norm]
    )
    for copy in more["relay"]:
        copy.wait_recv()
    dout_near.wait_recv()
    more["dout"].wait_recv()
    spill.put(douts, dout_hbm)
    layer_rest(1, near, far, [nothing] * 6, ready_out(1))
    mail.close()
    spill.close()


def forward_both(arrays, sizes):
    tokens, depth, units, feats, states, tall, small, high = sizes
    width = units + LANES
    group = tokens * GROUP
    rows = tall * GROUP + high + small * GROUP * units // depth
    shape = jax.ShapeDtypeStruct
    two = lambda *dims: (LAYERS,) + dims
    spilled = [
        (two(GROUP, tokens, depth), bf16), (two(group, units), bf16), (two(group, units), bf16),
        (two(group, units), bf16), (two(group, feats), bf16),
        (two(group, LANES), f32), (two(group, LANES), f32),
        (two(depth, width), bf16), (two(units, depth), bf16), (two(feats, units), bf16),
        ((GROUP, tokens, depth), bf16),
    ]
    kept = [
        ((tokens, depth), f32), ((tokens, depth), bf16), ((tokens, depth), f32), (two(8, depth), f32),
        (two(tokens, LANES), f32),
        (two(states, LANES), bf16), ((GROUP, tokens, LANES), bf16),
    ]
    sems = 160
    return pl.pallas_call(
        partial(forward_kernel, sizes),
        out_shape=[shape(*s) for s in kept + spilled],
        in_specs=[pl.BlockSpec(memory_space=VMEM)] * len(arrays),
        out_specs=[pl.BlockSpec(memory_space=VMEM)] * len(kept)
        + [pl.BlockSpec(memory_space=pl.ANY)] * len(spilled),
        scratch_shapes=[
            VMEM(two(GROUP - 1, tall + small, depth), bf16),
            VMEM(two(GROUP - 1, small, depth), bf16),
            VMEM(two(LINE, 2, rows, depth), bf16),
            VMEM((GROUP * RINGS, tall - small, LANES), f32),
            VMEM(two(depth, width), bf16),
            VMEM(two(units, depth), bf16),
            VMEM(two(feats, units), bf16),
            VMEM((GROUP, tokens, depth), bf16),
            VMEM(two(GROUP, tokens, depth), bf16),
            VMEM((GROUP, tokens, depth), bf16),
            VMEM(two(group, units), bf16),
            VMEM(two(group, units), bf16),
            VMEM(two(group, units), bf16),
            VMEM(two(group, feats), bf16),
            VMEM(two(group, LANES), f32),
            VMEM(two(group, LANES), f32),
            VMEM(two(GROUP, tokens, LANES), bf16),
            VMEM(two(GROUP - 1, GROUP, tokens, LANES), bf16),
            VMEM((GROUP, tokens, depth), bf16),
            VMEM(two(2, tokens, depth), bf16),
            VMEM((tokens, depth), bf16),
            VMEM((tokens, depth), bf16),
            VMEM((tokens, depth), f32),
            VMEM((tokens, width), f32),
            VMEM((tokens, LANES), f32),
            VMEM((8, PAD + tokens, LANES), f32),
            VMEM((tokens, LANES), f32),
            VMEM((tall - small, LANES), f32),
            VMEM((tokens // 2, states), bf16),
            VMEM((tokens // 2, states), bf16),
            pltpu.SemaphoreType.DMA((sems,)),
            pltpu.SemaphoreType.DMA((sems,)),
            pltpu.SemaphoreType.DMA((32,)),
        ],
        compiler_params=pltpu.CompilerParams(
            vmem_limit_bytes=60 << 20, collective_id=1, has_side_effects=True
        ),
        cost_estimate=cost(120.0),
        name="forward_both",
    )(*arrays)


class Fetch:
    def __init__(self, sem):
        self.sem, self.count = sem, 0

    def get(self, src, dst):
        copy = pltpu.make_async_copy(src, dst, self.sem.at[self.count])
        self.count += 1
        copy.start()
        return copy


class Reduce:
    def __init__(self, mail, packs, ysum, zin, zother, l, begin, cut, end, lanes, spot):
        self.mail, self.packs, self.ysum, self.zin, self.zother = mail, packs, ysum, zin, zother
        self.l, self.early, self.late, self.lanes = l, slice(begin, cut), slice(cut, end), lanes
        self.has_early = cut > begin
        self.other = slice(spot, spot + cut - begin)
        self.over, self.steps = [], {}
        z = mail.z
        low = z < LINE // 2
        self.order = [
            jnp.where(low, 3, 0), jnp.where(low, 2, 1), jnp.where(low, 1 - z, 5 - z), z,
        ]

    def at(self, z, y, rows):
        return self.packs.at[self.l, z, y, rows, self.lanes]

    def add(self, z, y, rows, more):
        ref = self.at(z, y, rows)
        ref[...] = (ref[...].astype(f32) + more[...].astype(f32)).astype(bf16)

    def slots(self, step, early):
        out = []
        m = self.mail
        rows = self.early if early else self.late
        for side, way in enumerate((1, -1)):
            held = 4 + m.z - step if way == 1 else m.z - 4 + step
            if way == 1:
                can = (m.z + 1 <= step) & (m.z < LINE - 1)
            else:
                can = (LINE - m.z <= step) & (m.z > 0)
            at = jnp.clip(held, 0, LINE - 1)
            out.append((way, side, can, at, m.y, rows, self.zin.at[self.l, step - 1, side, rows, self.lanes], 0))
            if early:
                spot = self.zother.at[self.l, step - 1, side, self.other, self.lanes]
                out.append((way, side, can, at, 1 - m.y, rows, spot, 1))
        return out

    def pass_on(self, step, early):
        for way, side, can, at, y, rows, spot, which in self.slots(step, early):
            copy = self.mail.copy(self.at(at, y, rows), spot, self.mail.along(way))
            self.mail.start(copy, can)
            self.steps[early, step, side, which] = copy

    def take(self, step, early):
        z = self.mail.z
        for way, side, can, at, y, rows, spot, which in self.slots(step, early):
            copy = self.steps[early, step, side, which]
            if way == 1:
                when, mine = (z >= 1) & (step >= z), 3 + z - step
            else:
                when, mine = (z <= LINE - 2) & (step >= LINE - 1 - z), z - 3 + step

            def arrive(copy=copy, mine=mine, y=y, rows=rows, spot=spot):
                copy.wait_recv()
                self.add(jnp.clip(mine, 0, LINE - 1), y, rows, spot)

            only(when, arrive)

    def begin(self):
        m = self.mail
        if self.has_early:
            self.pass_on(1, True)
        for i, z in enumerate(self.order):
            copy = m.copy(
                self.at(z, 1 - m.y, self.late), self.ysum.at[self.l, i, self.late, self.lanes], m.peer(1)
            )
            m.start(copy)
            self.over.append(copy)

    def step(self, i):
        m = self.mail
        if i < LINE:
            self.over[i].wait_recv()
            self.add(self.order[i], m.y, self.late, self.ysum.at[self.l, i, self.late, self.lanes])
            if i:
                self.take(i, False)
            if i < LINE - 1:
                self.pass_on(i + 1, False)
            if self.has_early and i:
                self.take(i, True)
                if i < LINE - 1:
                    self.pass_on(i + 1, True)
                else:
                    self.last = m.copy(
                        self.at(m.z, 1 - m.y, self.early), self.ysum.at[self.l, 0, self.early, self.lanes], m.peer(1)
                    )
                    m.start(self.last)
        elif self.has_early:
            self.last.wait_recv()
            self.add(m.z, m.y, self.early, self.ysum.at[self.l, 0, self.early, self.lanes])


class Direct:
    def __init__(self, mail, packs, ysum, zin, l, begin, end, lanes):
        self.mail, self.packs, self.ysum, self.zin, self.l = mail, packs, ysum, zin, l
        self.rows, self.lanes = slice(begin, end), lanes
        self.order = (1, 2, 3, 0)
        self.over, self.came = [], []

    def at(self, far, y):
        return self.packs.at[self.l, self.mail.z ^ far, y, self.rows, self.lanes]

    def begin(self):
        m = self.mail
        for far in self.order:
            dst = self.ysum.at[self.l, far, self.rows, self.lanes]
            copy = m.copy(self.at(far, 1 - m.y), dst, m.peer(1))
            m.start(copy)
            self.over.append(copy)

    def step(self, i):
        m = self.mail
        if i < LINE:
            far = self.order[i]
            self.over[i].wait_recv()
            ref = self.at(far, m.y)
            more = self.ysum[self.l, far, self.rows, self.lanes]
            ref[...] = (ref[...].astype(f32) + more.astype(f32)).astype(bf16)
            if far:
                copy = m.copy(ref, self.zin.at[self.l, far - 1, 0, self.rows, self.lanes], m.peer(2 * far))
                m.start(copy)
                self.came.append(copy)
        else:
            for copy in self.came:
                copy.wait_recv()
            ref = self.at(0, m.y)
            total = ref[...].astype(f32)
            for far in range(1, LINE):
                total = total + self.zin[self.l, far - 1, 0, self.rows, self.lanes].astype(f32)
            ref[...] = total.astype(bf16)


def backward_kernel(sizes, *refs):
    tokens, depth, units, feats, states, tall, small, high = sizes
    width = units + LANES
    top = tall * GROUP
    rows = top + high + small * GROUP * units // depth
    devices = GROUP * RINGS
    (
        cot_ref, x_ref, later_ref, rows_ref, filt_ref, mixn_ref, auxs, oadd_ref,
        norm_hbm, value_hbm, gp_hbm, c_hbm, full_hbm, z_hbm, g2_hbm, vw_hbm, ow_hbm, ew_hbm, dout_hbm,
    ) = refs[:19]
    dx_ref, vmine_ref, vtotal_ref, o_ref, raw_hbm, ofar_hbm = refs[19:25]
    (
        norm, value, gp, cbuf, full, z, g2, vw, ow, ew, dout, dcb, da,
        qe, qo, near, cross, far, ofar, dnbuf, din, dadd, dfar,
        packs, ysum, zin, zother, gsend, grecv, vsend, vin, vgrp,
        rem_scr, shifted, dz_scr, corr, y_scr, w_scr, o_scr, m_scr,
        send_sem, recv_sem, hbm_sem,
    ) = refs[25:]
    mail = Mail(send_sem, recv_sem)
    fetch = Fetch(hbm_sem)
    dp, z_at, y_at = mail.dp, mail.z, mail.y
    thirds = units // 256
    across = depth // 256
    strips = tokens // STRIP

    def lanes(at, size):
        return pl.ds(pl.multiple_of(at * size, LANES), size)

    def block(j):
        return pl.ds(pl.multiple_of(j * tokens, tokens), tokens)

    def load_out(l):
        return [
            fetch.get(ow_hbm.at[l], ow), fetch.get(ew_hbm.at[l], ew), fetch.get(value_hbm.at[l], value),
            fetch.get(gp_hbm.at[l], gp), fetch.get(c_hbm.at[l], cbuf), fetch.get(full_hbm.at[l], full),
        ]

    def load_in(l):
        return [
            fetch.get(z_hbm.at[l], z), fetch.get(g2_hbm.at[l], g2), fetch.get(vw_hbm.at[l], vw),
            fetch.get(norm_hbm.at[l], norm),
        ]

    first = fetch.get(dout_hbm, dout)
    loads = load_out(LAYERS - 1)
    more_loads = load_in(LAYERS - 1)
    vsend[...] = jnp.zeros(vsend.shape, f32)
    for b in range(8):
        shifted[b, tokens:, :] = jnp.zeros((PAD, LANES), f32)

    def start_dx(i, carry):
        at = pl.ds(pl.multiple_of(i * STRIP, STRIP), STRIP)
        up = cot_ref[at, :].astype(f32)
        dx_ref[at, :] = up
        low = (up * auxs[0, at, 2:3].astype(f32)).astype(bf16).astype(f32)
        return carry + jnp.sum(low, axis=0, keepdims=True)

    vsend[LAYERS - 1, 2:3, :] = lax.fori_loop(0, strips, start_dx, jnp.zeros((1, depth), f32))

    mail.greet((CORE, CHIP, BOTH, 1, 2, 3, 4, 5, 6, 7))

    def back_out(l, j):
        at = block(j)
        dgated = nt(dout[at, :], ow[...])
        val = value[at, :].astype(f32)
        gate = cbuf[at, :].astype(f32)
        dc = (dgated * val).astype(bf16)
        dcb[at, :] = dc
        da[at, :units] = (dgated * gate * gp[at, :].astype(f32)).astype(bf16)

        def keep():
            cbuf[at, :] = (gate * val).astype(bf16)

        pl.when(j < 2)(keep)
        vsend[l, 5:6, :units] += jnp.sum(dc.astype(f32), axis=0, keepdims=True)
        y_scr[...] = nt(dc, ew[...])
        for k in range(GROUP):
            part = y_scr[:, lanes(dp ^ k, LANES)].astype(bf16)
            if k % 2:
                qo[k // 2, j ^ 1] = part
            else:
                qe[k // 2, j] = part

    def back_in(l, j, middle):
        at = block(j)
        rem_scr[...] = jnp.broadcast_to(auxs[j, :, 1:2].astype(f32), (tokens, LANES))
        dy = qe[0, j].astype(f32) + near[0, j].astype(f32) + far[j].astype(f32)
        for b in range(8):
            shifted[b, :tokens, :] = dy if b == 0 else pltpu.roll(dy, tokens - b, 0)
        for s in range(strips):
            rem = rem_scr[s * STRIP : (s + 1) * STRIP, :]
            past = z[pl.ds(pl.multiple_of(j * tokens + s * STRIP, STRIP), STRIP), :]

            def lags(a, acc, s=s, rem=rem, past=past):
                base = pl.multiple_of(a * 8, 8)
                left = rem - (a * 8).astype(f32)
                for b in range(8):
                    row = filt_ref[l, pl.ds(base + b, 1), :]
                    later = shifted[b, pl.ds(pl.multiple_of(s * STRIP + base, 8), STRIP), :]
                    later = jnp.where(left >= b, later, 0.0)
                    acc = acc + later * row
                    pair = later * past
                    corr[pl.ds(pl.multiple_of(base * 8 + b * 8, 8), 8), :] += (pair[0:8] + pair[8:16]) + (
                        pair[16:24] + pair[24:32]
                    )
                return acc

            dz_scr[s * STRIP : (s + 1) * STRIP, :] = lax.fori_loop(
                0, (strips - s) * (STRIP // 8), lags, jnp.zeros((STRIP, LANES), f32)
            )
            if s == 2:
                middle()
        da2 = (dz_scr[...] + rows_ref[l, 5:6, :LANES] * dy) * g2[at, :]
        da[at, units:] = da2.astype(bf16)
        vsend[l, 5:6, units:width] += jnp.sum(z[at, :] * dy, axis=0, keepdims=True)
        vsend[l, 4:5, :width] += jnp.sum(da[at, :].astype(f32), axis=0, keepdims=True)
        dnbuf[j] = nt(da[at, :], vw[...]).astype(bf16)

    def grads_proj(l):
        half, wide = 2 * tokens, high * GROUP
        for j in (2, 3):
            at = slice(j * tokens, (j + 1) * tokens)
            dcb[at, :] = (cbuf[at, :].astype(f32) * value[at, :].astype(f32)).astype(bf16)
        for i in range(RINGS // GROUP):
            lane = slice(i * wide, (i + 1) * wide)
            o_scr[...] = (tn(cbuf[:half, lane], dout[:half, :]) + tn(dcb[half:, lane], dout[half:, :])).astype(bf16)
            for g in range(GROUP):
                at = i * GROUP + g
                packs[l, at // 2, at % 2, top : top + high, :] = o_scr[g * high : (g + 1) * high, :]
        sums[l]["proj"].begin()

    def grads_expand(l):
        for t in range(thirds):
            w_scr[: 2 * tokens, :256] = tn(full[...], dcb[:, t * 256 : (t + 1) * 256]).astype(bf16)
            for j in range(RINGS):
                for k in range(GROUP):
                    r, c = divmod(k * thirds + t, across)
                    owner = (dp ^ k) * RINGS + j
                    base = top + high + small * r
                    packs[l, j // 2, j % 2, base : base + small, c * 256 : (c + 1) * 256] = w_scr[
                        pl.ds(pl.multiple_of(owner * small, small), small), :256
                    ]
        sums[l]["expand"].begin()

    def grads_in_of(l, lane):
        wide = depth // GROUP
        size = lane.stop - lane.start
        for d in range(GROUP):
            w_scr[:wide, :size] = tn(norm[:, d * wide : (d + 1) * wide], da[:, lane]).astype(bf16)
            at = pl.ds(pl.multiple_of((dp ^ d) * tall, tall), tall)
            for j in range(RINGS):
                packs[l, j // 2, j % 2, at, lane] = w_scr[j * tall : (j + 1) * tall, :size]

    def mixing_of(l):
        lag = lax.broadcasted_iota(jnp.int32, (tokens, tokens * 8), 0)
        part = lax.broadcasted_iota(jnp.int32, (tokens, tokens * 8), 1) // 8
        total = nn((lag == part).astype(bf16), corr[...].astype(bf16))
        steps = lax.broadcasted_iota(jnp.int32, (tokens, states), 0).astype(f32)
        powers = jnp.exp(-steps * rows_ref[l, 3:4, :states]).astype(bf16)
        m_scr[...] = tn(powers, total.astype(bf16)).astype(bf16)
        for j in range(RINGS):
            for k in range(GROUP):
                owner = (dp ^ k) * RINGS + j
                side = packs.at[l, j // 2, j % 2, k * tall : (k + 1) * tall]
                side[:small, width:] = m_scr[pl.ds(pl.multiple_of(owner * small, small), small), :]
                side[small:, width:] = jnp.zeros((tall - small, LANES), bf16)
        steps = lax.broadcasted_iota(jnp.int32, (tokens, LANES), 0).astype(f32)
        terms = tn(powers, (total * steps).astype(bf16)) * mixn_ref[l].astype(f32)
        vsend[l, 3:4, :states] = -lax.dot_general(
            jnp.ones((8, LANES), f32), terms, cols_dims, precision=highest, preferred_element_type=f32
        )[0:1]

    state = {}
    bufs = (mail, packs, ysum, zin, zother)
    sums = [
        {
            "proj": Reduce(*bufs, l, top, top + 16, top + high, slice(0, depth), 16),
            "expand": Reduce(*bufs, l, top + high, top + high + 16, rows, slice(0, depth), 32),
            "value": Reduce(*bufs, l, 0, 16, top, slice(0, units), 0),
            "rest": Direct(*bufs[:4], l, 0, top, slice(units, depth)),
        }
        for l in range(LAYERS)
    ]

    def own(l, at, lane=slice(None)):
        return packs[l, z_at, y_at, at, lane]

    def group_proj(l):
        sums[l]["proj"].step(4)
        o_ref[l] = own(l, slice(top, top + high))

    def group_out(l):
        sums[l]["expand"].step(4)
        for k in range(GROUP):
            dst = grecv.at[l, 0, tall : tall + small] if k == 0 else gsend.at[l, k - 1]
            for t in range(thirds):
                r, c = divmod(k * thirds + t, across)
                base = top + high + small * r
                dst[:, t * 256 : (t + 1) * 256] = own(l, slice(base, base + small), slice(c * 256, (c + 1) * 256))
            dst[:, units:] = jnp.zeros((small, depth - units), bf16)
            if k:
                state[l, "out", k] = mail.send(
                    gsend.at[l, k - 1], grecv.at[l, k, tall : tall + small], k * RINGS
                )

    def group_in(l, name):
        sums[l][name].step(4)
        lane = sums[l][name].lanes
        for k in (2, 3, 1):
            state[l, name, k] = mail.send(
                packs.at[l, z_at, y_at, k * tall : (k + 1) * tall, lane], grecv.at[l, k, 0:tall, lane], k * RINGS
            )
        grecv[l, 0, :tall, lane] = own(l, slice(0, tall), lane)

    def group_last(l):
        for name in ("out", "value", "rest"):
            for k in range(1, GROUP):
                state[l, name, k].wait_recv()
        state[l, "raw"] = fetch.get(grecv.at[l], raw_hbm.at[l])

    def vector_rest(l):
        state[l, "vr"] = [mail.send(vsend.at[l], vin.at[l, j - 1], j) for j in range(1, RINGS)]

    def vector_group(l):
        for copy in state[l, "vr"]:
            copy.wait_recv()
        total = vsend[l]
        for j in range(RINGS - 1):
            total = total + vin[l, j]
        vmine_ref[l] = total
        vgrp[l, 0] = total
        state[l, "vg"] = [mail.send(vgrp.at[l, 0], vgrp.at[l, k], k * RINGS) for k in range(1, GROUP)]

    def vector_last(l):
        for copy in state[l, "vg"]:
            copy.wait_recv()
        total = vgrp[l, 0]
        for k in range(1, GROUP):
            total = total + vgrp[l, k]
        vtotal_ref[l] = total

    def pair(fn, lo):
        def body(i, carry):
            fn(lo + i)
            return carry

        lax.fori_loop(0, 2, body, 0)

    def exchange_dy(half):
        return mail.send(qo.at[:, half], near.at[:, half], CORE)

    def cross_dy(half, other, copy):
        copy.wait_recv()
        cross[half] = (qe[1, half].astype(f32) + near[1, half].astype(f32)).astype(bf16)
        return mail.send(cross.at[half], far.at[other], CHIP)

    lo, hi = slice(0, 2), slice(2, 4)
    halves = [slice(h * tokens // 2, (h + 1) * tokens // 2) for h in range(2)]

    def grads_value(l):
        grads_in_of(l, slice(0, units))
        sums[l]["value"].begin()

    def grads_rest(l):
        grads_in_of(l, slice(units, width))
        mixing_of(l)
        sums[l]["rest"].begin()

    def layer(l, loads, more_loads, events, wait_far):
        def due():
            if events:
                events.pop(0)()

        for copy in loads:
            copy.wait()
        corr[...] = jnp.zeros(corr.shape, f32)
        pair(lambda j: back_out(l, j), 0)
        near_lo = exchange_dy(lo)
        wait_far()
        grads_proj(l)
        pair(lambda j: back_out(l, j), 2)
        near_hi = exchange_dy(hi)
        cross_lo = cross_dy(lo, hi, near_lo)
        cross_hi = cross_dy(hi, lo, near_hi)
        if l:
            state["o"] = mail.send(oadd_ref, ofar, CHIP)
        due()
        grads_expand(l)
        next_loads = load_out(l - 1) if l else []
        for copy in more_loads:
            copy.wait()
        due()
        grads_value(l)
        due()
        cross_lo.wait_recv()
        back_in(l, 3, due)
        core_hi = mail.send(dnbuf.at[3], din.at[0], CORE)
        due()
        back_in(l, 2, due)
        core_hi.wait_recv()
        chip = []
        for at in halves:
            dadd[at] = (dnbuf[2, at].astype(f32) + din[0, at].astype(f32)).astype(bf16)
            chip.append(mail.send(dadd.at[at], dfar.at[at], CHIP))
        due()
        cross_hi.wait_recv()
        back_in(l, 1, due)
        core_lo = mail.send(dnbuf.at[1], din.at[1], CORE)
        due()
        back_in(l, 0, due)
        due()
        if l == 0:
            grads_rest(l)
        due()
        core_lo.wait_recv()

        def strip(i, carry):
            gain_sum, shift_sum, out_sum = carry
            at = pl.ds(pl.multiple_of(i * STRIP, STRIP), STRIP)
            v = later_ref[at, :] if l else x_ref[at, :].astype(f32)
            center = v - jnp.mean(v, axis=1, keepdims=True)
            scale = lax.rsqrt(jnp.mean(center * center, axis=1, keepdims=True) + 1e-05)
            normed = center * scale
            grad = dnbuf[0, at, :].astype(f32) + din[1, at, :].astype(f32) + dfar[at, :].astype(f32)
            q = grad * rows_ref[l, 0:1, :]
            tilt = q - jnp.mean(q, axis=1, keepdims=True) - normed * jnp.mean(q * normed, axis=1, keepdims=True)
            up = dx_ref[at, :] + tilt * scale
            dx_ref[at, :] = up
            if l:
                low = (up * auxs[0, at, 2:3].astype(f32)).astype(bf16)
                dout[at, :] = low
                out_sum = out_sum + jnp.sum(low.astype(f32), axis=0, keepdims=True)
            return (
                gain_sum + jnp.sum(grad * normed, axis=0, keepdims=True),
                shift_sum + jnp.sum(grad, axis=0, keepdims=True),
                out_sum,
            )

        zero = jnp.zeros((1, depth), f32)
        sums_now = (zero, zero, zero)
        for h, at in enumerate(halves):
            chip[h].wait_recv()
            sums_now = lax.fori_loop(h * strips // 2, (h + 1) * strips // 2, strip, sums_now)
            if l:
                state["dout", h] = mail.send(dout.at[at], dout.at[slice(2 * tokens + at.start, 2 * tokens + at.stop)], CHIP)
        gain_sum, shift_sum, out_sum = sums_now
        vsend[l, 0:1, :] = gain_sum
        vsend[l, 1:2, :] = shift_sum
        if l:
            vsend[l - 1, 2:3, :] = out_sum
        for copy in (near_lo, near_hi, cross_lo, cross_hi, core_hi, core_lo, *chip):
            mail.finish(copy)
        return next_loads

    first.wait()

    def then(*steps):
        def event():
            for step in steps:
                step()

        return event

    nothing = then()

    def step(l, name, i):
        return lambda: sums[l][name].step(i)

    def steps(l, name, *which):
        return then(*(step(l, name, i) for i in which))

    events = [
        then(),
        then(),
        then(step(1, "proj", 0)),
        then(),
        then(step(1, "proj", 1)),
        then(),
        then(step(1, "proj", 2), step(1, "expand", 0)),
        then(),
        then(step(1, "proj", 3), step(1, "expand", 1)),
        then(),
        then(step(1, "expand", 2), step(1, "value", 0)),
        then(lambda: group_proj(1), step(1, "expand", 3)),
    ]
    loads = layer(1, loads, more_loads, events, nothing)

    dout_core = mail.send(dout.at[pl.ds(0, tokens)], dout.at[pl.ds(tokens, tokens)], CORE)
    grads_rest(1)
    more_loads = load_in(0)
    vector_rest(1)
    state["o"].wait_recv()
    far_out = fetch.get(ofar, ofar_hbm)

    step(1, "value", 1)()

    def dout_far():
        group_out(1)
        step(1, "value", 2)()
        relays = []
        for h, at in enumerate(halves):
            state["dout", h].wait_recv()
            src = dout.at[slice(2 * tokens + at.start, 2 * tokens + at.stop)]
            relays.append(mail.send(src, dout.at[slice(3 * tokens + at.start, 3 * tokens + at.stop)], CORE))
        step(1, "value", 3)()
        step(1, "rest", 0)()
        for relay in relays:
            relay.wait_recv()

    events = [
        then(step(1, "rest", 1)),
        then(step(0, "proj", 0)),
        then(lambda: group_in(1, "value"), step(1, "rest", 2)),
        then(step(0, "proj", 1)),
        then(lambda: vector_group(1), step(1, "rest", 3)),
        then(step(0, "proj", 2), step(0, "expand", 0)),
        then(lambda: group_in(1, "rest")),
        then(step(0, "proj", 3), step(0, "expand", 1)),
        then(step(0, "value", 0)),
        then(step(0, "expand", 2), lambda: group_proj(0), step(0, "value", 1)),
        then(lambda: vector_last(1)),
        then(step(0, "expand", 3), step(0, "value", 2), lambda: group_last(1)),
    ]
    dout_core.wait_recv()
    layer(0, loads, more_loads, events, dout_far)
    step(0, "value", 3)()
    vector_rest(0)
    step(0, "rest", 0)()
    group_out(0)
    group_in(0, "value")
    step(0, "rest", 1)()
    vector_group(0)
    steps(0, "rest", 2, 3)()
    group_in(0, "rest")
    vector_last(0)
    group_last(0)
    mail.close()
    far_out.wait()
    for l in range(LAYERS):
        state[l, "raw"].wait()


def backward_both(arrays, sizes):
    tokens, depth, units, feats, states, tall, small, high = sizes
    width = units + LANES
    group = tokens * GROUP
    rows = tall * GROUP + high + small * GROUP * units // depth
    shape = jax.ShapeDtypeStruct
    two = lambda *dims: (LAYERS,) + dims
    outs = [
        ((tokens, depth), f32), (two(8, depth), f32), (two(8, depth), f32), (two(high, depth), bf16),
        (two(GROUP, tall + small, depth), bf16), ((tokens, depth), bf16),
    ]
    return pl.pallas_call(
        partial(backward_kernel, sizes),
        out_shape=[shape(*s) for s in outs],
        in_specs=[pl.BlockSpec(memory_space=VMEM)] * 8 + [pl.BlockSpec(memory_space=pl.ANY)] * 11,
        out_specs=[pl.BlockSpec(memory_space=VMEM)] * 4 + [pl.BlockSpec(memory_space=pl.ANY)] * 2,
        scratch_shapes=[
            VMEM((group, depth), bf16),
            VMEM((group, units), bf16),
            VMEM((group, units), bf16),
            VMEM((group, units), bf16),
            VMEM((group, feats), bf16),
            VMEM((group, LANES), f32),
            VMEM((group, LANES), f32),
            VMEM((depth, width), bf16),
            VMEM((units, depth), bf16),
            VMEM((feats, units), bf16),
            VMEM((group, depth), bf16),
            VMEM((group, units), bf16),
            VMEM((group, width), bf16),
            VMEM((2, GROUP, tokens, LANES), bf16),
            VMEM((2, GROUP, tokens, LANES), bf16),
            VMEM((2, GROUP, tokens, LANES), bf16),
            VMEM((GROUP, tokens, LANES), bf16),
            VMEM((GROUP, tokens, LANES), bf16),
            VMEM((tokens, depth), bf16),
            VMEM((GROUP, tokens, depth), bf16),
            VMEM((2, tokens, depth), bf16),
            VMEM((tokens, depth), bf16),
            VMEM((tokens, depth), bf16),
            VMEM(two(LINE, 2, rows, depth), bf16),
            VMEM(two(LINE, rows, depth), bf16),
            VMEM(two(LINE - 1, 2, rows, depth), bf16),
            VMEM(two(LINE - 1, 2, 48, depth), bf16),
            VMEM(two(GROUP - 1, small, depth), bf16),
            VMEM(two(GROUP, tall + small, depth), bf16),
            VMEM(two(8, depth), f32),
            VMEM(two(RINGS - 1, 8, depth), f32),
            VMEM(two(GROUP, 8, depth), f32),
            VMEM((tokens, LANES), f32),
            VMEM((8, PAD + tokens, LANES), f32),
            VMEM((tokens, LANES), f32),
            VMEM((tokens * 8, LANES), f32),
            VMEM((tokens, feats), f32),
            VMEM((2 * tokens, width), bf16),
            VMEM((high * GROUP, depth), bf16),
            VMEM((states, LANES), bf16),
            pltpu.SemaphoreType.DMA((220,)),
            pltpu.SemaphoreType.DMA((220,)),
            pltpu.SemaphoreType.DMA((26,)),
        ],
        compiler_params=pltpu.CompilerParams(
            vmem_limit_bytes=60 << 20, collective_id=2, has_side_effects=True
        ),
        cost_estimate=cost(140.0),
        name="backward_both",
    )(*arrays)


def finish(me, arrays, sizes):
    tokens, depth, units, feats, states, tall, small, high = sizes
    width = units + LANES
    devices = GROUP * RINGS
    hidden = units * GROUP

    def kernel(me_ref, *refs):
        hbm = refs[: len(arrays)]
        (
            last_ref, dx_ref, gain_ref, shift_ref, v_ref, vb_ref, r_ref, rb_ref, dec_ref, si_out, so_out,
            skip_ref, e_ref, eb_ref, o_ref, ob_ref,
        ) = refs[len(arrays) : len(arrays) + 16]
        here, sem = refs[len(arrays) + 16 : -1], refs[-1]
        to = (*here, dx_ref)
        copies = [pltpu.make_async_copy(a, b, sem.at[i]) for i, (a, b) in enumerate(zip(hbm, to))]
        for copy in copies:
            copy.start()
        raw, out_part, mine_ref, total_ref, last_in, far_in, aux_ref, si_ref, so_ref = here
        for copy in copies[:-1]:
            copy.wait()
        dp, fs = me_ref[0], me_ref[1]
        index = dp * RINGS + fs

        def lanes(at, size):
            return pl.ds(pl.multiple_of(at * size, LANES), size)

        flags = aux_ref[0, :, 2:3].astype(f32)
        last_ref[...] = (last_in[...] + flags * far_in[...].astype(f32)).astype(bf16)
        o_ref[...] = out_part[...].astype(f32)
        apart = lax.broadcasted_iota(jnp.int32, (depth, LANES), 0) - lax.broadcasted_iota(
            jnp.int32, (depth, LANES), 1
        )
        both = jnp.concatenate([total_ref[0], total_ref[1], mine_ref[0], mine_ref[1]], axis=0)
        high_part = both.astype(bf16)
        low_part = (both - high_part.astype(f32)).astype(bf16)

        def pick(start):
            chosen = (apart == start).astype(bf16)
            return nn(high_part, chosen) + nn(low_part, chosen)

        short, mid = states // devices, units // RINGS
        long_all, short_all = pick(index * (depth // devices)), pick(index * short)
        mid_all, rest_all = pick(fs * mid), pick(units + fs * short)
        for l in range(LAYERS):
            for k in range(GROUP):
                q = dp ^ k
                v_ref[l, :, lanes(q, units)] = raw[l, k, :tall, :units].astype(f32)
                r_ref[l, :, lanes(q, LANES)] = raw[l, k, :tall, units:width].astype(f32)
                e_ref[l, :, lanes(q, units)] = raw[l, k, tall:, :units].astype(f32)
                part = raw[l, k, :small, width:].astype(f32)
                si_out[l, :, lanes(q, LANES)] = part * so_ref[l, :, lanes(q, LANES)].astype(f32)
                so_out[l, :, lanes(q, LANES)] = part * si_ref[l, :, lanes(q, LANES)].astype(f32)

            for r, ref in enumerate((gain_ref, shift_ref, ob_ref)):
                ref[l : l + 1, :] = long_all[8 * l + r : 8 * l + r + 1, : depth // devices]
            dec_ref[l : l + 1, :] = short_all[8 * l + 3 : 8 * l + 4, :short]
            own = 8 * (LAYERS + l)
            vb_ref[l : l + 1, :] = mid_all[own + 4 : own + 5, :mid]
            eb_ref[l : l + 1, :] = mid_all[own + 5 : own + 6, :mid]
            rb_ref[l : l + 1, :] = rest_all[own + 4 : own + 5, :short]
            skip_ref[l : l + 1, :] = rest_all[own + 5 : own + 6, :short]
        copies[-1].wait()

    two = lambda *dims: (LAYERS,) + dims
    outs = [
        (tokens, depth), two(depth // devices), two(depth // devices), two(tall, hidden), two(units // RINGS),
        two(tall, feats), two(LANES // RINGS), two(states // devices), two(small, feats), two(small, feats),
        two(LANES // RINGS), two(small, hidden), two(units // RINGS), two(high, depth), two(depth // devices),
    ]
    return pl.pallas_call(
        kernel,
        out_shape=[jax.ShapeDtypeStruct((tokens, depth), bf16)] + [jax.ShapeDtypeStruct(s, f32) for s in outs],
        in_specs=[pl.BlockSpec(memory_space=pltpu.SMEM)] + [pl.BlockSpec(memory_space=pl.ANY)] * len(arrays),
        out_specs=[pl.BlockSpec(memory_space=VMEM)] * 16,
        scratch_shapes=[VMEM(a.shape, a.dtype) for a in arrays[:-1]] + [pltpu.SemaphoreType.DMA((len(arrays),))],
        compiler_params=pltpu.CompilerParams(vmem_limit_bytes=60 << 20),
        cost_estimate=cost(4.0),
        name="finish",
    )(me, *arrays)


def mixer(labels, signal, decays, stateinput, stateoutput, skipgain):
    rows = signal.shape[0]
    width = min(32, rows)
    count = rows // width
    mixing = stateinput * stateoutput
    offsets = jnp.arange(width, dtype=jnp.float32)
    powers = jnp.exp(-offsets[:, None] * decays[None, :])
    kernel = jnp.dot(powers, mixing, precision=highest)
    positions = jnp.arange(width, dtype=jnp.int32)
    lagged = jnp.maximum(positions[:, None] - positions[None, :], 0)
    toeplitz = jnp.take(kernel, lagged, axis=0)
    causal = positions[:, None] >= positions[None, :]
    leading = jnp.exp(-(offsets[:, None] + 1.0) * decays[None, :])
    trailing = jnp.exp(-(width - 1.0 - offsets[:, None]) * decays[None, :])
    across = jnp.exp(-width * decays)

    def advance(carry, pieces):
        state, before = carry
        block, marks = pieces
        same = jnp.logical_and(marks[:, None] == marks[None, :], causal).astype(signal.dtype)
        inner = jnp.sum(toeplitz * same[:, :, None] * block[None, :, :], axis=1)
        joined = (marks == before).astype(signal.dtype)
        carried = jnp.dot(leading, mixing * state, precision=highest) * joined[:, None]
        final = marks[width - 1]
        keep = (final == before).astype(signal.dtype)
        fresh = (marks == final).astype(signal.dtype)
        state = across[:, None] * state * keep + lax.dot_general(
            trailing * fresh[:, None], block, rows_dims, precision=highest
        )
        return ((state, final), inner + carried)

    start = (jnp.zeros(mixing.shape, signal.dtype), jnp.array(-1, jnp.int32))
    ending, mixed = lax.scan(
        jax.checkpoint(advance),
        start,
        (signal.reshape(count, width, -1), labels.reshape(count, width)),
    )
    return mixed.reshape(rows, -1) + skipgain[None, :] * signal


def normalize(rows, gain, shift):
    center = rows - jnp.mean(rows, axis=1, keepdims=True)
    spread = jnp.mean(center * center, axis=1, keepdims=True)
    return center * lax.rsqrt(spread + 1e-05) * gain + shift


def smooth(values):
    return jax.nn.gelu(values, approximate=False)


def gather_forward(shards, depth):
    return (
        lax.all_gather(shards[0][depth], ("dp", "fsdp"), axis=0, tiled=True),
        lax.all_gather(shards[1][depth], ("dp", "fsdp"), axis=0, tiled=True),
        lax.all_gather(shards[2][depth], ("dp", "fsdp"), axis=0, tiled=True),
        lax.all_gather(shards[3][depth], ("dp", "fsdp"), axis=0, tiled=True),
        lax.all_gather(shards[4][depth], ("dp", "fsdp"), axis=0, tiled=True),
        lax.all_gather(shards[5][depth], ("dp", "fsdp"), axis=0, tiled=True),
        lax.all_gather(shards[6][depth], ("dp", "fsdp"), axis=0, tiled=True),
        lax.all_gather(shards[7][depth], ("dp", "fsdp"), axis=0, tiled=True),
        lax.all_gather(shards[8][depth], ("dp", "fsdp"), axis=0, tiled=True),
        lax.all_gather(shards[9][depth], ("dp", "fsdp"), axis=0, tiled=True),
        lax.all_gather(shards[10][depth], ("dp", "fsdp"), axis=0, tiled=True),
        lax.all_gather(shards[11][depth], ("dp", "fsdp"), axis=0, tiled=True),
        lax.all_gather(shards[12][depth], ("dp", "fsdp"), axis=0, tiled=True),
        lax.all_gather(shards[13][depth], ("dp", "fsdp"), axis=0, tiled=True),
    )


def gather_backward(shards, depth):
    return (
        lax.all_gather(shards[0][depth], ("dp", "fsdp"), axis=0, tiled=True),
        lax.all_gather(shards[1][depth], ("dp", "fsdp"), axis=0, tiled=True),
        lax.all_gather(shards[2][depth], ("dp", "fsdp"), axis=0, tiled=True),
        lax.all_gather(shards[3][depth], ("dp", "fsdp"), axis=0, tiled=True),
        lax.all_gather(shards[4][depth], ("dp", "fsdp"), axis=0, tiled=True),
        lax.all_gather(shards[5][depth], ("dp", "fsdp"), axis=0, tiled=True),
        lax.all_gather(shards[6][depth], ("dp", "fsdp"), axis=0, tiled=True),
        lax.all_gather(shards[7][depth], ("dp", "fsdp"), axis=0, tiled=True),
        lax.all_gather(shards[8][depth], ("dp", "fsdp"), axis=0, tiled=True),
        lax.all_gather(shards[9][depth], ("dp", "fsdp"), axis=0, tiled=True),
        lax.all_gather(shards[10][depth], ("dp", "fsdp"), axis=0, tiled=True),
        lax.all_gather(shards[11][depth], ("dp", "fsdp"), axis=0, tiled=True),
        lax.all_gather(shards[12][depth], ("dp", "fsdp"), axis=0, tiled=True),
        lax.all_gather(shards[13][depth], ("dp", "fsdp"), axis=0, tiled=True),
    )


def scatter_layer(terms):
    return (
        lax.psum_scatter(terms[0], ("dp", "fsdp"), scatter_dimension=0, tiled=True),
        lax.psum_scatter(terms[1], ("dp", "fsdp"), scatter_dimension=0, tiled=True),
        lax.psum_scatter(terms[2], ("dp", "fsdp"), scatter_dimension=0, tiled=True),
        lax.psum_scatter(terms[3], ("dp", "fsdp"), scatter_dimension=0, tiled=True),
        lax.psum_scatter(terms[4], ("dp", "fsdp"), scatter_dimension=0, tiled=True),
        lax.psum_scatter(terms[5], ("dp", "fsdp"), scatter_dimension=0, tiled=True),
        lax.psum_scatter(terms[6], ("dp", "fsdp"), scatter_dimension=0, tiled=True),
        lax.psum_scatter(terms[7], ("dp", "fsdp"), scatter_dimension=0, tiled=True),
        lax.psum_scatter(terms[8], ("dp", "fsdp"), scatter_dimension=0, tiled=True),
        lax.psum_scatter(terms[9], ("dp", "fsdp"), scatter_dimension=0, tiled=True),
        lax.psum_scatter(terms[10], ("dp", "fsdp"), scatter_dimension=0, tiled=True),
        lax.psum_scatter(terms[11], ("dp", "fsdp"), scatter_dimension=0, tiled=True),
        lax.psum_scatter(terms[12], ("dp", "fsdp"), scatter_dimension=0, tiled=True),
        lax.psum_scatter(terms[13], ("dp", "fsdp"), scatter_dimension=0, tiled=True),
    )


def layer_forward(current, labels, flags, weights):
    (
        normgain,
        normbias,
        valueproj,
        valuebias,
        reduceproj,
        reducebias,
        decays,
        stateinput,
        stateoutput,
        skipgain,
        expandproj,
        expandbias,
        outproj,
        outbias,
    ) = weights
    normed, norm_back = jax.vjp(
        normalize, current, normgain.astype(jnp.float32), normbias.astype(jnp.float32)
    )
    normed_low = normed.astype(jnp.bfloat16)
    opened = jnp.dot(normed_low, valueproj, preferred_element_type=jnp.float32) + valuebias.astype(
        jnp.float32
    )
    values, value_back = jax.vjp(smooth, opened)
    reduced = jnp.dot(
        normed_low, reduceproj, preferred_element_type=jnp.float32
    ) + reducebias.astype(jnp.float32)
    smoothed, reduce_back = jax.vjp(smooth, reduced)
    signal = smoothed * flags
    mixed, mix_back = jax.vjp(
        partial(mixer, labels),
        signal,
        decays.astype(jnp.float32),
        stateinput.astype(jnp.float32),
        stateoutput.astype(jnp.float32),
        skipgain.astype(jnp.float32),
    )
    mixed_low = mixed.astype(jnp.bfloat16)
    expanded = jnp.dot(
        mixed_low, expandproj, preferred_element_type=jnp.float32
    ) + expandbias.astype(jnp.float32)
    gated = (expanded * values).astype(jnp.bfloat16)
    branch = jnp.dot(gated, outproj, preferred_element_type=jnp.float32) + outbias.astype(
        jnp.float32
    )
    saved = (
        normed_low,
        values,
        value_back,
        reduce_back,
        mix_back,
        mixed_low,
        expanded,
        gated,
        norm_back,
    )
    return (current + flags * branch, saved)


def layer_backward(upstream, flags, weights, saved):
    (
        normgain,
        normbias,
        valueproj,
        valuebias,
        reduceproj,
        reducebias,
        decays,
        stateinput,
        stateoutput,
        skipgain,
        expandproj,
        expandbias,
        outproj,
        outbias,
    ) = weights
    normed_low, values, value_back, reduce_back, mix_back, mixed_low, expanded, gated, norm_back = (
        saved
    )
    dout = (flags * upstream).astype(jnp.bfloat16)
    outproj_term = lax.dot_general(gated, dout, rows_dims, preferred_element_type=jnp.float32)
    outbias_term = jnp.sum(dout, axis=0, dtype=jnp.float32)
    dgated = lax.dot_general(dout, outproj, cols_dims, preferred_element_type=jnp.float32)
    dexpanded = (dgated * values).astype(jnp.bfloat16)
    dvalues = dgated * expanded
    expandproj_term = lax.dot_general(
        mixed_low, dexpanded, rows_dims, preferred_element_type=jnp.float32
    )
    expandbias_term = jnp.sum(dexpanded, axis=0, dtype=jnp.float32)
    dmixed = lax.dot_general(dexpanded, expandproj, cols_dims, preferred_element_type=jnp.float32)
    dsignal, decays_term, stateinput_term, stateoutput_term, skipgain_term = mix_back(dmixed)
    (dreduced,) = reduce_back(dsignal * flags)
    dreduced_low = dreduced.astype(jnp.bfloat16)
    (dopened,) = value_back(dvalues)
    dopened_low = dopened.astype(jnp.bfloat16)
    valueproj_term = lax.dot_general(
        normed_low, dopened_low, rows_dims, preferred_element_type=jnp.float32
    )
    valuebias_term = jnp.sum(dopened_low, axis=0, dtype=jnp.float32)
    reduceproj_term = lax.dot_general(
        normed_low, dreduced_low, rows_dims, preferred_element_type=jnp.float32
    )
    reducebias_term = jnp.sum(dreduced_low, axis=0, dtype=jnp.float32)
    dnormed = lax.dot_general(dopened_low, valueproj, cols_dims, preferred_element_type=jnp.float32)
    dnormed = dnormed + lax.dot_general(
        dreduced_low, reduceproj, cols_dims, preferred_element_type=jnp.float32
    )
    dcurrent, normgain_term, normbias_term = norm_back(dnormed)
    terms = (
        normgain_term,
        normbias_term,
        valueproj_term,
        valuebias_term,
        reduceproj_term,
        reducebias_term,
        decays_term,
        stateinput_term,
        stateoutput_term,
        skipgain_term,
        expandproj_term,
        expandbias_term,
        outproj_term,
        outbias_term,
    )
    return (upstream + dcurrent, terms)


def plain(
    inputs,
    segment_ids,
    token_mask,
    cotangent,
    normgain,
    normbias,
    valueproj,
    valuebias,
    reduceproj,
    reducebias,
    decays,
    stateinput,
    stateoutput,
    skipgain,
    expandproj,
    expandbias,
    outproj,
    outbias,
):
    shards = (
        normgain,
        normbias,
        valueproj,
        valuebias,
        reduceproj,
        reducebias,
        decays,
        stateinput,
        stateoutput,
        skipgain,
        expandproj,
        expandbias,
        outproj,
        outbias,
    )
    flags = token_mask.astype(jnp.float32)[:, None]
    current = inputs.astype(jnp.float32)
    fetched = []
    stored = []
    for depth in range(LAYERS):
        weights = gather_forward(shards, depth)
        current, saved = layer_forward(current, segment_ids, flags, weights)
        fetched.append(weights)
        stored.append(saved)
    outputs = current.astype(jnp.bfloat16)
    upstream = cotangent.astype(jnp.float32)
    scattered = [None] * LAYERS
    for depth in reversed(range(LAYERS)):
        weights = gather_backward(shards, depth)
        upstream, terms = layer_backward(upstream, flags, weights, stored[depth])
        scattered[depth] = scatter_layer(terms)
    results = tuple(
        (jnp.stack([scattered[depth][index] for depth in range(LAYERS)]) for index in range(14))
    )
    return (outputs, upstream) + tuple(results)


def fast(
    inputs, segment_ids, token_mask, cotangent, normgain, normbias, valueproj, valuebias,
    reduceproj, reducebias, decays, stateinput, stateoutput, skipgain, expandproj, expandbias,
    outproj, outbias,
):
    tokens, depth = inputs.shape
    tall = valueproj.shape[1]
    small = stateinput.shape[1]
    high = outproj.shape[1]
    units = valueproj.shape[2] // GROUP
    feats = reduceproj.shape[2]
    states = stateinput.shape[1] * GROUP * RINGS
    group = tokens * GROUP
    sizes = (tokens, depth, units, feats, states, tall, small, high)

    lined = lambda v: v.reshape(tokens // LANES, LANES)
    shorts = (normgain, normbias, outbias, decays, valuebias, reducebias, skipgain, expandbias)
    (
        last, across, later, rows, filt, mixes, auxes,
        norms, value, slope, gate, full, z, slope2, value_w, out_w, expand_w, douts,
    ) = forward_both(
        (
            inputs, lined(segment_ids), lined(token_mask), cotangent, valueproj, reduceproj, expandproj,
            outproj, stateinput, stateoutput, *shorts, *tables(GROUP * RINGS),
        ),
        sizes,
    )
    dx, mine, total, out_part, raw, arrived = backward_both(
        (
            cotangent, inputs, later, rows, filt, mixes, auxes, across,
            norms.reshape(LAYERS, group, depth), value, slope, gate, full, z, slope2,
            value_w, out_w, expand_w, douts.reshape(group, depth),
        ),
        sizes,
    )
    me = jnp.stack([lax.axis_index("dp"), lax.axis_index("fsdp")]).astype(jnp.int32)
    arrays = (raw, out_part, mine, total, last, arrived, auxes, stateinput, stateoutput, dx)
    return tuple(finish(me, arrays, sizes))


def solution(mesh):
    placed = (
        P(("dp", "fsdp"), None),
        P(("dp", "fsdp")),
        P(("dp", "fsdp")),
        P(("dp", "fsdp"), None),
        P(None, ("dp", "fsdp")),
        P(None, ("dp", "fsdp")),
        P(None, ("dp", "fsdp"), None),
        P(None, ("dp", "fsdp")),
        P(None, ("dp", "fsdp"), None),
        P(None, ("dp", "fsdp")),
        P(None, ("dp", "fsdp")),
        P(None, ("dp", "fsdp"), None),
        P(None, ("dp", "fsdp"), None),
        P(None, ("dp", "fsdp")),
        P(None, ("dp", "fsdp"), None),
        P(None, ("dp", "fsdp")),
        P(None, ("dp", "fsdp"), None),
        P(None, ("dp", "fsdp")),
    )
    small = mesh.shape["dp"] == GROUP and mesh.shape["fsdp"] == RINGS
    return jax.shard_map(
        fast if small else plain,
        mesh=mesh,
        in_specs=placed,
        out_specs=(
            P(("dp", "fsdp"), None),
            P(("dp", "fsdp"), None),
            P(None, ("dp", "fsdp")),
            P(None, ("dp", "fsdp")),
            P(None, ("dp", "fsdp"), None),
            P(None, ("dp", "fsdp")),
            P(None, ("dp", "fsdp"), None),
            P(None, ("dp", "fsdp")),
            P(None, ("dp", "fsdp")),
            P(None, ("dp", "fsdp"), None),
            P(None, ("dp", "fsdp"), None),
            P(None, ("dp", "fsdp")),
            P(None, ("dp", "fsdp"), None),
            P(None, ("dp", "fsdp")),
            P(None, ("dp", "fsdp"), None),
            P(None, ("dp", "fsdp")),
        ),
        check_vma=False,
    )
```

```python
from functools import partial

import jax
import jax.numpy as jnp
import numpy as np
from jax import lax
from jax.experimental import pallas as pl
from jax.experimental.pallas import tpu as pltpu
from jax.sharding import PartitionSpec as P

LAYERS = 2
AXES = ("dp", "fsdp")
GROUP = 4
RINGS = 8
LANES = 128
STRIP = 32
PAD = 32

f32 = jnp.float32
bf16 = jnp.bfloat16
highest = lax.Precision.HIGHEST
rows_dims = (((0,), (0,)), ((), ()))
cols_dims = (((1,), (1,)), ((), ()))

VMEM = pltpu.VMEM


def cost(micros):
    return pl.CostEstimate(
        flops=int(micros * 1.0e9), bytes_accessed=1 << 20, transcendentals=0
    )


def nt(a, b):
    return lax.dot_general(a, b, cols_dims, preferred_element_type=f32)


def tn(a, b):
    return lax.dot_general(a, b, rows_dims, preferred_element_type=f32)


def nn(a, b):
    return jnp.dot(a, b, preferred_element_type=f32)


def tables(devices):
    out = []
    for count, size in ((devices, 32), (RINGS, 96), (devices, 16)):
        at = np.arange(count * size)
        out.append(jnp.asarray((np.arange(LANES)[:, None] == at[None, :] % size), bf16))
        out.append(jnp.asarray((np.arange(count)[:, None] == at[None, :] // size), f32))
    return out


class Mail:
    def __init__(self, send_sem, recv_sem):
        self.dp, self.fs = lax.axis_index("dp"), lax.axis_index("fsdp")
        self.z, self.y = self.fs // 2, self.fs % 2
        self.send_sem, self.recv_sem, self.count, self.sent = send_sem, recv_sem, 0, []

    def peer(self, flip):
        return (self.dp ^ (flip // RINGS), self.fs ^ (flip % RINGS))

    def along(self, way):
        return (self.dp, self.fs + 2 * way)

    def greet(self, flips):
        barrier = pltpu.get_barrier_semaphore()

        def hail(device):
            pl.semaphore_signal(barrier, inc=1, device_id=device, device_id_type=pl.DeviceIdType.MESH)

        for flip in flips:
            hail(self.peer(flip))
        ahead, behind = self.z < LINE - 1, self.z > 0
        pl.when(ahead)(lambda: hail(self.along(1)))
        pl.when(behind)(lambda: hail(self.along(-1)))
        pl.semaphore_wait(barrier, len(flips) + ahead.astype(jnp.int32) + behind.astype(jnp.int32))

    def copy(self, src, dst, device):
        made = pltpu.make_async_remote_copy(
            src_ref=src, dst_ref=dst, send_sem=self.send_sem.at[self.count],
            recv_sem=self.recv_sem.at[self.count], device_id=device,
            device_id_type=pl.DeviceIdType.MESH,
        )
        self.count += 1
        return made

    def start(self, copy, when=None):
        only(when, copy.start)
        self.sent.append((copy, when))

    def send(self, src, dst, flip):
        copy = self.copy(src, dst, self.peer(flip))
        self.start(copy)
        return copy

    def finish(self, copy):
        copy.wait_send()
        self.sent = [(c, w) for c, w in self.sent if c is not copy]

    def close(self):
        for copy, when in self.sent:
            only(when, copy.wait_send)


def only(when, step):
    if when is None:
        step()
    else:
        pl.when(when)(step)


class Gather:
    def __init__(self, mail, packs, l, begin, cut, end):
        self.mail, self.packs, self.l = mail, packs, l
        self.early, self.late = slice(begin, cut), slice(cut, end)
        self.steps, self.across = {}, []

    def line(self, rows, both, step):
        m = self.mail
        for way in (1, -1):
            held = m.z - way * (step - 1)
            can = (held >= 0) & (m.z < LINE - 1) if way == 1 else (held <= LINE - 1) & (m.z > 0)
            at = jnp.clip(held, 0, LINE - 1)
            ref = self.packs.at[self.l, at, :, rows] if both else self.packs.at[self.l, at, m.y, rows]
            copy = m.copy(ref, ref, m.along(way))
            m.start(copy, can)
            self.steps[both, step, way] = copy

    def over(self, rows, at, when):
        m = self.mail
        ref = self.packs.at[self.l, at, m.y, rows]
        copy = m.copy(ref, ref, m.peer(1))
        m.start(copy, when)
        self.across.append((copy, when))
        return copy

    def begin(self):
        self.first = self.over(self.early, self.mail.z, None)
        self.across = []
        self.line(self.late, False, 1)
        self.over(self.late, self.mail.z, None)

    def come(self, both, step):
        m = self.mail
        out = []
        for way in (1, -1):
            source = m.z - way * step
            when = source >= 0 if way == 1 else source <= LINE - 1
            only(when, self.steps[both, step, way].wait_recv)
            out.append((jnp.clip(source, 0, LINE - 1), when))
        return out

    def step(self, step):
        held = self.come(False, step)
        if step < LINE - 1:
            self.line(self.late, False, step + 1)
        for at, when in held:
            self.over(self.late, at, when)
        if step == 1:
            self.first.wait_recv()
        else:
            self.come(True, step - 1)
        self.line(self.early, True, step)

    def end(self):
        self.come(True, LINE - 1)
        for copy, when in self.across:
            only(when, copy.wait_recv)


class Spill:
    def __init__(self, sem):
        self.sem, self.open = sem, []

    def put(self, src, dst):
        copy = pltpu.make_async_copy(src, dst, self.sem.at[len(self.open)])
        copy.start()
        self.open.append(copy)

    def close(self):
        for copy in self.open:
            copy.wait()


CORE, CHIP, BOTH = RINGS, 2 * RINGS, 3 * RINGS
FLIPS = (CORE, CHIP, BOTH, 1)
LINE = RINGS // 2


def forward_kernel(sizes, *refs):
    tokens, depth, units, feats, states, tall, small, high = sizes
    width = units + LANES
    top = tall * GROUP
    rows = top + high + small * GROUP * units // depth
    (
        x_ref, seg_ref, mask_ref, cot_ref, v_ref, r_ref, e_ref, o_ref, si_ref, so_ref,
        *short_refs, rep32, put32, rep96, put96, rep16, put16,
    ) = refs[:24]
    (
        out_ref, cross_ref, later_ref, rows_ref, filt_ref, mixn_ref, auxs,
        norm_hbm, value_hbm, gp_hbm, c_hbm, full_hbm, z_hbm, g2_hbm,
        vw_hbm, ow_hbm, ew_hbm, dout_hbm,
    ) = refs[24:42]
    (
        pieces, ein, packs, vecn, vw, ow, ew, xin, norm, douts,
        value, gp, cbuf, full, z, g2, ybuf, yin, obuf, oin, oadd, ofar, xcur,
        a_scr, age_scr, shifted, y_scr, vec_scr, lead_scr, trail_scr, send_sem, recv_sem, hbm_sem,
    ) = refs[42:]
    mail = Mail(send_sem, recv_sem)
    spill = Spill(hbm_sem)
    dp, z_at, y_at = mail.dp, mail.z, mail.y
    thirds = units // 256
    across = depth // 256

    def lanes(index, size):
        return pl.ds(pl.multiple_of(index * size, LANES), size)

    def place_expand(l, k, part):
        for t in range(thirds):
            r, c = divmod(k * thirds + t, across)
            at = top + high + small * r
            packs[l, z_at, y_at, at : at + small, c * 256 : (c + 1) * 256] = part[:, t * 256 : (t + 1) * 256]

    vec_scr[...] = jnp.zeros(vec_scr.shape, f32)
    for l in range(LAYERS):
        for r, ref in enumerate(short_refs):
            vec_scr[8 * l + r : 8 * l + r + 1, : ref.shape[1]] = ref[l : l + 1, :].astype(f32)
    for l in range(LAYERS):
        a_scr[:small, :feats] = si_ref[l].astype(f32) * so_ref[l].astype(f32)
        for k in range(GROUP):
            q = dp ^ k
            dst = packs.at[l, z_at, y_at, 0:tall] if k == 0 else pieces.at[l, k - 1, 0:tall]
            dst[:, :units] = v_ref[l, :, lanes(q, units)]
            dst[:, units:width] = r_ref[l, :, lanes(q, LANES)]
            dst[:small, width:] = a_scr[:small, lanes(q, LANES)].astype(bf16)
            dst[small:, width:] = vec_scr[...].astype(bf16)
            part = e_ref[l, :, lanes(q, units)]
            if k == 0:
                place_expand(l, 0, part)
            else:
                pieces[l, k - 1, tall:, :units] = part
                pieces[l, k - 1, tall:, units:] = jnp.zeros((small, depth - units), bf16)
        packs[l, z_at, y_at, top : top + high, :] = o_ref[l]

    mail.greet(FLIPS)

    def to_group(l, ks):
        return [
            (
                k,
                mail.send(
                    pieces.at[l, k - 1, 0:tall], packs.at[l, z_at, y_at, k * tall : (k + 1) * tall], k * RINGS
                ),
                mail.send(pieces.at[l, k - 1, tall : tall + small], ein.at[l, k - 1], k * RINGS),
            )
            for k in ks
        ]

    def from_group(l, copies):
        for k, one, two in copies:
            one.wait_recv()
            two.wait_recv()
            place_expand(l, k, ein[l, k - 1, :, :units])

    gathers = [
        [Gather(mail, packs, l, 0, 16, top), Gather(mail, packs, l, top, top + 32, rows)] for l in range(LAYERS)
    ]
    first = to_group(0, (2, 3, 1))
    xin[0] = x_ref[...]

    def line_up(ref):
        row = jnp.concatenate([ref[i : i + 1, :] for i in range(tokens // LANES)], axis=1).astype(f32)
        return jnp.broadcast_to(row, (tokens, tokens))

    ids = line_up(seg_ref)
    here = lax.broadcasted_iota(jnp.int32, (tokens, tokens), 0)
    there = lax.broadcasted_iota(jnp.int32, (tokens, tokens), 1)
    same = (ids == ids.T).astype(f32)
    age = jnp.sum(jnp.where(there < here, same, 0.0), axis=1, keepdims=True)
    rest = jnp.sum(jnp.where(there > here, same, 0.0), axis=1, keepdims=True)
    mask = line_up(mask_ref).T[:, :LANES]
    lane = lax.broadcasted_iota(jnp.int32, (tokens, LANES), 1)
    auxs[0] = jnp.where(lane == 0, age, jnp.where(lane == 1, rest, jnp.where(lane == 2, mask, 0.0))).astype(bf16)
    age_scr[...] = mask

    from_group(0, first)
    gathers[0][0].begin()
    aux_in = [mail.send(auxs.at[0], auxs.at[k], k * RINGS) for k in (1, 2, 3)]
    x_near = mail.send(x_ref, xin.at[1], CORE)
    x_far = mail.send(x_ref, xin.at[2], CHIP)
    second = to_group(1, (1,))

    def start_dout(i, carry):
        at = pl.ds(pl.multiple_of(i * STRIP, STRIP), STRIP)
        flags = jnp.broadcast_to(age_scr[at, 0:1], (STRIP, depth))
        douts[0, at, :] = (cot_ref[at, :].astype(f32) * flags).astype(bf16)
        return carry

    lax.fori_loop(0, tokens // STRIP, start_dout, 0)
    dout_near = mail.send(douts.at[0], douts.at[1], CORE)
    gathers[0][0].step(1)
    gathers[0][0].step(2)
    gathers[0][1].begin()
    x_far.wait_recv()
    x_relay = mail.send(xin.at[2], xin.at[3], CORE)
    second += to_group(1, (2, 3))
    dout_far = mail.send(douts.at[0], douts.at[2], CHIP)
    gathers[0][0].step(3)

    def open_value(l):
        for j in range(RINGS):
            for k in range(GROUP):
                index = (dp ^ k) * RINGS + j
                at = slice(k * tall, (k + 1) * tall)
                source = packs.at[l, j // 2, j % 2]
                vw[l, pl.ds(pl.multiple_of(index * tall, tall), tall), :] = source[at, :width]
                mixn_ref[l, pl.ds(pl.multiple_of(index * small, small), small), :] = source[
                    k * tall : k * tall + small, width:
                ]
                if l == 0:
                    vecn[index] = source[k * tall + small : (k + 1) * tall, width:].astype(f32)

        if l == 0:
            for each in range(LAYERS):
                open_vectors(each)
        lag = lax.broadcasted_iota(jnp.int32, (tokens, states), 0).astype(f32)
        filt_ref[l] = nn(jnp.exp(-lag * rows_ref[l, 3:4, :states]).astype(bf16), mixn_ref[l])
        half = tokens // 2
        step = lax.broadcasted_iota(jnp.int32, (half, states), 0).astype(f32)
        lead_scr[...] = jnp.exp(-(step + 1.0) * rows_ref[l, 3:4, :states]).astype(bf16)
        trail_scr[...] = jnp.exp(-(half - 1.0 - step) * rows_ref[l, 3:4, :states]).astype(bf16)

    def open_vectors(l):
        def line(r, rep, put, group=False):
            r = r + 8 * l
            short = vecn[pl.ds(dp * RINGS, RINGS), r, :] if group else vecn[:, r, :]
            return jnp.sum(nn(short.astype(bf16), rep) * put, axis=0, keepdims=True)

        rows_ref[l] = jnp.zeros(rows_ref.shape[1:], f32)
        for r in range(3):
            rows_ref[l, r : r + 1, :] = line(r, rep32[...], put32[...])
        rows_ref[l, 3:4, :states] = line(3, rep16[...], put16[...])
        rows_ref[l, 4:5, :units] = line(4, rep96[...], put96[...], True)
        rows_ref[l, 4:5, units:width] = line(5, rep16[:, :LANES], put16[:RINGS, :LANES], True)
        rows_ref[l, 5:6, :LANES] = line(6, rep16[:, :LANES], put16[:RINGS, :LANES], True)
        rows_ref[l, 6:7, :units] = line(7, rep96[...], put96[...], True)

    def open_out(l):
        for j in range(RINGS):
            source = packs.at[l, j // 2, j % 2]
            ow[l, j * high : (j + 1) * high, :] = source[top : top + high, :]
            for k in range(GROUP):
                index = (dp ^ k) * RINGS + j
                at = pl.ds(pl.multiple_of(index * small, small), small)
                for t in range(thirds):
                    r, c = divmod(k * thirds + t, across)
                    base = top + high + small * r
                    ew[l, at, t * 256 : (t + 1) * 256] = source[
                        base : base + small, c * 256 : (c + 1) * 256
                    ]

    halves = [slice(h * tokens // 2, (h + 1) * tokens // 2) for h in range(2)]

    def normalize(l, read, dst, begin=0, end=tokens // STRIP):
        def strip(i, carry):
            at = pl.ds(pl.multiple_of(i * STRIP, STRIP), STRIP)
            v = read(at)
            center = v - jnp.mean(v, axis=1, keepdims=True)
            scale = lax.rsqrt(jnp.mean(center * center, axis=1, keepdims=True) + 1e-05)
            dst[at, :] = (center * scale * rows_ref[l, 0:1, :] + rows_ref[l, 1:2, :]).astype(bf16)
            return carry

        lax.fori_loop(begin, end, strip, 0)

    def branch_in(l, j, middle):
        base = j * tokens
        a_scr[...] = nn(norm[l, j], vw[l])
        half = tokens // 2
        spot = lax.broadcasted_iota(jnp.int32, (tokens, LANES), 0)
        ages = jnp.broadcast_to(auxs[j, :, 0:1].astype(f32), (tokens, LANES))
        age_scr[...] = jnp.minimum(ages, (spot % half).astype(f32))

        def smooth(i, carry):
            here = pl.ds(pl.multiple_of(i * STRIP, STRIP), STRIP)
            there = pl.ds(pl.multiple_of(base + i * STRIP, STRIP), STRIP)
            v = a_scr[here, :] + rows_ref[l, 4:5, :width]
            cdf = 0.5 + 0.5 * lax.erf(v * 0.7071067811865476)
            slope = cdf + v * (0.3989422804014327 * jnp.exp(-0.5 * v * v))
            act = v * cdf
            value[l, there, :] = act[:, :units].astype(bf16)
            gp[l, there, :] = slope[:, :units].astype(bf16)
            mask = jnp.broadcast_to(auxs[j, here, 2:3].astype(f32), (STRIP, LANES))
            z[l, there, :] = act[:, units:] * mask
            g2[l, there, :] = slope[:, units:] * mask
            return carry

        lax.fori_loop(0, tokens // STRIP, smooth, 0)
        middle()
        signal = z[l, base : base + tokens, :]
        for b in range(8):
            shifted[b, PAD:, :] = signal if b == 0 else pltpu.roll(signal, b, 0)

        for s in range(tokens // STRIP):
            age = age_scr[s * STRIP : (s + 1) * STRIP, :]

            def lags(a, acc, s=s, age=age):
                start = pl.multiple_of(a * 8, 8)
                left = age - (a * 8).astype(f32)
                for b in range(8):
                    row = filt_ref[l, pl.ds(start + b, 1), :]
                    past = shifted[b, pl.ds(pl.multiple_of(PAD + s * STRIP - start, 8), STRIP), :]
                    acc = acc + jnp.where(left >= b, past, 0.0) * row
                return acc

            y_scr[s * STRIP : (s + 1) * STRIP, :] = lax.fori_loop(
                0, (s % (half // STRIP) + 1) * (STRIP // 8), lags, jnp.zeros((STRIP, LANES), f32)
            )
        place = lax.broadcasted_iota(jnp.int32, (half, LANES), 0).astype(f32)
        left = jnp.broadcast_to(auxs[j, :half, 1:2].astype(f32), (half, LANES))
        ages = jnp.broadcast_to(auxs[j, half:, 0:1].astype(f32), (half, LANES))
        carry = jnp.where(place + left >= half - 1.0, signal[:half, :], 0.0).astype(bf16)
        held = (tn(trail_scr[...], carry) * mixn_ref[l].astype(f32)).astype(bf16)
        y_scr[half:, :] += jnp.where(place + 1.0 <= ages, nn(lead_scr[...], held), 0.0)
        ybuf[l, j] = (y_scr[...] + rows_ref[l, 5:6, :LANES] * signal).astype(bf16)

    def branch_out(l, j):
        at = slice(j * tokens, (j + 1) * tokens)
        for k, part in ((0, ybuf[l, j]), (1, yin[l, 0, j ^ 1]), (2, yin[l, 1, j ^ 2]), (3, yin[l, 2, j ^ 3])):
            full[l, at, lanes(dp ^ k, LANES)] = part
        c = nn(full[l, at, :], ew[l]) + rows_ref[l, 6:7, :units]
        product = (c * value[l, at, :].astype(f32)).astype(bf16)
        cbuf[l, at, :] = c.astype(bf16)
        obuf[j] = nn(product, ow[l]).astype(bf16)

    for b in range(8):
        shifted[b, :PAD, :] = jnp.zeros((PAD, LANES), f32)

    def layer(l, events):
        def due():
            if events:
                events.pop(0)()

        branch_in(l, 0, due)
        due()
        branch_in(l, 1, due)
        near = [mail.send(ybuf.at[l, 0:2], yin.at[l, 0, 0:2], CORE)]
        far = [mail.send(ybuf.at[l, 0:2], yin.at[l, 1, 0:2], CHIP)]
        due()
        return near, far

    n_far = []

    def on_half(h):
        size = tokens // STRIP // 2
        normalize(1, lambda at: xcur[at, :], norm.at[1, 0], h * size, (h + 1) * size)
        n_far.append(mail.send(norm.at[1, 0, halves[h]], norm.at[1, 2, halves[h]], CHIP))

    def layer_rest(l, near, far, events, ready):
        def due():
            if events:
                events.pop(0)()

        branch_in(l, 2, due)
        due()
        branch_in(l, 3, due)
        near.append(mail.send(ybuf.at[l, 2:4], yin.at[l, 0, 2:4], CORE))
        far.append(mail.send(ybuf.at[l, 2:4], yin.at[l, 1, 2:4], CHIP))
        far[0].wait_recv()
        relay = [mail.send(yin.at[l, 1, 0:2], yin.at[l, 2, 0:2], CORE)]
        due()
        ready()
        near[1].wait_recv()
        relay[0].wait_recv()
        branch_out(l, 3)
        core_hi = mail.send(obuf.at[3], oin.at[l, 0], CORE)
        branch_out(l, 2)
        core_hi.wait_recv()
        if l == 0:
            cross = []
            for at in halves:
                oadd[at] = (obuf[2, at].astype(f32) + oin[l, 0, at].astype(f32)).astype(bf16)
                cross.append(mail.send(oadd.at[at], ofar.at[at], CHIP))
        else:
            cross_ref[...] = (obuf[2].astype(f32) + oin[l, 0].astype(f32)).astype(bf16)
        due()
        far[1].wait_recv()
        relay.append(mail.send(yin.at[l, 1, 2:4], yin.at[l, 2, 2:4], CORE))
        near[0].wait_recv()
        relay[1].wait_recv()
        branch_out(l, 1)
        core_lo = mail.send(obuf.at[1], oin.at[l, 1], CORE)
        branch_out(l, 0)
        core_lo.wait_recv()
        due()

        def strip(i, carry):
            at = pl.ds(pl.multiple_of(i * STRIP, STRIP), STRIP)
            branch = obuf[0, at, :].astype(f32) + oin[l, 1, at, :].astype(f32)
            if l == 0:
                branch = branch + ofar[at, :].astype(f32)
            mask = auxs[0, at, 2:3].astype(f32)
            before = x_ref[at, :].astype(f32) if l == 0 else xcur[at, :]
            now = before + mask * (branch + rows_ref[l, 2:3, :])
            if l == 0:
                xcur[at, :] = now
                later_ref[at, :] = now
            else:
                out_ref[at, :] = now
            return carry

        for h in range(2):
            if l == 0:
                cross[h].wait_recv()
            lax.fori_loop(h * tokens // STRIP // 2, (h + 1) * tokens // STRIP // 2, strip, 0)
            if l == 0:
                on_half(h)
        mail.finish(core_hi)
        mail.finish(core_lo)
        for buf, hbm in ((cbuf, c_hbm), (full, full_hbm)):
            spill.put(buf.at[l], hbm.at[l])

    def spill_in(l):
        for buf, hbm in ((norm, norm_hbm), (value, value_hbm), (gp, gp_hbm), (z, z_hbm), (g2, g2_hbm)):
            spill.put(buf.at[l], hbm.at[l])

    def then(*steps):
        def event():
            for step in steps:
                step()

        return event

    nothing = then()

    gathers[0][0].end()
    open_value(0)
    spill.put(vw.at[0], vw_hbm.at[0])
    for copy in aux_in:
        copy.wait_recv()
    x_near.wait_recv()
    for j in (0, 1):
        normalize(0, lambda at, j=j: xin[j, at, :].astype(f32), norm.at[0, j])
    gathers[0][1].step(1)

    more = {}

    def next_value():
        from_group(1, second)
        gathers[1][0].begin()

    def relay_dout():
        dout_far.wait_recv()
        more["dout"] = mail.send(douts.at[2], douts.at[3], CORE)

    near, far = layer(
        0, [nothing, lambda: gathers[0][1].step(2), next_value, lambda: gathers[0][1].step(3)]
    )
    x_relay.wait_recv()
    for j in (2, 3):
        normalize(0, lambda at, j=j: xin[j, at, :].astype(f32), norm.at[0, j])

    def ready_out(l):
        def event():
            gathers[l][1].end()
            open_out(l)
            spill.put(ow.at[l], ow_hbm.at[l])
            spill.put(ew.at[l], ew_hbm.at[l])
            spill_in(l)

        return event

    events = [
        relay_dout,
        lambda: gathers[1][0].step(1),
        nothing,
        lambda: gathers[1][0].step(2),
        then(lambda: gathers[1][1].begin(), lambda: gathers[1][0].step(3)),
        lambda: gathers[1][1].step(1),
    ]
    layer_rest(0, near, far, events, ready_out(0))

    n_near = mail.send(norm.at[1, 0], norm.at[1, 1], CORE)
    gathers[1][0].end()
    open_value(1)
    spill.put(vw.at[1], vw_hbm.at[1])
    def relay_norm():
        more["relay"] = []
        for at, copy in zip(halves, n_far):
            copy.wait_recv()
            more["relay"].append(mail.send(norm.at[1, 2, at], norm.at[1, 3, at], CORE))

    n_near.wait_recv()
    near, far = layer(
        1, [lambda: gathers[1][1].step(2), nothing, relay_norm, lambda: gathers[1][1].step(3)]
    )
    for copy in more["relay"]:
        copy.wait_recv()
    dout_near.wait_recv()
    more["dout"].wait_recv()
    spill.put(douts, dout_hbm)
    layer_rest(1, near, far, [nothing] * 6, ready_out(1))
    mail.close()
    spill.close()


def forward_both(arrays, sizes):
    tokens, depth, units, feats, states, tall, small, high = sizes
    width = units + LANES
    group = tokens * GROUP
    rows = tall * GROUP + high + small * GROUP * units // depth
    shape = jax.ShapeDtypeStruct
    two = lambda *dims: (LAYERS,) + dims
    spilled = [
        (two(GROUP, tokens, depth), bf16), (two(group, units), bf16), (two(group, units), bf16),
        (two(group, units), bf16), (two(group, feats), bf16),
        (two(group, LANES), f32), (two(group, LANES), f32),
        (two(depth, width), bf16), (two(units, depth), bf16), (two(feats, units), bf16),
        ((GROUP, tokens, depth), bf16),
    ]
    kept = [
        ((tokens, depth), f32), ((tokens, depth), bf16), ((tokens, depth), f32), (two(8, depth), f32),
        (two(tokens, LANES), f32),
        (two(states, LANES), bf16), ((GROUP, tokens, LANES), bf16),
    ]
    sems = 160
    return pl.pallas_call(
        partial(forward_kernel, sizes),
        out_shape=[shape(*s) for s in kept + spilled],
        in_specs=[pl.BlockSpec(memory_space=VMEM)] * len(arrays),
        out_specs=[pl.BlockSpec(memory_space=VMEM)] * len(kept)
        + [pl.BlockSpec(memory_space=pl.ANY)] * len(spilled),
        scratch_shapes=[
            VMEM(two(GROUP - 1, tall + small, depth), bf16),
            VMEM(two(GROUP - 1, small, depth), bf16),
            VMEM(two(LINE, 2, rows, depth), bf16),
            VMEM((GROUP * RINGS, tall - small, LANES), f32),
            VMEM(two(depth, width), bf16),
            VMEM(two(units, depth), bf16),
            VMEM(two(feats, units), bf16),
            VMEM((GROUP, tokens, depth), bf16),
            VMEM(two(GROUP, tokens, depth), bf16),
            VMEM((GROUP, tokens, depth), bf16),
            VMEM(two(group, units), bf16),
            VMEM(two(group, units), bf16),
            VMEM(two(group, units), bf16),
            VMEM(two(group, feats), bf16),
            VMEM(two(group, LANES), f32),
            VMEM(two(group, LANES), f32),
            VMEM(two(GROUP, tokens, LANES), bf16),
            VMEM(two(GROUP - 1, GROUP, tokens, LANES), bf16),
            VMEM((GROUP, tokens, depth), bf16),
            VMEM(two(2, tokens, depth), bf16),
            VMEM((tokens, depth), bf16),
            VMEM((tokens, depth), bf16),
            VMEM((tokens, depth), f32),
            VMEM((tokens, width), f32),
            VMEM((tokens, LANES), f32),
            VMEM((8, PAD + tokens, LANES), f32),
            VMEM((tokens, LANES), f32),
            VMEM((tall - small, LANES), f32),
            VMEM((tokens // 2, states), bf16),
            VMEM((tokens // 2, states), bf16),
            pltpu.SemaphoreType.DMA((sems,)),
            pltpu.SemaphoreType.DMA((sems,)),
            pltpu.SemaphoreType.DMA((32,)),
        ],
        compiler_params=pltpu.CompilerParams(
            vmem_limit_bytes=60 << 20, collective_id=1, has_side_effects=True
        ),
        cost_estimate=cost(120.0),
        name="forward_both",
    )(*arrays)


class Fetch:
    def __init__(self, sem):
        self.sem, self.count = sem, 0

    def get(self, src, dst):
        copy = pltpu.make_async_copy(src, dst, self.sem.at[self.count])
        self.count += 1
        copy.start()
        return copy


class Reduce:
    def __init__(self, mail, packs, ysum, zin, zother, l, begin, cut, end, lanes, spot):
        self.mail, self.packs, self.ysum, self.zin, self.zother = mail, packs, ysum, zin, zother
        self.l, self.early, self.late, self.lanes = l, slice(begin, cut), slice(cut, end), lanes
        self.has_early = cut > begin
        self.other = slice(spot, spot + cut - begin)
        self.over, self.steps = [], {}
        z = mail.z
        low = z < LINE // 2
        self.order = [
            jnp.where(low, 3, 0), jnp.where(low, 2, 1), jnp.where(low, 1 - z, 5 - z), z,
        ]

    def at(self, z, y, rows):
        return self.packs.at[self.l, z, y, rows, self.lanes]

    def add(self, z, y, rows, more):
        ref = self.at(z, y, rows)
        ref[...] = (ref[...].astype(f32) + more[...].astype(f32)).astype(bf16)

    def slots(self, step, early):
        out = []
        m = self.mail
        rows = self.early if early else self.late
        for side, way in enumerate((1, -1)):
            held = 4 + m.z - step if way == 1 else m.z - 4 + step
            if way == 1:
                can = (m.z + 1 <= step) & (m.z < LINE - 1)
            else:
                can = (LINE - m.z <= step) & (m.z > 0)
            at = jnp.clip(held, 0, LINE - 1)
            out.append((way, side, can, at, m.y, rows, self.zin.at[self.l, step - 1, side, rows, self.lanes], 0))
            if early:
                spot = self.zother.at[self.l, step - 1, side, self.other, self.lanes]
                out.append((way, side, can, at, 1 - m.y, rows, spot, 1))
        return out

    def pass_on(self, step, early):
        for way, side, can, at, y, rows, spot, which in self.slots(step, early):
            copy = self.mail.copy(self.at(at, y, rows), spot, self.mail.along(way))
            self.mail.start(copy, can)
            self.steps[early, step, side, which] = copy

    def take(self, step, early):
        z = self.mail.z
        for way, side, can, at, y, rows, spot, which in self.slots(step, early):
            copy = self.steps[early, step, side, which]
            if way == 1:
                when, mine = (z >= 1) & (step >= z), 3 + z - step
            else:
                when, mine = (z <= LINE - 2) & (step >= LINE - 1 - z), z - 3 + step

            def arrive(copy=copy, mine=mine, y=y, rows=rows, spot=spot):
                copy.wait_recv()
                self.add(jnp.clip(mine, 0, LINE - 1), y, rows, spot)

            only(when, arrive)

    def begin(self):
        m = self.mail
        if self.has_early:
            self.pass_on(1, True)
        for i, z in enumerate(self.order):
            copy = m.copy(
                self.at(z, 1 - m.y, self.late), self.ysum.at[self.l, i, self.late, self.lanes], m.peer(1)
            )
            m.start(copy)
            self.over.append(copy)

    def step(self, i):
        m = self.mail
        if i < LINE:
            self.over[i].wait_recv()
            self.add(self.order[i], m.y, self.late, self.ysum.at[self.l, i, self.late, self.lanes])
            if i:
                self.take(i, False)
            if i < LINE - 1:
                self.pass_on(i + 1, False)
            if self.has_early and i:
                self.take(i, True)
                if i < LINE - 1:
                    self.pass_on(i + 1, True)
                else:
                    self.last = m.copy(
                        self.at(m.z, 1 - m.y, self.early), self.ysum.at[self.l, 0, self.early, self.lanes], m.peer(1)
                    )
                    m.start(self.last)
        elif self.has_early:
            self.last.wait_recv()
            self.add(m.z, m.y, self.early, self.ysum.at[self.l, 0, self.early, self.lanes])


class Direct:
    def __init__(self, mail, packs, ysum, zin, l, begin, end, lanes):
        self.mail, self.packs, self.ysum, self.zin, self.l = mail, packs, ysum, zin, l
        self.rows, self.lanes = slice(begin, end), lanes
        self.order = (1, 2, 3, 0)
        self.over, self.came = [], []

    def at(self, far, y):
        return self.packs.at[self.l, self.mail.z ^ far, y, self.rows, self.lanes]

    def begin(self):
        m = self.mail
        for far in self.order:
            dst = self.ysum.at[self.l, far, self.rows, self.lanes]
            copy = m.copy(self.at(far, 1 - m.y), dst, m.peer(1))
            m.start(copy)
            self.over.append(copy)

    def step(self, i):
        m = self.mail
        if i < LINE:
            far = self.order[i]
            self.over[i].wait_recv()
            ref = self.at(far, m.y)
            more = self.ysum[self.l, far, self.rows, self.lanes]
            ref[...] = (ref[...].astype(f32) + more.astype(f32)).astype(bf16)
            if far:
                copy = m.copy(ref, self.zin.at[self.l, far - 1, 0, self.rows, self.lanes], m.peer(2 * far))
                m.start(copy)
                self.came.append(copy)
        else:
            for copy in self.came:
                copy.wait_recv()
            ref = self.at(0, m.y)
            total = ref[...].astype(f32)
            for far in range(1, LINE):
                total = total + self.zin[self.l, far - 1, 0, self.rows, self.lanes].astype(f32)
            ref[...] = total.astype(bf16)


def backward_kernel(sizes, *refs):
    tokens, depth, units, feats, states, tall, small, high = sizes
    width = units + LANES
    top = tall * GROUP
    rows = top + high + small * GROUP * units // depth
    devices = GROUP * RINGS
    (
        cot_ref, x_ref, later_ref, rows_ref, filt_ref, mixn_ref, auxs, oadd_ref,
        norm_hbm, value_hbm, gp_hbm, c_hbm, full_hbm, z_hbm, g2_hbm, vw_hbm, ow_hbm, ew_hbm, dout_hbm,
    ) = refs[:19]
    dx_ref, vmine_ref, vtotal_ref, o_ref, raw_hbm, ofar_hbm = refs[19:25]
    (
        norm, value, gp, cbuf, full, z, g2, vw, ow, ew, dout, dcb, da,
        qe, qo, near, cross, far, ofar, dnbuf, din, dadd, dfar,
        packs, ysum, zin, zother, gsend, grecv, vsend, vin, vgrp,
        rem_scr, shifted, dz_scr, corr, y_scr, w_scr, o_scr, m_scr,
        send_sem, recv_sem, hbm_sem,
    ) = refs[25:]
    mail = Mail(send_sem, recv_sem)
    fetch = Fetch(hbm_sem)
    dp, z_at, y_at = mail.dp, mail.z, mail.y
    thirds = units // 256
    across = depth // 256
    strips = tokens // STRIP

    def lanes(at, size):
        return pl.ds(pl.multiple_of(at * size, LANES), size)

    def block(j):
        return pl.ds(pl.multiple_of(j * tokens, tokens), tokens)

    def load_out(l):
        return [
            fetch.get(ow_hbm.at[l], ow), fetch.get(ew_hbm.at[l], ew), fetch.get(value_hbm.at[l], value),
            fetch.get(gp_hbm.at[l], gp), fetch.get(c_hbm.at[l], cbuf), fetch.get(full_hbm.at[l], full),
        ]

    def load_in(l):
        return [
            fetch.get(z_hbm.at[l], z), fetch.get(g2_hbm.at[l], g2), fetch.get(vw_hbm.at[l], vw),
            fetch.get(norm_hbm.at[l], norm),
        ]

    first = fetch.get(dout_hbm, dout)
    loads = load_out(LAYERS - 1)
    more_loads = load_in(LAYERS - 1)
    vsend[...] = jnp.zeros(vsend.shape, f32)
    for b in range(8):
        shifted[b, tokens:, :] = jnp.zeros((PAD, LANES), f32)

    def start_dx(i, carry):
        at = pl.ds(pl.multiple_of(i * STRIP, STRIP), STRIP)
        up = cot_ref[at, :].astype(f32)
        dx_ref[at, :] = up
        low = (up * auxs[0, at, 2:3].astype(f32)).astype(bf16).astype(f32)
        return carry + jnp.sum(low, axis=0, keepdims=True)

    vsend[LAYERS - 1, 2:3, :] = lax.fori_loop(0, strips, start_dx, jnp.zeros((1, depth), f32))

    mail.greet((CORE, CHIP, BOTH, 1, 2, 3, 4, 5, 6, 7))

    def back_out(l, j):
        at = block(j)
        dgated = nt(dout[at, :], ow[...])
        val = value[at, :].astype(f32)
        gate = cbuf[at, :].astype(f32)
        dc = (dgated * val).astype(bf16)
        dcb[at, :] = dc
        da[at, :units] = (dgated * gate * gp[at, :].astype(f32)).astype(bf16)

        def keep():
            cbuf[at, :] = (gate * val).astype(bf16)

        pl.when(j < 2)(keep)
        vsend[l, 5:6, :units] += jnp.sum(dc.astype(f32), axis=0, keepdims=True)
        y_scr[...] = nt(dc, ew[...])
        for k in range(GROUP):
            part = y_scr[:, lanes(dp ^ k, LANES)].astype(bf16)
            if k % 2:
                qo[k // 2, j ^ 1] = part
            else:
                qe[k // 2, j] = part

    def back_in(l, j, middle):
        at = block(j)
        rem_scr[...] = jnp.broadcast_to(auxs[j, :, 1:2].astype(f32), (tokens, LANES))
        dy = qe[0, j].astype(f32) + near[0, j].astype(f32) + far[j].astype(f32)
        for b in range(8):
            shifted[b, :tokens, :] = dy if b == 0 else pltpu.roll(dy, tokens - b, 0)
        for s in range(strips):
            rem = rem_scr[s * STRIP : (s + 1) * STRIP, :]
            past = z[pl.ds(pl.multiple_of(j * tokens + s * STRIP, STRIP), STRIP), :]

            def lags(a, acc, s=s, rem=rem, past=past):
                base = pl.multiple_of(a * 8, 8)
                left = rem - (a * 8).astype(f32)
                for b in range(8):
                    row = filt_ref[l, pl.ds(base + b, 1), :]
                    later = shifted[b, pl.ds(pl.multiple_of(s * STRIP + base, 8), STRIP), :]
                    later = jnp.where(left >= b, later, 0.0)
                    acc = acc + later * row
                    pair = later * past
                    corr[pl.ds(pl.multiple_of(base * 8 + b * 8, 8), 8), :] += (pair[0:8] + pair[8:16]) + (
                        pair[16:24] + pair[24:32]
                    )
                return acc

            dz_scr[s * STRIP : (s + 1) * STRIP, :] = lax.fori_loop(
                0, (strips - s) * (STRIP // 8), lags, jnp.zeros((STRIP, LANES), f32)
            )
            if s == 2:
                middle()
        da2 = (dz_scr[...] + rows_ref[l, 5:6, :LANES] * dy) * g2[at, :]
        da[at, units:] = da2.astype(bf16)
        vsend[l, 5:6, units:width] += jnp.sum(z[at, :] * dy, axis=0, keepdims=True)
        vsend[l, 4:5, :width] += jnp.sum(da[at, :].astype(f32), axis=0, keepdims=True)
        dnbuf[j] = nt(da[at, :], vw[...]).astype(bf16)

    def grads_proj(l):
        half, wide = 2 * tokens, high * GROUP
        for j in (2, 3):
            at = slice(j * tokens, (j + 1) * tokens)
            dcb[at, :] = (cbuf[at, :].astype(f32) * value[at, :].astype(f32)).astype(bf16)
        for i in range(RINGS // GROUP):
            lane = slice(i * wide, (i + 1) * wide)
            o_scr[...] = (tn(cbuf[:half, lane], dout[:half, :]) + tn(dcb[half:, lane], dout[half:, :])).astype(bf16)
            for g in range(GROUP):
                at = i * GROUP + g
                packs[l, at // 2, at % 2, top : top + high, :] = o_scr[g * high : (g + 1) * high, :]
        sums[l]["proj"].begin()

    def grads_expand(l):
        for t in range(thirds):
            w_scr[: 2 * tokens, :256] = tn(full[...], dcb[:, t * 256 : (t + 1) * 256]).astype(bf16)
            for j in range(RINGS):
                for k in range(GROUP):
                    r, c = divmod(k * thirds + t, across)
                    owner = (dp ^ k) * RINGS + j
                    base = top + high + small * r
                    packs[l, j // 2, j % 2, base : base + small, c * 256 : (c + 1) * 256] = w_scr[
                        pl.ds(pl.multiple_of(owner * small, small), small), :256
                    ]
        sums[l]["expand"].begin()

    def grads_in_of(l, lane):
        wide = depth // GROUP
        size = lane.stop - lane.start
        for d in range(GROUP):
            w_scr[:wide, :size] = tn(norm[:, d * wide : (d + 1) * wide], da[:, lane]).astype(bf16)
            at = pl.ds(pl.multiple_of((dp ^ d) * tall, tall), tall)
            for j in range(RINGS):
                packs[l, j // 2, j % 2, at, lane] = w_scr[j * tall : (j + 1) * tall, :size]

    def mixing_of(l):
        lag = lax.broadcasted_iota(jnp.int32, (tokens, tokens * 8), 0)
        part = lax.broadcasted_iota(jnp.int32, (tokens, tokens * 8), 1) // 8
        total = nn((lag == part).astype(bf16), corr[...].astype(bf16))
        steps = lax.broadcasted_iota(jnp.int32, (tokens, states), 0).astype(f32)
        powers = jnp.exp(-steps * rows_ref[l, 3:4, :states]).astype(bf16)
        m_scr[...] = tn(powers, total.astype(bf16)).astype(bf16)
        for j in range(RINGS):
            for k in range(GROUP):
                owner = (dp ^ k) * RINGS + j
                side = packs.at[l, j // 2, j % 2, k * tall : (k + 1) * tall]
                side[:small, width:] = m_scr[pl.ds(pl.multiple_of(owner * small, small), small), :]
                side[small:, width:] = jnp.zeros((tall - small, LANES), bf16)
        steps = lax.broadcasted_iota(jnp.int32, (tokens, LANES), 0).astype(f32)
        terms = tn(powers, (total * steps).astype(bf16)) * mixn_ref[l].astype(f32)
        vsend[l, 3:4, :states] = -lax.dot_general(
            jnp.ones((8, LANES), f32), terms, cols_dims, precision=highest, preferred_element_type=f32
        )[0:1]

    state = {}
    bufs = (mail, packs, ysum, zin, zother)
    sums = [
        {
            "proj": Reduce(*bufs, l, top, top + 16, top + high, slice(0, depth), 16),
            "expand": Reduce(*bufs, l, top + high, top + high + 16, rows, slice(0, depth), 32),
            "value": Reduce(*bufs, l, 0, 16, top, slice(0, units), 0),
            "rest": Direct(*bufs[:4], l, 0, top, slice(units, depth)),
        }
        for l in range(LAYERS)
    ]

    def own(l, at, lane=slice(None)):
        return packs[l, z_at, y_at, at, lane]

    def group_proj(l):
        sums[l]["proj"].step(4)
        o_ref[l] = own(l, slice(top, top + high))

    def group_out(l):
        sums[l]["expand"].step(4)
        for k in range(GROUP):
            dst = grecv.at[l, 0, tall : tall + small] if k == 0 else gsend.at[l, k - 1]
            for t in range(thirds):
                r, c = divmod(k * thirds + t, across)
                base = top + high + small * r
                dst[:, t * 256 : (t + 1) * 256] = own(l, slice(base, base + small), slice(c * 256, (c + 1) * 256))
            dst[:, units:] = jnp.zeros((small, depth - units), bf16)
            if k:
                state[l, "out", k] = mail.send(
                    gsend.at[l, k - 1], grecv.at[l, k, tall : tall + small], k * RINGS
                )

    def group_in(l, name):
        sums[l][name].step(4)
        lane = sums[l][name].lanes
        for k in (2, 3, 1):
            state[l, name, k] = mail.send(
                packs.at[l, z_at, y_at, k * tall : (k + 1) * tall, lane], grecv.at[l, k, 0:tall, lane], k * RINGS
            )
        grecv[l, 0, :tall, lane] = own(l, slice(0, tall), lane)

    def group_last(l):
        for name in ("out", "value", "rest"):
            for k in range(1, GROUP):
                state[l, name, k].wait_recv()
        state[l, "raw"] = fetch.get(grecv.at[l], raw_hbm.at[l])

    def vector_rest(l):
        state[l, "vr"] = [mail.send(vsend.at[l], vin.at[l, j - 1], j) for j in range(1, RINGS)]

    def vector_group(l):
        for copy in state[l, "vr"]:
            copy.wait_recv()
        total = vsend[l]
        for j in range(RINGS - 1):
            total = total + vin[l, j]
        vmine_ref[l] = total
        vgrp[l, 0] = total
        state[l, "vg"] = [mail.send(vgrp.at[l, 0], vgrp.at[l, k], k * RINGS) for k in range(1, GROUP)]

    def vector_last(l):
        for copy in state[l, "vg"]:
            copy.wait_recv()
        total = vgrp[l, 0]
        for k in range(1, GROUP):
            total = total + vgrp[l, k]
        vtotal_ref[l] = total

    def pair(fn, lo):
        def body(i, carry):
            fn(lo + i)
            return carry

        lax.fori_loop(0, 2, body, 0)

    def exchange_dy(half):
        return mail.send(qo.at[:, half], near.at[:, half], CORE)

    def cross_dy(half, other, copy):
        copy.wait_recv()
        cross[half] = (qe[1, half].astype(f32) + near[1, half].astype(f32)).astype(bf16)
        return mail.send(cross.at[half], far.at[other], CHIP)

    lo, hi = slice(0, 2), slice(2, 4)
    halves = [slice(h * tokens // 2, (h + 1) * tokens // 2) for h in range(2)]

    def grads_value(l):
        grads_in_of(l, slice(0, units))
        sums[l]["value"].begin()

    def grads_rest(l):
        grads_in_of(l, slice(units, width))
        mixing_of(l)
        sums[l]["rest"].begin()

    def layer(l, loads, more_loads, events, wait_far):
        def due():
            if events:
                events.pop(0)()

        for copy in loads:
            copy.wait()
        corr[...] = jnp.zeros(corr.shape, f32)
        pair(lambda j: back_out(l, j), 0)
        near_lo = exchange_dy(lo)
        wait_far()
        grads_proj(l)
        pair(lambda j: back_out(l, j), 2)
        near_hi = exchange_dy(hi)
        cross_lo = cross_dy(lo, hi, near_lo)
        cross_hi = cross_dy(hi, lo, near_hi)
        if l:
            state["o"] = mail.send(oadd_ref, ofar, CHIP)
        due()
        grads_expand(l)
        next_loads = load_out(l - 1) if l else []
        for copy in more_loads:
            copy.wait()
        due()
        grads_value(l)
        due()
        cross_lo.wait_recv()
        back_in(l, 3, due)
        core_hi = mail.send(dnbuf.at[3], din.at[0], CORE)
        due()
        back_in(l, 2, due)
        core_hi.wait_recv()
        chip = []
        for at in halves:
            dadd[at] = (dnbuf[2, at].astype(f32) + din[0, at].astype(f32)).astype(bf16)
            chip.append(mail.send(dadd.at[at], dfar.at[at], CHIP))
        due()
        cross_hi.wait_recv()
        back_in(l, 1, due)
        core_lo = mail.send(dnbuf.at[1], din.at[1], CORE)
        due()
        back_in(l, 0, due)
        due()
        if l == 0:
            grads_rest(l)
        due()
        core_lo.wait_recv()

        def strip(i, carry):
            gain_sum, shift_sum, out_sum = carry
            at = pl.ds(pl.multiple_of(i * STRIP, STRIP), STRIP)
            v = later_ref[at, :] if l else x_ref[at, :].astype(f32)
            center = v - jnp.mean(v, axis=1, keepdims=True)
            scale = lax.rsqrt(jnp.mean(center * center, axis=1, keepdims=True) + 1e-05)
            normed = center * scale
            grad = dnbuf[0, at, :].astype(f32) + din[1, at, :].astype(f32) + dfar[at, :].astype(f32)
            q = grad * rows_ref[l, 0:1, :]
            tilt = q - jnp.mean(q, axis=1, keepdims=True) - normed * jnp.mean(q * normed, axis=1, keepdims=True)
            up = dx_ref[at, :] + tilt * scale
            dx_ref[at, :] = up
            if l:
                low = (up * auxs[0, at, 2:3].astype(f32)).astype(bf16)
                dout[at, :] = low
                out_sum = out_sum + jnp.sum(low.astype(f32), axis=0, keepdims=True)
            return (
                gain_sum + jnp.sum(grad * normed, axis=0, keepdims=True),
                shift_sum + jnp.sum(grad, axis=0, keepdims=True),
                out_sum,
            )

        zero = jnp.zeros((1, depth), f32)
        sums_now = (zero, zero, zero)
        for h, at in enumerate(halves):
            chip[h].wait_recv()
            sums_now = lax.fori_loop(h * strips // 2, (h + 1) * strips // 2, strip, sums_now)
            if l:
                state["dout", h] = mail.send(dout.at[at], dout.at[slice(2 * tokens + at.start, 2 * tokens + at.stop)], CHIP)
        gain_sum, shift_sum, out_sum = sums_now
        vsend[l, 0:1, :] = gain_sum
        vsend[l, 1:2, :] = shift_sum
        if l:
            vsend[l - 1, 2:3, :] = out_sum
        for copy in (near_lo, near_hi, cross_lo, cross_hi, core_hi, core_lo, *chip):
            mail.finish(copy)
        return next_loads

    first.wait()

    def then(*steps):
        def event():
            for step in steps:
                step()

        return event

    nothing = then()

    def step(l, name, i):
        return lambda: sums[l][name].step(i)

    def steps(l, name, *which):
        return then(*(step(l, name, i) for i in which))

    events = [
        then(),
        then(),
        then(step(1, "proj", 0)),
        then(),
        then(step(1, "proj", 1)),
        then(),
        then(step(1, "proj", 2), step(1, "expand", 0)),
        then(),
        then(step(1, "proj", 3), step(1, "expand", 1)),
        then(),
        then(step(1, "expand", 2), step(1, "value", 0)),
        then(lambda: group_proj(1), step(1, "expand", 3)),
    ]
    loads = layer(1, loads, more_loads, events, nothing)

    dout_core = mail.send(dout.at[pl.ds(0, tokens)], dout.at[pl.ds(tokens, tokens)], CORE)
    grads_rest(1)
    more_loads = load_in(0)
    vector_rest(1)
    state["o"].wait_recv()
    far_out = fetch.get(ofar, ofar_hbm)

    step(1, "value", 1)()

    def dout_far():
        group_out(1)
        step(1, "value", 2)()
        relays = []
        for h, at in enumerate(halves):
            state["dout", h].wait_recv()
            src = dout.at[slice(2 * tokens + at.start, 2 * tokens + at.stop)]
            relays.append(mail.send(src, dout.at[slice(3 * tokens + at.start, 3 * tokens + at.stop)], CORE))
        step(1, "value", 3)()
        step(1, "rest", 0)()
        for relay in relays:
            relay.wait_recv()

    events = [
        then(step(1, "rest", 1)),
        then(step(0, "proj", 0)),
        then(lambda: group_in(1, "value"), step(1, "rest", 2)),
        then(step(0, "proj", 1)),
        then(lambda: vector_group(1), step(1, "rest", 3)),
        then(step(0, "proj", 2), step(0, "expand", 0)),
        then(lambda: group_in(1, "rest")),
        then(step(0, "proj", 3), step(0, "expand", 1)),
        then(step(0, "value", 0)),
        then(step(0, "expand", 2), lambda: group_proj(0), step(0, "value", 1)),
        then(lambda: vector_last(1)),
        then(step(0, "expand", 3), step(0, "value", 2), lambda: group_last(1)),
    ]
    dout_core.wait_recv()
    layer(0, loads, more_loads, events, dout_far)
    step(0, "value", 3)()
    vector_rest(0)
    step(0, "rest", 0)()
    group_out(0)
    group_in(0, "value")
    step(0, "rest", 1)()
    vector_group(0)
    steps(0, "rest", 2, 3)()
    group_in(0, "rest")
    vector_last(0)
    group_last(0)
    mail.close()
    far_out.wait()
    for l in range(LAYERS):
        state[l, "raw"].wait()


def backward_both(arrays, sizes):
    tokens, depth, units, feats, states, tall, small, high = sizes
    width = units + LANES
    group = tokens * GROUP
    rows = tall * GROUP + high + small * GROUP * units // depth
    shape = jax.ShapeDtypeStruct
    two = lambda *dims: (LAYERS,) + dims
    outs = [
        ((tokens, depth), f32), (two(8, depth), f32), (two(8, depth), f32), (two(high, depth), bf16),
        (two(GROUP, tall + small, depth), bf16), ((tokens, depth), bf16),
    ]
    return pl.pallas_call(
        partial(backward_kernel, sizes),
        out_shape=[shape(*s) for s in outs],
        in_specs=[pl.BlockSpec(memory_space=VMEM)] * 8 + [pl.BlockSpec(memory_space=pl.ANY)] * 11,
        out_specs=[pl.BlockSpec(memory_space=VMEM)] * 4 + [pl.BlockSpec(memory_space=pl.ANY)] * 2,
        scratch_shapes=[
            VMEM((group, depth), bf16),
            VMEM((group, units), bf16),
            VMEM((group, units), bf16),
            VMEM((group, units), bf16),
            VMEM((group, feats), bf16),
            VMEM((group, LANES), f32),
            VMEM((group, LANES), f32),
            VMEM((depth, width), bf16),
            VMEM((units, depth), bf16),
            VMEM((feats, units), bf16),
            VMEM((group, depth), bf16),
            VMEM((group, units), bf16),
            VMEM((group, width), bf16),
            VMEM((2, GROUP, tokens, LANES), bf16),
            VMEM((2, GROUP, tokens, LANES), bf16),
            VMEM((2, GROUP, tokens, LANES), bf16),
            VMEM((GROUP, tokens, LANES), bf16),
            VMEM((GROUP, tokens, LANES), bf16),
            VMEM((tokens, depth), bf16),
            VMEM((GROUP, tokens, depth), bf16),
            VMEM((2, tokens, depth), bf16),
            VMEM((tokens, depth), bf16),
            VMEM((tokens, depth), bf16),
            VMEM(two(LINE, 2, rows, depth), bf16),
            VMEM(two(LINE, rows, depth), bf16),
            VMEM(two(LINE - 1, 2, rows, depth), bf16),
            VMEM(two(LINE - 1, 2, 48, depth), bf16),
            VMEM(two(GROUP - 1, small, depth), bf16),
            VMEM(two(GROUP, tall + small, depth), bf16),
            VMEM(two(8, depth), f32),
            VMEM(two(RINGS - 1, 8, depth), f32),
            VMEM(two(GROUP, 8, depth), f32),
            VMEM((tokens, LANES), f32),
            VMEM((8, PAD + tokens, LANES), f32),
            VMEM((tokens, LANES), f32),
            VMEM((tokens * 8, LANES), f32),
            VMEM((tokens, feats), f32),
            VMEM((2 * tokens, width), bf16),
            VMEM((high * GROUP, depth), bf16),
            VMEM((states, LANES), bf16),
            pltpu.SemaphoreType.DMA((220,)),
            pltpu.SemaphoreType.DMA((220,)),
            pltpu.SemaphoreType.DMA((26,)),
        ],
        compiler_params=pltpu.CompilerParams(
            vmem_limit_bytes=60 << 20, collective_id=2, has_side_effects=True
        ),
        cost_estimate=cost(140.0),
        name="backward_both",
    )(*arrays)


def finish(me, arrays, sizes):
    tokens, depth, units, feats, states, tall, small, high = sizes
    width = units + LANES
    devices = GROUP * RINGS
    hidden = units * GROUP

    def kernel(me_ref, *refs):
        hbm = refs[: len(arrays)]
        (
            last_ref, dx_ref, gain_ref, shift_ref, v_ref, vb_ref, r_ref, rb_ref, dec_ref, si_out, so_out,
            skip_ref, e_ref, eb_ref, o_ref, ob_ref,
        ) = refs[len(arrays) : len(arrays) + 16]
        here, sem = refs[len(arrays) + 16 : -1], refs[-1]
        to = (*here, dx_ref)
        copies = [pltpu.make_async_copy(a, b, sem.at[i]) for i, (a, b) in enumerate(zip(hbm, to))]
        for copy in copies:
            copy.start()
        raw, out_part, mine_ref, total_ref, last_in, far_in, aux_ref, si_ref, so_ref = here
        for copy in copies[:-1]:
            copy.wait()
        dp, fs = me_ref[0], me_ref[1]
        index = dp * RINGS + fs

        def lanes(at, size):
            return pl.ds(pl.multiple_of(at * size, LANES), size)

        flags = aux_ref[0, :, 2:3].astype(f32)
        last_ref[...] = (last_in[...] + flags * far_in[...].astype(f32)).astype(bf16)
        o_ref[...] = out_part[...].astype(f32)
        apart = lax.broadcasted_iota(jnp.int32, (depth, LANES), 0) - lax.broadcasted_iota(
            jnp.int32, (depth, LANES), 1
        )
        both = jnp.concatenate([total_ref[0], total_ref[1], mine_ref[0], mine_ref[1]], axis=0)
        high_part = both.astype(bf16)
        low_part = (both - high_part.astype(f32)).astype(bf16)

        def pick(start):
            chosen = (apart == start).astype(bf16)
            return nn(high_part, chosen) + nn(low_part, chosen)

        short, mid = states // devices, units // RINGS
        long_all, short_all = pick(index * (depth // devices)), pick(index * short)
        mid_all, rest_all = pick(fs * mid), pick(units + fs * short)
        for l in range(LAYERS):
            for k in range(GROUP):
                q = dp ^ k
                v_ref[l, :, lanes(q, units)] = raw[l, k, :tall, :units].astype(f32)
                r_ref[l, :, lanes(q, LANES)] = raw[l, k, :tall, units:width].astype(f32)
                e_ref[l, :, lanes(q, units)] = raw[l, k, tall:, :units].astype(f32)
                part = raw[l, k, :small, width:].astype(f32)
                si_out[l, :, lanes(q, LANES)] = part * so_ref[l, :, lanes(q, LANES)].astype(f32)
                so_out[l, :, lanes(q, LANES)] = part * si_ref[l, :, lanes(q, LANES)].astype(f32)

            for r, ref in enumerate((gain_ref, shift_ref, ob_ref)):
                ref[l : l + 1, :] = long_all[8 * l + r : 8 * l + r + 1, : depth // devices]
            dec_ref[l : l + 1, :] = short_all[8 * l + 3 : 8 * l + 4, :short]
            own = 8 * (LAYERS + l)
            vb_ref[l : l + 1, :] = mid_all[own + 4 : own + 5, :mid]
            eb_ref[l : l + 1, :] = mid_all[own + 5 : own + 6, :mid]
            rb_ref[l : l + 1, :] = rest_all[own + 4 : own + 5, :short]
            skip_ref[l : l + 1, :] = rest_all[own + 5 : own + 6, :short]
        copies[-1].wait()

    two = lambda *dims: (LAYERS,) + dims
    outs = [
        (tokens, depth), two(depth // devices), two(depth // devices), two(tall, hidden), two(units // RINGS),
        two(tall, feats), two(LANES // RINGS), two(states // devices), two(small, feats), two(small, feats),
        two(LANES // RINGS), two(small, hidden), two(units // RINGS), two(high, depth), two(depth // devices),
    ]
    return pl.pallas_call(
        kernel,
        out_shape=[jax.ShapeDtypeStruct((tokens, depth), bf16)] + [jax.ShapeDtypeStruct(s, f32) for s in outs],
        in_specs=[pl.BlockSpec(memory_space=pltpu.SMEM)] + [pl.BlockSpec(memory_space=pl.ANY)] * len(arrays),
        out_specs=[pl.BlockSpec(memory_space=VMEM)] * 16,
        scratch_shapes=[VMEM(a.shape, a.dtype) for a in arrays[:-1]] + [pltpu.SemaphoreType.DMA((len(arrays),))],
        compiler_params=pltpu.CompilerParams(vmem_limit_bytes=60 << 20),
        cost_estimate=cost(4.0),
        name="finish",
    )(me, *arrays)


def mixer(labels, signal, decays, stateinput, stateoutput, skipgain):
    rows = signal.shape[0]
    width = min(32, rows)
    count = rows // width
    mixing = stateinput * stateoutput
    offsets = jnp.arange(width, dtype=jnp.float32)
    powers = jnp.exp(-offsets[:, None] * decays[None, :])
    kernel = jnp.dot(powers, mixing, precision=highest)
    positions = jnp.arange(width, dtype=jnp.int32)
    lagged = jnp.maximum(positions[:, None] - positions[None, :], 0)
    toeplitz = jnp.take(kernel, lagged, axis=0)
    causal = positions[:, None] >= positions[None, :]
    leading = jnp.exp(-(offsets[:, None] + 1.0) * decays[None, :])
    trailing = jnp.exp(-(width - 1.0 - offsets[:, None]) * decays[None, :])
    across = jnp.exp(-width * decays)

    def advance(carry, pieces):
        state, before = carry
        block, marks = pieces
        same = jnp.logical_and(marks[:, None] == marks[None, :], causal).astype(signal.dtype)
        inner = jnp.sum(toeplitz * same[:, :, None] * block[None, :, :], axis=1)
        joined = (marks == before).astype(signal.dtype)
        carried = jnp.dot(leading, mixing * state, precision=highest) * joined[:, None]
        final = marks[width - 1]
        keep = (final == before).astype(signal.dtype)
        fresh = (marks == final).astype(signal.dtype)
        state = across[:, None] * state * keep + lax.dot_general(
            trailing * fresh[:, None], block, rows_dims, precision=highest
        )
        return ((state, final), inner + carried)

    start = (jnp.zeros(mixing.shape, signal.dtype), jnp.array(-1, jnp.int32))
    ending, mixed = lax.scan(
        jax.checkpoint(advance),
        start,
        (signal.reshape(count, width, -1), labels.reshape(count, width)),
    )
    return mixed.reshape(rows, -1) + skipgain[None, :] * signal


def normalize(rows, gain, shift):
    center = rows - jnp.mean(rows, axis=1, keepdims=True)
    spread = jnp.mean(center * center, axis=1, keepdims=True)
    return center * lax.rsqrt(spread + 1e-05) * gain + shift


def smooth(values):
    return jax.nn.gelu(values, approximate=False)


def gather_forward(shards, depth):
    return (
        lax.all_gather(shards[0][depth], ("dp", "fsdp"), axis=0, tiled=True),
        lax.all_gather(shards[1][depth], ("dp", "fsdp"), axis=0, tiled=True),
        lax.all_gather(shards[2][depth], ("dp", "fsdp"), axis=0, tiled=True),
        lax.all_gather(shards[3][depth], ("dp", "fsdp"), axis=0, tiled=True),
        lax.all_gather(shards[4][depth], ("dp", "fsdp"), axis=0, tiled=True),
        lax.all_gather(shards[5][depth], ("dp", "fsdp"), axis=0, tiled=True),
        lax.all_gather(shards[6][depth], ("dp", "fsdp"), axis=0, tiled=True),
        lax.all_gather(shards[7][depth], ("dp", "fsdp"), axis=0, tiled=True),
        lax.all_gather(shards[8][depth], ("dp", "fsdp"), axis=0, tiled=True),
        lax.all_gather(shards[9][depth], ("dp", "fsdp"), axis=0, tiled=True),
        lax.all_gather(shards[10][depth], ("dp", "fsdp"), axis=0, tiled=True),
        lax.all_gather(shards[11][depth], ("dp", "fsdp"), axis=0, tiled=True),
        lax.all_gather(shards[12][depth], ("dp", "fsdp"), axis=0, tiled=True),
        lax.all_gather(shards[13][depth], ("dp", "fsdp"), axis=0, tiled=True),
    )


def gather_backward(shards, depth):
    return (
        lax.all_gather(shards[0][depth], ("dp", "fsdp"), axis=0, tiled=True),
        lax.all_gather(shards[1][depth], ("dp", "fsdp"), axis=0, tiled=True),
        lax.all_gather(shards[2][depth], ("dp", "fsdp"), axis=0, tiled=True),
        lax.all_gather(shards[3][depth], ("dp", "fsdp"), axis=0, tiled=True),
        lax.all_gather(shards[4][depth], ("dp", "fsdp"), axis=0, tiled=True),
        lax.all_gather(shards[5][depth], ("dp", "fsdp"), axis=0, tiled=True),
        lax.all_gather(shards[6][depth], ("dp", "fsdp"), axis=0, tiled=True),
        lax.all_gather(shards[7][depth], ("dp", "fsdp"), axis=0, tiled=True),
        lax.all_gather(shards[8][depth], ("dp", "fsdp"), axis=0, tiled=True),
        lax.all_gather(shards[9][depth], ("dp", "fsdp"), axis=0, tiled=True),
        lax.all_gather(shards[10][depth], ("dp", "fsdp"), axis=0, tiled=True),
        lax.all_gather(shards[11][depth], ("dp", "fsdp"), axis=0, tiled=True),
        lax.all_gather(shards[12][depth], ("dp", "fsdp"), axis=0, tiled=True),
        lax.all_gather(shards[13][depth], ("dp", "fsdp"), axis=0, tiled=True),
    )


def scatter_layer(terms):
    return (
        lax.psum_scatter(terms[0], ("dp", "fsdp"), scatter_dimension=0, tiled=True),
        lax.psum_scatter(terms[1], ("dp", "fsdp"), scatter_dimension=0, tiled=True),
        lax.psum_scatter(terms[2], ("dp", "fsdp"), scatter_dimension=0, tiled=True),
        lax.psum_scatter(terms[3], ("dp", "fsdp"), scatter_dimension=0, tiled=True),
        lax.psum_scatter(terms[4], ("dp", "fsdp"), scatter_dimension=0, tiled=True),
        lax.psum_scatter(terms[5], ("dp", "fsdp"), scatter_dimension=0, tiled=True),
        lax.psum_scatter(terms[6], ("dp", "fsdp"), scatter_dimension=0, tiled=True),
        lax.psum_scatter(terms[7], ("dp", "fsdp"), scatter_dimension=0, tiled=True),
        lax.psum_scatter(terms[8], ("dp", "fsdp"), scatter_dimension=0, tiled=True),
        lax.psum_scatter(terms[9], ("dp", "fsdp"), scatter_dimension=0, tiled=True),
        lax.psum_scatter(terms[10], ("dp", "fsdp"), scatter_dimension=0, tiled=True),
        lax.psum_scatter(terms[11], ("dp", "fsdp"), scatter_dimension=0, tiled=True),
        lax.psum_scatter(terms[12], ("dp", "fsdp"), scatter_dimension=0, tiled=True),
        lax.psum_scatter(terms[13], ("dp", "fsdp"), scatter_dimension=0, tiled=True),
    )


def layer_forward(current, labels, flags, weights):
    (
        normgain,
        normbias,
        valueproj,
        valuebias,
        reduceproj,
        reducebias,
        decays,
        stateinput,
        stateoutput,
        skipgain,
        expandproj,
        expandbias,
        outproj,
        outbias,
    ) = weights
    normed, norm_back = jax.vjp(
        normalize, current, normgain.astype(jnp.float32), normbias.astype(jnp.float32)
    )
    normed_low = normed.astype(jnp.bfloat16)
    opened = jnp.dot(normed_low, valueproj, preferred_element_type=jnp.float32) + valuebias.astype(
        jnp.float32
    )
    values, value_back = jax.vjp(smooth, opened)
    reduced = jnp.dot(
        normed_low, reduceproj, preferred_element_type=jnp.float32
    ) + reducebias.astype(jnp.float32)
    smoothed, reduce_back = jax.vjp(smooth, reduced)
    signal = smoothed * flags
    mixed, mix_back = jax.vjp(
        partial(mixer, labels),
        signal,
        decays.astype(jnp.float32),
        stateinput.astype(jnp.float32),
        stateoutput.astype(jnp.float32),
        skipgain.astype(jnp.float32),
    )
    mixed_low = mixed.astype(jnp.bfloat16)
    expanded = jnp.dot(
        mixed_low, expandproj, preferred_element_type=jnp.float32
    ) + expandbias.astype(jnp.float32)
    gated = (expanded * values).astype(jnp.bfloat16)
    branch = jnp.dot(gated, outproj, preferred_element_type=jnp.float32) + outbias.astype(
        jnp.float32
    )
    saved = (
        normed_low,
        values,
        value_back,
        reduce_back,
        mix_back,
        mixed_low,
        expanded,
        gated,
        norm_back,
    )
    return (current + flags * branch, saved)


def layer_backward(upstream, flags, weights, saved):
    (
        normgain,
        normbias,
        valueproj,
        valuebias,
        reduceproj,
        reducebias,
        decays,
        stateinput,
        stateoutput,
        skipgain,
        expandproj,
        expandbias,
        outproj,
        outbias,
    ) = weights
    normed_low, values, value_back, reduce_back, mix_back, mixed_low, expanded, gated, norm_back = (
        saved
    )
    dout = (flags * upstream).astype(jnp.bfloat16)
    outproj_term = lax.dot_general(gated, dout, rows_dims, preferred_element_type=jnp.float32)
    outbias_term = jnp.sum(dout, axis=0, dtype=jnp.float32)
    dgated = lax.dot_general(dout, outproj, cols_dims, preferred_element_type=jnp.float32)
    dexpanded = (dgated * values).astype(jnp.bfloat16)
    dvalues = dgated * expanded
    expandproj_term = lax.dot_general(
        mixed_low, dexpanded, rows_dims, preferred_element_type=jnp.float32
    )
    expandbias_term = jnp.sum(dexpanded, axis=0, dtype=jnp.float32)
    dmixed = lax.dot_general(dexpanded, expandproj, cols_dims, preferred_element_type=jnp.float32)
    dsignal, decays_term, stateinput_term, stateoutput_term, skipgain_term = mix_back(dmixed)
    (dreduced,) = reduce_back(dsignal * flags)
    dreduced_low = dreduced.astype(jnp.bfloat16)
    (dopened,) = value_back(dvalues)
    dopened_low = dopened.astype(jnp.bfloat16)
    valueproj_term = lax.dot_general(
        normed_low, dopened_low, rows_dims, preferred_element_type=jnp.float32
    )
    valuebias_term = jnp.sum(dopened_low, axis=0, dtype=jnp.float32)
    reduceproj_term = lax.dot_general(
        normed_low, dreduced_low, rows_dims, preferred_element_type=jnp.float32
    )
    reducebias_term = jnp.sum(dreduced_low, axis=0, dtype=jnp.float32)
    dnormed = lax.dot_general(dopened_low, valueproj, cols_dims, preferred_element_type=jnp.float32)
    dnormed = dnormed + lax.dot_general(
        dreduced_low, reduceproj, cols_dims, preferred_element_type=jnp.float32
    )
    dcurrent, normgain_term, normbias_term = norm_back(dnormed)
    terms = (
        normgain_term,
        normbias_term,
        valueproj_term,
        valuebias_term,
        reduceproj_term,
        reducebias_term,
        decays_term,
        stateinput_term,
        stateoutput_term,
        skipgain_term,
        expandproj_term,
        expandbias_term,
        outproj_term,
        outbias_term,
    )
    return (upstream + dcurrent, terms)


def plain(
    inputs,
    segment_ids,
    token_mask,
    cotangent,
    normgain,
    normbias,
    valueproj,
    valuebias,
    reduceproj,
    reducebias,
    decays,
    stateinput,
    stateoutput,
    skipgain,
    expandproj,
    expandbias,
    outproj,
    outbias,
):
    shards = (
        normgain,
        normbias,
        valueproj,
        valuebias,
        reduceproj,
        reducebias,
        decays,
        stateinput,
        stateoutput,
        skipgain,
        expandproj,
        expandbias,
        outproj,
        outbias,
    )
    flags = token_mask.astype(jnp.float32)[:, None]
    current = inputs.astype(jnp.float32)
    fetched = []
    stored = []
    for depth in range(LAYERS):
        weights = gather_forward(shards, depth)
        current, saved = layer_forward(current, segment_ids, flags, weights)
        fetched.append(weights)
        stored.append(saved)
    outputs = current.astype(jnp.bfloat16)
    upstream = cotangent.astype(jnp.float32)
    scattered = [None] * LAYERS
    for depth in reversed(range(LAYERS)):
        weights = gather_backward(shards, depth)
        upstream, terms = layer_backward(upstream, flags, weights, stored[depth])
        scattered[depth] = scatter_layer(terms)
    results = tuple(
        (jnp.stack([scattered[depth][index] for depth in range(LAYERS)]) for index in range(14))
    )
    return (outputs, upstream) + tuple(results)


def fast(
    inputs, segment_ids, token_mask, cotangent, normgain, normbias, valueproj, valuebias,
    reduceproj, reducebias, decays, stateinput, stateoutput, skipgain, expandproj, expandbias,
    outproj, outbias,
):
    tokens, depth = inputs.shape
    tall = valueproj.shape[1]
    small = stateinput.shape[1]
    high = outproj.shape[1]
    units = valueproj.shape[2] // GROUP
    feats = reduceproj.shape[2]
    states = stateinput.shape[1] * GROUP * RINGS
    group = tokens * GROUP
    sizes = (tokens, depth, units, feats, states, tall, small, high)

    lined = lambda v: v.reshape(tokens // LANES, LANES)
    shorts = (normgain, normbias, outbias, decays, valuebias, reducebias, skipgain, expandbias)
    (
        last, across, later, rows, filt, mixes, auxes,
        norms, value, slope, gate, full, z, slope2, value_w, out_w, expand_w, douts,
    ) = forward_both(
        (
            inputs, lined(segment_ids), lined(token_mask), cotangent, valueproj, reduceproj, expandproj,
            outproj, stateinput, stateoutput, *shorts, *tables(GROUP * RINGS),
        ),
        sizes,
    )
    dx, mine, total, out_part, raw, arrived = backward_both(
        (
            cotangent, inputs, later, rows, filt, mixes, auxes, across,
            norms.reshape(LAYERS, group, depth), value, slope, gate, full, z, slope2,
            value_w, out_w, expand_w, douts.reshape(group, depth),
        ),
        sizes,
    )
    me = jnp.stack([lax.axis_index("dp"), lax.axis_index("fsdp")]).astype(jnp.int32)
    arrays = (raw, out_part, mine, total, last, arrived, auxes, stateinput, stateoutput, dx)
    return tuple(finish(me, arrays, sizes))


def solution(mesh):
    placed = (
        P(("dp", "fsdp"), None),
        P(("dp", "fsdp")),
        P(("dp", "fsdp")),
        P(("dp", "fsdp"), None),
        P(None, ("dp", "fsdp")),
        P(None, ("dp", "fsdp")),
        P(None, ("dp", "fsdp"), None),
        P(None, ("dp", "fsdp")),
        P(None, ("dp", "fsdp"), None),
        P(None, ("dp", "fsdp")),
        P(None, ("dp", "fsdp")),
        P(None, ("dp", "fsdp"), None),
        P(None, ("dp", "fsdp"), None),
        P(None, ("dp", "fsdp")),
        P(None, ("dp", "fsdp"), None),
        P(None, ("dp", "fsdp")),
        P(None, ("dp", "fsdp"), None),
        P(None, ("dp", "fsdp")),
    )
    small = mesh.shape["dp"] == GROUP and mesh.shape["fsdp"] == RINGS
    return jax.shard_map(
        fast if small else plain,
        mesh=mesh,
        in_specs=placed,
        out_specs=(
            P(("dp", "fsdp"), None),
            P(("dp", "fsdp"), None),
            P(None, ("dp", "fsdp")),
            P(None, ("dp", "fsdp")),
            P(None, ("dp", "fsdp"), None),
            P(None, ("dp", "fsdp")),
            P(None, ("dp", "fsdp"), None),
            P(None, ("dp", "fsdp")),
            P(None, ("dp", "fsdp")),
            P(None, ("dp", "fsdp"), None),
            P(None, ("dp", "fsdp"), None),
            P(None, ("dp", "fsdp")),
            P(None, ("dp", "fsdp"), None),
            P(None, ("dp", "fsdp")),
            P(None, ("dp", "fsdp"), None),
            P(None, ("dp", "fsdp")),
        ),
        check_vma=False,
    )
```
